32 devices in a mesh: rows: 16 (over z, x, core), cols: 2 (over y).
Axes of the slice: x: 2, y: 2, z: 4, core: 2. Of those that a mesh axis runs over, the one named last changes fastest.
Arguments:
- features: bfloat16 [49152, 256], P(('rows', 'cols')), may hold values from -6 to 6
- adj_values: bfloat16 [384, 3, 128, 128], P(('rows', 'cols')), may hold values from -0.3125 to 0.3125
- adj_offset: int32 [384, 3], P(('rows', 'cols')), may hold values from -2 to 2, as said below
- adj_count: int32 [384], P(('rows', 'cols')), may hold values from 1 to 3, as said below
- weight: bfloat16 [256, 256], replicated, may hold values from -0.375 to 0.375
- bias_vector: float32 [256], replicated, may hold values from -4 to 4
- cotangent: bfloat16 [49152, 256], P(('rows', 'cols')), may hold values from -6 to 6
Outputs:
- activated: bfloat16 [49152, 256], P(('rows', 'cols'))
- grad_features: bfloat16 [49152, 256], P(('rows', 'cols'))
- grad_weight: float32 [256, 256], replicated
- grad_bias: float32 [256], replicated
The draws below stay inside these ranges and needn't reach their ends.
Inputs may be any that keep to these rules, and one draw needn't show every extreme that they name: Slot 0 of every row block has offset 0; the offsets of one row block are distinct, and for row block i every i + adj_offset[i, s] lies in 0 to 383. Row block i uses its slots 0 to adj_count[i] - 1; the values and offsets of its other slots are ignored. In every draw all row blocks of one device, drawn from the seed, use all 3 slots.
All inputs are finite; a program needn't handle non-finite values.
Results may differ from the reference program's by a relative error of at most 0.0075.
Values may be sent and summed in bfloat16 or wider, within the bound.
No kernel may reach another device: no remote copies, remote signals or barrier semaphores. Data moves between devices by JAX's collectives and lax.ppermute only.
A program may use at most 64 MiB of HBM per device.

```python
import math
import jax
import jax.numpy as jnp
from jax import lax

F = 256
BLK = 128
BAND = 2
ROW_SLOTS = 3
BLK_DEV = 12
NBLK = 384
NODES = 49152


def draw_adj_offset(key, part):
    candidates = jnp.concatenate([jnp.arange(-BAND, 0, dtype=jnp.int32), jnp.arange(1, BAND + 1, dtype=jnp.int32)])
    row_index = jnp.arange(NBLK, dtype=jnp.int32)[:, None]
    landing = row_index + candidates[None, :]
    inside = (landing >= 0) & (landing < NBLK)
    scores = jax.random.randint(jax.random.fold_in(key, 11), (NBLK, 2 * BAND), 0, 1 << 20) * (2 * BAND)
    scores = scores + jnp.arange(2 * BAND, dtype=jnp.int32)[None, :]
    scores = scores + jnp.where(inside, 1 << 26, 0).astype(jnp.int32)
    unused_scores, chosen = lax.top_k(scores, ROW_SLOTS - 1)
    picked = candidates[chosen]
    return jnp.concatenate([jnp.zeros((NBLK, 1), jnp.int32), picked], 1).astype(jnp.int32)


def draw_adj_count(key, part):
    base_count = jax.random.randint(jax.random.fold_in(key, 21), (NBLK,), 1, ROW_SLOTS + 1)
    busiest = jax.random.randint(jax.random.fold_in(key, 22), (), 0, NBLK // BLK_DEV)
    owner = jnp.arange(NBLK, dtype=jnp.int32) // BLK_DEV
    return jnp.where(owner == busiest, ROW_SLOTS, base_count).astype(jnp.int32)


def steps_of(rng, extent, split, smallest, largest):
    loudness, own = 1.0, jax.random.fold_in(rng, 6)
    for dim, shards_of in split:
        heights = jnp.exp(jax.random.uniform(jax.random.fold_in(own, dim), (shards_of,), jnp.float32, smallest / len(split), largest / len(split)))
        loudness = loudness * jnp.repeat(heights, extent[dim] // shards_of).reshape([-1 if axis == dim else 1 for axis in range(len(extent))])
    return loudness


def gaussian(own_key, shape, scale, reach, cuts=(), kind=jnp.bfloat16):
    entries = scale * jax.random.normal(own_key, shape, jnp.float32)
    if cuts:
        entries = entries * steps_of(own_key, shape, cuts, -0.22, 0.18)
    return jnp.clip(entries, -reach, reach).astype(kind)


def setup_inputs(seed: int = 0) -> dict:
    keys = jax.random.split(jax.random.key(seed), 8)
    features = gaussian(keys[0], (NODES, F), 1.0, 6.0, ((0, 32),))
    adj_values = gaussian(keys[1], (NBLK, ROW_SLOTS, BLK, BLK), (BLK * ROW_SLOTS) ** -0.5, 0.3125, ((0, 32),))
    adj_offset = draw_adj_offset(jax.random.fold_in(keys[7], 71), 0)
    adj_count = draw_adj_count(jax.random.fold_in(keys[7], 71), 0)
    weight = gaussian(keys[4], (F, F), F ** -0.5, 0.375)
    bias_vector = gaussian(keys[5], (F,), 1.0, 4.0, (), jnp.float32)
    cotangent = gaussian(keys[6], (NODES, F), 1.0, 6.0, ((0, 32),))
    return dict(features=features, adj_values=adj_values, adj_offset=adj_offset, adj_count=adj_count, weight=weight, bias_vector=bias_vector, cotangent=cotangent)


def reference(features, adj_values, adj_offset, adj_count, weight, bias_vector, cotangent):
    group_total = NBLK // BLK_DEV
    span_blocks = BLK_DEV + 2 * BAND
    feat_blocks = features.reshape(NBLK, BLK, F)
    border = jnp.zeros((BAND, BLK, F), features.dtype)
    padded = jnp.concatenate([border, feat_blocks, border], 0)
    values_grouped = adj_values.reshape(group_total, BLK_DEV, ROW_SLOTS, BLK, BLK)
    offset_grouped = adj_offset.reshape(group_total, BLK_DEV, ROW_SLOTS)
    count_grouped = adj_count.reshape(group_total, BLK_DEV)
    slot_index = jnp.arange(ROW_SLOTS, dtype=jnp.int32)
    block_index = jnp.arange(BLK_DEV, dtype=jnp.int32)
    group_ids = jnp.arange(group_total, dtype=jnp.int32)

    def aggregate(inputs):
        group, values, offsets, counts = inputs
        window = lax.dynamic_slice_in_dim(padded, (group * BLK_DEV).astype(jnp.int32), span_blocks, 0)
        target = block_index[:, None] + BAND + offsets
        active = slot_index[None, :] < counts[:, None]
        picked = window[target]
        picked = jnp.where(active[:, :, None, None], picked, jnp.zeros_like(picked))
        return jnp.einsum('bsac,bscf->baf', values.astype(jnp.float32), picked.astype(jnp.float32))
    summed = lax.map(aggregate, (group_ids, values_grouped, offset_grouped, count_grouped))
    aggregated = summed.reshape(NODES, F).astype(jnp.bfloat16)
    preact = jnp.dot(aggregated, weight, preferred_element_type=jnp.float32) + bias_vector
    activated = jax.nn.silu(preact).astype(jnp.bfloat16)
    sigmoid_pre = jax.nn.sigmoid(preact)
    grad_pre = (cotangent.astype(jnp.float32) * sigmoid_pre * (1.0 + preact * (1.0 - sigmoid_pre))).astype(jnp.bfloat16)
    norm_scale = 1.0 / math.sqrt(NODES)
    grad_weight = jnp.dot(aggregated.T, grad_pre, preferred_element_type=jnp.float32) * norm_scale
    grad_bias = lax.optimization_barrier(jnp.sum(grad_pre.astype(jnp.float32), axis=0)) * norm_scale
    upstream = jnp.dot(grad_pre, weight.T, preferred_element_type=jnp.float32).astype(jnp.bfloat16)
    upstream_grouped = upstream.reshape(group_total, BLK_DEV, BLK, F)

    def spread(inputs):
        values, offsets, counts, grads = inputs
        target = block_index[:, None] + BAND + offsets
        active = slot_index[None, :] < counts[:, None]
        slot_terms = jnp.einsum('bsac,baf->bscf', values.astype(jnp.float32), grads.astype(jnp.float32))
        slot_terms = jnp.where(active[:, :, None, None], slot_terms, jnp.zeros_like(slot_terms))
        empty = jnp.zeros((span_blocks, BLK, F), jnp.float32)
        return empty.at[target.reshape(-1)].add(slot_terms.reshape(-1, BLK, F))

    def advance(carry, inputs):
        pending, upper_prev = carry
        extended = spread(inputs)
        lower_part = extended[:BAND]
        middle = extended[BAND:BAND + BLK_DEV]
        upper_part = extended[BAND + BLK_DEV:]
        finished = pending.at[BLK_DEV - BAND:].add(lower_part)
        pending_next = middle.at[:BAND].add(upper_prev)
        return ((pending_next, upper_part), finished)
    start_state = (jnp.zeros((BLK_DEV, BLK, F), jnp.float32), jnp.zeros((BAND, BLK, F), jnp.float32))
    (last_pending, upper_last), finished = lax.scan(advance, start_state, (values_grouped, offset_grouped, count_grouped, upstream_grouped))
    grad_blocks = jnp.concatenate([finished[1:], last_pending[None]], 0)
    grad_features = grad_blocks.reshape(NODES, F).astype(jnp.bfloat16)
    return (activated, grad_features, grad_weight, grad_bias)
```

```python
import math

import jax
import jax.numpy as jnp
from jax import lax
from jax.experimental import pallas as pl
from jax.experimental.pallas import tpu as pltpu
from jax.sharding import PartitionSpec as P

BAND = 2
AXES = ("rows", "cols")
LANES = 128


def targets(off_ref, cnt_ref, block, slots, blocks):
    dump = blocks + 2 * BAND
    return [
        jnp.where(slot < cnt_ref[block], block + BAND + off_ref[block, slot], dump)
        for slot in range(slots)
    ]


def forward_kernel(
    off_ref, cnt_ref, feat_ref, lower_ref, upper_ref, adj_ref, weight_ref, bias_ref, cot_ref,
    act_ref, upstream_ref, partial_ref,
    window, agg_all, grad_all,
):
    blocks, slots, block_rows, _ = adj_ref.shape
    width = feat_ref.shape[1]
    rim = BAND * block_rows
    rows = blocks * block_rows
    window[:rim] = lower_ref[...]
    window[rim : rim + rows] = feat_ref[...]
    window[rim + rows : 2 * rim + rows] = upper_ref[...]
    window[2 * rim + rows :] = jnp.zeros((block_rows, width), jnp.bfloat16)
    weight = weight_ref[...]
    bias = bias_ref[...]
    bias_sum = jnp.zeros((8, width), jnp.float32)
    for block in range(blocks):
        here = pl.ds(block * block_rows, block_rows)
        picked = jnp.concatenate(
            [
                window[pl.ds(pl.multiple_of(target * block_rows, block_rows), block_rows)]
                for target in targets(off_ref, cnt_ref, block, slots, blocks)
            ],
            0,
        )
        row = jnp.concatenate([adj_ref[block, slot] for slot in range(slots)], 1)
        agg = jnp.dot(row, picked, preferred_element_type=jnp.float32).astype(jnp.bfloat16)
        agg_all[here] = agg
        preact = jnp.dot(agg, weight, preferred_element_type=jnp.float32) + bias
        gate = 1.0 / (1.0 + jnp.exp(-preact))
        act_ref[here] = (preact * gate).astype(jnp.bfloat16)
        grad = cot_ref[here].astype(jnp.float32) * gate * (1.0 + preact * (1.0 - gate))
        grad = grad.astype(jnp.bfloat16)
        grad_all[here] = grad
        bias_sum = bias_sum + jnp.sum(
            grad.astype(jnp.float32).reshape(block_rows // 8, 8, width), axis=0
        )
        upstream_ref[block] = lax.dot_general(
            weight, grad, (((1,), (1,)), ((), ())), preferred_element_type=jnp.float32
        ).astype(jnp.bfloat16)
    partial = lax.dot_general(
        agg_all[...], grad_all[...], (((0,), (0,)), ((), ())), preferred_element_type=jnp.float32
    )
    partial_ref[:, :width] = partial.astype(jnp.bfloat16)
    bias_row = jnp.sum(bias_sum, axis=0, keepdims=True)
    partial_ref[:, width:] = jnp.broadcast_to(bias_row, (LANES, width)).T.astype(jnp.bfloat16)


def backward_kernel(
    off_ref, cnt_ref, adj_ref, upstream_ref, grad_ref, edge_ref, lower_ref, upper_ref, spread
):
    blocks, slots, block_rows, _ = adj_ref.shape
    spread[...] = jnp.zeros_like(spread)
    for block in range(blocks):
        row = jnp.concatenate([adj_ref[block, slot] for slot in range(slots)], 1)
        terms = jnp.dot(upstream_ref[block], row, preferred_element_type=jnp.float32)
        for slot, target in enumerate(targets(off_ref, cnt_ref, block, slots, blocks)):
            spread[target] += terms[:, slot * block_rows : (slot + 1) * block_rows]
    for block in range(BAND):
        here = pl.ds(block * block_rows, block_rows)
        lower_ref[here] = spread[block].T.astype(jnp.bfloat16)
        upper_ref[here] = spread[BAND + blocks + block].T.astype(jnp.bfloat16)
    for block in range(blocks):
        value = spread[BAND + block].T
        if block < BAND:
            edge_ref[block * block_rows : (block + 1) * block_rows] = value
        elif block >= blocks - BAND:
            place = block - blocks + 2 * BAND
            edge_ref[place * block_rows : (place + 1) * block_rows] = value
        else:
            grad_ref[block * block_rows : (block + 1) * block_rows] = value.astype(jnp.bfloat16)


def edge_kernel(whole_ref, edge_ref, spill_ref, out_ref):
    out_ref[...] = (edge_ref[...] + spill_ref[...].astype(jnp.float32)).astype(jnp.bfloat16)


def reduce_kernel(gathered_ref, spread_ref):
    count = gathered_ref.shape[0]
    total = jnp.sum(gathered_ref[...].astype(jnp.float32), axis=0).astype(jnp.bfloat16)
    spread_ref[...] = jnp.broadcast_to(total[None], (count,) + total.shape)


def neighbour(value, steps, count):
    initial, last = max(0, -steps), min(count, count - steps)
    return lax.ppermute(value, AXES, [(source, source + steps) for source in range(initial, last)])


def sum_devices(partial, count):
    rows, lanes = partial.shape
    axes = AXES
    if rows % count:
        axes = "rows"
        count = lax.axis_size("rows")
    gathered = lax.all_to_all(partial, axes, 0, 0, tiled=True).reshape(count, rows // count, lanes)
    if axes == "rows":
        share = jnp.sum(gathered.astype(jnp.float32), axis=0)
        share = lax.psum(share, "cols").astype(jnp.bfloat16)
        shares = jnp.broadcast_to(share[None], gathered.shape)
    else:
        shares = pl.pallas_call(
            reduce_kernel,
            out_shape=jax.ShapeDtypeStruct(gathered.shape, jnp.bfloat16),
            name="reduce_share",
        )(gathered)
    return lax.all_to_all(shares.reshape(rows, lanes), axes, 0, 0, tiled=True)


def on_device(features, adj_values, adj_offset, adj_count, weight, bias_vector, cotangent):
    blocks, slots = adj_offset.shape
    block_rows = adj_values.shape[2]
    rows, width = features.shape
    rim = BAND * block_rows
    count = lax.axis_size("rows") * lax.axis_size("cols")
    smem = pl.BlockSpec(memory_space=pltpu.SMEM)
    vmem = pl.BlockSpec(memory_space=pltpu.VMEM)
    params = pltpu.CompilerParams(vmem_limit_bytes=40 * 1024 * 1024)

    from_below = neighbour(features[rows - rim :], 1, count)
    from_above = neighbour(features[:rim], -1, count)
    activated, upstream, partial = pl.pallas_call(
        forward_kernel,
        out_shape=(
            jax.ShapeDtypeStruct((rows, width), jnp.bfloat16),
            jax.ShapeDtypeStruct((blocks, width, block_rows), jnp.bfloat16),
            jax.ShapeDtypeStruct((width, width + LANES), jnp.bfloat16),
        ),
        in_specs=[smem, smem] + [vmem] * 7,
        out_specs=(vmem, vmem, vmem),
        scratch_shapes=[
            pltpu.VMEM((rows + 2 * rim + block_rows, width), jnp.bfloat16),
            pltpu.VMEM((rows, width), jnp.bfloat16),
            pltpu.VMEM((rows, width), jnp.bfloat16),
        ],
        compiler_params=params,
        cost_estimate=pl.CostEstimate(
            flops=1_000_000_000, bytes_accessed=5_000_000, transcendentals=800_000
        ),
        name="layer_forward",
    )(
        adj_offset, adj_count, features, from_below, from_above, adj_values, weight,
        bias_vector.reshape(1, width), cotangent,
    )
    grad_inner, edges, lower_part, upper_part = pl.pallas_call(
        backward_kernel,
        out_shape=(
            jax.ShapeDtypeStruct((rows, width), jnp.bfloat16),
            jax.ShapeDtypeStruct((2 * rim, width), jnp.float32),
            jax.ShapeDtypeStruct((rim, width), jnp.bfloat16),
            jax.ShapeDtypeStruct((rim, width), jnp.bfloat16),
        ),
        in_specs=[smem, smem, vmem, vmem],
        out_specs=(vmem, vmem, vmem, vmem),
        scratch_shapes=[
            pltpu.VMEM((blocks + 2 * BAND + 1, width, block_rows), jnp.float32),
        ],
        compiler_params=params,
        cost_estimate=pl.CostEstimate(
            flops=400_000_000, bytes_accessed=4_000_000, transcendentals=0
        ),
        name="layer_backward",
    )(adj_offset, adj_count, adj_values, upstream)
    from_above_dev = neighbour(lower_part, -1, count)
    from_below_dev = neighbour(upper_part, 1, count)
    summed = sum_devices(partial, count)
    norm_scale = 1.0 / math.sqrt(rows * count)
    grad_weight = summed[:, :width].astype(jnp.float32) * norm_scale
    grad_bias = summed[:, width].astype(jnp.float32) * norm_scale
    last = rows // rim - 1
    spills = jnp.concatenate([from_below_dev, from_above_dev], 0)
    grad_features = pl.pallas_call(
        edge_kernel,
        grid=(2,),
        out_shape=jax.ShapeDtypeStruct((rows, width), jnp.bfloat16),
        in_specs=[
            pl.BlockSpec(memory_space=pl.ANY),
            pl.BlockSpec((rim, width), lambda step: (step, 0)),
            pl.BlockSpec((rim, width), lambda step: (step, 0)),
        ],
        out_specs=pl.BlockSpec((rim, width), lambda step: (step * last, 0)),
        input_output_aliases={0: 0},
        name="join_edges",
    )(grad_inner, edges, spills)
    return (activated, grad_features, grad_weight, grad_bias)


def solution(mesh):
    return jax.shard_map(
        on_device,
        mesh=mesh,
        in_specs=(
            P(AXES, None),
            P(AXES, None, None, None),
            P(AXES, None),
            P(AXES),
            P(),
            P(),
            P(AXES, None),
        ),
        out_specs=(P(AXES, None), P(AXES, None), P(), P()),
        check_vma=False,
    )
```

```python
import math

import jax
import jax.numpy as jnp
from jax import lax
from jax.experimental import pallas as pl
from jax.experimental.pallas import tpu as pltpu
from jax.sharding import Mesh, PartitionSpec as P

BAND = 2
AXES = ("outer", "inner", "cols")
GROUP = ("inner", "cols")
LANES = 128
MIB = 1024 * 1024


def row_of(adj_ref, block, slots):
    return jnp.concatenate([adj_ref[block, slot] for slot in range(slots)], 1)


def pick(source, places, block_rows):
    return jnp.concatenate(
        [
            source[pl.ds(pl.multiple_of(place * block_rows, block_rows), block_rows)]
            for place in places
        ],
        0,
    )


def places_of(off_ref, cnt_ref, block, shift, dump, slots):
    return [
        jnp.where(slot < cnt_ref[block], block + shift + off_ref[slot, block], dump)
        for slot in range(slots)
    ]


def activate(preact, cotangent):
    gate = 1.0 / (1.0 + jnp.exp(-preact))
    grad = cotangent.astype(jnp.float32) * gate * (1.0 + preact * (1.0 - gate))
    return (preact * gate).astype(jnp.bfloat16), grad.astype(jnp.bfloat16)


def column_sums(grad):
    rows, width = grad.shape
    return jnp.sum(grad.astype(jnp.float32).reshape(rows // 8, 8, width), axis=0)


def to_upstream(weight, grad):
    return lax.dot_general(
        weight, grad, (((1,), (1,)), ((), ())), preferred_element_type=jnp.float32
    ).astype(jnp.bfloat16)


def weight_terms(agg, grad):
    return lax.dot_general(
        agg, grad, (((0,), (0,)), ((), ())), preferred_element_type=jnp.float32
    )


def inner_kernel(
    off_ref, cnt_ref, weight_hbm, bias_hbm, feat_hbm, adj_hbm, cot_hbm,
    act_hbm, grad_hbm, spread, partial_ref, sums_ref, weight_ref, bias_ref, feat_rim, adj_rim,
    cot_rim,
    feat, adj, cot, act, out, agg_all, grad_all, sems,
):
    blocks, slots, block_rows, _ = adj_hbm.shape
    rows, width = feat_hbm.shape
    count = blocks - 2 * BAND
    rim = BAND * block_rows
    half = 2 * rim
    inner = count * block_rows
    copies = [
        pltpu.make_async_copy(feat_hbm, feat.at[pl.ds(0, rows)], sems.at[0]),
        pltpu.make_async_copy(adj_hbm.at[pl.ds(BAND, count)], adj, sems.at[1]),
        pltpu.make_async_copy(weight_hbm, weight_ref, sems.at[11]),
        pltpu.make_async_copy(bias_hbm, bias_ref, sems.at[12]),
        pltpu.make_async_copy(cot_hbm.at[pl.ds(rim, inner)], cot, sems.at[2]),
        pltpu.make_async_copy(feat_hbm.at[pl.ds(0, half)], feat_rim.at[pl.ds(0, half)], sems.at[3]),
        pltpu.make_async_copy(
            feat_hbm.at[pl.ds(rows - half, half)], feat_rim.at[pl.ds(half, half)], sems.at[4]
        ),
        pltpu.make_async_copy(adj_hbm.at[pl.ds(0, BAND)], adj_rim.at[pl.ds(0, BAND)], sems.at[5]),
        pltpu.make_async_copy(
            adj_hbm.at[pl.ds(blocks - BAND, BAND)], adj_rim.at[pl.ds(BAND, BAND)], sems.at[6]
        ),
        pltpu.make_async_copy(cot_hbm.at[pl.ds(0, rim)], cot_rim.at[pl.ds(0, rim)], sems.at[7]),
        pltpu.make_async_copy(
            cot_hbm.at[pl.ds(rows - rim, rim)], cot_rim.at[pl.ds(rim, rim)], sems.at[8]
        ),
    ]
    for copy in copies:
        copy.start()
    feat[rows:] = jnp.zeros((block_rows, width), jnp.bfloat16)
    spread[...] = jnp.zeros_like(spread)
    for copy in copies[:5]:
        copy.wait()
    weight = weight_ref[...]
    bias = bias_ref[...]
    sums = jnp.zeros((8, width), jnp.float32)
    for step in range(count):
        here = pl.ds(step * block_rows, block_rows)
        places = places_of(off_ref, cnt_ref, step + BAND, 0, blocks, slots)
        row = row_of(adj, step, slots)
        agg = jnp.dot(row, pick(feat, places, block_rows), preferred_element_type=jnp.float32)
        agg = agg.astype(jnp.bfloat16)
        agg_all[here] = agg
        preact = jnp.dot(agg, weight, preferred_element_type=jnp.float32) + bias
        act[here], grad = activate(preact, cot[here])
        grad_all[here] = grad
        sums = sums + column_sums(grad)
        terms = jnp.dot(to_upstream(weight, grad), row, preferred_element_type=jnp.float32)
        for slot, place in enumerate(places):
            spread[place] += terms[:, slot * block_rows : (slot + 1) * block_rows]
    act_out = pltpu.make_async_copy(act, act_hbm.at[pl.ds(rim, inner)], sems.at[9])
    act_out.start()
    done = blocks - 4 * BAND
    for step in range(done):
        here = pl.ds(step * block_rows, block_rows)
        out[here] = spread[2 * BAND + step].T.astype(jnp.bfloat16)
    grad_out = pltpu.make_async_copy(
        out, grad_hbm.at[pl.ds(half, done * block_rows)], sems.at[10]
    )
    grad_out.start()
    sums_ref[...] = sums
    partial_ref[...] = weight_terms(agg_all[...], grad_all[...])
    for copy in copies[5:]:
        copy.wait()
    act_out.wait()
    grad_out.wait()


def rim_places(off_ref, cnt_ref, step, blocks, slots):
    if step < BAND:
        return places_of(off_ref, cnt_ref, step, BAND, 6 * BAND, slots)
    block = blocks - 2 * BAND + step
    return places_of(off_ref, cnt_ref, block, 5 * BAND - blocks, 6 * BAND, slots)


def rim_kernel(
    off_ref, cnt_ref, weight_ref, bias_ref, feat_ref, lower_ref, upper_ref, adj_ref, cot_ref,
    partial_ref, sums_ref,
    act_ref, grad_ref, payload_ref,
    window, agg_all,
):
    blocks = off_ref.shape[1]
    steps, slots, block_rows, _ = adj_ref.shape
    width = feat_ref.shape[1]
    rim = BAND * block_rows
    window[:rim] = lower_ref[...]
    window[rim : 5 * rim] = feat_ref[...]
    window[5 * rim : 6 * rim] = upper_ref[...]
    window[6 * rim :] = jnp.zeros((block_rows, width), jnp.bfloat16)
    weight = weight_ref[...]
    bias = bias_ref[...]
    sums = sums_ref[...]
    for step in range(steps):
        here = pl.ds(step * block_rows, block_rows)
        places = rim_places(off_ref, cnt_ref, step, blocks, slots)
        agg = jnp.dot(
            row_of(adj_ref, step, slots), pick(window, places, block_rows),
            preferred_element_type=jnp.float32,
        ).astype(jnp.bfloat16)
        agg_all[here] = agg
        preact = jnp.dot(agg, weight, preferred_element_type=jnp.float32) + bias
        act_ref[here], grad = activate(preact, cot_ref[here])
        grad_ref[here] = grad
        sums = sums + column_sums(grad)
    partial = partial_ref[...] + weight_terms(agg_all[...], grad_ref[...])
    payload_ref[:, :width] = partial.astype(jnp.bfloat16)
    sum_row = jnp.sum(sums, axis=0, keepdims=True)
    payload_ref[:, width:] = jnp.broadcast_to(sum_row, (LANES, width)).T.astype(jnp.bfloat16)


def rim_back_kernel(
    off_ref, cnt_ref, weight_ref, adj_ref, grad_ref, act_ref, inner_ref, act_in, whole_in,
    act_hbm, whole_hbm, edge_ref, lower_ref, upper_ref,
    spread, out, sems,
):
    blocks = off_ref.shape[1]
    steps, slots, block_rows, _ = adj_ref.shape
    rim = BAND * block_rows
    rows = blocks * block_rows
    copies = [
        pltpu.make_async_copy(act_ref.at[pl.ds(0, rim)], act_hbm.at[pl.ds(0, rim)], sems.at[0]),
        pltpu.make_async_copy(
            act_ref.at[pl.ds(rim, rim)], act_hbm.at[pl.ds(rows - rim, rim)], sems.at[1]
        ),
    ]
    for copy in copies:
        copy.start()
    zero = jnp.zeros((BAND,) + spread.shape[1:], jnp.float32)
    spread[:BAND] = zero
    spread[BAND : 3 * BAND] = inner_ref[: 2 * BAND]
    spread[3 * BAND : 5 * BAND] = inner_ref[blocks - 2 * BAND : blocks]
    spread[5 * BAND : 6 * BAND] = zero
    weight = weight_ref[...]
    for step in range(steps):
        here = pl.ds(step * block_rows, block_rows)
        places = rim_places(off_ref, cnt_ref, step, blocks, slots)
        terms = jnp.dot(
            to_upstream(weight, grad_ref[here]), row_of(adj_ref, step, slots),
            preferred_element_type=jnp.float32,
        )
        for slot, place in enumerate(places):
            spread[place] += terms[:, slot * block_rows : (slot + 1) * block_rows]
    for block in range(BAND):
        here = pl.ds(block * block_rows, block_rows)
        after = pl.ds(rim + block * block_rows, block_rows)
        lower_ref[here] = spread[block].T.astype(jnp.bfloat16)
        upper_ref[here] = spread[5 * BAND + block].T.astype(jnp.bfloat16)
        edge_ref[here] = spread[BAND + block].T
        edge_ref[after] = spread[4 * BAND + block].T
        out[here] = spread[2 * BAND + block].T.astype(jnp.bfloat16)
        out[after] = spread[3 * BAND + block].T.astype(jnp.bfloat16)
    finals = [
        pltpu.make_async_copy(out.at[pl.ds(0, rim)], whole_hbm.at[pl.ds(rim, rim)], sems.at[2]),
        pltpu.make_async_copy(
            out.at[pl.ds(rim, rim)], whole_hbm.at[pl.ds(rows - 2 * rim, rim)], sems.at[3]
        ),
    ]
    for copy in finals:
        copy.start()
    for copy in copies + finals:
        copy.wait()


def share_kernel(gathered_ref, spread_ref):
    total = jnp.sum(gathered_ref[...].astype(jnp.float32), axis=0).astype(jnp.bfloat16)
    spread_ref[...] = jnp.broadcast_to(total[None], spread_ref.shape)


def last_kernel(
    scale, summed_ref, edge_ref, below_ref, above_ref, whole_in,
    weight_out, bias_out, whole_hbm, out, sems,
):
    width = weight_out.shape[1]
    rim = below_ref.shape[0]
    rows = whole_hbm.shape[0]
    out[:rim] = (edge_ref[:rim] + below_ref[...].astype(jnp.float32)).astype(jnp.bfloat16)
    out[rim:] = (edge_ref[rim:] + above_ref[...].astype(jnp.float32)).astype(jnp.bfloat16)
    copies = [
        pltpu.make_async_copy(out.at[pl.ds(0, rim)], whole_hbm.at[pl.ds(0, rim)], sems.at[0]),
        pltpu.make_async_copy(
            out.at[pl.ds(rim, rim)], whole_hbm.at[pl.ds(rows - rim, rim)], sems.at[1]
        ),
    ]
    for copy in copies:
        copy.start()
    weight_out[...] = summed_ref[:, :width].astype(jnp.float32) * scale
    bias_out[...] = summed_ref[:, width:].astype(jnp.float32).T[:1] * scale
    for copy in copies:
        copy.wait()


def neighbour(value, steps, count):
    initial, last = max(0, -steps), min(count, count - steps)
    return lax.ppermute(value, AXES, [(source, source + steps) for source in range(initial, last)])


def add_up(gathered, copies):
    return pl.pallas_call(
        share_kernel,
        out_shape=jax.ShapeDtypeStruct((copies,) + gathered.shape[1:], jnp.bfloat16),
        compiler_params=pltpu.CompilerParams(vmem_limit_bytes=4 * MIB),
        cost_estimate=pl.CostEstimate(
            flops=gathered.size, bytes_accessed=4 * gathered.size, transcendentals=0
        ),
        name="add_up",
    )(gathered)


def sum_devices(payload):
    rows, lanes = payload.shape
    group = lax.axis_size("inner") * lax.axis_size("cols")
    outer = lax.axis_size("outer")
    parts = lax.all_to_all(payload, GROUP, 0, 0, tiled=True).reshape(group, rows // group, lanes)
    shares = add_up(parts, outer).reshape(outer * (rows // group), lanes)
    shares = lax.all_to_all(shares, "outer", 0, 0, tiled=True).reshape(outer, rows // group, lanes)
    return lax.all_to_all(add_up(shares, group).reshape(rows, lanes), GROUP, 0, 0, tiled=True)


def on_device(features, adj_values, adj_offset, adj_count, weight, bias_vector, cotangent):
    blocks, slots = adj_offset.shape
    block_rows = adj_values.shape[2]
    rows, width = features.shape
    rim = BAND * block_rows
    inner = rows - 2 * rim
    count = lax.axis_size("outer") * lax.axis_size("inner") * lax.axis_size("cols")
    smem = pl.BlockSpec(memory_space=pltpu.SMEM)
    vmem = pl.BlockSpec(memory_space=pltpu.VMEM)
    hbm = pl.BlockSpec(memory_space=pltpu.HBM)
    bias_row = bias_vector.reshape(1, width)

    def in_hbm(value):
        return pltpu.with_memory_space_constraint(value, pltpu.HBM)

    def shape(*sizes, dtype=jnp.bfloat16):
        return jax.ShapeDtypeStruct(sizes, dtype)

    def params(mib):
        return pltpu.CompilerParams(vmem_limit_bytes=mib * MIB)

    def cost(share):
        return pl.CostEstimate(
            flops=int(1.2e9 * share), bytes_accessed=int(6e6 * share),
            transcendentals=int(8e5 * share),
        )

    offsets = in_hbm(adj_offset.T)
    counts = in_hbm(adj_count)
    from_below = neighbour(features[rows - rim :], 1, count)
    from_above = neighbour(features[:rim], -1, count)
    (
        activated, grad_whole, spread, partial, sums, weight_near, bias_near, feat_rim, adj_rim,
        cot_rim,
    ) = pl.pallas_call(
        inner_kernel,
        out_shape=(
            shape(rows, width),
            shape(rows, width),
            shape(blocks + 1, width, block_rows, dtype=jnp.float32),
            shape(width, width, dtype=jnp.float32),
            shape(8, width, dtype=jnp.float32),
            shape(width, width),
            shape(1, width, dtype=jnp.float32),
            shape(4 * rim, width),
            shape(2 * BAND, slots, block_rows, block_rows),
            shape(2 * rim, width),
        ),
        in_specs=[smem, smem] + [hbm] * 5,
        out_specs=(hbm, hbm) + (vmem,) * 8,
        scratch_shapes=[
            pltpu.VMEM((rows + block_rows, width), jnp.bfloat16),
            pltpu.VMEM((blocks - 2 * BAND, slots, block_rows, block_rows), jnp.bfloat16),
            pltpu.VMEM((inner, width), jnp.bfloat16),
            pltpu.VMEM((inner, width), jnp.bfloat16),
            pltpu.VMEM((rows - 4 * rim, width), jnp.bfloat16),
            pltpu.VMEM((inner, width), jnp.bfloat16),
            pltpu.VMEM((inner, width), jnp.bfloat16),
            pltpu.SemaphoreType.DMA((13,)),
        ],
        compiler_params=params(20),
        cost_estimate=cost(0.7),
        name="inner_rows",
    )(
        offsets, counts,
        *(in_hbm(x) for x in (weight, bias_row, features, adj_values, cotangent)),
    )
    act_rim, grad_rim, payload = pl.pallas_call(
        rim_kernel,
        out_shape=(shape(2 * rim, width), shape(2 * rim, width), shape(width, width + LANES)),
        in_specs=[smem, smem] + [vmem] * 9,
        out_specs=(vmem,) * 3,
        scratch_shapes=[
            pltpu.VMEM((6 * rim + block_rows, width), jnp.bfloat16),
            pltpu.VMEM((2 * rim, width), jnp.bfloat16),
        ],
        compiler_params=params(12),
        cost_estimate=cost(0.15),
        name="rim_rows",
    )(
        offsets, counts, weight_near, bias_near, feat_rim, from_below, from_above, adj_rim,
        cot_rim, partial, sums,
    )
    activated, grad_whole, edges, lower_part, upper_part = pl.pallas_call(
        rim_back_kernel,
        out_shape=(
            shape(rows, width),
            shape(rows, width),
            shape(2 * rim, width, dtype=jnp.float32),
            shape(rim, width),
            shape(rim, width),
        ),
        in_specs=[smem, smem] + [vmem] * 5 + [hbm, hbm],
        out_specs=(hbm, hbm, vmem, vmem, vmem),
        scratch_shapes=[
            pltpu.VMEM((6 * BAND + 1, width, block_rows), jnp.float32),
            pltpu.VMEM((2 * rim, width), jnp.bfloat16),
            pltpu.SemaphoreType.DMA((4,)),
        ],
        input_output_aliases={7: 0, 8: 1},
        compiler_params=params(12),
        cost_estimate=cost(0.15),
        name="rim_rows_back",
    )(
        offsets, counts, weight_near, adj_rim, grad_rim, act_rim, spread, activated, grad_whole
    )
    from_above_dev = neighbour(lower_part, -1, count)
    from_below_dev = neighbour(upper_part, 1, count)
    summed = sum_devices(payload)
    norm_scale = 1.0 / math.sqrt(rows * count)
    grad_weight, grad_bias, grad_features = pl.pallas_call(
        lambda *refs: last_kernel(norm_scale, *refs),
        out_shape=(
            shape(width, width, dtype=jnp.float32),
            shape(1, width, dtype=jnp.float32),
            shape(rows, width),
        ),
        in_specs=[vmem] * 4 + [hbm],
        out_specs=(vmem, vmem, hbm),
        scratch_shapes=[
            pltpu.VMEM((2 * rim, width), jnp.bfloat16),
            pltpu.SemaphoreType.DMA((2,)),
        ],
        input_output_aliases={4: 2},
        compiler_params=params(8),
        name="last_step",
    )(summed, edges, from_below_dev, from_above_dev, grad_whole)
    return (activated, grad_features, grad_weight, grad_bias.reshape(width))


def solution(mesh):
    rows, cols = mesh.devices.shape
    inner = math.gcd(rows, 4)
    parts = Mesh(mesh.devices.reshape(rows // inner, inner, cols), AXES)
    return jax.shard_map(
        on_device,
        mesh=parts,
        in_specs=(
            P(AXES, None),
            P(AXES, None, None, None),
            P(AXES, None),
            P(AXES),
            P(),
            P(),
            P(AXES, None),
        ),
        out_specs=(P(AXES, None), P(AXES, None), P(), P()),
        check_vma=False,
    )
```

```python
import math

import jax
import jax.numpy as jnp
from jax import lax
from jax.experimental import pallas as pl
from jax.experimental.pallas import tpu as pltpu
from jax.sharding import PartitionSpec as P

BAND = 2
TAIL = 16
AXES = ("rows", "cols")
MIB = 1024 * 1024


def row_of(adj_ref, block, slots):
    return jnp.concatenate([adj_ref[block, slot] for slot in range(slots)], 1)


def pick(source, places, block_rows):
    return jnp.concatenate(
        [
            source[pl.ds(pl.multiple_of(place * block_rows, block_rows), block_rows)]
            for place in places
        ],
        0,
    )


def places_of(off_ref, cnt_ref, block, shift, dump, slots):
    return [
        jnp.where(slot < cnt_ref[block], block + shift + off_ref[slot, block], dump)
        for slot in range(slots)
    ]


def activate(preact, cotangent):
    gate = 1.0 / (1.0 + jnp.exp(-preact))
    grad = cotangent.astype(jnp.float32) * gate * (1.0 + preact * (1.0 - gate))
    return (preact * gate).astype(jnp.bfloat16), grad.astype(jnp.bfloat16)


def column_sums(grad):
    rows, width = grad.shape
    return jnp.sum(grad.astype(jnp.float32).reshape(rows // 8, 8, width), axis=0)


def to_upstream(weight, grad):
    return lax.dot_general(
        weight, grad, (((1,), (1,)), ((), ())), preferred_element_type=jnp.float32
    ).astype(jnp.bfloat16)


def weight_terms(agg, grad):
    return lax.dot_general(
        agg, grad, (((0,), (0,)), ((), ())), preferred_element_type=jnp.float32
    )


def inner_kernel(
    off_ref, cnt_ref, weight_hbm, bias_hbm, feat_hbm, adj_hbm, cot_hbm,
    act_hbm, grad_ref, partial_ref, sums_ref, weight_ref, bias_ref, feat_rim, adj_rim, cot_rim,
    feat, adj, cot, act, agg_all, sems,
):
    blocks, slots, block_rows, _ = adj_hbm.shape
    rows, width = feat_hbm.shape
    count = blocks - 2 * BAND
    rim = BAND * block_rows
    half = 2 * rim
    inner = count * block_rows
    copies = [
        pltpu.make_async_copy(feat_hbm, feat.at[pl.ds(0, rows)], sems.at[0]),
        pltpu.make_async_copy(adj_hbm.at[pl.ds(BAND, count)], adj, sems.at[1]),
        pltpu.make_async_copy(weight_hbm, weight_ref, sems.at[2]),
        pltpu.make_async_copy(bias_hbm, bias_ref, sems.at[3]),
        pltpu.make_async_copy(cot_hbm.at[pl.ds(rim, inner)], cot, sems.at[4]),
        pltpu.make_async_copy(feat_hbm.at[pl.ds(0, half)], feat_rim.at[pl.ds(0, half)], sems.at[5]),
        pltpu.make_async_copy(
            feat_hbm.at[pl.ds(rows - half, half)], feat_rim.at[pl.ds(half, half)], sems.at[6]
        ),
        pltpu.make_async_copy(adj_hbm.at[pl.ds(0, BAND)], adj_rim.at[pl.ds(0, BAND)], sems.at[7]),
        pltpu.make_async_copy(
            adj_hbm.at[pl.ds(blocks - BAND, BAND)], adj_rim.at[pl.ds(BAND, BAND)], sems.at[8]
        ),
        pltpu.make_async_copy(cot_hbm.at[pl.ds(0, rim)], cot_rim.at[pl.ds(0, rim)], sems.at[9]),
        pltpu.make_async_copy(
            cot_hbm.at[pl.ds(rows - rim, rim)], cot_rim.at[pl.ds(rim, rim)], sems.at[10]
        ),
    ]
    for copy in copies:
        copy.start()
    feat[rows:] = jnp.zeros((block_rows, width), jnp.bfloat16)
    for copy in copies[:5]:
        copy.wait()
    weight = weight_ref[...]
    bias = bias_ref[...]
    sums = jnp.zeros((8, width), jnp.float32)
    for step in range(0, count, 2):
        for block in (step, step + 1):
            places = places_of(off_ref, cnt_ref, block + BAND, 0, blocks, slots)
            agg_all[block * block_rows : (block + 1) * block_rows] = jnp.dot(
                row_of(adj, block, slots), pick(feat, places, block_rows),
                preferred_element_type=jnp.float32,
            ).astype(jnp.bfloat16)
        here = pl.ds(step * block_rows, 2 * block_rows)
        preact = jnp.dot(agg_all[here], weight, preferred_element_type=jnp.float32) + bias
        act[here], grad = activate(preact, cot[here])
        grad_ref[here] = grad
        sums = sums + column_sums(grad)
    act_out = pltpu.make_async_copy(act, act_hbm.at[pl.ds(rim, inner)], sems.at[11])
    act_out.start()
    sums_ref[...] = sums
    partial_ref[...] = weight_terms(agg_all[...], grad_ref[...])
    for copy in copies[5:]:
        copy.wait()
    act_out.wait()


def rim_places(off_ref, cnt_ref, step, blocks, slots):
    if step < BAND:
        return places_of(off_ref, cnt_ref, step, BAND, 6 * BAND, slots)
    block = blocks - 2 * BAND + step
    return places_of(off_ref, cnt_ref, block, 5 * BAND - blocks, 6 * BAND, slots)


def rim_kernel(
    off_ref, cnt_ref, side_ref, weight_ref, bias_ref, feat_ref, lower_ref, upper_ref, adj_ref,
    cot_ref, partial_ref, sums_ref,
    act_ref, grad_ref, send_ref, keep_ref,
    window, agg_all, payload,
):
    blocks = off_ref.shape[1]
    steps, slots, block_rows, _ = adj_ref.shape
    width = feat_ref.shape[1]
    rim = BAND * block_rows
    window[:rim] = lower_ref[...]
    window[rim : 5 * rim] = feat_ref[...]
    window[5 * rim : 6 * rim] = upper_ref[...]
    window[6 * rim :] = jnp.zeros((block_rows, width), jnp.bfloat16)
    weight = weight_ref[...]
    bias = bias_ref[...]
    sums = sums_ref[...]
    for step in range(0, steps, 2):
        for block in (step, step + 1):
            places = rim_places(off_ref, cnt_ref, block, blocks, slots)
            agg_all[block * block_rows : (block + 1) * block_rows] = jnp.dot(
                row_of(adj_ref, block, slots), pick(window, places, block_rows),
                preferred_element_type=jnp.float32,
            ).astype(jnp.bfloat16)
        here = pl.ds(step * block_rows, 2 * block_rows)
        preact = jnp.dot(agg_all[here], weight, preferred_element_type=jnp.float32) + bias
        act_ref[here], grad = activate(preact, cot_ref[here])
        grad_ref[here] = grad
        sums = sums + column_sums(grad)
    half = width // 2
    partial = partial_ref[...] + weight_terms(agg_all[...], grad_ref[...])
    payload[0, :half] = partial[:half]
    payload[1, :half] = partial[half:]
    tail = jnp.zeros((TAIL, width), jnp.float32)
    payload[0, half:] = jnp.broadcast_to(jnp.sum(sums, axis=0, keepdims=True), tail.shape)
    payload[1, half:] = tail
    side = side_ref[0]
    keep_ref[...] = payload[side]
    send_ref[...] = payload[1 - side]


def rim_back_kernel(
    off_ref, cnt_ref, weight_ref, adj_ref, grad_ref, act_ref, act_in,
    act_hbm, spread, lower_ref, upper_ref, mark_ref,
    sems,
):
    blocks = off_ref.shape[1]
    steps, slots, block_rows, _ = adj_ref.shape
    rim = BAND * block_rows
    rows = blocks * block_rows
    copies = [
        pltpu.make_async_copy(act_ref.at[pl.ds(0, rim)], act_hbm.at[pl.ds(0, rim)], sems.at[0]),
        pltpu.make_async_copy(
            act_ref.at[pl.ds(rim, rim)], act_hbm.at[pl.ds(rows - rim, rim)], sems.at[1]
        ),
    ]
    for copy in copies:
        copy.start()
    spread[...] = jnp.zeros_like(spread)
    weight = weight_ref[...]
    for step in range(steps):
        here = pl.ds(step * block_rows, block_rows)
        places = rim_places(off_ref, cnt_ref, step, blocks, slots)
        terms = jnp.dot(
            to_upstream(weight, grad_ref[here]), row_of(adj_ref, step, slots),
            preferred_element_type=jnp.float32,
        )
        for slot, place in enumerate(places):
            spread[place] += terms[:, slot * block_rows : (slot + 1) * block_rows]
    for block in range(BAND):
        here = pl.ds(block * block_rows, block_rows)
        lower_ref[here] = spread[block].T.astype(jnp.bfloat16)
        upper_ref[here] = spread[5 * BAND + block].T.astype(jnp.bfloat16)
    mark_ref[...] = jnp.zeros_like(mark_ref)
    for copy in copies:
        copy.wait()


def inner_back_kernel(
    off_ref, cnt_ref, weight_ref, adj_hbm, grad_ref, rim_spread,
    whole_hbm, edge_ref, mark_ref,
    adj, spread, out, sems,
):
    blocks, slots, block_rows, _ = adj_hbm.shape
    count = blocks - 2 * BAND
    rim = BAND * block_rows
    fetch = pltpu.make_async_copy(adj_hbm.at[pl.ds(BAND, count)], adj, sems.at[0])
    fetch.start()
    spread[: 2 * BAND] = rim_spread[BAND : 3 * BAND]
    spread[2 * BAND :] = jnp.zeros_like(spread[2 * BAND :])
    spread[blocks - 2 * BAND : blocks] = rim_spread[3 * BAND : 5 * BAND]
    weight = weight_ref[...]
    fetch.wait()
    for step in range(count):
        here = pl.ds(step * block_rows, block_rows)
        places = places_of(off_ref, cnt_ref, step + BAND, 0, blocks, slots)
        terms = jnp.dot(
            to_upstream(weight, grad_ref[here]), row_of(adj, step, slots),
            preferred_element_type=jnp.float32,
        )
        for slot, place in enumerate(places):
            spread[place] += terms[:, slot * block_rows : (slot + 1) * block_rows]
    for step in range(count):
        here = pl.ds(step * block_rows, block_rows)
        out[here] = spread[BAND + step].T.astype(jnp.bfloat16)
    finish = pltpu.make_async_copy(out, whole_hbm.at[pl.ds(rim, count * block_rows)], sems.at[1])
    finish.start()
    mark_ref[...] = jnp.zeros_like(mark_ref)
    for block in range(BAND):
        edge_ref[block * block_rows : (block + 1) * block_rows] = spread[block].T
        after = BAND + block
        edge_ref[after * block_rows : (after + 1) * block_rows] = spread[blocks - BAND + block].T
    finish.wait()


def edge_kernel(edge_ref, below_ref, above_ref, whole_in, whole_hbm, mark_ref, out, sems):
    rim = below_ref.shape[0]
    rows = whole_hbm.shape[0]
    out[:rim] = (edge_ref[:rim] + below_ref[...].astype(jnp.float32)).astype(jnp.bfloat16)
    out[rim:] = (edge_ref[rim:] + above_ref[...].astype(jnp.float32)).astype(jnp.bfloat16)
    copies = [
        pltpu.make_async_copy(out.at[pl.ds(0, rim)], whole_hbm.at[pl.ds(0, rim)], sems.at[0]),
        pltpu.make_async_copy(
            out.at[pl.ds(rim, rim)], whole_hbm.at[pl.ds(rows - rim, rim)], sems.at[1]
        ),
    ]
    for copy in copies:
        copy.start()
    mark_ref[...] = jnp.zeros_like(mark_ref)
    for copy in copies:
        copy.wait()


def add_kernel(left_ref, right_ref, *rest):
    total_ref = rest[-1]
    total = left_ref[...].astype(jnp.float32) + right_ref[...].astype(jnp.float32)
    total_ref[...] = total.astype(total_ref.dtype)


def last_kernel(scale, side_ref, own_ref, other_ref, weight_out, bias_out):
    half = weight_out.shape[0] // 2
    side = side_ref[0]
    own_rows = pl.ds(pl.multiple_of(side * half, half), half)
    other_rows = pl.ds(pl.multiple_of((1 - side) * half, half), half)
    weight_out[own_rows] = own_ref[:half] * scale
    weight_out[other_rows] = other_ref[:half] * scale
    first = jnp.where(side == 0, own_ref[half : half + 1], other_ref[half : half + 1])
    bias_out[...] = first * scale


def neighbour(value, steps, count):
    initial, last = max(0, -steps), min(count, count - steps)
    return lax.ppermute(value, AXES, [(source, source + steps) for source in range(initial, last)])


def add(left, right, dtype, after=()):
    return pl.pallas_call(
        add_kernel,
        out_shape=jax.ShapeDtypeStruct(left.shape, dtype),
        in_specs=[pl.BlockSpec(memory_space=pltpu.VMEM)] * 2
        + [pl.BlockSpec(memory_space=pl.ANY)] * len(after),
        compiler_params=pltpu.CompilerParams(vmem_limit_bytes=2 * MIB),
        cost_estimate=pl.CostEstimate(
            flops=left.size, bytes_accessed=6 * left.size, transcendentals=0
        ),
        name="add_halves",
    )(left, right, *after)


def swap(value, bits):
    return lax.ppermute(value, AXES, [(i, i ^ (1 << bit)) for i, bit in enumerate(bits)])


def sum_halves(send, keep, count, core_bit, marks):
    others = [bit for bit in range(count.bit_length() - 1) if bit != core_bit]
    orders = (others, others[::-1])
    total = add(keep, swap(send, [core_bit] * count), jnp.bfloat16, marks.get(0, ()))
    for step in range(len(others)):
        bits = [orders[(i >> core_bit) & 1][step] for i in range(count)]
        last = step == len(others) - 1
        dtype = jnp.float32 if last else jnp.bfloat16
        total = add(total, swap(total, bits), dtype, marks.get(-1 if last else step + 1, ()))
    return total


def on_device(features, adj_values, adj_offset, adj_count, weight, bias_vector, cotangent):
    blocks, slots = adj_offset.shape
    block_rows = adj_values.shape[2]
    rows, width = features.shape
    rim = BAND * block_rows
    inner = rows - 2 * rim
    cols = lax.axis_size("cols")
    count = lax.axis_size("rows") * cols
    smem = pl.BlockSpec(memory_space=pltpu.SMEM)
    vmem = pl.BlockSpec(memory_space=pltpu.VMEM)
    hbm = pl.BlockSpec(memory_space=pltpu.HBM)
    bias_row = bias_vector.reshape(1, width)

    def in_hbm(value):
        return pltpu.with_memory_space_constraint(value, pltpu.HBM)

    def shape(*sizes, dtype=jnp.bfloat16):
        return jax.ShapeDtypeStruct(sizes, dtype)

    def params(mib):
        return pltpu.CompilerParams(vmem_limit_bytes=mib * MIB)

    def cost(share):
        return pl.CostEstimate(
            flops=int(1.2e9 * share), bytes_accessed=int(6e6 * share),
            transcendentals=int(8e5 * share),
        )

    offsets = in_hbm(adj_offset.T)
    counts = in_hbm(adj_count)
    core_bit = cols.bit_length() - 1
    side = (lax.axis_index("rows") & 1).reshape(1)
    from_below = neighbour(features[rows - rim :], 1, count)
    from_above = neighbour(features[:rim], -1, count)
    (
        activated, grad_inner, partial, sums, weight_near, bias_near, feat_rim, adj_rim, cot_rim,
    ) = pl.pallas_call(
        inner_kernel,
        out_shape=(
            shape(rows, width),
            shape(inner, width),
            shape(width, width, dtype=jnp.float32),
            shape(8, width, dtype=jnp.float32),
            shape(width, width),
            shape(1, width, dtype=jnp.float32),
            shape(4 * rim, width),
            shape(2 * BAND, slots, block_rows, block_rows),
            shape(2 * rim, width),
        ),
        in_specs=[smem, smem] + [hbm] * 5,
        out_specs=(hbm,) + (vmem,) * 8,
        scratch_shapes=[
            pltpu.VMEM((rows + block_rows, width), jnp.bfloat16),
            pltpu.VMEM((blocks - 2 * BAND, slots, block_rows, block_rows), jnp.bfloat16),
            pltpu.VMEM((inner, width), jnp.bfloat16),
            pltpu.VMEM((inner, width), jnp.bfloat16),
            pltpu.VMEM((inner, width), jnp.bfloat16),
            pltpu.SemaphoreType.DMA((12,)),
        ],
        compiler_params=params(20),
        cost_estimate=cost(0.5),
        name="inner_rows",
    )(
        offsets, counts,
        *(in_hbm(x) for x in (weight, bias_row, features, adj_values, cotangent)),
    )
    half_shape = (width // 2 + TAIL, width)
    act_rim, grad_rim, send, keep = pl.pallas_call(
        rim_kernel,
        out_shape=(
            shape(2 * rim, width),
            shape(2 * rim, width),
            shape(*half_shape, dtype=jnp.float32),
            shape(*half_shape, dtype=jnp.float32),
        ),
        in_specs=[smem] * 3 + [vmem] * 9,
        out_specs=(vmem,) * 4,
        scratch_shapes=[
            pltpu.VMEM((6 * rim + block_rows, width), jnp.bfloat16),
            pltpu.VMEM((2 * rim, width), jnp.bfloat16),
            pltpu.VMEM((2,) + half_shape, jnp.float32),
        ],
        compiler_params=params(12),
        cost_estimate=cost(0.2),
        name="rim_rows",
    )(
        offsets, counts, side, weight_near, bias_near, feat_rim, from_below, from_above, adj_rim,
        cot_rim, partial, sums,
    )
    mark = shape(8, 128, dtype=jnp.float32)
    activated, rim_spread, lower_part, upper_part, first_mark = pl.pallas_call(
        rim_back_kernel,
        out_shape=(
            shape(rows, width),
            shape(6 * BAND + 1, width, block_rows, dtype=jnp.float32),
            shape(rim, width),
            shape(rim, width),
            mark,
        ),
        in_specs=[smem, smem] + [vmem] * 4 + [hbm],
        out_specs=(hbm,) + (vmem,) * 4,
        scratch_shapes=[pltpu.SemaphoreType.DMA((2,))],
        input_output_aliases={6: 0},
        compiler_params=params(12),
        cost_estimate=cost(0.2),
        name="rim_rows_back",
    )(offsets, counts, weight_near, adj_rim, grad_rim, act_rim, activated)
    from_above_dev = neighbour(lower_part, -1, count)
    from_below_dev = neighbour(upper_part, 1, count)
    grad_whole, edges, second_mark = pl.pallas_call(
        inner_back_kernel,
        out_shape=(shape(rows, width), shape(2 * rim, width, dtype=jnp.float32), mark),
        in_specs=[smem, smem, vmem, hbm, vmem, vmem],
        out_specs=(hbm, vmem, vmem),
        scratch_shapes=[
            pltpu.VMEM((blocks - 2 * BAND, slots, block_rows, block_rows), jnp.bfloat16),
            pltpu.VMEM((blocks + 1, width, block_rows), jnp.float32),
            pltpu.VMEM((inner, width), jnp.bfloat16),
            pltpu.SemaphoreType.DMA((2,)),
        ],
        compiler_params=params(12),
        cost_estimate=cost(0.3),
        name="inner_rows_back",
    )(offsets, counts, weight_near, in_hbm(adj_values), grad_inner, rim_spread)
    grad_features, third_mark = pl.pallas_call(
        edge_kernel,
        out_shape=(shape(rows, width), mark),
        in_specs=[vmem] * 3 + [hbm],
        out_specs=(hbm, vmem),
        scratch_shapes=[
            pltpu.VMEM((2 * rim, width), jnp.bfloat16),
            pltpu.SemaphoreType.DMA((2,)),
        ],
        input_output_aliases={3: 0},
        compiler_params=params(8),
        cost_estimate=cost(0.05),
        name="join_edges",
    )(edges, from_below_dev, from_above_dev, grad_whole)
    marks = {0: (first_mark,), 2: (second_mark,), -1: (third_mark,)}
    own_half = sum_halves(send, keep, count, core_bit, marks)
    other_half = swap(own_half, [core_bit] * count)
    norm_scale = 1.0 / math.sqrt(rows * count)
    grad_weight, grad_bias = pl.pallas_call(
        lambda *refs: last_kernel(norm_scale, *refs),
        out_shape=(
            shape(width, width, dtype=jnp.float32),
            shape(1, width, dtype=jnp.float32),
        ),
        in_specs=[smem, vmem, vmem],
        out_specs=(vmem, vmem),
        compiler_params=params(8),
        name="last_step",
    )(side, own_half, other_half)
    return (activated, grad_features, grad_weight, grad_bias.reshape(width))


def solution(mesh):
    return jax.shard_map(
        on_device,
        mesh=mesh,
        in_specs=(
            P(AXES, None),
            P(AXES, None, None, None),
            P(AXES, None),
            P(AXES),
            P(),
            P(),
            P(AXES, None),
        ),
        out_specs=(P(AXES, None), P(AXES, None), P(), P()),
        check_vma=False,
    )
```

```python
import functools
import math

import jax
import jax.numpy as jnp
from jax import lax
from jax.experimental import pallas as pl
from jax.experimental.pallas import tpu as pltpu
from jax.sharding import PartitionSpec as P

BAND = 2
TAIL = 16
AXES = ("rows", "cols")
MIB = 1024 * 1024


def row_of(adj_ref, block, slots):
    return jnp.concatenate([adj_ref[block, slot] for slot in range(slots)], 1)


def pick(source, places, block_rows):
    return jnp.concatenate(
        [
            source[pl.ds(pl.multiple_of(place * block_rows, block_rows), block_rows)]
            for place in places
        ],
        0,
    )


def places_of(off_ref, cnt_ref, block, shift, dump, slots):
    return [
        jnp.where(slot < cnt_ref[block], block + shift + off_ref[slot, block], dump)
        for slot in range(slots)
    ]


def place_in_mesh():
    return lax.axis_index("rows") * lax.axis_size("cols") + lax.axis_index("cols")


def core_side():
    return lax.axis_index("rows") & 1


def halo_kernel(feat_hbm, first_ref, second_ref, sems):
    rows = feat_hbm.shape[0]
    rim = first_ref.shape[0]
    odd = place_in_mesh() & 1
    last = rows - rim
    starts = ((1 - odd) * last, odd * last)
    copies = [
        pltpu.make_async_copy(
            feat_hbm.at[pl.ds(pl.multiple_of(start, rim), rim)], out_ref, sems.at[i]
        )
        for i, (start, out_ref) in enumerate(zip(starts, (first_ref, second_ref)))
    ]
    for copy in copies:
        copy.start()
    for copy in copies:
        copy.wait()


def activate(preact, cotangent):
    gate = 1.0 / (1.0 + jnp.exp(-preact))
    grad = cotangent.astype(jnp.float32) * gate * (1.0 + preact * (1.0 - gate))
    return (preact * gate).astype(jnp.bfloat16), grad.astype(jnp.bfloat16)


def column_sums(grad):
    rows, width = grad.shape
    return jnp.sum(grad.astype(jnp.float32).reshape(rows // 8, 8, width), axis=0)


def to_upstream(weight, grad):
    return lax.dot_general(
        weight, grad, (((1,), (1,)), ((), ())), preferred_element_type=jnp.float32
    ).astype(jnp.bfloat16)


def weight_terms(agg, grad):
    return lax.dot_general(
        agg, grad, (((0,), (0,)), ((), ())), preferred_element_type=jnp.float32
    )


def inner_kernel(
    off_ref, cnt_ref, weight_hbm, bias_hbm, feat_hbm, adj_hbm, cot_hbm,
    act_hbm, grad_ref, partial_ref, sums_ref, weight_ref, bias_ref, feat_rim, adj_rim, cot_rim,
    feat, adj, cot, act, agg_all, sems,
):
    blocks, slots, block_rows, _ = adj_hbm.shape
    rows, width = feat_hbm.shape
    count = blocks - 2 * BAND
    rim = BAND * block_rows
    half = 2 * rim
    inner = count * block_rows
    copies = [
        pltpu.make_async_copy(feat_hbm, feat.at[pl.ds(0, rows)], sems.at[0]),
        pltpu.make_async_copy(adj_hbm.at[pl.ds(BAND, count)], adj, sems.at[1]),
        pltpu.make_async_copy(weight_hbm, weight_ref, sems.at[2]),
        pltpu.make_async_copy(bias_hbm, bias_ref, sems.at[3]),
        pltpu.make_async_copy(cot_hbm.at[pl.ds(rim, inner)], cot, sems.at[4]),
        pltpu.make_async_copy(feat_hbm.at[pl.ds(0, half)], feat_rim.at[pl.ds(0, half)], sems.at[5]),
        pltpu.make_async_copy(
            feat_hbm.at[pl.ds(rows - half, half)], feat_rim.at[pl.ds(half, half)], sems.at[6]
        ),
        pltpu.make_async_copy(adj_hbm.at[pl.ds(0, BAND)], adj_rim.at[pl.ds(0, BAND)], sems.at[7]),
        pltpu.make_async_copy(
            adj_hbm.at[pl.ds(blocks - BAND, BAND)], adj_rim.at[pl.ds(BAND, BAND)], sems.at[8]
        ),
        pltpu.make_async_copy(cot_hbm.at[pl.ds(0, rim)], cot_rim.at[pl.ds(0, rim)], sems.at[9]),
        pltpu.make_async_copy(
            cot_hbm.at[pl.ds(rows - rim, rim)], cot_rim.at[pl.ds(rim, rim)], sems.at[10]
        ),
    ]
    for copy in copies:
        copy.start()
    feat[rows:] = jnp.zeros((block_rows, width), jnp.bfloat16)
    for copy in copies[:5]:
        copy.wait()
    weight = weight_ref[...]
    bias = bias_ref[...]
    sums = jnp.zeros((8, width), jnp.float32)
    for step in range(0, count, 2):
        for block in (step, step + 1):
            places = places_of(off_ref, cnt_ref, block + BAND, 0, blocks, slots)
            agg_all[block * block_rows : (block + 1) * block_rows] = jnp.dot(
                row_of(adj, block, slots), pick(feat, places, block_rows),
                preferred_element_type=jnp.float32,
            ).astype(jnp.bfloat16)
        here = pl.ds(step * block_rows, 2 * block_rows)
        preact = jnp.dot(agg_all[here], weight, preferred_element_type=jnp.float32) + bias
        act[here], grad = activate(preact, cot[here])
        grad_ref[here] = grad
        sums = sums + column_sums(grad)
    act_out = pltpu.make_async_copy(act, act_hbm.at[pl.ds(rim, inner)], sems.at[11])
    act_out.start()
    sums_ref[...] = sums
    partial_ref[...] = weight_terms(agg_all[...], grad_ref[...])
    for copy in copies[5:]:
        copy.wait()
    act_out.wait()


def rim_places(off_ref, cnt_ref, step, blocks, slots):
    if step < BAND:
        return places_of(off_ref, cnt_ref, step, BAND, 6 * BAND, slots)
    block = blocks - 2 * BAND + step
    return places_of(off_ref, cnt_ref, block, 5 * BAND - blocks, 6 * BAND, slots)


def rim_kernel(
    off_ref, cnt_ref, weight_ref, bias_ref, feat_ref, first_ref, second_ref, adj_ref,
    cot_ref, partial_ref, sums_ref,
    act_ref, grad_ref, send_ref, keep_ref,
    window, agg_all, payload,
):
    blocks = off_ref.shape[1]
    steps, slots, block_rows, _ = adj_ref.shape
    width = feat_ref.shape[1]
    rim = BAND * block_rows
    odd = place_in_mesh() & 1
    window[pl.ds(pl.multiple_of((1 - odd) * 5 * rim, rim), rim)] = first_ref[...]
    window[pl.ds(pl.multiple_of(odd * 5 * rim, rim), rim)] = second_ref[...]
    window[rim : 5 * rim] = feat_ref[...]
    window[6 * rim :] = jnp.zeros((block_rows, width), jnp.bfloat16)
    weight = weight_ref[...]
    bias = bias_ref[...]
    sums = sums_ref[...]
    for step in range(0, steps, 2):
        for block in (step, step + 1):
            places = rim_places(off_ref, cnt_ref, block, blocks, slots)
            agg_all[block * block_rows : (block + 1) * block_rows] = jnp.dot(
                row_of(adj_ref, block, slots), pick(window, places, block_rows),
                preferred_element_type=jnp.float32,
            ).astype(jnp.bfloat16)
        here = pl.ds(step * block_rows, 2 * block_rows)
        preact = jnp.dot(agg_all[here], weight, preferred_element_type=jnp.float32) + bias
        act_ref[here], grad = activate(preact, cot_ref[here])
        grad_ref[here] = grad
        sums = sums + column_sums(grad)
    half = width // 2
    partial = partial_ref[...] + weight_terms(agg_all[...], grad_ref[...])
    payload[0, :half] = partial[:half]
    payload[1, :half] = partial[half:]
    tail = jnp.zeros((TAIL, width), jnp.float32)
    payload[0, half:] = jnp.broadcast_to(jnp.sum(sums, axis=0, keepdims=True), tail.shape)
    payload[1, half:] = tail
    side = core_side()
    keep_ref[...] = payload[side]
    send_ref[...] = payload[1 - side]


def rim_back_kernel(
    off_ref, cnt_ref, weight_ref, adj_ref, grad_ref, act_ref, act_in,
    act_hbm, spread, first_ref, second_ref, mark_ref,
    sems,
):
    blocks = off_ref.shape[1]
    steps, slots, block_rows, _ = adj_ref.shape
    rim = BAND * block_rows
    rows = blocks * block_rows
    copies = [
        pltpu.make_async_copy(act_ref.at[pl.ds(0, rim)], act_hbm.at[pl.ds(0, rim)], sems.at[0]),
        pltpu.make_async_copy(
            act_ref.at[pl.ds(rim, rim)], act_hbm.at[pl.ds(rows - rim, rim)], sems.at[1]
        ),
    ]
    for copy in copies:
        copy.start()
    spread[...] = jnp.zeros_like(spread)
    weight = weight_ref[...]
    for step in range(steps):
        here = pl.ds(step * block_rows, block_rows)
        places = rim_places(off_ref, cnt_ref, step, blocks, slots)
        terms = jnp.dot(
            to_upstream(weight, grad_ref[here]), row_of(adj_ref, step, slots),
            preferred_element_type=jnp.float32,
        )
        for slot, place in enumerate(places):
            spread[place] += terms[:, slot * block_rows : (slot + 1) * block_rows]
    odd = place_in_mesh() & 1
    for block in range(BAND):
        here = pl.ds(block * block_rows, block_rows)
        first_ref[here] = spread[(1 - odd) * 5 * BAND + block].T.astype(jnp.bfloat16)
        second_ref[here] = spread[odd * 5 * BAND + block].T.astype(jnp.bfloat16)
    mark_ref[...] = jnp.zeros_like(mark_ref)
    for copy in copies:
        copy.wait()


def scatter_rows(off_ref, cnt_ref, weight, adj, grad_ref, spread, steps, blocks, slots):
    block_rows = adj.shape[2]
    for i, step in enumerate(steps):
        here = pl.ds(step * block_rows, block_rows)
        places = places_of(off_ref, cnt_ref, step + BAND, 0, blocks, slots)
        terms = jnp.dot(
            to_upstream(weight, grad_ref[here]), row_of(adj, i, slots),
            preferred_element_type=jnp.float32,
        )
        for slot, place in enumerate(places):
            spread[place] += terms[:, slot * block_rows : (slot + 1) * block_rows]


def inner_back_first(
    off_ref, cnt_ref, weight_ref, adj_hbm, grad_ref, rim_spread, spread, mark_ref, adj, sems
):
    blocks, slots, _, _ = adj_hbm.shape
    count = adj.shape[0]
    fetch = pltpu.make_async_copy(adj_hbm.at[pl.ds(BAND, count)], adj, sems.at[0])
    fetch.start()
    spread[: 2 * BAND] = rim_spread[BAND : 3 * BAND]
    spread[2 * BAND :] = jnp.zeros_like(spread[2 * BAND :])
    spread[blocks - 2 * BAND : blocks] = rim_spread[3 * BAND : 5 * BAND]
    mark_ref[...] = jnp.zeros_like(mark_ref)
    fetch.wait()
    scatter_rows(
        off_ref, cnt_ref, weight_ref[...], adj, grad_ref, spread, range(count), blocks, slots
    )


def inner_back_second(
    off_ref, cnt_ref, weight_ref, adj_hbm, grad_ref, half_spread,
    whole_hbm, edge_ref, mark_ref,
    adj, spread, out, sems,
):
    blocks, slots, block_rows, _ = adj_hbm.shape
    count = blocks - 2 * BAND
    first = count - adj.shape[0]
    rim = BAND * block_rows
    fetch = pltpu.make_async_copy(
        adj_hbm.at[pl.ds(BAND + first, count - first)], adj, sems.at[0]
    )
    fetch.start()
    spread[...] = half_spread[...]
    mark_ref[...] = jnp.zeros_like(mark_ref)
    fetch.wait()
    scatter_rows(
        off_ref, cnt_ref, weight_ref[...], adj, grad_ref, spread, range(first, count), blocks,
        slots,
    )
    for step in range(count):
        here = pl.ds(step * block_rows, block_rows)
        out[here] = spread[BAND + step].T.astype(jnp.bfloat16)
    finish = pltpu.make_async_copy(out, whole_hbm.at[pl.ds(rim, count * block_rows)], sems.at[1])
    finish.start()
    for block in range(BAND):
        edge_ref[block * block_rows : (block + 1) * block_rows] = spread[block].T
        after = BAND + block
        edge_ref[after * block_rows : (after + 1) * block_rows] = spread[blocks - BAND + block].T
    finish.wait()


def edge_kernel(edge_ref, first_ref, second_ref, whole_in, whole_hbm, mark_ref, out, sems):
    rim = first_ref.shape[0]
    rows = whole_hbm.shape[0]
    odd = place_in_mesh() & 1
    for base, spill_ref in (((1 - odd) * rim, first_ref), (odd * rim, second_ref)):
        here = pl.ds(pl.multiple_of(base, rim), rim)
        out[here] = (edge_ref[here] + spill_ref[...].astype(jnp.float32)).astype(jnp.bfloat16)
    copies = [
        pltpu.make_async_copy(out.at[pl.ds(0, rim)], whole_hbm.at[pl.ds(0, rim)], sems.at[0]),
        pltpu.make_async_copy(
            out.at[pl.ds(rim, rim)], whole_hbm.at[pl.ds(rows - rim, rim)], sems.at[1]
        ),
    ]
    for copy in copies:
        copy.start()
    mark_ref[...] = jnp.zeros_like(mark_ref)
    for copy in copies:
        copy.wait()


def add_kernel(parts, *refs):
    values = [ref[...].astype(jnp.float32) for ref in refs[:parts]]
    total = values[0] + values[1]
    if parts == 4:
        total = total + (values[2] + values[3])
    refs[-1][...] = total.astype(refs[-1].dtype)


def last_kernel(scale, own_ref, other_ref, weight_out, bias_out):
    half = weight_out.shape[0] // 2
    side = core_side()
    own_rows = pl.ds(pl.multiple_of(side * half, half), half)
    other_rows = pl.ds(pl.multiple_of((1 - side) * half, half), half)
    weight_out[own_rows] = own_ref[:half] * scale
    weight_out[other_rows] = other_ref[:half] * scale
    first = jnp.where(side == 0, own_ref[half : half + 1], other_ref[half : half + 1])
    bias_out[...] = first * scale


def add(values, dtype, after=()):
    size = values[0].size
    return pl.pallas_call(
        functools.partial(add_kernel, len(values)),
        out_shape=jax.ShapeDtypeStruct(values[0].shape, dtype),
        in_specs=[pl.BlockSpec(memory_space=pltpu.VMEM)] * len(values)
        + [pl.BlockSpec(memory_space=pl.ANY)] * len(after),
        compiler_params=pltpu.CompilerParams(vmem_limit_bytes=2 * MIB),
        cost_estimate=pl.CostEstimate(
            flops=size * len(values), bytes_accessed=8 * size, transcendentals=0
        ),
        name="add_halves",
    )(*values, *after)


def swap(value, masks):
    pairs = [(i, i ^ mask) for i, mask in enumerate(masks) if mask]
    return lax.ppermute(value, AXES, pairs)


def with_next(value, count):
    pairs = [(i, i + 1 if i & 1 else i - 1) for i in range(1, count - 1)]
    return lax.ppermute(value, AXES, pairs)


def sum_halves(send, keep, count, core_bit, marks):
    others = [bit for bit in range(count.bit_length() - 1) if bit != core_bit]
    groups = [others[i : i + 2] for i in range(0, len(others), 2)]
    total = add([keep, swap(send, [1 << core_bit] * count)], jnp.bfloat16, marks.get("core", ()))
    for step in range(len(groups)):
        masks = []
        for group in (groups[step], groups[len(groups) - 1 - step]):
            if len(groups[0]) != len(groups[-1]):
                group = groups[step]
            low = 1 << group[0]
            masks.append((low, 1 << group[1], low | 1 << group[1]) if group[1:] else (low,))
        parts = [total] + [
            swap(total, [masks[(i >> core_bit) & 1][k] for i in range(count)])
            for k in range(len(masks[0]))
        ]
        last = step == len(groups) - 1
        name = "last" if last else step
        total = add(parts, jnp.float32 if last else jnp.bfloat16, marks.get(name, ()))
    return total


def on_device(features, adj_values, adj_offset, adj_count, weight, bias_vector, cotangent):
    blocks, slots = adj_offset.shape
    block_rows = adj_values.shape[2]
    rows, width = features.shape
    rim = BAND * block_rows
    inner = rows - 2 * rim
    cols = lax.axis_size("cols")
    count = lax.axis_size("rows") * cols
    smem = pl.BlockSpec(memory_space=pltpu.SMEM)
    vmem = pl.BlockSpec(memory_space=pltpu.VMEM)
    hbm = pl.BlockSpec(memory_space=pltpu.HBM)
    bias_row = bias_vector.reshape(1, width)

    def in_hbm(value):
        return pltpu.with_memory_space_constraint(value, pltpu.HBM)

    def shape(*sizes, dtype=jnp.bfloat16):
        return jax.ShapeDtypeStruct(sizes, dtype)

    def params(mib):
        return pltpu.CompilerParams(vmem_limit_bytes=mib * MIB)

    def cost(share):
        return pl.CostEstimate(
            flops=int(1.2e9 * share), bytes_accessed=int(6e6 * share),
            transcendentals=int(8e5 * share),
        )

    offsets = in_hbm(adj_offset.T)
    counts = in_hbm(adj_count)
    core_bit = cols.bit_length() - 1
    first_rim, second_rim = pl.pallas_call(
        halo_kernel,
        out_shape=(shape(rim, width), shape(rim, width)),
        in_specs=[hbm],
        out_specs=(vmem, vmem),
        scratch_shapes=[pltpu.SemaphoreType.DMA((2,))],
        compiler_params=params(2),
        cost_estimate=cost(0.05),
        name="halo_rows",
    )(in_hbm(features))
    first_halo = swap(first_rim, [1] * count)
    second_halo = with_next(second_rim, count)
    (
        activated, grad_inner, partial, sums, weight_near, bias_near, feat_rim, adj_rim, cot_rim,
    ) = pl.pallas_call(
        inner_kernel,
        out_shape=(
            shape(rows, width),
            shape(inner, width),
            shape(width, width, dtype=jnp.float32),
            shape(8, width, dtype=jnp.float32),
            shape(width, width),
            shape(1, width, dtype=jnp.float32),
            shape(4 * rim, width),
            shape(2 * BAND, slots, block_rows, block_rows),
            shape(2 * rim, width),
        ),
        in_specs=[smem, smem] + [hbm] * 5,
        out_specs=(hbm,) + (vmem,) * 8,
        scratch_shapes=[
            pltpu.VMEM((rows + block_rows, width), jnp.bfloat16),
            pltpu.VMEM((blocks - 2 * BAND, slots, block_rows, block_rows), jnp.bfloat16),
            pltpu.VMEM((inner, width), jnp.bfloat16),
            pltpu.VMEM((inner, width), jnp.bfloat16),
            pltpu.VMEM((inner, width), jnp.bfloat16),
            pltpu.SemaphoreType.DMA((12,)),
        ],
        compiler_params=params(20),
        cost_estimate=cost(0.5),
        name="inner_rows",
    )(
        offsets, counts,
        *(in_hbm(x) for x in (weight, bias_row, features, adj_values, cotangent)),
    )
    half_shape = (width // 2 + TAIL, width)
    act_rim, grad_rim, send, keep = pl.pallas_call(
        rim_kernel,
        out_shape=(
            shape(2 * rim, width),
            shape(2 * rim, width),
            shape(*half_shape, dtype=jnp.float32),
            shape(*half_shape, dtype=jnp.float32),
        ),
        in_specs=[smem] * 2 + [vmem] * 9,
        out_specs=(vmem,) * 4,
        scratch_shapes=[
            pltpu.VMEM((6 * rim + block_rows, width), jnp.bfloat16),
            pltpu.VMEM((2 * rim, width), jnp.bfloat16),
            pltpu.VMEM((2,) + half_shape, jnp.float32),
        ],
        compiler_params=params(12),
        cost_estimate=cost(0.2),
        name="rim_rows",
    )(
        offsets, counts, weight_near, bias_near, feat_rim, first_halo, second_halo, adj_rim,
        cot_rim, partial, sums,
    )
    mark = shape(8, 128, dtype=jnp.float32)
    activated, rim_spread, first_spill, second_spill, first_mark = pl.pallas_call(
        rim_back_kernel,
        out_shape=(
            shape(rows, width),
            shape(6 * BAND + 1, width, block_rows, dtype=jnp.float32),
            shape(rim, width),
            shape(rim, width),
            mark,
        ),
        in_specs=[smem, smem] + [vmem] * 4 + [hbm],
        out_specs=(hbm,) + (vmem,) * 4,
        scratch_shapes=[pltpu.SemaphoreType.DMA((2,))],
        input_output_aliases={6: 0},
        compiler_params=params(12),
        cost_estimate=cost(0.2),
        name="rim_rows_back",
    )(offsets, counts, weight_near, adj_rim, grad_rim, act_rim, activated)
    first_part = swap(first_spill, [1] * count)
    second_part = with_next(second_spill, count)
    spread_shape = (blocks + 1, width, block_rows)
    steps = inner // block_rows
    half_spread, second_mark = pl.pallas_call(
        inner_back_first,
        out_shape=(shape(*spread_shape, dtype=jnp.float32), mark),
        in_specs=[smem, smem, vmem, hbm, vmem, vmem],
        out_specs=(vmem, vmem),
        scratch_shapes=[
            pltpu.VMEM((steps // 2, slots, block_rows, block_rows), jnp.bfloat16),
            pltpu.SemaphoreType.DMA((1,)),
        ],
        compiler_params=params(12),
        cost_estimate=cost(0.15),
        name="inner_back_first",
    )(offsets, counts, weight_near, in_hbm(adj_values), grad_inner, rim_spread)
    grad_whole, edges, third_mark = pl.pallas_call(
        inner_back_second,
        out_shape=(shape(rows, width), shape(2 * rim, width, dtype=jnp.float32), mark),
        in_specs=[smem, smem, vmem, hbm, vmem, vmem],
        out_specs=(hbm, vmem, vmem),
        scratch_shapes=[
            pltpu.VMEM((steps - steps // 2, slots, block_rows, block_rows), jnp.bfloat16),
            pltpu.VMEM(spread_shape, jnp.float32),
            pltpu.VMEM((inner, width), jnp.bfloat16),
            pltpu.SemaphoreType.DMA((2,)),
        ],
        compiler_params=params(12),
        cost_estimate=cost(0.15),
        name="inner_back_second",
    )(offsets, counts, weight_near, in_hbm(adj_values), grad_inner, half_spread)
    grad_features, last_mark = pl.pallas_call(
        edge_kernel,
        out_shape=(shape(rows, width), mark),
        in_specs=[vmem] * 3 + [hbm],
        out_specs=(hbm, vmem),
        scratch_shapes=[
            pltpu.VMEM((2 * rim, width), jnp.bfloat16),
            pltpu.SemaphoreType.DMA((2,)),
        ],
        input_output_aliases={3: 0},
        compiler_params=params(8),
        cost_estimate=cost(0.05),
        name="join_edges",
    )(edges, first_part, second_part, grad_whole)
    marks = {"core": (first_mark,), 0: (second_mark,), "last": (third_mark, last_mark)}
    own_half = sum_halves(send, keep, count, core_bit, marks)
    other_half = swap(own_half, [1 << core_bit] * count)
    norm_scale = 1.0 / math.sqrt(rows * count)
    grad_weight, grad_bias = pl.pallas_call(
        functools.partial(last_kernel, norm_scale),
        out_shape=(
            shape(width, width, dtype=jnp.float32),
            shape(1, width, dtype=jnp.float32),
        ),
        in_specs=[vmem, vmem],
        out_specs=(vmem, vmem),
        compiler_params=params(8),
        name="last_step",
    )(own_half, other_half)
    return (activated, grad_features, grad_weight, grad_bias.reshape(width))


def solution(mesh):
    return jax.shard_map(
        on_device,
        mesh=mesh,
        in_specs=(
            P(AXES, None),
            P(AXES, None, None, None),
            P(AXES, None),
            P(AXES),
            P(),
            P(),
            P(AXES, None),
        ),
        out_specs=(P(AXES, None), P(AXES, None), P(), P()),
        check_vma=False,
    )
```

```python
import functools
import math

import jax
import jax.numpy as jnp
from jax import lax
from jax.experimental import pallas as pl
from jax.experimental.pallas import tpu as pltpu
from jax.sharding import PartitionSpec as P

BAND = 2
TAIL = 16
AXES = ("rows", "cols")
MIB = 1024 * 1024


def row_of(adj_ref, block, slots):
    return jnp.concatenate([adj_ref[block, slot] for slot in range(slots)], 1)


def pick(source, places, block_rows):
    return jnp.concatenate(
        [
            source[pl.ds(pl.multiple_of(place * block_rows, block_rows), block_rows)]
            for place in places
        ],
        0,
    )


def write_places(off_ref, cnt_ref, place_ref, blocks, slots):
    for block in range(blocks):
        if block < BAND:
            shift, dump = BAND, 6 * BAND
        elif block < blocks - BAND:
            shift, dump = 0, blocks
        else:
            shift, dump = 5 * BAND - blocks, 6 * BAND
        for slot in range(slots):
            place_ref[block * slots + slot] = jnp.where(
                slot < cnt_ref[block], block + shift + off_ref[slot, block], dump
            )


def places_of(place_ref, block, slots):
    return [place_ref[block * slots + slot] for slot in range(slots)]


def rim_block(step, blocks):
    return step if step < BAND else blocks - 2 * BAND + step


def place_in_mesh():
    return lax.axis_index("rows") * lax.axis_size("cols") + lax.axis_index("cols")


def core_side():
    return lax.axis_index("rows") & 1


def halo_kernel(feat_hbm, first_ref, second_ref, sems):
    rows = feat_hbm.shape[0]
    rim = first_ref.shape[0]
    odd = place_in_mesh() & 1
    last = rows - rim
    starts = ((1 - odd) * last, odd * last)
    copies = [
        pltpu.make_async_copy(
            feat_hbm.at[pl.ds(pl.multiple_of(start, rim), rim)], out_ref, sems.at[i]
        )
        for i, (start, out_ref) in enumerate(zip(starts, (first_ref, second_ref)))
    ]
    for copy in copies:
        copy.start()
    for copy in copies:
        copy.wait()


def activate(preact, cotangent):
    gate = 1.0 / (1.0 + jnp.exp(-preact))
    grad = cotangent.astype(jnp.float32) * gate * (1.0 + preact * (1.0 - gate))
    return (preact * gate).astype(jnp.bfloat16), grad.astype(jnp.bfloat16)


def column_sums(grad):
    rows, width = grad.shape
    return jnp.sum(grad.astype(jnp.float32).reshape(rows // 8, 8, width), axis=0)


def to_upstream(weight, grad):
    return lax.dot_general(
        weight, grad, (((1,), (1,)), ((), ())), preferred_element_type=jnp.float32
    ).astype(jnp.bfloat16)


def weight_terms(agg, grad):
    return lax.dot_general(
        agg, grad, (((0,), (0,)), ((), ())), preferred_element_type=jnp.float32
    )


def inner_kernel(
    off_ref, cnt_ref, weight_hbm, bias_hbm, feat_hbm, adj_hbm, cot_hbm,
    act_hbm, place_ref, grad_ref, partial_ref, sums_ref, weight_ref, bias_ref, feat_rim, adj_rim,
    cot_rim, adj,
    feat, cot, act, agg_all, sems,
):
    blocks, slots, block_rows, _ = adj_hbm.shape
    rows, width = feat_hbm.shape
    count = blocks - 2 * BAND
    rim = BAND * block_rows
    half = 2 * rim
    inner = count * block_rows
    copies = [
        pltpu.make_async_copy(feat_hbm, feat.at[pl.ds(0, rows)], sems.at[0]),
        pltpu.make_async_copy(adj_hbm.at[pl.ds(BAND, count)], adj, sems.at[1]),
        pltpu.make_async_copy(weight_hbm, weight_ref, sems.at[2]),
        pltpu.make_async_copy(bias_hbm, bias_ref, sems.at[3]),
        pltpu.make_async_copy(cot_hbm.at[pl.ds(rim, inner)], cot, sems.at[4]),
        pltpu.make_async_copy(feat_hbm.at[pl.ds(0, half)], feat_rim.at[pl.ds(0, half)], sems.at[5]),
        pltpu.make_async_copy(
            feat_hbm.at[pl.ds(rows - half, half)], feat_rim.at[pl.ds(half, half)], sems.at[6]
        ),
        pltpu.make_async_copy(adj_hbm.at[pl.ds(0, BAND)], adj_rim.at[pl.ds(0, BAND)], sems.at[7]),
        pltpu.make_async_copy(
            adj_hbm.at[pl.ds(blocks - BAND, BAND)], adj_rim.at[pl.ds(BAND, BAND)], sems.at[8]
        ),
        pltpu.make_async_copy(cot_hbm.at[pl.ds(0, rim)], cot_rim.at[pl.ds(0, rim)], sems.at[9]),
        pltpu.make_async_copy(
            cot_hbm.at[pl.ds(rows - rim, rim)], cot_rim.at[pl.ds(rim, rim)], sems.at[10]
        ),
    ]
    for copy in copies:
        copy.start()
    feat[rows:] = jnp.zeros((block_rows, width), jnp.bfloat16)
    write_places(off_ref, cnt_ref, place_ref, blocks, slots)
    for copy in copies[:5]:
        copy.wait()
    weight = weight_ref[...]
    bias = bias_ref[...]
    sums = jnp.zeros((8, width), jnp.float32)
    for step in range(0, count, 2):
        for block in (step, step + 1):
            places = places_of(place_ref, block + BAND, slots)
            agg_all[block * block_rows : (block + 1) * block_rows] = jnp.dot(
                row_of(adj, block, slots), pick(feat, places, block_rows),
                preferred_element_type=jnp.float32,
            ).astype(jnp.bfloat16)
        here = pl.ds(step * block_rows, 2 * block_rows)
        preact = jnp.dot(agg_all[here], weight, preferred_element_type=jnp.float32) + bias
        act[here], grad = activate(preact, cot[here])
        grad_ref[here] = grad
        sums = sums + column_sums(grad)
    act_out = pltpu.make_async_copy(act, act_hbm.at[pl.ds(rim, inner)], sems.at[11])
    act_out.start()
    sums_ref[...] = sums
    partial_ref[...] = weight_terms(agg_all[...], grad_ref[...])
    for copy in copies[5:]:
        copy.wait()
    act_out.wait()


def rim_kernel(
    place_ref, weight_ref, bias_ref, feat_ref, first_ref, second_ref, adj_ref, cot_ref,
    partial_ref, sums_ref,
    act_ref, grad_ref, send_ref, keep_ref,
    window, agg_all, payload,
):
    steps, slots, block_rows, _ = adj_ref.shape
    blocks = place_ref.shape[0] // slots
    width = feat_ref.shape[1]
    rim = BAND * block_rows
    odd = place_in_mesh() & 1
    window[pl.ds(pl.multiple_of((1 - odd) * 5 * rim, rim), rim)] = first_ref[...]
    window[pl.ds(pl.multiple_of(odd * 5 * rim, rim), rim)] = second_ref[...]
    window[rim : 5 * rim] = feat_ref[...]
    window[6 * rim :] = jnp.zeros((block_rows, width), jnp.bfloat16)
    weight = weight_ref[...]
    bias = bias_ref[...]
    sums = sums_ref[...]
    for step in range(0, steps, 2):
        for block in (step, step + 1):
            places = places_of(place_ref, rim_block(block, blocks), slots)
            agg_all[block * block_rows : (block + 1) * block_rows] = jnp.dot(
                row_of(adj_ref, block, slots), pick(window, places, block_rows),
                preferred_element_type=jnp.float32,
            ).astype(jnp.bfloat16)
        here = pl.ds(step * block_rows, 2 * block_rows)
        preact = jnp.dot(agg_all[here], weight, preferred_element_type=jnp.float32) + bias
        act_ref[here], grad = activate(preact, cot_ref[here])
        grad_ref[here] = grad
        sums = sums + column_sums(grad)
    half = width // 2
    partial = partial_ref[...] + weight_terms(agg_all[...], grad_ref[...])
    payload[0, :half] = partial[:half]
    payload[1, :half] = partial[half:]
    tail = jnp.zeros((TAIL, width), jnp.float32)
    payload[0, half:] = jnp.broadcast_to(jnp.sum(sums, axis=0, keepdims=True), tail.shape)
    payload[1, half:] = tail
    side = core_side()
    keep_ref[...] = payload[side]
    send_ref[...] = payload[1 - side]


def scatter_rows(places, weight_ref, adj_ref, grad_ref, spread):
    _, slots, block_rows, _ = adj_ref.shape
    upstream = to_upstream(weight_ref[...], grad_ref[...])
    for step, targets in enumerate(places):
        terms = jnp.dot(
            upstream[:, step * block_rows : (step + 1) * block_rows],
            row_of(adj_ref, step, slots),
            preferred_element_type=jnp.float32,
        )
        for slot, target in enumerate(targets):
            spread[target] += terms[:, slot * block_rows : (slot + 1) * block_rows]


def rim_back_kernel(
    place_ref, weight_ref, adj_ref, grad_ref, act_ref, act_in,
    act_hbm, spread, first_ref, second_ref, mark_ref,
    sems,
):
    steps, slots, block_rows, _ = adj_ref.shape
    blocks = place_ref.shape[0] // slots
    rim = BAND * block_rows
    rows = blocks * block_rows
    copies = [
        pltpu.make_async_copy(act_ref.at[pl.ds(0, rim)], act_hbm.at[pl.ds(0, rim)], sems.at[0]),
        pltpu.make_async_copy(
            act_ref.at[pl.ds(rim, rim)], act_hbm.at[pl.ds(rows - rim, rim)], sems.at[1]
        ),
    ]
    for copy in copies:
        copy.start()
    spread[...] = jnp.zeros_like(spread)
    scatter_rows(
        [places_of(place_ref, rim_block(step, blocks), slots) for step in range(steps)],
        weight_ref, adj_ref, grad_ref, spread,
    )
    odd = place_in_mesh() & 1
    for block in range(BAND):
        here = pl.ds(block * block_rows, block_rows)
        first_ref[here] = spread[(1 - odd) * 5 * BAND + block].T.astype(jnp.bfloat16)
        second_ref[here] = spread[odd * 5 * BAND + block].T.astype(jnp.bfloat16)
    mark_ref[...] = jnp.zeros_like(mark_ref)
    for copy in copies:
        copy.wait()


def inner_back_kernel(
    place_ref, weight_ref, adj_ref, grad_ref, rim_spread,
    whole_hbm, edge_ref, mark_ref,
    spread, out, sems,
):
    count, slots, block_rows, _ = adj_ref.shape
    blocks = place_ref.shape[0] // slots
    rim = BAND * block_rows
    spread[: 2 * BAND] = rim_spread[BAND : 3 * BAND]
    spread[2 * BAND :] = jnp.zeros_like(spread[2 * BAND :])
    spread[blocks - 2 * BAND : blocks] = rim_spread[3 * BAND : 5 * BAND]
    mark_ref[...] = jnp.zeros_like(mark_ref)
    scatter_rows(
        [places_of(place_ref, step + BAND, slots) for step in range(count)],
        weight_ref, adj_ref, grad_ref, spread,
    )
    for step in range(count):
        here = pl.ds(step * block_rows, block_rows)
        out[here] = spread[BAND + step].T.astype(jnp.bfloat16)
    finish = pltpu.make_async_copy(out, whole_hbm.at[pl.ds(rim, count * block_rows)], sems.at[0])
    finish.start()
    for block in range(BAND):
        edge_ref[block * block_rows : (block + 1) * block_rows] = spread[block].T
        after = BAND + block
        edge_ref[after * block_rows : (after + 1) * block_rows] = spread[blocks - BAND + block].T
    finish.wait()


def add_kernel(parts, *refs):
    values = [ref[...].astype(jnp.float32) for ref in refs[:parts]]
    total = values[0] + values[1]
    if parts == 4:
        total = total + (values[2] + values[3])
    refs[-1][...] = total.astype(refs[-1].dtype)


def last_kernel(
    scale, own_ref, other_ref, edge_ref, first_ref, second_ref, whole_in,
    weight_out, bias_out, whole_hbm,
    out, sums, sems,
):
    half = sums.shape[0] // 2
    rim = first_ref.shape[0]
    rows = whole_hbm.shape[0]
    odd = place_in_mesh() & 1
    for base, spill_ref in (((1 - odd) * rim, first_ref), (odd * rim, second_ref)):
        here = pl.ds(pl.multiple_of(base, rim), rim)
        out[here] = (edge_ref[here] + spill_ref[...].astype(jnp.float32)).astype(jnp.bfloat16)
    copies = [
        pltpu.make_async_copy(out.at[pl.ds(0, rim)], whole_hbm.at[pl.ds(0, rim)], sems.at[0]),
        pltpu.make_async_copy(
            out.at[pl.ds(rim, rim)], whole_hbm.at[pl.ds(rows - rim, rim)], sems.at[1]
        ),
        pltpu.make_async_copy(sums, weight_out, sems.at[2]),
    ]
    for copy in copies[:2]:
        copy.start()
    side = core_side()
    own_rows = pl.ds(pl.multiple_of(side * half, half), half)
    other_rows = pl.ds(pl.multiple_of((1 - side) * half, half), half)
    sums[own_rows] = own_ref[:half] * scale
    sums[other_rows] = other_ref[:half] * scale
    copies[2].start()
    first = jnp.where(side == 0, own_ref[half : half + 1], other_ref[half : half + 1])
    bias_out[...] = first * scale
    for copy in copies:
        copy.wait()


def add(values, dtype, after=()):
    size = values[0].size
    return pl.pallas_call(
        functools.partial(add_kernel, len(values)),
        out_shape=jax.ShapeDtypeStruct(values[0].shape, dtype),
        in_specs=[pl.BlockSpec(memory_space=pltpu.VMEM)] * len(values)
        + [pl.BlockSpec(memory_space=pl.ANY)] * len(after),
        compiler_params=pltpu.CompilerParams(vmem_limit_bytes=2 * MIB),
        cost_estimate=pl.CostEstimate(
            flops=size * len(values), bytes_accessed=8 * size, transcendentals=0
        ),
        name="add_halves",
    )(*values, *after)


def swap(value, masks):
    pairs = [(i, i ^ mask) for i, mask in enumerate(masks) if mask]
    return lax.ppermute(value, AXES, pairs)


def with_next(value, count):
    pairs = [(i, i + 1 if i & 1 else i - 1) for i in range(1, count - 1)]
    return lax.ppermute(value, AXES, pairs)


def sum_halves(send, keep, count, core_bit, marks):
    others = [bit for bit in range(count.bit_length() - 1) if bit != core_bit]
    groups = [others[i : i + 2] for i in range(0, len(others), 2)]
    total = add([keep, swap(send, [1 << core_bit] * count)], jnp.bfloat16, marks.get("core", ()))
    for step in range(len(groups)):
        masks = []
        for group in (groups[step], groups[len(groups) - 1 - step]):
            if len(groups[0]) != len(groups[-1]):
                group = groups[step]
            low = 1 << group[0]
            masks.append((low, 1 << group[1], low | 1 << group[1]) if group[1:] else (low,))
        parts = [total] + [
            swap(total, [masks[(i >> core_bit) & 1][k] for i in range(count)])
            for k in range(len(masks[0]))
        ]
        last = step == len(groups) - 1
        name = "last" if last else step
        total = add(parts, jnp.float32 if last else jnp.bfloat16, marks.get(name, ()))
    return total


def on_device(features, adj_values, adj_offset, adj_count, weight, bias_vector, cotangent):
    blocks, slots = adj_offset.shape
    block_rows = adj_values.shape[2]
    rows, width = features.shape
    rim = BAND * block_rows
    inner = rows - 2 * rim
    cols = lax.axis_size("cols")
    count = lax.axis_size("rows") * cols
    smem = pl.BlockSpec(memory_space=pltpu.SMEM)
    vmem = pl.BlockSpec(memory_space=pltpu.VMEM)
    hbm = pl.BlockSpec(memory_space=pltpu.HBM)
    bias_row = bias_vector.reshape(1, width)

    def in_hbm(value):
        return pltpu.with_memory_space_constraint(value, pltpu.HBM)

    def shape(*sizes, dtype=jnp.bfloat16):
        return jax.ShapeDtypeStruct(sizes, dtype)

    def params(mib):
        return pltpu.CompilerParams(vmem_limit_bytes=mib * MIB)

    def cost(share):
        return pl.CostEstimate(
            flops=int(1.2e9 * share), bytes_accessed=int(6e6 * share),
            transcendentals=int(8e5 * share),
        )

    offsets = in_hbm(adj_offset.T)
    counts = in_hbm(adj_count)
    core_bit = cols.bit_length() - 1
    first_rim, second_rim = pl.pallas_call(
        halo_kernel,
        out_shape=(shape(rim, width), shape(rim, width)),
        in_specs=[hbm],
        out_specs=(vmem, vmem),
        scratch_shapes=[pltpu.SemaphoreType.DMA((2,))],
        compiler_params=params(2),
        cost_estimate=cost(0.05),
        name="halo_rows",
    )(in_hbm(features))
    first_halo = swap(first_rim, [1] * count)
    second_halo = with_next(second_rim, count)
    (
        activated, places, grad_inner, partial, sums, weight_near, bias_near, feat_rim, adj_rim,
        cot_rim, adj_inner,
    ) = pl.pallas_call(
        inner_kernel,
        out_shape=(
            shape(rows, width),
            shape(blocks * slots, dtype=jnp.int32),
            shape(inner, width),
            shape(width, width, dtype=jnp.float32),
            shape(8, width, dtype=jnp.float32),
            shape(width, width),
            shape(1, width, dtype=jnp.float32),
            shape(4 * rim, width),
            shape(2 * BAND, slots, block_rows, block_rows),
            shape(2 * rim, width),
            shape(blocks - 2 * BAND, slots, block_rows, block_rows),
        ),
        in_specs=[smem, smem] + [hbm] * 5,
        out_specs=(hbm, smem) + (vmem,) * 9,
        scratch_shapes=[
            pltpu.VMEM((rows + block_rows, width), jnp.bfloat16),
            pltpu.VMEM((inner, width), jnp.bfloat16),
            pltpu.VMEM((inner, width), jnp.bfloat16),
            pltpu.VMEM((inner, width), jnp.bfloat16),
            pltpu.SemaphoreType.DMA((12,)),
        ],
        compiler_params=params(20),
        cost_estimate=cost(0.5),
        name="inner_rows",
    )(
        offsets, counts,
        *(in_hbm(x) for x in (weight, bias_row, features, adj_values, cotangent)),
    )
    half_shape = (width // 2 + TAIL, width)
    act_rim, grad_rim, send, keep = pl.pallas_call(
        rim_kernel,
        out_shape=(
            shape(2 * rim, width),
            shape(2 * rim, width),
            shape(*half_shape, dtype=jnp.float32),
            shape(*half_shape, dtype=jnp.float32),
        ),
        in_specs=[smem] + [vmem] * 9,
        out_specs=(vmem,) * 4,
        scratch_shapes=[
            pltpu.VMEM((6 * rim + block_rows, width), jnp.bfloat16),
            pltpu.VMEM((2 * rim, width), jnp.bfloat16),
            pltpu.VMEM((2,) + half_shape, jnp.float32),
        ],
        compiler_params=params(12),
        cost_estimate=cost(0.2),
        name="rim_rows",
    )(
        places, weight_near, bias_near, feat_rim, first_halo, second_halo, adj_rim, cot_rim,
        partial, sums,
    )
    mark = shape(8, 128, dtype=jnp.float32)
    activated, rim_spread, first_spill, second_spill, first_mark = pl.pallas_call(
        rim_back_kernel,
        out_shape=(
            shape(rows, width),
            shape(6 * BAND + 1, width, block_rows, dtype=jnp.float32),
            shape(rim, width),
            shape(rim, width),
            mark,
        ),
        in_specs=[smem] + [vmem] * 4 + [hbm],
        out_specs=(hbm,) + (vmem,) * 4,
        scratch_shapes=[pltpu.SemaphoreType.DMA((2,))],
        input_output_aliases={5: 0},
        compiler_params=params(12),
        cost_estimate=cost(0.2),
        name="rim_rows_back",
    )(places, weight_near, adj_rim, grad_rim, act_rim, activated)
    first_part = swap(first_spill, [1] * count)
    second_part = with_next(second_spill, count)
    grad_whole, edges, second_mark = pl.pallas_call(
        inner_back_kernel,
        out_shape=(shape(rows, width), shape(2 * rim, width, dtype=jnp.float32), mark),
        in_specs=[smem] + [vmem] * 4,
        out_specs=(hbm, vmem, vmem),
        scratch_shapes=[
            pltpu.VMEM((blocks + 1, width, block_rows), jnp.float32),
            pltpu.VMEM((inner, width), jnp.bfloat16),
            pltpu.SemaphoreType.DMA((1,)),
        ],
        compiler_params=params(12),
        cost_estimate=cost(0.3),
        name="inner_rows_back",
    )(places, weight_near, adj_inner, grad_inner, rim_spread)
    marks = {"core": (first_mark,), "last": (second_mark,)}
    own_half = sum_halves(send, keep, count, core_bit, marks)
    other_half = swap(own_half, [1 << core_bit] * count)
    norm_scale = 1.0 / math.sqrt(rows * count)
    grad_weight, grad_bias, grad_features = pl.pallas_call(
        functools.partial(last_kernel, norm_scale),
        out_shape=(
            shape(width, width, dtype=jnp.float32),
            shape(1, width, dtype=jnp.float32),
            shape(rows, width),
        ),
        in_specs=[vmem] * 5 + [hbm],
        out_specs=(hbm, vmem, hbm),
        scratch_shapes=[
            pltpu.VMEM((2 * rim, width), jnp.bfloat16),
            pltpu.VMEM((width, width), jnp.float32),
            pltpu.SemaphoreType.DMA((3,)),
        ],
        input_output_aliases={5: 2},
        compiler_params=params(8),
        name="last_step",
    )(own_half, other_half, edges, first_part, second_part, grad_whole)
    return (activated, grad_features, grad_weight, grad_bias.reshape(width))


def solution(mesh):
    return jax.shard_map(
        on_device,
        mesh=mesh,
        in_specs=(
            P(AXES, None),
            P(AXES, None, None, None),
            P(AXES, None),
            P(AXES),
            P(),
            P(),
            P(AXES, None),
        ),
        out_specs=(P(AXES, None), P(AXES, None), P(), P()),
        check_vma=False,
    )
```

```python
import functools
import math

import jax
import jax.numpy as jnp
from jax import lax
from jax.experimental import pallas as pl
from jax.experimental.pallas import tpu as pltpu
from jax.sharding import PartitionSpec as P

BAND = 2
TAIL = 16
AXES = ("rows", "cols")
MIB = 1024 * 1024


def row_of(adj_ref, block, slots):
    return jnp.concatenate([adj_ref[block, slot] for slot in range(slots)], 1)


def pick(source, places, block_rows):
    return jnp.concatenate(
        [
            source[pl.ds(pl.multiple_of(place * block_rows, block_rows), block_rows)]
            for place in places
        ],
        0,
    )


def write_places(off_ref, cnt_ref, place_ref, blocks, slots):
    for block in range(blocks):
        if block < BAND:
            shift, dump = BAND, 6 * BAND
        elif block < blocks - BAND:
            shift, dump = 0, blocks
        else:
            shift, dump = 5 * BAND - blocks, 6 * BAND
        for slot in range(slots):
            place_ref[block * slots + slot] = jnp.where(
                slot < cnt_ref[block], block + shift + off_ref[slot, block], dump
            )


def places_of(place_ref, block, slots):
    return [place_ref[block * slots + slot] for slot in range(slots)]


def rim_block(step, blocks):
    return step if step < BAND else blocks - 2 * BAND + step


def place_in_mesh():
    return lax.axis_index("rows") * lax.axis_size("cols") + lax.axis_index("cols")


def core_side():
    return lax.axis_index("rows") & 1


def halo_kernel(feat_hbm, first_ref, second_ref, sems):
    rows = feat_hbm.shape[0]
    rim = first_ref.shape[0]
    odd = place_in_mesh() & 1
    last = rows - rim
    starts = ((1 - odd) * last, odd * last)
    copies = [
        pltpu.make_async_copy(
            feat_hbm.at[pl.ds(pl.multiple_of(start, rim), rim)], out_ref, sems.at[i]
        )
        for i, (start, out_ref) in enumerate(zip(starts, (first_ref, second_ref)))
    ]
    for copy in copies:
        copy.start()
    for copy in copies:
        copy.wait()


def activate(preact, cotangent):
    gate = 1.0 / (1.0 + jnp.exp(-preact))
    grad = cotangent.astype(jnp.float32) * gate * (1.0 + preact * (1.0 - gate))
    return (preact * gate).astype(jnp.bfloat16), grad.astype(jnp.bfloat16)


def column_sums(grad):
    rows, width = grad.shape
    return jnp.sum(grad.astype(jnp.float32).reshape(rows // 8, 8, width), axis=0)


def to_upstream(weight, grad):
    return lax.dot_general(
        weight, grad, (((1,), (1,)), ((), ())), preferred_element_type=jnp.float32
    ).astype(jnp.bfloat16)


def weight_terms(agg, grad):
    return lax.dot_general(
        agg, grad, (((0,), (0,)), ((), ())), preferred_element_type=jnp.float32
    )


def inner_kernel(
    off_ref, cnt_ref, weight_hbm, bias_hbm, feat_hbm, adj_hbm, cot_hbm,
    act_hbm, place_ref, grad_ref, partial_ref, sums_ref, weight_ref, bias_ref, feat_rim, adj_rim,
    cot_rim, adj,
    feat, cot, act, agg_all, sems,
):
    blocks, slots, block_rows, _ = adj_hbm.shape
    rows, width = feat_hbm.shape
    count = blocks - 2 * BAND
    rim = BAND * block_rows
    half = 2 * rim
    inner = count * block_rows
    copies = [
        pltpu.make_async_copy(feat_hbm, feat.at[pl.ds(0, rows)], sems.at[0]),
        pltpu.make_async_copy(adj_hbm.at[pl.ds(BAND, count)], adj, sems.at[1]),
        pltpu.make_async_copy(weight_hbm, weight_ref, sems.at[2]),
        pltpu.make_async_copy(bias_hbm, bias_ref, sems.at[3]),
        pltpu.make_async_copy(cot_hbm.at[pl.ds(rim, inner)], cot, sems.at[4]),
        pltpu.make_async_copy(feat_hbm.at[pl.ds(0, half)], feat_rim.at[pl.ds(0, half)], sems.at[5]),
        pltpu.make_async_copy(
            feat_hbm.at[pl.ds(rows - half, half)], feat_rim.at[pl.ds(half, half)], sems.at[6]
        ),
        pltpu.make_async_copy(adj_hbm.at[pl.ds(0, BAND)], adj_rim.at[pl.ds(0, BAND)], sems.at[7]),
        pltpu.make_async_copy(
            adj_hbm.at[pl.ds(blocks - BAND, BAND)], adj_rim.at[pl.ds(BAND, BAND)], sems.at[8]
        ),
        pltpu.make_async_copy(cot_hbm.at[pl.ds(0, rim)], cot_rim.at[pl.ds(0, rim)], sems.at[9]),
        pltpu.make_async_copy(
            cot_hbm.at[pl.ds(rows - rim, rim)], cot_rim.at[pl.ds(rim, rim)], sems.at[10]
        ),
    ]
    for copy in copies:
        copy.start()
    feat[rows:] = jnp.zeros((block_rows, width), jnp.bfloat16)
    write_places(off_ref, cnt_ref, place_ref, blocks, slots)
    for copy in copies[:5]:
        copy.wait()
    weight = weight_ref[...]
    bias = bias_ref[...]
    sums = jnp.zeros((8, width), jnp.float32)
    for step in range(0, count, 2):
        for block in (step, step + 1):
            places = places_of(place_ref, block + BAND, slots)
            agg_all[block * block_rows : (block + 1) * block_rows] = jnp.dot(
                row_of(adj, block, slots), pick(feat, places, block_rows),
                preferred_element_type=jnp.float32,
            ).astype(jnp.bfloat16)
        here = pl.ds(step * block_rows, 2 * block_rows)
        preact = jnp.dot(agg_all[here], weight, preferred_element_type=jnp.float32) + bias
        act[here], grad = activate(preact, cot[here])
        grad_ref[here] = grad
        sums = sums + column_sums(grad)
    act_out = pltpu.make_async_copy(act, act_hbm.at[pl.ds(rim, inner)], sems.at[11])
    act_out.start()
    sums_ref[...] = sums
    partial_ref[...] = weight_terms(agg_all[...], grad_ref[...])
    for copy in copies[5:]:
        copy.wait()
    act_out.wait()


def rim_kernel(
    place_ref, weight_ref, bias_ref, feat_ref, first_ref, second_ref, adj_ref, cot_ref,
    partial_ref, sums_ref,
    act_ref, grad_ref, send_ref, keep_ref,
    window, agg_all, payload,
):
    steps, slots, block_rows, _ = adj_ref.shape
    blocks = place_ref.shape[0] // slots
    width = feat_ref.shape[1]
    rim = BAND * block_rows
    odd = place_in_mesh() & 1
    window[pl.ds(pl.multiple_of((1 - odd) * 5 * rim, rim), rim)] = first_ref[...]
    window[pl.ds(pl.multiple_of(odd * 5 * rim, rim), rim)] = second_ref[...]
    window[rim : 5 * rim] = feat_ref[...]
    window[6 * rim :] = jnp.zeros((block_rows, width), jnp.bfloat16)
    weight = weight_ref[...]
    bias = bias_ref[...]
    sums = sums_ref[...]
    for step in range(0, steps, 2):
        for block in (step, step + 1):
            places = places_of(place_ref, rim_block(block, blocks), slots)
            agg_all[block * block_rows : (block + 1) * block_rows] = jnp.dot(
                row_of(adj_ref, block, slots), pick(window, places, block_rows),
                preferred_element_type=jnp.float32,
            ).astype(jnp.bfloat16)
        here = pl.ds(step * block_rows, 2 * block_rows)
        preact = jnp.dot(agg_all[here], weight, preferred_element_type=jnp.float32) + bias
        act_ref[here], grad = activate(preact, cot_ref[here])
        grad_ref[here] = grad
        sums = sums + column_sums(grad)
    half = width // 2
    partial = partial_ref[...] + weight_terms(agg_all[...], grad_ref[...])
    payload[0, :half] = partial[:half]
    payload[1, :half] = partial[half:]
    tail = jnp.zeros((TAIL, width), jnp.float32)
    payload[0, half:] = jnp.broadcast_to(jnp.sum(sums, axis=0, keepdims=True), tail.shape)
    payload[1, half:] = tail
    side = core_side()
    keep_ref[...] = payload[side]
    send_ref[...] = payload[1 - side]


def scatter_rows(places, weight_ref, adj_ref, grad_ref, spread):
    _, slots, block_rows, _ = adj_ref.shape
    upstream = to_upstream(weight_ref[...], grad_ref[...])
    for step, targets in enumerate(places):
        terms = jnp.dot(
            upstream[:, step * block_rows : (step + 1) * block_rows],
            row_of(adj_ref, step, slots),
            preferred_element_type=jnp.float32,
        )
        for slot, target in enumerate(targets):
            spread[target] += terms[:, slot * block_rows : (slot + 1) * block_rows]


def rim_back_kernel(
    place_ref, weight_ref, adj_ref, grad_ref, act_ref, act_in,
    act_hbm, spread, first_ref, second_ref, mark_ref,
    sems,
):
    steps, slots, block_rows, _ = adj_ref.shape
    blocks = place_ref.shape[0] // slots
    rim = BAND * block_rows
    rows = blocks * block_rows
    copies = [
        pltpu.make_async_copy(act_ref.at[pl.ds(0, rim)], act_hbm.at[pl.ds(0, rim)], sems.at[0]),
        pltpu.make_async_copy(
            act_ref.at[pl.ds(rim, rim)], act_hbm.at[pl.ds(rows - rim, rim)], sems.at[1]
        ),
    ]
    for copy in copies:
        copy.start()
    spread[...] = jnp.zeros_like(spread)
    scatter_rows(
        [places_of(place_ref, rim_block(step, blocks), slots) for step in range(steps)],
        weight_ref, adj_ref, grad_ref, spread,
    )
    odd = place_in_mesh() & 1
    for block in range(BAND):
        here = pl.ds(block * block_rows, block_rows)
        first_ref[here] = spread[(1 - odd) * 5 * BAND + block].T.astype(jnp.bfloat16)
        second_ref[here] = spread[odd * 5 * BAND + block].T.astype(jnp.bfloat16)
    mark_ref[...] = jnp.zeros_like(mark_ref)
    for copy in copies:
        copy.wait()


def inner_back_kernel(
    place_ref, weight_ref, adj_ref, grad_ref, rim_spread,
    whole_hbm, edge_ref, mark_ref,
    spread, out, sems,
):
    count, slots, block_rows, _ = adj_ref.shape
    blocks = place_ref.shape[0] // slots
    rim = BAND * block_rows
    spread[: 2 * BAND] = rim_spread[BAND : 3 * BAND]
    spread[2 * BAND :] = jnp.zeros_like(spread[2 * BAND :])
    spread[blocks - 2 * BAND : blocks] = rim_spread[3 * BAND : 5 * BAND]
    mark_ref[...] = jnp.zeros_like(mark_ref)
    scatter_rows(
        [places_of(place_ref, step + BAND, slots) for step in range(count)],
        weight_ref, adj_ref, grad_ref, spread,
    )
    for step in range(count):
        here = pl.ds(step * block_rows, block_rows)
        out[here] = spread[BAND + step].T.astype(jnp.bfloat16)
    finish = pltpu.make_async_copy(out, whole_hbm.at[pl.ds(rim, count * block_rows)], sems.at[0])
    finish.start()
    for block in range(BAND):
        edge_ref[block * block_rows : (block + 1) * block_rows] = spread[block].T
        after = BAND + block
        edge_ref[after * block_rows : (after + 1) * block_rows] = spread[blocks - BAND + block].T
    finish.wait()


def add_kernel(parts, *refs):
    values = [ref[...].astype(jnp.float32) for ref in refs[:parts]]
    total = values[0] + values[1]
    if parts == 4:
        total = total + (values[2] + values[3])
    refs[-1][...] = total.astype(refs[-1].dtype)


def last_kernel(
    scale, own_ref, other_ref, edge_ref, first_ref, second_ref, whole_in,
    weight_out, bias_out, whole_hbm,
    out, sums, sems,
):
    half = sums.shape[0] // 2
    rim = first_ref.shape[0]
    rows = whole_hbm.shape[0]
    odd = place_in_mesh() & 1
    for base, spill_ref in (((1 - odd) * rim, first_ref), (odd * rim, second_ref)):
        here = pl.ds(pl.multiple_of(base, rim), rim)
        out[here] = (edge_ref[here] + spill_ref[...].astype(jnp.float32)).astype(jnp.bfloat16)
    copies = [
        pltpu.make_async_copy(out.at[pl.ds(0, rim)], whole_hbm.at[pl.ds(0, rim)], sems.at[0]),
        pltpu.make_async_copy(
            out.at[pl.ds(rim, rim)], whole_hbm.at[pl.ds(rows - rim, rim)], sems.at[1]
        ),
        pltpu.make_async_copy(sums, weight_out, sems.at[2]),
    ]
    for copy in copies[:2]:
        copy.start()
    side = core_side()
    own_rows = pl.ds(pl.multiple_of(side * half, half), half)
    other_rows = pl.ds(pl.multiple_of((1 - side) * half, half), half)
    sums[own_rows] = own_ref[:half] * scale
    sums[other_rows] = other_ref[:half] * scale
    copies[2].start()
    first = jnp.where(side == 0, own_ref[half : half + 1], other_ref[half : half + 1])
    bias_out[...] = first * scale
    for copy in copies:
        copy.wait()


def add(values, dtype, after=()):
    size = values[0].size
    return pl.pallas_call(
        functools.partial(add_kernel, len(values)),
        out_shape=jax.ShapeDtypeStruct(values[0].shape, dtype),
        in_specs=[pl.BlockSpec(memory_space=pltpu.VMEM)] * len(values)
        + [pl.BlockSpec(memory_space=pl.ANY)] * len(after),
        compiler_params=pltpu.CompilerParams(vmem_limit_bytes=2 * MIB),
        cost_estimate=pl.CostEstimate(
            flops=size * len(values), bytes_accessed=8 * size, transcendentals=0
        ),
        name="add_halves",
    )(*values, *after)


def swap(value, masks):
    pairs = [(i, i ^ mask) for i, mask in enumerate(masks) if mask]
    return lax.ppermute(value, AXES, pairs)


def with_next(value, count):
    pairs = [(i, i + 1 if i & 1 else i - 1) for i in range(1, count - 1)]
    return lax.ppermute(value, AXES, pairs)


def sum_halves(send, keep, count, core_bit, marks):
    others = [bit for bit in range(count.bit_length() - 1) if bit != core_bit]
    groups = [others[i : i + 2] for i in range(0, len(others), 2)]
    total = add([keep, swap(send, [1 << core_bit] * count)], jnp.bfloat16, marks.get("core", ()))
    for step in range(len(groups)):
        masks = []
        for group in (groups[step], groups[len(groups) - 1 - step]):
            if len(groups[0]) != len(groups[-1]):
                group = groups[step]
            low = 1 << group[0]
            masks.append((low, 1 << group[1], low | 1 << group[1]) if group[1:] else (low,))
        parts = [total] + [
            swap(total, [masks[(i >> core_bit) & 1][k] for i in range(count)])
            for k in range(len(masks[0]))
        ]
        last = step == len(groups) - 1
        name = "last" if last else step
        total = add(parts, jnp.float32 if last else jnp.bfloat16, marks.get(name, ()))
    return total


def on_device(features, adj_values, adj_offset, adj_count, weight, bias_vector, cotangent):
    blocks, slots = adj_offset.shape
    block_rows = adj_values.shape[2]
    rows, width = features.shape
    rim = BAND * block_rows
    inner = rows - 2 * rim
    cols = lax.axis_size("cols")
    count = lax.axis_size("rows") * cols
    smem = pl.BlockSpec(memory_space=pltpu.SMEM)
    vmem = pl.BlockSpec(memory_space=pltpu.VMEM)
    hbm = pl.BlockSpec(memory_space=pltpu.HBM)
    bias_row = bias_vector.reshape(1, width)

    def in_hbm(value):
        return pltpu.with_memory_space_constraint(value, pltpu.HBM)

    def shape(*sizes, dtype=jnp.bfloat16):
        return jax.ShapeDtypeStruct(sizes, dtype)

    def params(mib):
        return pltpu.CompilerParams(vmem_limit_bytes=mib * MIB)

    def cost(share):
        return pl.CostEstimate(
            flops=int(1.2e9 * share), bytes_accessed=int(6e6 * share),
            transcendentals=int(8e5 * share),
        )

    offsets = in_hbm(adj_offset.T)
    counts = in_hbm(adj_count)
    core_bit = cols.bit_length() - 1
    first_rim, second_rim = pl.pallas_call(
        halo_kernel,
        out_shape=(shape(rim, width), shape(rim, width)),
        in_specs=[hbm],
        out_specs=(vmem, vmem),
        scratch_shapes=[pltpu.SemaphoreType.DMA((2,))],
        compiler_params=params(2),
        cost_estimate=cost(0.05),
        name="halo_rows",
    )(in_hbm(features))
    first_halo = swap(first_rim, [1] * count)
    second_halo = with_next(second_rim, count)
    (
        activated, places, grad_inner, partial, sums, weight_near, bias_near, feat_rim, adj_rim,
        cot_rim, adj_inner,
    ) = pl.pallas_call(
        inner_kernel,
        out_shape=(
            shape(rows, width),
            shape(blocks * slots, dtype=jnp.int32),
            shape(inner, width),
            shape(width, width, dtype=jnp.float32),
            shape(8, width, dtype=jnp.float32),
            shape(width, width),
            shape(1, width, dtype=jnp.float32),
            shape(4 * rim, width),
            shape(2 * BAND, slots, block_rows, block_rows),
            shape(2 * rim, width),
            shape(blocks - 2 * BAND, slots, block_rows, block_rows),
        ),
        in_specs=[smem, smem] + [hbm] * 5,
        out_specs=(hbm, smem) + (vmem,) * 9,
        scratch_shapes=[
            pltpu.VMEM((rows + block_rows, width), jnp.bfloat16),
            pltpu.VMEM((inner, width), jnp.bfloat16),
            pltpu.VMEM((inner, width), jnp.bfloat16),
            pltpu.VMEM((inner, width), jnp.bfloat16),
            pltpu.SemaphoreType.DMA((12,)),
        ],
        compiler_params=params(20),
        cost_estimate=cost(0.5),
        name="inner_rows",
    )(
        offsets, counts,
        *(in_hbm(x) for x in (weight, bias_row, features, adj_values, cotangent)),
    )
    half_shape = (width // 2 + TAIL, width)
    act_rim, grad_rim, send, keep = pl.pallas_call(
        rim_kernel,
        out_shape=(
            shape(2 * rim, width),
            shape(2 * rim, width),
            shape(*half_shape, dtype=jnp.float32),
            shape(*half_shape, dtype=jnp.float32),
        ),
        in_specs=[smem] + [vmem] * 9,
        out_specs=(vmem,) * 4,
        scratch_shapes=[
            pltpu.VMEM((6 * rim + block_rows, width), jnp.bfloat16),
            pltpu.VMEM((2 * rim, width), jnp.bfloat16),
            pltpu.VMEM((2,) + half_shape, jnp.float32),
        ],
        compiler_params=params(12),
        cost_estimate=cost(0.2),
        name="rim_rows",
    )(
        places, weight_near, bias_near, feat_rim, first_halo, second_halo, adj_rim, cot_rim,
        partial, sums,
    )
    mark = shape(8, 128, dtype=jnp.float32)
    activated, rim_spread, first_spill, second_spill, first_mark = pl.pallas_call(
        rim_back_kernel,
        out_shape=(
            shape(rows, width),
            shape(6 * BAND + 1, width, block_rows, dtype=jnp.float32),
            shape(rim, width),
            shape(rim, width),
            mark,
        ),
        in_specs=[smem] + [vmem] * 4 + [hbm],
        out_specs=(hbm,) + (vmem,) * 4,
        scratch_shapes=[pltpu.SemaphoreType.DMA((2,))],
        input_output_aliases={5: 0},
        compiler_params=params(12),
        cost_estimate=cost(0.2),
        name="rim_rows_back",
    )(places, weight_near, adj_rim, grad_rim, act_rim, activated)
    first_part = swap(first_spill, [1] * count)
    second_part = with_next(second_spill, count)
    grad_whole, edges, second_mark = pl.pallas_call(
        inner_back_kernel,
        out_shape=(shape(rows, width), shape(2 * rim, width, dtype=jnp.float32), mark),
        in_specs=[smem] + [vmem] * 4,
        out_specs=(hbm, vmem, vmem),
        scratch_shapes=[
            pltpu.VMEM((blocks + 1, width, block_rows), jnp.float32),
            pltpu.VMEM((inner, width), jnp.bfloat16),
            pltpu.SemaphoreType.DMA((1,)),
        ],
        compiler_params=params(12),
        cost_estimate=cost(0.3),
        name="inner_rows_back",
    )(places, weight_near, adj_inner, grad_inner, rim_spread)
    marks = {"core": (first_mark,), "last": (second_mark, first_part, second_part)}
    own_half = sum_halves(send, keep, count, core_bit, marks)
    other_half = swap(own_half, [1 << core_bit] * count)
    norm_scale = 1.0 / math.sqrt(rows * count)
    grad_weight, grad_bias, grad_features = pl.pallas_call(
        functools.partial(last_kernel, norm_scale),
        out_shape=(
            shape(width, width, dtype=jnp.float32),
            shape(1, width, dtype=jnp.float32),
            shape(rows, width),
        ),
        in_specs=[vmem] * 5 + [hbm],
        out_specs=(hbm, vmem, hbm),
        scratch_shapes=[
            pltpu.VMEM((2 * rim, width), jnp.bfloat16),
            pltpu.VMEM((width, width), jnp.float32),
            pltpu.SemaphoreType.DMA((3,)),
        ],
        input_output_aliases={5: 2},
        compiler_params=params(8),
        name="last_step",
    )(own_half, other_half, edges, first_part, second_part, grad_whole)
    return (activated, grad_features, grad_weight, grad_bias.reshape(width))


def solution(mesh):
    return jax.shard_map(
        on_device,
        mesh=mesh,
        in_specs=(
            P(AXES, None),
            P(AXES, None, None, None),
            P(AXES, None),
            P(AXES),
            P(),
            P(),
            P(AXES, None),
        ),
        out_specs=(P(AXES, None), P(AXES, None), P(), P()),
        check_vma=False,
    )
```

```python
import functools
import math

import jax
import jax.numpy as jnp
from jax import lax
from jax.experimental import pallas as pl
from jax.experimental.pallas import tpu as pltpu
from jax.sharding import PartitionSpec as P

BAND = 2
TAIL = 16
AXES = ("rows", "cols")
MIB = 1024 * 1024


def row_of(adj_ref, block, slots):
    return jnp.concatenate([adj_ref[block, slot] for slot in range(slots)], 1)


def pick(source, places, block_rows):
    return jnp.concatenate(
        [
            source[pl.ds(pl.multiple_of(place * block_rows, block_rows), block_rows)]
            for place in places
        ],
        0,
    )


def write_places(off_ref, cnt_ref, place_ref, blocks, slots):
    for block in range(blocks):
        if block < BAND:
            shift, dump = BAND, 6 * BAND
        elif block < blocks - BAND:
            shift, dump = 0, blocks
        else:
            shift, dump = 5 * BAND - blocks, 6 * BAND
        for slot in range(slots):
            place_ref[block * slots + slot] = jnp.where(
                slot < cnt_ref[block], block + shift + off_ref[slot, block], dump
            )


def places_of(place_ref, block, slots):
    return [place_ref[block * slots + slot] for slot in range(slots)]


def rim_block(step, blocks):
    return step if step < BAND else blocks - 2 * BAND + step


def place_in_mesh():
    return lax.axis_index("rows") * lax.axis_size("cols") + lax.axis_index("cols")


def core_side():
    return lax.axis_index("rows") & 1


def halo_kernel(feat_hbm, first_ref, second_ref, sems):
    rows = feat_hbm.shape[0]
    rim = first_ref.shape[0]
    odd = place_in_mesh() & 1
    last = rows - rim
    starts = ((1 - odd) * last, odd * last)
    copies = [
        pltpu.make_async_copy(
            feat_hbm.at[pl.ds(pl.multiple_of(start, rim), rim)], out_ref, sems.at[i]
        )
        for i, (start, out_ref) in enumerate(zip(starts, (first_ref, second_ref)))
    ]
    for copy in copies:
        copy.start()
    for copy in copies:
        copy.wait()


def activate(preact, cotangent):
    gate = 1.0 / (1.0 + jnp.exp(-preact))
    grad = cotangent.astype(jnp.float32) * gate * (1.0 + preact * (1.0 - gate))
    return (preact * gate).astype(jnp.bfloat16), grad.astype(jnp.bfloat16)


def column_sums(grad):
    rows, width = grad.shape
    return jnp.sum(grad.astype(jnp.float32).reshape(rows // 8, 8, width), axis=0)


def to_upstream(weight, grad):
    return lax.dot_general(
        weight, grad, (((1,), (1,)), ((), ())), preferred_element_type=jnp.float32
    ).astype(jnp.bfloat16)


def weight_terms(agg, grad):
    return lax.dot_general(
        agg, grad, (((0,), (0,)), ((), ())), preferred_element_type=jnp.float32
    )


def inner_kernel(
    off_hbm, cnt_hbm, weight_hbm, bias_hbm, feat_hbm, adj_hbm, cot_hbm,
    act_hbm, place_out, grad_ref, partial_ref, sums_ref, weight_ref, bias_ref, feat_rim, adj_rim,
    cot_rim, adj,
    off_ref, cnt_ref, place_ref, feat, cot, act, agg_all, sems,
):
    blocks, slots, block_rows, _ = adj_hbm.shape
    rows, width = feat_hbm.shape
    count = blocks - 2 * BAND
    rim = BAND * block_rows
    half = 2 * rim
    inner = count * block_rows
    scalars = [
        pltpu.make_async_copy(off_hbm, off_ref, sems.at[12]),
        pltpu.make_async_copy(cnt_hbm, cnt_ref, sems.at[13]),
    ]
    copies = [
        pltpu.make_async_copy(feat_hbm, feat.at[pl.ds(0, rows)], sems.at[0]),
        pltpu.make_async_copy(adj_hbm.at[pl.ds(BAND, count)], adj, sems.at[1]),
        pltpu.make_async_copy(weight_hbm, weight_ref, sems.at[2]),
        pltpu.make_async_copy(bias_hbm, bias_ref, sems.at[3]),
        pltpu.make_async_copy(cot_hbm.at[pl.ds(rim, inner)], cot, sems.at[4]),
        pltpu.make_async_copy(feat_hbm.at[pl.ds(0, half)], feat_rim.at[pl.ds(0, half)], sems.at[5]),
        pltpu.make_async_copy(
            feat_hbm.at[pl.ds(rows - half, half)], feat_rim.at[pl.ds(half, half)], sems.at[6]
        ),
        pltpu.make_async_copy(adj_hbm.at[pl.ds(0, BAND)], adj_rim.at[pl.ds(0, BAND)], sems.at[7]),
        pltpu.make_async_copy(
            adj_hbm.at[pl.ds(blocks - BAND, BAND)], adj_rim.at[pl.ds(BAND, BAND)], sems.at[8]
        ),
        pltpu.make_async_copy(cot_hbm.at[pl.ds(0, rim)], cot_rim.at[pl.ds(0, rim)], sems.at[9]),
        pltpu.make_async_copy(
            cot_hbm.at[pl.ds(rows - rim, rim)], cot_rim.at[pl.ds(rim, rim)], sems.at[10]
        ),
    ]
    for copy in scalars + copies:
        copy.start()
    feat[rows:] = jnp.zeros((block_rows, width), jnp.bfloat16)
    for copy in scalars:
        copy.wait()
    write_places(off_ref, cnt_ref, place_ref, blocks, slots)
    place_copy = pltpu.make_async_copy(place_ref, place_out, sems.at[14])
    place_copy.start()
    for copy in copies[:5]:
        copy.wait()
    weight = weight_ref[...]
    bias = bias_ref[...]
    sums = jnp.zeros((8, width), jnp.float32)
    for step in range(0, count, 2):
        for block in (step, step + 1):
            places = places_of(place_ref, block + BAND, slots)
            agg_all[block * block_rows : (block + 1) * block_rows] = jnp.dot(
                row_of(adj, block, slots), pick(feat, places, block_rows),
                preferred_element_type=jnp.float32,
            ).astype(jnp.bfloat16)
        here = pl.ds(step * block_rows, 2 * block_rows)
        preact = jnp.dot(agg_all[here], weight, preferred_element_type=jnp.float32) + bias
        act[here], grad = activate(preact, cot[here])
        grad_ref[here] = grad
        sums = sums + column_sums(grad)
    act_out = pltpu.make_async_copy(act, act_hbm.at[pl.ds(rim, inner)], sems.at[11])
    act_out.start()
    sums_ref[...] = sums
    partial_ref[...] = weight_terms(agg_all[...], grad_ref[...])
    for copy in copies[5:]:
        copy.wait()
    act_out.wait()
    place_copy.wait()


def rim_kernel(
    place_in, weight_ref, bias_ref, feat_ref, first_ref, second_ref, adj_ref, cot_ref,
    partial_ref, sums_ref,
    act_ref, grad_ref, send_ref, keep_ref,
    place_ref, window, agg_all, payload, sems,
):
    fetch = pltpu.make_async_copy(place_in, place_ref, sems.at[0])
    fetch.start()
    steps, slots, block_rows, _ = adj_ref.shape
    blocks = place_ref.shape[0] // slots
    width = feat_ref.shape[1]
    rim = BAND * block_rows
    odd = place_in_mesh() & 1
    window[pl.ds(pl.multiple_of((1 - odd) * 5 * rim, rim), rim)] = first_ref[...]
    window[pl.ds(pl.multiple_of(odd * 5 * rim, rim), rim)] = second_ref[...]
    window[rim : 5 * rim] = feat_ref[...]
    window[6 * rim :] = jnp.zeros((block_rows, width), jnp.bfloat16)
    weight = weight_ref[...]
    bias = bias_ref[...]
    sums = sums_ref[...]
    fetch.wait()
    for step in range(0, steps, 2):
        for block in (step, step + 1):
            places = places_of(place_ref, rim_block(block, blocks), slots)
            agg_all[block * block_rows : (block + 1) * block_rows] = jnp.dot(
                row_of(adj_ref, block, slots), pick(window, places, block_rows),
                preferred_element_type=jnp.float32,
            ).astype(jnp.bfloat16)
        here = pl.ds(step * block_rows, 2 * block_rows)
        preact = jnp.dot(agg_all[here], weight, preferred_element_type=jnp.float32) + bias
        act_ref[here], grad = activate(preact, cot_ref[here])
        grad_ref[here] = grad
        sums = sums + column_sums(grad)
    half = width // 2
    partial = partial_ref[...] + weight_terms(agg_all[...], grad_ref[...])
    payload[0, :half] = partial[:half]
    payload[1, :half] = partial[half:]
    tail = jnp.zeros((TAIL, width), jnp.float32)
    payload[0, half:] = jnp.broadcast_to(jnp.sum(sums, axis=0, keepdims=True), tail.shape)
    payload[1, half:] = tail
    side = core_side()
    keep_ref[...] = payload[side]
    send_ref[...] = payload[1 - side]


def scatter_rows(places, upstream, adj_ref, spread):
    _, slots, block_rows, _ = adj_ref.shape
    for step, targets in enumerate(places):
        terms = jnp.dot(
            upstream[:, step * block_rows : (step + 1) * block_rows],
            row_of(adj_ref, step, slots),
            preferred_element_type=jnp.float32,
        )
        for slot, target in enumerate(targets):
            spread[target] += terms[:, slot * block_rows : (slot + 1) * block_rows]


def rim_back_kernel(
    place_in, weight_ref, adj_ref, grad_ref, act_ref, act_in,
    act_hbm, spread, first_ref, second_ref, mark_ref,
    place_ref, sems,
):
    fetch = pltpu.make_async_copy(place_in, place_ref, sems.at[2])
    fetch.start()
    steps, slots, block_rows, _ = adj_ref.shape
    blocks = place_ref.shape[0] // slots
    rim = BAND * block_rows
    rows = blocks * block_rows
    copies = [
        pltpu.make_async_copy(act_ref.at[pl.ds(0, rim)], act_hbm.at[pl.ds(0, rim)], sems.at[0]),
        pltpu.make_async_copy(
            act_ref.at[pl.ds(rim, rim)], act_hbm.at[pl.ds(rows - rim, rim)], sems.at[1]
        ),
    ]
    for copy in copies:
        copy.start()
    spread[...] = jnp.zeros_like(spread)
    upstream = to_upstream(weight_ref[...], grad_ref[...])
    fetch.wait()
    scatter_rows(
        [places_of(place_ref, rim_block(step, blocks), slots) for step in range(steps)],
        upstream, adj_ref, spread,
    )
    odd = place_in_mesh() & 1
    for block in range(BAND):
        here = pl.ds(block * block_rows, block_rows)
        first_ref[here] = spread[(1 - odd) * 5 * BAND + block].T.astype(jnp.bfloat16)
        second_ref[here] = spread[odd * 5 * BAND + block].T.astype(jnp.bfloat16)
    mark_ref[...] = jnp.zeros_like(mark_ref)
    for copy in copies:
        copy.wait()


def inner_back_kernel(
    place_in, weight_ref, adj_ref, grad_ref, rim_spread,
    whole_hbm, edge_ref,
    place_ref, spread, out, sems,
):
    fetch = pltpu.make_async_copy(place_in, place_ref, sems.at[1])
    fetch.start()
    count, slots, block_rows, _ = adj_ref.shape
    blocks = place_ref.shape[0] // slots
    rim = BAND * block_rows
    spread[: 2 * BAND] = rim_spread[BAND : 3 * BAND]
    spread[2 * BAND :] = jnp.zeros_like(spread[2 * BAND :])
    spread[blocks - 2 * BAND : blocks] = rim_spread[3 * BAND : 5 * BAND]
    upstream = to_upstream(weight_ref[...], grad_ref[...])
    fetch.wait()
    scatter_rows(
        [places_of(place_ref, step + BAND, slots) for step in range(count)],
        upstream, adj_ref, spread,
    )
    for step in range(count):
        here = pl.ds(step * block_rows, block_rows)
        out[here] = spread[BAND + step].T.astype(jnp.bfloat16)
    finish = pltpu.make_async_copy(out, whole_hbm.at[pl.ds(rim, count * block_rows)], sems.at[0])
    finish.start()
    for block in range(BAND):
        edge_ref[block * block_rows : (block + 1) * block_rows] = spread[block].T
        after = BAND + block
        edge_ref[after * block_rows : (after + 1) * block_rows] = spread[blocks - BAND + block].T
    finish.wait()


def add_kernel(parts, *refs):
    values = [ref[...].astype(jnp.float32) for ref in refs[:parts]]
    total = values[0] + values[1]
    if parts == 4:
        total = total + (values[2] + values[3])
    refs[-1][...] = total.astype(refs[-1].dtype)


def last_kernel(
    scale, own_ref, other_ref, edge_ref, first_ref, second_ref, whole_in,
    weight_out, bias_out, whole_hbm,
    out, sums, bias, sems,
):
    half = sums.shape[0] // 2
    rim = first_ref.shape[0]
    rows = whole_hbm.shape[0]
    copies = [
        pltpu.make_async_copy(sums, weight_out, sems.at[0]),
        pltpu.make_async_copy(bias, bias_out, sems.at[1]),
        pltpu.make_async_copy(out.at[pl.ds(0, rim)], whole_hbm.at[pl.ds(0, rim)], sems.at[2]),
        pltpu.make_async_copy(
            out.at[pl.ds(rim, rim)], whole_hbm.at[pl.ds(rows - rim, rim)], sems.at[3]
        ),
    ]
    side = core_side()
    own_rows = pl.ds(pl.multiple_of(side * half, half), half)
    other_rows = pl.ds(pl.multiple_of((1 - side) * half, half), half)
    sums[own_rows] = own_ref[:half] * scale
    sums[other_rows] = other_ref[:half] * scale
    copies[0].start()
    first = jnp.where(side == 0, own_ref[half : half + 1], other_ref[half : half + 1])
    bias[...] = first * scale
    copies[1].start()
    odd = place_in_mesh() & 1
    for base, spill_ref in (((1 - odd) * rim, first_ref), (odd * rim, second_ref)):
        here = pl.ds(pl.multiple_of(base, rim), rim)
        out[here] = (edge_ref[here] + spill_ref[...].astype(jnp.float32)).astype(jnp.bfloat16)
    for copy in copies[2:]:
        copy.start()
    for copy in copies:
        copy.wait()


def add(values, dtype, after=()):
    size = values[0].size
    return pl.pallas_call(
        functools.partial(add_kernel, len(values)),
        out_shape=jax.ShapeDtypeStruct(values[0].shape, dtype),
        in_specs=[pl.BlockSpec(memory_space=pltpu.VMEM)] * len(values)
        + [pl.BlockSpec(memory_space=pl.ANY)] * len(after),
        compiler_params=pltpu.CompilerParams(vmem_limit_bytes=2 * MIB),
        cost_estimate=pl.CostEstimate(
            flops=size * len(values), bytes_accessed=8 * size, transcendentals=0
        ),
        name="add_halves",
    )(*values, *after)


def swap(value, masks):
    pairs = [(i, i ^ mask) for i, mask in enumerate(masks) if mask]
    return lax.ppermute(value, AXES, pairs)


def with_next(value, count):
    pairs = [(i, i + 1 if i & 1 else i - 1) for i in range(1, count - 1)]
    return lax.ppermute(value, AXES, pairs)


def sum_halves(send, keep, count, core_bit, marks):
    others = [bit for bit in range(count.bit_length() - 1) if bit != core_bit]
    groups = [others[i : i + 2] for i in range(0, len(others), 2)]
    total = add([keep, swap(send, [1 << core_bit] * count)], jnp.bfloat16, marks.get("core", ()))
    for step in range(len(groups)):
        masks = []
        for group in (groups[step], groups[len(groups) - 1 - step]):
            if len(groups[0]) != len(groups[-1]):
                group = groups[step]
            low = 1 << group[0]
            masks.append((low, 1 << group[1], low | 1 << group[1]) if group[1:] else (low,))
        parts = [total] + [
            swap(total, [masks[(i >> core_bit) & 1][k] for i in range(count)])
            for k in range(len(masks[0]))
        ]
        last = step == len(groups) - 1
        name = "last" if last else step
        total = add(parts, jnp.float32 if last else jnp.bfloat16, marks.get(name, ()))
    return total


def on_device(features, adj_values, adj_offset, adj_count, weight, bias_vector, cotangent):
    blocks, slots = adj_offset.shape
    block_rows = adj_values.shape[2]
    rows, width = features.shape
    rim = BAND * block_rows
    inner = rows - 2 * rim
    cols = lax.axis_size("cols")
    count = lax.axis_size("rows") * cols
    vmem = pl.BlockSpec(memory_space=pltpu.VMEM)
    hbm = pl.BlockSpec(memory_space=pltpu.HBM)
    anywhere = pl.BlockSpec(memory_space=pl.ANY)
    place_scratch = pltpu.SMEM((blocks * slots,), jnp.int32)
    bias_row = bias_vector.reshape(1, width)

    def in_hbm(value):
        return pltpu.with_memory_space_constraint(value, pltpu.HBM)

    def shape(*sizes, dtype=jnp.bfloat16):
        return jax.ShapeDtypeStruct(sizes, dtype)

    def params(mib):
        return pltpu.CompilerParams(vmem_limit_bytes=mib * MIB)

    def cost(share):
        return pl.CostEstimate(
            flops=int(1.2e9 * share), bytes_accessed=int(6e6 * share),
            transcendentals=int(8e5 * share),
        )

    offsets = in_hbm(adj_offset.T)
    counts = in_hbm(adj_count)
    core_bit = cols.bit_length() - 1
    first_rim, second_rim = pl.pallas_call(
        halo_kernel,
        out_shape=(shape(rim, width), shape(rim, width)),
        in_specs=[hbm],
        out_specs=(vmem, vmem),
        scratch_shapes=[pltpu.SemaphoreType.DMA((2,))],
        compiler_params=params(2),
        cost_estimate=cost(0.05),
        name="halo_rows",
    )(in_hbm(features))
    first_halo = swap(first_rim, [1] * count)
    second_halo = with_next(second_rim, count)
    (
        activated, places, grad_inner, partial, sums, weight_near, bias_near, feat_rim, adj_rim,
        cot_rim, adj_inner,
    ) = pl.pallas_call(
        inner_kernel,
        out_shape=(
            shape(rows, width),
            shape(blocks * slots, dtype=jnp.int32),
            shape(inner, width),
            shape(width, width, dtype=jnp.float32),
            shape(8, width, dtype=jnp.float32),
            shape(width, width),
            shape(1, width, dtype=jnp.float32),
            shape(4 * rim, width),
            shape(2 * BAND, slots, block_rows, block_rows),
            shape(2 * rim, width),
            shape(blocks - 2 * BAND, slots, block_rows, block_rows),
        ),
        in_specs=[hbm] * 7,
        out_specs=(hbm, anywhere) + (vmem,) * 9,
        scratch_shapes=[
            pltpu.SMEM((slots, blocks), jnp.int32),
            pltpu.SMEM((blocks,), jnp.int32),
            place_scratch,
            pltpu.VMEM((rows + block_rows, width), jnp.bfloat16),
            pltpu.VMEM((inner, width), jnp.bfloat16),
            pltpu.VMEM((inner, width), jnp.bfloat16),
            pltpu.VMEM((inner, width), jnp.bfloat16),
            pltpu.SemaphoreType.DMA((15,)),
        ],
        compiler_params=params(20),
        cost_estimate=cost(0.5),
        name="inner_rows",
    )(
        offsets, counts,
        *(in_hbm(x) for x in (weight, bias_row, features, adj_values, cotangent)),
    )
    half_shape = (width // 2 + TAIL, width)
    act_rim, grad_rim, send, keep = pl.pallas_call(
        rim_kernel,
        out_shape=(
            shape(2 * rim, width),
            shape(2 * rim, width),
            shape(*half_shape, dtype=jnp.float32),
            shape(*half_shape, dtype=jnp.float32),
        ),
        in_specs=[anywhere] + [vmem] * 9,
        out_specs=(vmem,) * 4,
        scratch_shapes=[
            place_scratch,
            pltpu.VMEM((6 * rim + block_rows, width), jnp.bfloat16),
            pltpu.VMEM((2 * rim, width), jnp.bfloat16),
            pltpu.VMEM((2,) + half_shape, jnp.float32),
            pltpu.SemaphoreType.DMA((1,)),
        ],
        compiler_params=params(12),
        cost_estimate=cost(0.2),
        name="rim_rows",
    )(
        places, weight_near, bias_near, feat_rim, first_halo, second_halo, adj_rim, cot_rim,
        partial, sums,
    )
    mark = shape(8, 128, dtype=jnp.float32)
    activated, rim_spread, first_spill, second_spill, first_mark = pl.pallas_call(
        rim_back_kernel,
        out_shape=(
            shape(rows, width),
            shape(6 * BAND + 1, width, block_rows, dtype=jnp.float32),
            shape(rim, width),
            shape(rim, width),
            mark,
        ),
        in_specs=[anywhere] + [vmem] * 4 + [hbm],
        out_specs=(hbm,) + (vmem,) * 4,
        scratch_shapes=[place_scratch, pltpu.SemaphoreType.DMA((3,))],
        input_output_aliases={5: 0},
        compiler_params=params(12),
        cost_estimate=cost(0.2),
        name="rim_rows_back",
    )(places, weight_near, adj_rim, grad_rim, act_rim, activated)
    first_part = swap(first_spill, [1] * count)
    second_part = with_next(second_spill, count)
    grad_whole, edges = pl.pallas_call(
        inner_back_kernel,
        out_shape=(shape(rows, width), shape(2 * rim, width, dtype=jnp.float32)),
        in_specs=[anywhere] + [vmem] * 4,
        out_specs=(hbm, vmem),
        scratch_shapes=[
            place_scratch,
            pltpu.VMEM((blocks + 1, width, block_rows), jnp.float32),
            pltpu.VMEM((inner, width), jnp.bfloat16),
            pltpu.SemaphoreType.DMA((2,)),
        ],
        compiler_params=params(12),
        cost_estimate=cost(2.0),
        name="inner_rows_back",
    )(places, weight_near, adj_inner, grad_inner, rim_spread)
    marks = {0: (first_mark,)}
    own_half = sum_halves(send, keep, count, core_bit, marks)
    other_half = swap(own_half, [1 << core_bit] * count)
    norm_scale = 1.0 / math.sqrt(rows * count)
    grad_weight, grad_bias, grad_features = pl.pallas_call(
        functools.partial(last_kernel, norm_scale),
        out_shape=(
            shape(width, width, dtype=jnp.float32),
            shape(1, width, dtype=jnp.float32),
            shape(rows, width),
        ),
        in_specs=[vmem] * 5 + [hbm],
        out_specs=(hbm, hbm, hbm),
        scratch_shapes=[
            pltpu.VMEM((2 * rim, width), jnp.bfloat16),
            pltpu.VMEM((width, width), jnp.float32),
            pltpu.VMEM((1, width), jnp.float32),
            pltpu.SemaphoreType.DMA((4,)),
        ],
        input_output_aliases={5: 2},
        compiler_params=params(8),
        name="last_step",
    )(own_half, other_half, edges, first_part, second_part, grad_whole)
    return (activated, grad_features, grad_weight, grad_bias.reshape(width))


def solution(mesh):
    return jax.shard_map(
        on_device,
        mesh=mesh,
        in_specs=(
            P(AXES, None),
            P(AXES, None, None, None),
            P(AXES, None),
            P(AXES),
            P(),
            P(),
            P(AXES, None),
        ),
        out_specs=(P(AXES, None), P(AXES, None), P(), P()),
        check_vma=False,
    )
```

```python
import functools
import math

import jax
import jax.numpy as jnp
from jax import lax
from jax.experimental import pallas as pl
from jax.experimental.pallas import tpu as pltpu
from jax.sharding import PartitionSpec as P

BAND = 2
TAIL = 16
AXES = ("rows", "cols")
MIB = 1024 * 1024


def row_of(adj_ref, block, slots):
    return jnp.concatenate([adj_ref[block, slot] for slot in range(slots)], 1)


def pick(source, places, block_rows):
    return jnp.concatenate(
        [
            source[pl.ds(pl.multiple_of(place * block_rows, block_rows), block_rows)]
            for place in places
        ],
        0,
    )


def write_places(off_ref, cnt_ref, place_ref, blocks, slots):
    for block in range(blocks):
        if block < BAND:
            shift, dump = BAND, 6 * BAND
        elif block < blocks - BAND:
            shift, dump = 0, blocks
        else:
            shift, dump = 5 * BAND - blocks, 6 * BAND
        for slot in range(slots):
            place_ref[block * slots + slot] = jnp.where(
                slot < cnt_ref[block], block + shift + off_ref[slot, block], dump
            )


def places_of(place_ref, block, slots):
    return [place_ref[block * slots + slot] for slot in range(slots)]


def place_in_mesh():
    return lax.axis_index("rows") * lax.axis_size("cols") + lax.axis_index("cols")


def core_side():
    return lax.axis_index("rows") & 1


def rim_start(rows, rim, order):
    odd = place_in_mesh() & 1
    return pl.multiple_of((odd if order else 1 - odd) * (rows - rim), rim)


def halo_kernel(feat_hbm, first_ref, sems):
    rows = feat_hbm.shape[0]
    rim = first_ref.shape[0]
    copy = pltpu.make_async_copy(
        feat_hbm.at[pl.ds(rim_start(rows, rim, 0), rim)], first_ref, sems.at[0]
    )
    copy.start()
    copy.wait()


def activate(preact, cotangent):
    gate = 1.0 / (1.0 + jnp.exp(-preact))
    grad = cotangent.astype(jnp.float32) * gate * (1.0 + preact * (1.0 - gate))
    return (preact * gate).astype(jnp.bfloat16), grad.astype(jnp.bfloat16)


def column_sums(grad):
    rows, width = grad.shape
    return jnp.sum(grad.astype(jnp.float32).reshape(rows // 8, 8, width), axis=0)


def to_upstream(weight, grad):
    return lax.dot_general(
        weight, grad, (((1,), (1,)), ((), ())), preferred_element_type=jnp.float32
    ).astype(jnp.bfloat16)


def weight_terms(agg, grad):
    return lax.dot_general(
        agg, grad, (((0,), (0,)), ((), ())), preferred_element_type=jnp.float32
    )


def forward_rows(place_ref, blocks, source, adj, weight, bias, cot, act, grad_ref, agg_all):
    _, slots, block_rows, _ = adj.shape
    sums = jnp.zeros((8, grad_ref.shape[1]), jnp.float32)
    for step in range(0, len(blocks), 2):
        for i in (step, step + 1):
            agg_all[i * block_rows : (i + 1) * block_rows] = jnp.dot(
                row_of(adj, blocks[i], slots),
                pick(source, places_of(place_ref, blocks[i], slots), block_rows),
                preferred_element_type=jnp.float32,
            ).astype(jnp.bfloat16)
        here = pl.ds(step * block_rows, 2 * block_rows)
        there = pl.ds(blocks[step] * block_rows, 2 * block_rows)
        preact = jnp.dot(agg_all[here], weight, preferred_element_type=jnp.float32) + bias
        act[here], grad = activate(preact, cot[there])
        grad_ref[here] = grad
        sums = sums + column_sums(grad)
    return sums


def inner_first_kernel(
    off_hbm, cnt_hbm, weight_hbm, bias_hbm, feat_hbm, adj_hbm, cot_hbm,
    place_out, second_ref, weight_ref, bias_ref, feat, adj, cot, act_ref, grad_ref, agg_ref,
    sums_ref,
    off_ref, cnt_ref, place_ref, sems,
):
    blocks, slots, block_rows, _ = adj_hbm.shape
    rows, width = feat_hbm.shape
    rim = BAND * block_rows
    split = blocks // 2
    cut = split * block_rows
    scalars = [
        pltpu.make_async_copy(off_hbm, off_ref, sems.at[0]),
        pltpu.make_async_copy(cnt_hbm, cnt_ref, sems.at[1]),
    ]
    early = [
        pltpu.make_async_copy(feat_hbm, feat.at[pl.ds(0, rows)], sems.at[2]),
        pltpu.make_async_copy(
            adj_hbm.at[pl.ds(0, split)], adj.at[pl.ds(0, split)], sems.at[3]
        ),
        pltpu.make_async_copy(weight_hbm, weight_ref, sems.at[4]),
        pltpu.make_async_copy(bias_hbm, bias_ref, sems.at[5]),
        pltpu.make_async_copy(cot_hbm.at[pl.ds(0, cut)], cot.at[pl.ds(0, cut)], sems.at[6]),
    ]
    late = [
        pltpu.make_async_copy(
            adj_hbm.at[pl.ds(split, blocks - split)], adj.at[pl.ds(split, blocks - split)],
            sems.at[7],
        ),
        pltpu.make_async_copy(
            cot_hbm.at[pl.ds(cut, rows - cut)], cot.at[pl.ds(cut, rows - cut)], sems.at[8]
        ),
    ]
    for copy in scalars + early + late:
        copy.start()
    feat[rows:] = jnp.zeros((block_rows, width), jnp.bfloat16)
    for copy in scalars:
        copy.wait()
    write_places(off_ref, cnt_ref, place_ref, blocks, slots)
    place_copy = pltpu.make_async_copy(place_ref, place_out, sems.at[9])
    place_copy.start()
    for copy in early:
        copy.wait()
    second_ref[...] = feat[pl.ds(rim_start(rows, rim, 1), rim)]
    sums_ref[...] = forward_rows(
        place_ref, range(BAND, split), feat, adj, weight_ref[...], bias_ref[...], cot, act_ref,
        grad_ref, agg_ref,
    )
    place_copy.wait()
    for copy in late:
        copy.wait()


def inner_second_kernel(
    place_in, weight_ref, bias_ref, feat, adj, cot, act_first, grad_first, agg_first, sums_first,
    act_hbm, grad_ref, partial_ref, sums_ref,
    place_ref, act, agg_all, sems,
):
    blocks, _, block_rows, _ = adj.shape
    rim = BAND * block_rows
    rows = blocks * block_rows
    cut = blocks // 2 * block_rows
    copies = [
        pltpu.make_async_copy(act_first, act_hbm.at[pl.ds(rim, cut - rim)], sems.at[0]),
        pltpu.make_async_copy(act, act_hbm.at[pl.ds(cut, rows - rim - cut)], sems.at[1]),
    ]
    fetch = pltpu.make_async_copy(place_in, place_ref, sems.at[2])
    fetch.start()
    copies[0].start()
    partial = weight_terms(agg_first[...], grad_first[...])
    fetch.wait()
    sums = forward_rows(
        place_ref, range(blocks // 2, blocks - BAND), feat, adj, weight_ref[...], bias_ref[...],
        cot, act, grad_ref, agg_all,
    )
    copies[1].start()
    sums_ref[...] = sums_first[...] + sums
    partial_ref[...] = partial + weight_terms(agg_all[...], grad_ref[...])
    for copy in copies:
        copy.wait()


def rim_kernel(
    place_in, weight_ref, bias_ref, feat, first_ref, second_ref, adj, cot, partial_ref, sums_ref,
    act_ref, grad_ref, send_ref, keep_ref,
    place_ref, window, agg_all, payload, sems,
):
    fetch = pltpu.make_async_copy(place_in, place_ref, sems.at[0])
    fetch.start()
    blocks, _, block_rows, _ = adj.shape
    width = feat.shape[1]
    rim = BAND * block_rows
    rows = blocks * block_rows
    odd = place_in_mesh() & 1
    window[pl.ds(pl.multiple_of((1 - odd) * 5 * rim, rim), rim)] = first_ref[...]
    window[pl.ds(pl.multiple_of(odd * 5 * rim, rim), rim)] = second_ref[...]
    window[rim : 3 * rim] = feat[: 2 * rim]
    window[3 * rim : 5 * rim] = feat[rows - 2 * rim : rows]
    window[6 * rim :] = jnp.zeros((block_rows, width), jnp.bfloat16)
    fetch.wait()
    rim_blocks = [*range(BAND), *range(blocks - BAND, blocks)]
    sums = sums_ref[...] + forward_rows(
        place_ref, rim_blocks, window, adj, weight_ref[...], bias_ref[...], cot, act_ref,
        grad_ref, agg_all,
    )
    half = width // 2
    partial = partial_ref[...] + weight_terms(agg_all[...], grad_ref[...])
    payload[0, :half] = partial[:half]
    payload[1, :half] = partial[half:]
    tail = jnp.zeros((TAIL, width), jnp.float32)
    payload[0, half:] = jnp.broadcast_to(jnp.sum(sums, axis=0, keepdims=True), tail.shape)
    payload[1, half:] = tail
    side = core_side()
    keep_ref[...] = payload[side]
    send_ref[...] = payload[1 - side]


def scatter_rows(place_ref, blocks, upstream, adj, spread):
    _, slots, block_rows, _ = adj.shape
    for step, block in enumerate(blocks):
        terms = jnp.dot(
            upstream[:, step * block_rows : (step + 1) * block_rows],
            row_of(adj, block, slots),
            preferred_element_type=jnp.float32,
        )
        for slot, target in enumerate(places_of(place_ref, block, slots)):
            spread[target] += terms[:, slot * block_rows : (slot + 1) * block_rows]


def rim_back_kernel(
    place_in, weight_ref, adj, grad_ref, act_ref, act_in,
    act_hbm, spread, first_ref, second_ref, mark_ref,
    place_ref, sems,
):
    fetch = pltpu.make_async_copy(place_in, place_ref, sems.at[2])
    fetch.start()
    blocks, _, block_rows, _ = adj.shape
    rim = BAND * block_rows
    rows = blocks * block_rows
    copies = [
        pltpu.make_async_copy(act_ref.at[pl.ds(0, rim)], act_hbm.at[pl.ds(0, rim)], sems.at[0]),
        pltpu.make_async_copy(
            act_ref.at[pl.ds(rim, rim)], act_hbm.at[pl.ds(rows - rim, rim)], sems.at[1]
        ),
    ]
    for copy in copies:
        copy.start()
    spread[...] = jnp.zeros_like(spread)
    upstream = to_upstream(weight_ref[...], grad_ref[...])
    fetch.wait()
    rim_blocks = [*range(BAND), *range(blocks - BAND, blocks)]
    scatter_rows(place_ref, rim_blocks, upstream, adj, spread)
    odd = place_in_mesh() & 1
    for block in range(BAND):
        here = pl.ds(block * block_rows, block_rows)
        first_ref[here] = spread[(1 - odd) * 5 * BAND + block].T.astype(jnp.bfloat16)
        second_ref[here] = spread[odd * 5 * BAND + block].T.astype(jnp.bfloat16)
    mark_ref[...] = jnp.zeros_like(mark_ref)
    for copy in copies:
        copy.wait()


def inner_back_kernel(
    place_in, weight_ref, adj, grad_first, grad_second, rim_spread,
    whole_hbm, edge_ref,
    place_ref, spread, out, sems,
):
    fetch = pltpu.make_async_copy(place_in, place_ref, sems.at[1])
    fetch.start()
    blocks, _, block_rows, _ = adj.shape
    count = blocks - 2 * BAND
    rim = BAND * block_rows
    spread[: 2 * BAND] = rim_spread[BAND : 3 * BAND]
    spread[2 * BAND :] = jnp.zeros_like(spread[2 * BAND :])
    spread[blocks - 2 * BAND : blocks] = rim_spread[3 * BAND : 5 * BAND]
    grad = jnp.concatenate([grad_first[...], grad_second[...]], 0)
    upstream = to_upstream(weight_ref[...], grad)
    fetch.wait()
    scatter_rows(place_ref, range(BAND, blocks - BAND), upstream, adj, spread)
    for step in range(count):
        here = pl.ds(step * block_rows, block_rows)
        out[here] = spread[BAND + step].T.astype(jnp.bfloat16)
    finish = pltpu.make_async_copy(out, whole_hbm.at[pl.ds(rim, count * block_rows)], sems.at[0])
    finish.start()
    for block in range(BAND):
        edge_ref[block * block_rows : (block + 1) * block_rows] = spread[block].T
        after = BAND + block
        edge_ref[after * block_rows : (after + 1) * block_rows] = spread[blocks - BAND + block].T
    finish.wait()


def add_kernel(parts, *refs):
    values = [ref[...].astype(jnp.float32) for ref in refs[:parts]]
    total = values[0] + values[1]
    if parts == 4:
        total = total + (values[2] + values[3])
    refs[-1][...] = total.astype(refs[-1].dtype)


def last_kernel(
    scale, own_ref, other_ref, edge_ref, first_ref, second_ref, whole_in,
    weight_out, bias_out, whole_hbm,
    out, sums, bias, sems,
):
    half = sums.shape[0] // 2
    rim = first_ref.shape[0]
    rows = whole_hbm.shape[0]
    copies = [
        pltpu.make_async_copy(sums, weight_out, sems.at[0]),
        pltpu.make_async_copy(bias, bias_out, sems.at[1]),
        pltpu.make_async_copy(out.at[pl.ds(0, rim)], whole_hbm.at[pl.ds(0, rim)], sems.at[2]),
        pltpu.make_async_copy(
            out.at[pl.ds(rim, rim)], whole_hbm.at[pl.ds(rows - rim, rim)], sems.at[3]
        ),
    ]
    side = core_side()
    own_rows = pl.ds(pl.multiple_of(side * half, half), half)
    other_rows = pl.ds(pl.multiple_of((1 - side) * half, half), half)
    sums[own_rows] = own_ref[:half] * scale
    sums[other_rows] = other_ref[:half] * scale
    copies[0].start()
    first = jnp.where(side == 0, own_ref[half : half + 1], other_ref[half : half + 1])
    bias[...] = first * scale
    copies[1].start()
    odd = place_in_mesh() & 1
    for base, spill_ref in (((1 - odd) * rim, first_ref), (odd * rim, second_ref)):
        here = pl.ds(pl.multiple_of(base, rim), rim)
        out[here] = (edge_ref[here] + spill_ref[...].astype(jnp.float32)).astype(jnp.bfloat16)
    for copy in copies[2:]:
        copy.start()
    for copy in copies:
        copy.wait()


def add(values, dtype, after=()):
    size = values[0].size
    return pl.pallas_call(
        functools.partial(add_kernel, len(values)),
        out_shape=jax.ShapeDtypeStruct(values[0].shape, dtype),
        in_specs=[pl.BlockSpec(memory_space=pltpu.VMEM)] * len(values)
        + [pl.BlockSpec(memory_space=pl.ANY)] * len(after),
        compiler_params=pltpu.CompilerParams(vmem_limit_bytes=2 * MIB),
        cost_estimate=pl.CostEstimate(
            flops=size * len(values), bytes_accessed=8 * size, transcendentals=0
        ),
        name="add_halves",
    )(*values, *after)


def swap(value, masks):
    pairs = [(i, i ^ mask) for i, mask in enumerate(masks) if mask]
    return lax.ppermute(value, AXES, pairs)


def with_next(value, count):
    pairs = [(i, i + 1 if i & 1 else i - 1) for i in range(1, count - 1)]
    return lax.ppermute(value, AXES, pairs)


def sum_halves(send, keep, count, core_bit, marks):
    others = [bit for bit in range(count.bit_length() - 1) if bit != core_bit]
    groups = [others[i : i + 2] for i in range(0, len(others), 2)]
    total = add([keep, swap(send, [1 << core_bit] * count)], jnp.bfloat16, marks.get("core", ()))
    for step in range(len(groups)):
        masks = []
        for group in (groups[step], groups[len(groups) - 1 - step]):
            if len(groups[0]) != len(groups[-1]):
                group = groups[step]
            low = 1 << group[0]
            masks.append((low, 1 << group[1], low | 1 << group[1]) if group[1:] else (low,))
        parts = [total] + [
            swap(total, [masks[(i >> core_bit) & 1][k] for i in range(count)])
            for k in range(len(masks[0]))
        ]
        last = step == len(groups) - 1
        name = "last" if last else step
        total = add(parts, jnp.float32 if last else jnp.bfloat16, marks.get(name, ()))
    return total


def on_device(features, adj_values, adj_offset, adj_count, weight, bias_vector, cotangent):
    blocks, slots = adj_offset.shape
    block_rows = adj_values.shape[2]
    rows, width = features.shape
    rim = BAND * block_rows
    inner = rows - 2 * rim
    cols = lax.axis_size("cols")
    count = lax.axis_size("rows") * cols
    vmem = pl.BlockSpec(memory_space=pltpu.VMEM)
    hbm = pl.BlockSpec(memory_space=pltpu.HBM)
    anywhere = pl.BlockSpec(memory_space=pl.ANY)
    place_scratch = pltpu.SMEM((blocks * slots,), jnp.int32)
    bias_row = bias_vector.reshape(1, width)

    def in_hbm(value):
        return pltpu.with_memory_space_constraint(value, pltpu.HBM)

    def shape(*sizes, dtype=jnp.bfloat16):
        return jax.ShapeDtypeStruct(sizes, dtype)

    def params(mib):
        return pltpu.CompilerParams(vmem_limit_bytes=mib * MIB)

    def cost(share):
        return pl.CostEstimate(
            flops=int(1.2e9 * share), bytes_accessed=int(6e6 * share),
            transcendentals=int(8e5 * share),
        )

    offsets = in_hbm(adj_offset.T)
    counts = in_hbm(adj_count)
    core_bit = cols.bit_length() - 1
    first_rim = pl.pallas_call(
        halo_kernel,
        out_shape=shape(rim, width),
        in_specs=[hbm],
        out_specs=vmem,
        scratch_shapes=[pltpu.SemaphoreType.DMA((1,))],
        compiler_params=params(2),
        cost_estimate=cost(0.05),
        name="halo_rows",
    )(in_hbm(features))
    first_halo = swap(first_rim, [1] * count)
    cut = blocks // 2 * block_rows
    (
        places, second_rim, weight_near, bias_near, feat_near, adj_near, cot_near, act_first,
        grad_first, agg_first, sums_first,
    ) = pl.pallas_call(
        inner_first_kernel,
        out_shape=(
            shape(blocks * slots, dtype=jnp.int32),
            shape(rim, width),
            shape(width, width),
            shape(1, width, dtype=jnp.float32),
            shape(rows + block_rows, width),
            shape(*adj_values.shape),
            shape(rows, width),
            shape(cut - rim, width),
            shape(cut - rim, width),
            shape(cut - rim, width),
            shape(8, width, dtype=jnp.float32),
        ),
        in_specs=[hbm] * 7,
        out_specs=(anywhere,) + (vmem,) * 10,
        scratch_shapes=[
            pltpu.SMEM((slots, blocks), jnp.int32),
            pltpu.SMEM((blocks,), jnp.int32),
            place_scratch,
            pltpu.SemaphoreType.DMA((10,)),
        ],
        compiler_params=params(12),
        cost_estimate=cost(0.25),
        name="inner_rows_first",
    )(
        offsets, counts,
        *(in_hbm(x) for x in (weight, bias_row, features, adj_values, cotangent)),
    )
    second_halo = with_next(second_rim, count)
    activated, grad_second, partial, sums = pl.pallas_call(
        inner_second_kernel,
        out_shape=(
            shape(rows, width),
            shape(rows - rim - cut, width),
            shape(width, width, dtype=jnp.float32),
            shape(8, width, dtype=jnp.float32),
        ),
        in_specs=[anywhere] + [vmem] * 9,
        out_specs=(hbm,) + (vmem,) * 3,
        scratch_shapes=[
            place_scratch,
            pltpu.VMEM((rows - rim - cut, width), jnp.bfloat16),
            pltpu.VMEM((rows - rim - cut, width), jnp.bfloat16),
            pltpu.SemaphoreType.DMA((3,)),
        ],
        compiler_params=params(12),
        cost_estimate=cost(0.25),
        name="inner_rows_second",
    )(
        places, weight_near, bias_near, feat_near, adj_near, cot_near, act_first, grad_first,
        agg_first, sums_first,
    )
    half_shape = (width // 2 + TAIL, width)
    act_rim, grad_rim, send, keep = pl.pallas_call(
        rim_kernel,
        out_shape=(
            shape(2 * rim, width),
            shape(2 * rim, width),
            shape(*half_shape, dtype=jnp.float32),
            shape(*half_shape, dtype=jnp.float32),
        ),
        in_specs=[anywhere] + [vmem] * 9,
        out_specs=(vmem,) * 4,
        scratch_shapes=[
            place_scratch,
            pltpu.VMEM((6 * rim + block_rows, width), jnp.bfloat16),
            pltpu.VMEM((2 * rim, width), jnp.bfloat16),
            pltpu.VMEM((2,) + half_shape, jnp.float32),
            pltpu.SemaphoreType.DMA((1,)),
        ],
        compiler_params=params(12),
        cost_estimate=cost(0.2),
        name="rim_rows",
    )(
        places, weight_near, bias_near, feat_near, first_halo, second_halo, adj_near, cot_near,
        partial, sums,
    )
    mark = shape(8, 128, dtype=jnp.float32)
    activated, rim_spread, first_spill, second_spill, first_mark = pl.pallas_call(
        rim_back_kernel,
        out_shape=(
            shape(rows, width),
            shape(6 * BAND + 1, width, block_rows, dtype=jnp.float32),
            shape(rim, width),
            shape(rim, width),
            mark,
        ),
        in_specs=[anywhere] + [vmem] * 4 + [hbm],
        out_specs=(hbm,) + (vmem,) * 4,
        scratch_shapes=[place_scratch, pltpu.SemaphoreType.DMA((3,))],
        input_output_aliases={5: 0},
        compiler_params=params(12),
        cost_estimate=cost(0.2),
        name="rim_rows_back",
    )(places, weight_near, adj_near, grad_rim, act_rim, activated)
    first_part = swap(first_spill, [1] * count)
    second_part = with_next(second_spill, count)
    grad_whole, edges = pl.pallas_call(
        inner_back_kernel,
        out_shape=(shape(rows, width), shape(2 * rim, width, dtype=jnp.float32)),
        in_specs=[anywhere] + [vmem] * 5,
        out_specs=(hbm, vmem),
        scratch_shapes=[
            place_scratch,
            pltpu.VMEM((blocks + 1, width, block_rows), jnp.float32),
            pltpu.VMEM((inner, width), jnp.bfloat16),
            pltpu.SemaphoreType.DMA((2,)),
        ],
        compiler_params=params(12),
        cost_estimate=cost(2.0),
        name="inner_rows_back",
    )(places, weight_near, adj_near, grad_first, grad_second, rim_spread)
    marks = {0: (first_mark,), "last": (first_part,)}
    own_half = sum_halves(send, keep, count, core_bit, marks)
    other_half = swap(own_half, [1 << core_bit] * count)
    norm_scale = 1.0 / math.sqrt(rows * count)
    grad_weight, grad_bias, grad_features = pl.pallas_call(
        functools.partial(last_kernel, norm_scale),
        out_shape=(
            shape(width, width, dtype=jnp.float32),
            shape(1, width, dtype=jnp.float32),
            shape(rows, width),
        ),
        in_specs=[vmem] * 5 + [hbm],
        out_specs=(hbm, hbm, hbm),
        scratch_shapes=[
            pltpu.VMEM((2 * rim, width), jnp.bfloat16),
            pltpu.VMEM((width, width), jnp.float32),
            pltpu.VMEM((1, width), jnp.float32),
            pltpu.SemaphoreType.DMA((4,)),
        ],
        input_output_aliases={5: 2},
        compiler_params=params(8),
        name="last_step",
    )(own_half, other_half, edges, first_part, second_part, grad_whole)
    return (activated, grad_features, grad_weight, grad_bias.reshape(width))


def solution(mesh):
    return jax.shard_map(
        on_device,
        mesh=mesh,
        in_specs=(
            P(AXES, None),
            P(AXES, None, None, None),
            P(AXES, None),
            P(AXES),
            P(),
            P(),
            P(AXES, None),
        ),
        out_specs=(P(AXES, None), P(AXES, None), P(), P()),
        check_vma=False,
    )
```

```python
import functools
import math

import jax
import jax.numpy as jnp
from jax import lax
from jax.experimental import pallas as pl
from jax.experimental.pallas import tpu as pltpu
from jax.sharding import PartitionSpec as P

BAND = 2
TAIL = 16
AXES = ("rows", "cols")
MIB = 1024 * 1024


def row_of(adj_ref, block, slots):
    return jnp.concatenate([adj_ref[block, slot] for slot in range(slots)], 1)


def pick(source, places, block_rows):
    return jnp.concatenate(
        [
            source[pl.ds(pl.multiple_of(place * block_rows, block_rows), block_rows)]
            for place in places
        ],
        0,
    )


def write_places(off_ref, cnt_ref, place_ref, blocks, slots):
    for block in range(blocks):
        if block < BAND:
            shift, dump = BAND, 6 * BAND
        elif block < blocks - BAND:
            shift, dump = 0, blocks
        else:
            shift, dump = 5 * BAND - blocks, 6 * BAND
        for slot in range(slots):
            place_ref[block * slots + slot] = jnp.where(
                slot < cnt_ref[block], block + shift + off_ref[slot, block], dump
            )


def places_of(place_ref, block, slots):
    return [place_ref[block * slots + slot] for slot in range(slots)]


def rim_block(step, blocks):
    return step if step < BAND else blocks - 2 * BAND + step


def place_in_mesh():
    return lax.axis_index("rows") * lax.axis_size("cols") + lax.axis_index("cols")


def core_side():
    return lax.axis_index("rows") & 1


def halo_kernel(feat_hbm, first_ref, second_ref, sems):
    rows = feat_hbm.shape[0]
    rim = first_ref.shape[0]
    odd = place_in_mesh() & 1
    last = rows - rim
    starts = ((1 - odd) * last, odd * last)
    copies = [
        pltpu.make_async_copy(
            feat_hbm.at[pl.ds(pl.multiple_of(start, rim), rim)], out_ref, sems.at[i]
        )
        for i, (start, out_ref) in enumerate(zip(starts, (first_ref, second_ref)))
    ]
    for copy in copies:
        copy.start()
    for copy in copies:
        copy.wait()


def activate(preact, cotangent):
    gate = 1.0 / (1.0 + jnp.exp(-preact))
    grad = cotangent.astype(jnp.float32) * gate * (1.0 + preact * (1.0 - gate))
    return (preact * gate).astype(jnp.bfloat16), grad.astype(jnp.bfloat16)


def column_sums(grad):
    rows, width = grad.shape
    return jnp.sum(grad.astype(jnp.float32).reshape(rows // 8, 8, width), axis=0)


def to_upstream(weight, grad):
    return lax.dot_general(
        weight, grad, (((1,), (1,)), ((), ())), preferred_element_type=jnp.float32
    ).astype(jnp.bfloat16)


def weight_terms(agg, grad):
    return lax.dot_general(
        agg, grad, (((0,), (0,)), ((), ())), preferred_element_type=jnp.float32
    )


def inner_kernel(
    off_hbm, cnt_hbm, weight_hbm, bias_hbm, feat_hbm, adj_hbm, cot_hbm,
    act_hbm, place_out, grad_ref, partial_ref, sums_ref, weight_ref, bias_ref, feat_rim, adj_rim,
    cot_rim, adj,
    off_ref, cnt_ref, place_ref, feat, cot, act, agg_all, sems,
):
    blocks, slots, block_rows, _ = adj_hbm.shape
    rows, width = feat_hbm.shape
    count = blocks - 2 * BAND
    rim = BAND * block_rows
    half = 2 * rim
    inner = count * block_rows
    scalars = [
        pltpu.make_async_copy(off_hbm, off_ref, sems.at[12]),
        pltpu.make_async_copy(cnt_hbm, cnt_ref, sems.at[13]),
    ]
    copies = [
        pltpu.make_async_copy(feat_hbm, feat.at[pl.ds(0, rows)], sems.at[0]),
        pltpu.make_async_copy(adj_hbm.at[pl.ds(BAND, count)], adj, sems.at[1]),
        pltpu.make_async_copy(weight_hbm, weight_ref, sems.at[2]),
        pltpu.make_async_copy(bias_hbm, bias_ref, sems.at[3]),
        pltpu.make_async_copy(cot_hbm.at[pl.ds(rim, inner)], cot, sems.at[4]),
        pltpu.make_async_copy(feat_hbm.at[pl.ds(0, half)], feat_rim.at[pl.ds(0, half)], sems.at[5]),
        pltpu.make_async_copy(
            feat_hbm.at[pl.ds(rows - half, half)], feat_rim.at[pl.ds(half, half)], sems.at[6]
        ),
        pltpu.make_async_copy(adj_hbm.at[pl.ds(0, BAND)], adj_rim.at[pl.ds(0, BAND)], sems.at[7]),
        pltpu.make_async_copy(
            adj_hbm.at[pl.ds(blocks - BAND, BAND)], adj_rim.at[pl.ds(BAND, BAND)], sems.at[8]
        ),
        pltpu.make_async_copy(cot_hbm.at[pl.ds(0, rim)], cot_rim.at[pl.ds(0, rim)], sems.at[9]),
        pltpu.make_async_copy(
            cot_hbm.at[pl.ds(rows - rim, rim)], cot_rim.at[pl.ds(rim, rim)], sems.at[10]
        ),
    ]
    for copy in scalars + copies:
        copy.start()
    feat[rows:] = jnp.zeros((block_rows, width), jnp.bfloat16)
    for copy in scalars:
        copy.wait()
    write_places(off_ref, cnt_ref, place_ref, blocks, slots)
    place_copy = pltpu.make_async_copy(place_ref, place_out, sems.at[14])
    place_copy.start()
    for copy in copies[:5]:
        copy.wait()
    weight = weight_ref[...]
    bias = bias_ref[...]
    sums = jnp.zeros((8, width), jnp.float32)
    for step in range(0, count, 2):
        for block in (step, step + 1):
            places = places_of(place_ref, block + BAND, slots)
            agg_all[block * block_rows : (block + 1) * block_rows] = jnp.dot(
                row_of(adj, block, slots), pick(feat, places, block_rows),
                preferred_element_type=jnp.float32,
            ).astype(jnp.bfloat16)
        here = pl.ds(step * block_rows, 2 * block_rows)
        preact = jnp.dot(agg_all[here], weight, preferred_element_type=jnp.float32) + bias
        act[here], grad = activate(preact, cot[here])
        grad_ref[here] = grad
        sums = sums + column_sums(grad)
    act_out = pltpu.make_async_copy(act, act_hbm.at[pl.ds(rim, inner)], sems.at[11])
    act_out.start()
    sums_ref[...] = sums
    partial_ref[...] = weight_terms(agg_all[...], grad_ref[...])
    for copy in copies[5:]:
        copy.wait()
    act_out.wait()
    place_copy.wait()


def rim_kernel(
    place_in, weight_ref, bias_ref, feat_ref, first_ref, second_ref, adj_ref, cot_ref,
    partial_ref, sums_ref,
    act_ref, grad_ref, send_ref, keep_ref,
    place_ref, window, agg_all, payload, sems,
):
    fetch = pltpu.make_async_copy(place_in, place_ref, sems.at[0])
    fetch.start()
    steps, slots, block_rows, _ = adj_ref.shape
    blocks = place_ref.shape[0] // slots
    width = feat_ref.shape[1]
    rim = BAND * block_rows
    odd = place_in_mesh() & 1
    window[pl.ds(pl.multiple_of((1 - odd) * 5 * rim, rim), rim)] = first_ref[...]
    window[pl.ds(pl.multiple_of(odd * 5 * rim, rim), rim)] = second_ref[...]
    window[rim : 5 * rim] = feat_ref[...]
    window[6 * rim :] = jnp.zeros((block_rows, width), jnp.bfloat16)
    weight = weight_ref[...]
    bias = bias_ref[...]
    sums = sums_ref[...]
    fetch.wait()
    for step in range(0, steps, 2):
        for block in (step, step + 1):
            places = places_of(place_ref, rim_block(block, blocks), slots)
            agg_all[block * block_rows : (block + 1) * block_rows] = jnp.dot(
                row_of(adj_ref, block, slots), pick(window, places, block_rows),
                preferred_element_type=jnp.float32,
            ).astype(jnp.bfloat16)
        here = pl.ds(step * block_rows, 2 * block_rows)
        preact = jnp.dot(agg_all[here], weight, preferred_element_type=jnp.float32) + bias
        act_ref[here], grad = activate(preact, cot_ref[here])
        grad_ref[here] = grad
        sums = sums + column_sums(grad)
    half = width // 2
    partial = partial_ref[...] + weight_terms(agg_all[...], grad_ref[...])
    payload[0, :half] = partial[:half]
    payload[1, :half] = partial[half:]
    tail = jnp.zeros((TAIL, width), jnp.float32)
    payload[0, half:] = jnp.broadcast_to(jnp.sum(sums, axis=0, keepdims=True), tail.shape)
    payload[1, half:] = tail
    side = core_side()
    keep_ref[...] = payload[side]
    send_ref[...] = payload[1 - side]


def scatter_rows(places, upstream, adj_ref, spread):
    _, slots, block_rows, _ = adj_ref.shape
    for step, targets in enumerate(places):
        terms = jnp.dot(
            upstream[:, step * block_rows : (step + 1) * block_rows],
            row_of(adj_ref, step, slots),
            preferred_element_type=jnp.float32,
        )
        for slot, target in enumerate(targets):
            spread[target] += terms[:, slot * block_rows : (slot + 1) * block_rows]


def rim_back_kernel(
    place_in, weight_ref, adj_ref, grad_ref, act_ref, act_in,
    act_hbm, spread, first_ref, second_ref, mark_ref,
    place_ref, sems,
):
    fetch = pltpu.make_async_copy(place_in, place_ref, sems.at[2])
    fetch.start()
    steps, slots, block_rows, _ = adj_ref.shape
    blocks = place_ref.shape[0] // slots
    rim = BAND * block_rows
    rows = blocks * block_rows
    copies = [
        pltpu.make_async_copy(act_ref.at[pl.ds(0, rim)], act_hbm.at[pl.ds(0, rim)], sems.at[0]),
        pltpu.make_async_copy(
            act_ref.at[pl.ds(rim, rim)], act_hbm.at[pl.ds(rows - rim, rim)], sems.at[1]
        ),
    ]
    for copy in copies:
        copy.start()
    spread[...] = jnp.zeros_like(spread)
    upstream = to_upstream(weight_ref[...], grad_ref[...])
    fetch.wait()
    scatter_rows(
        [places_of(place_ref, rim_block(step, blocks), slots) for step in range(steps)],
        upstream, adj_ref, spread,
    )
    odd = place_in_mesh() & 1
    for block in range(BAND):
        here = pl.ds(block * block_rows, block_rows)
        first_ref[here] = spread[(1 - odd) * 5 * BAND + block].T.astype(jnp.bfloat16)
        second_ref[here] = spread[odd * 5 * BAND + block].T.astype(jnp.bfloat16)
    mark_ref[...] = jnp.zeros_like(mark_ref)
    for copy in copies:
        copy.wait()


def inner_back_kernel(
    place_in, weight_ref, adj_ref, grad_ref, rim_spread,
    whole_hbm, edge_ref,
    place_ref, spread, out, sems,
):
    fetch = pltpu.make_async_copy(place_in, place_ref, sems.at[1])
    fetch.start()
    count, slots, block_rows, _ = adj_ref.shape
    blocks = place_ref.shape[0] // slots
    rim = BAND * block_rows
    spread[: 2 * BAND] = rim_spread[BAND : 3 * BAND]
    spread[2 * BAND :] = jnp.zeros_like(spread[2 * BAND :])
    spread[blocks - 2 * BAND : blocks] = rim_spread[3 * BAND : 5 * BAND]
    upstream = to_upstream(weight_ref[...], grad_ref[...])
    fetch.wait()
    scatter_rows(
        [places_of(place_ref, step + BAND, slots) for step in range(count)],
        upstream, adj_ref, spread,
    )
    for step in range(count):
        here = pl.ds(step * block_rows, block_rows)
        out[here] = spread[BAND + step].T.astype(jnp.bfloat16)
    finish = pltpu.make_async_copy(out, whole_hbm.at[pl.ds(rim, count * block_rows)], sems.at[0])
    finish.start()
    for block in range(BAND):
        edge_ref[block * block_rows : (block + 1) * block_rows] = spread[block].T
        after = BAND + block
        edge_ref[after * block_rows : (after + 1) * block_rows] = spread[blocks - BAND + block].T
    finish.wait()


def add_kernel(parts, *refs):
    values = [ref[...].astype(jnp.float32) for ref in refs[:parts]]
    total = values[0] + values[1]
    if parts == 4:
        total = total + (values[2] + values[3])
    refs[-1][...] = total.astype(refs[-1].dtype)


def last_kernel(
    scale, own_ref, other_ref, edge_ref, first_ref, second_ref, whole_in,
    weight_out, bias_out, whole_hbm,
    out, sums, bias, sems,
):
    half = sums.shape[0] // 2
    rim = first_ref.shape[0]
    rows = whole_hbm.shape[0]
    copies = [
        pltpu.make_async_copy(sums, weight_out, sems.at[0]),
        pltpu.make_async_copy(bias, bias_out, sems.at[1]),
        pltpu.make_async_copy(out.at[pl.ds(0, rim)], whole_hbm.at[pl.ds(0, rim)], sems.at[2]),
        pltpu.make_async_copy(
            out.at[pl.ds(rim, rim)], whole_hbm.at[pl.ds(rows - rim, rim)], sems.at[3]
        ),
    ]
    side = core_side()
    own_rows = pl.ds(pl.multiple_of(side * half, half), half)
    other_rows = pl.ds(pl.multiple_of((1 - side) * half, half), half)
    sums[own_rows] = own_ref[:half] * scale
    sums[other_rows] = other_ref[:half] * scale
    copies[0].start()
    first = jnp.where(side == 0, own_ref[half : half + 1], other_ref[half : half + 1])
    bias[...] = first * scale
    copies[1].start()
    odd = place_in_mesh() & 1
    for base, spill_ref in (((1 - odd) * rim, first_ref), (odd * rim, second_ref)):
        here = pl.ds(pl.multiple_of(base, rim), rim)
        out[here] = (edge_ref[here] + spill_ref[...].astype(jnp.float32)).astype(jnp.bfloat16)
    for copy in copies[2:]:
        copy.start()
    for copy in copies:
        copy.wait()


def add(values, dtype, after=()):
    size = values[0].size
    return pl.pallas_call(
        functools.partial(add_kernel, len(values)),
        out_shape=jax.ShapeDtypeStruct(values[0].shape, dtype),
        in_specs=[pl.BlockSpec(memory_space=pltpu.VMEM)] * len(values)
        + [pl.BlockSpec(memory_space=pl.ANY)] * len(after),
        compiler_params=pltpu.CompilerParams(vmem_limit_bytes=2 * MIB),
        cost_estimate=pl.CostEstimate(
            flops=size * len(values), bytes_accessed=8 * size, transcendentals=0
        ),
        name="add_halves",
    )(*values, *after)


def swap(value, masks):
    pairs = [(i, i ^ mask) for i, mask in enumerate(masks) if mask]
    return lax.ppermute(value, AXES, pairs)


def with_next(value, count):
    pairs = [(i, (i + 1 if i & 1 else i - 1) % count) for i in range(count)]
    return lax.ppermute(value, AXES, pairs)


def sum_halves(send, keep, count, core_bit, marks):
    others = [bit for bit in range(count.bit_length() - 1) if bit != core_bit]
    groups = [others[i : i + 2] for i in range(0, len(others), 2)]
    total = add([keep, swap(send, [1 << core_bit] * count)], jnp.bfloat16, marks.get("core", ()))
    for step in range(len(groups)):
        masks = []
        for group in (groups[step], groups[len(groups) - 1 - step]):
            if len(groups[0]) != len(groups[-1]):
                group = groups[step]
            low = 1 << group[0]
            masks.append((low, 1 << group[1], low | 1 << group[1]) if group[1:] else (low,))
        parts = [total] + [
            swap(total, [masks[(i >> core_bit) & 1][k] for i in range(count)])
            for k in range(len(masks[0]))
        ]
        last = step == len(groups) - 1
        name = "last" if last else step
        total = add(parts, jnp.float32 if last else jnp.bfloat16, marks.get(name, ()))
    return total


def on_device(features, adj_values, adj_offset, adj_count, weight, bias_vector, cotangent):
    blocks, slots = adj_offset.shape
    block_rows = adj_values.shape[2]
    rows, width = features.shape
    rim = BAND * block_rows
    inner = rows - 2 * rim
    cols = lax.axis_size("cols")
    count = lax.axis_size("rows") * cols
    vmem = pl.BlockSpec(memory_space=pltpu.VMEM)
    hbm = pl.BlockSpec(memory_space=pltpu.HBM)
    anywhere = pl.BlockSpec(memory_space=pl.ANY)
    place_scratch = pltpu.SMEM((blocks * slots,), jnp.int32)
    bias_row = bias_vector.reshape(1, width)

    def in_hbm(value):
        return pltpu.with_memory_space_constraint(value, pltpu.HBM)

    def shape(*sizes, dtype=jnp.bfloat16):
        return jax.ShapeDtypeStruct(sizes, dtype)

    def params(mib):
        return pltpu.CompilerParams(vmem_limit_bytes=mib * MIB)

    def cost(share):
        return pl.CostEstimate(
            flops=int(1.2e9 * share), bytes_accessed=int(6e6 * share),
            transcendentals=int(8e5 * share),
        )

    offsets = in_hbm(adj_offset.T)
    counts = in_hbm(adj_count)
    core_bit = cols.bit_length() - 1
    first_rim, second_rim = pl.pallas_call(
        halo_kernel,
        out_shape=(shape(rim, width), shape(rim, width)),
        in_specs=[hbm],
        out_specs=(vmem, vmem),
        scratch_shapes=[pltpu.SemaphoreType.DMA((2,))],
        compiler_params=params(2),
        cost_estimate=cost(0.05),
        name="halo_rows",
    )(in_hbm(features))
    first_halo = swap(first_rim, [1] * count)
    second_halo = with_next(second_rim, count)
    (
        activated, places, grad_inner, partial, sums, weight_near, bias_near, feat_rim, adj_rim,
        cot_rim, adj_inner,
    ) = pl.pallas_call(
        inner_kernel,
        out_shape=(
            shape(rows, width),
            shape(blocks * slots, dtype=jnp.int32),
            shape(inner, width),
            shape(width, width, dtype=jnp.float32),
            shape(8, width, dtype=jnp.float32),
            shape(width, width),
            shape(1, width, dtype=jnp.float32),
            shape(4 * rim, width),
            shape(2 * BAND, slots, block_rows, block_rows),
            shape(2 * rim, width),
            shape(blocks - 2 * BAND, slots, block_rows, block_rows),
        ),
        in_specs=[hbm] * 7,
        out_specs=(hbm, anywhere) + (vmem,) * 9,
        scratch_shapes=[
            pltpu.SMEM((slots, blocks), jnp.int32),
            pltpu.SMEM((blocks,), jnp.int32),
            place_scratch,
            pltpu.VMEM((rows + block_rows, width), jnp.bfloat16),
            pltpu.VMEM((inner, width), jnp.bfloat16),
            pltpu.VMEM((inner, width), jnp.bfloat16),
            pltpu.VMEM((inner, width), jnp.bfloat16),
            pltpu.SemaphoreType.DMA((15,)),
        ],
        compiler_params=params(20),
        cost_estimate=cost(0.5),
        name="inner_rows",
    )(
        offsets, counts,
        *(in_hbm(x) for x in (weight, bias_row, features, adj_values, cotangent)),
    )
    half_shape = (width // 2 + TAIL, width)
    act_rim, grad_rim, send, keep = pl.pallas_call(
        rim_kernel,
        out_shape=(
            shape(2 * rim, width),
            shape(2 * rim, width),
            shape(*half_shape, dtype=jnp.float32),
            shape(*half_shape, dtype=jnp.float32),
        ),
        in_specs=[anywhere] + [vmem] * 9,
        out_specs=(vmem,) * 4,
        scratch_shapes=[
            place_scratch,
            pltpu.VMEM((6 * rim + block_rows, width), jnp.bfloat16),
            pltpu.VMEM((2 * rim, width), jnp.bfloat16),
            pltpu.VMEM((2,) + half_shape, jnp.float32),
            pltpu.SemaphoreType.DMA((1,)),
        ],
        compiler_params=params(12),
        cost_estimate=cost(0.2),
        name="rim_rows",
    )(
        places, weight_near, bias_near, feat_rim, first_halo, second_halo, adj_rim, cot_rim,
        partial, sums,
    )
    mark = shape(8, 128, dtype=jnp.float32)
    activated, rim_spread, first_spill, second_spill, first_mark = pl.pallas_call(
        rim_back_kernel,
        out_shape=(
            shape(rows, width),
            shape(6 * BAND + 1, width, block_rows, dtype=jnp.float32),
            shape(rim, width),
            shape(rim, width),
            mark,
        ),
        in_specs=[anywhere] + [vmem] * 4 + [hbm],
        out_specs=(hbm,) + (vmem,) * 4,
        scratch_shapes=[place_scratch, pltpu.SemaphoreType.DMA((3,))],
        input_output_aliases={5: 0},
        compiler_params=params(12),
        cost_estimate=cost(0.2),
        name="rim_rows_back",
    )(places, weight_near, adj_rim, grad_rim, act_rim, activated)
    first_part = swap(first_spill, [1] * count)
    second_part = with_next(second_spill, count)
    grad_whole, edges = pl.pallas_call(
        inner_back_kernel,
        out_shape=(shape(rows, width), shape(2 * rim, width, dtype=jnp.float32)),
        in_specs=[anywhere] + [vmem] * 4,
        out_specs=(hbm, vmem),
        scratch_shapes=[
            place_scratch,
            pltpu.VMEM((blocks + 1, width, block_rows), jnp.float32),
            pltpu.VMEM((inner, width), jnp.bfloat16),
            pltpu.SemaphoreType.DMA((2,)),
        ],
        compiler_params=params(12),
        cost_estimate=cost(2.0),
        name="inner_rows_back",
    )(places, weight_near, adj_inner, grad_inner, rim_spread)
    marks = {0: (first_mark,)}
    own_half = sum_halves(send, keep, count, core_bit, marks)
    other_half = swap(own_half, [1 << core_bit] * count)
    norm_scale = 1.0 / math.sqrt(rows * count)
    grad_weight, grad_bias, grad_features = pl.pallas_call(
        functools.partial(last_kernel, norm_scale),
        out_shape=(
            shape(width, width, dtype=jnp.float32),
            shape(1, width, dtype=jnp.float32),
            shape(rows, width),
        ),
        in_specs=[vmem] * 5 + [hbm],
        out_specs=(hbm, hbm, hbm),
        scratch_shapes=[
            pltpu.VMEM((2 * rim, width), jnp.bfloat16),
            pltpu.VMEM((width, width), jnp.float32),
            pltpu.VMEM((1, width), jnp.float32),
            pltpu.SemaphoreType.DMA((4,)),
        ],
        input_output_aliases={5: 2},
        compiler_params=params(8),
        name="last_step",
    )(own_half, other_half, edges, first_part, second_part, grad_whole)
    return (activated, grad_features, grad_weight, grad_bias.reshape(width))


def solution(mesh):
    return jax.shard_map(
        on_device,
        mesh=mesh,
        in_specs=(
            P(AXES, None),
            P(AXES, None, None, None),
            P(AXES, None),
            P(AXES),
            P(),
            P(),
            P(AXES, None),
        ),
        out_specs=(P(AXES, None), P(AXES, None), P(), P()),
        check_vma=False,
    )
```

```python
import functools
import math

import jax
import jax.numpy as jnp
from jax import lax
from jax.experimental import pallas as pl
from jax.experimental.pallas import tpu as pltpu
from jax.sharding import PartitionSpec as P

BAND = 2
TAIL = 16
AXES = ("rows", "cols")
MIB = 1024 * 1024


def row_of(adj_ref, block, slots):
    return jnp.concatenate([adj_ref[block, slot] for slot in range(slots)], 1)


def pick(source, places, block_rows):
    return jnp.concatenate(
        [
            source[pl.ds(pl.multiple_of(place * block_rows, block_rows), block_rows)]
            for place in places
        ],
        0,
    )


def write_places(off_ref, cnt_ref, place_ref, blocks, slots):
    for block in range(blocks):
        if block < BAND:
            shift, dump = BAND, 6 * BAND
        elif block < blocks - BAND:
            shift, dump = 0, blocks
        else:
            shift, dump = 5 * BAND - blocks, 6 * BAND
        for slot in range(slots):
            place_ref[block * slots + slot] = jnp.where(
                slot < cnt_ref[block], block + shift + off_ref[slot, block], dump
            )


def places_of(place_ref, block, slots):
    return [place_ref[block * slots + slot] for slot in range(slots)]


def rim_block(step, blocks):
    return step if step < BAND else blocks - 2 * BAND + step


def place_in_mesh():
    return lax.axis_index("rows") * lax.axis_size("cols") + lax.axis_index("cols")


def core_side():
    return lax.axis_index("rows") & 1


def halo_kernel(feat_hbm, first_ref, second_ref, sems):
    rows = feat_hbm.shape[0]
    rim = first_ref.shape[0]
    odd = place_in_mesh() & 1
    last = rows - rim
    starts = ((1 - odd) * last, odd * last)
    copies = [
        pltpu.make_async_copy(
            feat_hbm.at[pl.ds(pl.multiple_of(start, rim), rim)], out_ref, sems.at[i]
        )
        for i, (start, out_ref) in enumerate(zip(starts, (first_ref, second_ref)))
    ]
    for copy in copies:
        copy.start()
    for copy in copies:
        copy.wait()


def activate(preact, cotangent):
    gate = 1.0 / (1.0 + jnp.exp(-preact))
    grad = cotangent.astype(jnp.float32) * gate * (1.0 + preact * (1.0 - gate))
    return (preact * gate).astype(jnp.bfloat16), grad.astype(jnp.bfloat16)


def column_sums(grad):
    rows, width = grad.shape
    return jnp.sum(grad.astype(jnp.float32).reshape(rows // 8, 8, width), axis=0)


def to_upstream(weight, grad):
    return lax.dot_general(
        weight, grad, (((1,), (1,)), ((), ())), preferred_element_type=jnp.float32
    ).astype(jnp.bfloat16)


def weight_terms(agg, grad):
    return lax.dot_general(
        agg, grad, (((0,), (0,)), ((), ())), preferred_element_type=jnp.float32
    )


def inner_kernel(
    off_hbm, cnt_hbm, weight_hbm, bias_hbm, feat_hbm, adj_hbm, cot_hbm,
    act_hbm, place_out, grad_ref, partial_ref, sums_ref, weight_ref, bias_ref, feat_rim, adj_rim,
    cot_rim, adj,
    off_ref, cnt_ref, place_ref, feat, cot, act, agg_all, sems,
):
    blocks, slots, block_rows, _ = adj_hbm.shape
    rows, width = feat_hbm.shape
    count = blocks - 2 * BAND
    rim = BAND * block_rows
    half = 2 * rim
    inner = count * block_rows
    scalars = [
        pltpu.make_async_copy(off_hbm, off_ref, sems.at[12]),
        pltpu.make_async_copy(cnt_hbm, cnt_ref, sems.at[13]),
    ]
    copies = [
        pltpu.make_async_copy(feat_hbm, feat.at[pl.ds(0, rows)], sems.at[0]),
        pltpu.make_async_copy(adj_hbm.at[pl.ds(BAND, count)], adj, sems.at[1]),
        pltpu.make_async_copy(weight_hbm, weight_ref, sems.at[2]),
        pltpu.make_async_copy(bias_hbm, bias_ref, sems.at[3]),
        pltpu.make_async_copy(cot_hbm.at[pl.ds(rim, inner)], cot, sems.at[4]),
        pltpu.make_async_copy(feat_hbm.at[pl.ds(0, half)], feat_rim.at[pl.ds(0, half)], sems.at[5]),
        pltpu.make_async_copy(
            feat_hbm.at[pl.ds(rows - half, half)], feat_rim.at[pl.ds(half, half)], sems.at[6]
        ),
        pltpu.make_async_copy(adj_hbm.at[pl.ds(0, BAND)], adj_rim.at[pl.ds(0, BAND)], sems.at[7]),
        pltpu.make_async_copy(
            adj_hbm.at[pl.ds(blocks - BAND, BAND)], adj_rim.at[pl.ds(BAND, BAND)], sems.at[8]
        ),
        pltpu.make_async_copy(cot_hbm.at[pl.ds(0, rim)], cot_rim.at[pl.ds(0, rim)], sems.at[9]),
        pltpu.make_async_copy(
            cot_hbm.at[pl.ds(rows - rim, rim)], cot_rim.at[pl.ds(rim, rim)], sems.at[10]
        ),
    ]
    for copy in scalars + copies:
        copy.start()
    feat[rows:] = jnp.zeros((block_rows, width), jnp.bfloat16)
    for copy in scalars:
        copy.wait()
    write_places(off_ref, cnt_ref, place_ref, blocks, slots)
    place_copy = pltpu.make_async_copy(place_ref, place_out, sems.at[14])
    place_copy.start()
    for copy in copies[:5]:
        copy.wait()
    weight = weight_ref[...]
    bias = bias_ref[...]
    sums = jnp.zeros((8, width), jnp.float32)
    for step in range(0, count, 2):
        for block in (step, step + 1):
            places = places_of(place_ref, block + BAND, slots)
            agg_all[block * block_rows : (block + 1) * block_rows] = jnp.dot(
                row_of(adj, block, slots), pick(feat, places, block_rows),
                preferred_element_type=jnp.float32,
            ).astype(jnp.bfloat16)
        here = pl.ds(step * block_rows, 2 * block_rows)
        preact = jnp.dot(agg_all[here], weight, preferred_element_type=jnp.float32) + bias
        act[here], grad = activate(preact, cot[here])
        grad_ref[here] = grad
        sums = sums + column_sums(grad)
    act_out = pltpu.make_async_copy(act, act_hbm.at[pl.ds(rim, inner)], sems.at[11])
    act_out.start()
    sums_ref[...] = sums
    partial_ref[...] = weight_terms(agg_all[...], grad_ref[...])
    for copy in copies[5:]:
        copy.wait()
    act_out.wait()
    place_copy.wait()


def rim_kernel(
    place_in, weight_ref, bias_ref, feat_ref, first_ref, second_ref, adj_ref, cot_ref,
    partial_ref, sums_ref,
    act_ref, grad_ref, send_ref, keep_ref,
    place_ref, window, agg_all, payload, sems,
):
    fetch = pltpu.make_async_copy(place_in, place_ref, sems.at[0])
    fetch.start()
    steps, slots, block_rows, _ = adj_ref.shape
    blocks = place_ref.shape[0] // slots
    width = feat_ref.shape[1]
    rim = BAND * block_rows
    odd = place_in_mesh() & 1
    window[pl.ds(pl.multiple_of((1 - odd) * 5 * rim, rim), rim)] = first_ref[...]
    window[pl.ds(pl.multiple_of(odd * 5 * rim, rim), rim)] = second_ref[...]
    window[rim : 5 * rim] = feat_ref[...]
    window[6 * rim :] = jnp.zeros((block_rows, width), jnp.bfloat16)
    weight = weight_ref[...]
    bias = bias_ref[...]
    sums = sums_ref[...]
    fetch.wait()
    for step in range(0, steps, 2):
        for block in (step, step + 1):
            places = places_of(place_ref, rim_block(block, blocks), slots)
            agg_all[block * block_rows : (block + 1) * block_rows] = jnp.dot(
                row_of(adj_ref, block, slots), pick(window, places, block_rows),
                preferred_element_type=jnp.float32,
            ).astype(jnp.bfloat16)
        here = pl.ds(step * block_rows, 2 * block_rows)
        preact = jnp.dot(agg_all[here], weight, preferred_element_type=jnp.float32) + bias
        act_ref[here], grad = activate(preact, cot_ref[here])
        grad_ref[here] = grad
        sums = sums + column_sums(grad)
    half = width // 2
    partial = partial_ref[...] + weight_terms(agg_all[...], grad_ref[...])
    payload[0, :half] = partial[:half]
    payload[1, :half] = partial[half:]
    tail = jnp.zeros((TAIL, width), jnp.float32)
    payload[0, half:] = jnp.broadcast_to(jnp.sum(sums, axis=0, keepdims=True), tail.shape)
    payload[1, half:] = tail
    side = core_side()
    keep_ref[...] = payload[side]
    send_ref[...] = payload[1 - side]


def scatter_rows(places, upstream, adj_ref, spread):
    _, slots, block_rows, _ = adj_ref.shape
    for step, targets in enumerate(places):
        terms = jnp.dot(
            upstream[:, step * block_rows : (step + 1) * block_rows],
            row_of(adj_ref, step, slots),
            preferred_element_type=jnp.float32,
        )
        for slot, target in enumerate(targets):
            spread[target] += terms[:, slot * block_rows : (slot + 1) * block_rows]


def rim_back_kernel(
    place_in, weight_ref, adj_ref, grad_ref, act_ref, act_in,
    act_hbm, spread, first_ref, second_ref, mark_ref,
    place_ref, sems,
):
    fetch = pltpu.make_async_copy(place_in, place_ref, sems.at[2])
    fetch.start()
    steps, slots, block_rows, _ = adj_ref.shape
    blocks = place_ref.shape[0] // slots
    rim = BAND * block_rows
    rows = blocks * block_rows
    copies = [
        pltpu.make_async_copy(act_ref.at[pl.ds(0, rim)], act_hbm.at[pl.ds(0, rim)], sems.at[0]),
        pltpu.make_async_copy(
            act_ref.at[pl.ds(rim, rim)], act_hbm.at[pl.ds(rows - rim, rim)], sems.at[1]
        ),
    ]
    for copy in copies:
        copy.start()
    spread[...] = jnp.zeros_like(spread)
    upstream = to_upstream(weight_ref[...], grad_ref[...])
    fetch.wait()
    scatter_rows(
        [places_of(place_ref, rim_block(step, blocks), slots) for step in range(steps)],
        upstream, adj_ref, spread,
    )
    odd = place_in_mesh() & 1
    for block in range(BAND):
        here = pl.ds(block * block_rows, block_rows)
        first_ref[here] = spread[(1 - odd) * 5 * BAND + block].T.astype(jnp.bfloat16)
        second_ref[here] = spread[odd * 5 * BAND + block].T.astype(jnp.bfloat16)
    mark_ref[...] = jnp.zeros_like(mark_ref)
    for copy in copies:
        copy.wait()


def inner_back_kernel(
    place_in, weight_ref, adj_ref, grad_ref, rim_spread,
    whole_hbm, edge_ref, mark_ref,
    place_ref, spread, out, sems,
):
    fetch = pltpu.make_async_copy(place_in, place_ref, sems.at[1])
    fetch.start()
    count, slots, block_rows, _ = adj_ref.shape
    blocks = place_ref.shape[0] // slots
    rim = BAND * block_rows
    spread[: 2 * BAND] = rim_spread[BAND : 3 * BAND]
    spread[2 * BAND :] = jnp.zeros_like(spread[2 * BAND :])
    spread[blocks - 2 * BAND : blocks] = rim_spread[3 * BAND : 5 * BAND]
    upstream = to_upstream(weight_ref[...], grad_ref[...])
    fetch.wait()
    scatter_rows(
        [places_of(place_ref, step + BAND, slots) for step in range(count)],
        upstream, adj_ref, spread,
    )
    for step in range(count):
        here = pl.ds(step * block_rows, block_rows)
        out[here] = spread[BAND + step].T.astype(jnp.bfloat16)
    finish = pltpu.make_async_copy(out, whole_hbm.at[pl.ds(rim, count * block_rows)], sems.at[0])
    finish.start()
    mark_ref[...] = jnp.zeros_like(mark_ref)
    for block in range(BAND):
        edge_ref[block * block_rows : (block + 1) * block_rows] = spread[block].T
        after = BAND + block
        edge_ref[after * block_rows : (after + 1) * block_rows] = spread[blocks - BAND + block].T
    finish.wait()


def add_kernel(parts, *refs):
    values = [ref[...].astype(jnp.float32) for ref in refs[:parts]]
    total = values[0] + values[1]
    if parts == 4:
        total = total + (values[2] + values[3])
    refs[-1][...] = total.astype(refs[-1].dtype)


def last_kernel(
    scale, own_ref, other_ref, edge_ref, first_ref, second_ref, whole_in,
    weight_out, bias_out, whole_hbm,
    out, sums, bias, sems,
):
    half = sums.shape[0] // 2
    rim = first_ref.shape[0]
    rows = whole_hbm.shape[0]
    copies = [
        pltpu.make_async_copy(sums, weight_out, sems.at[0]),
        pltpu.make_async_copy(bias, bias_out, sems.at[1]),
        pltpu.make_async_copy(out.at[pl.ds(0, rim)], whole_hbm.at[pl.ds(0, rim)], sems.at[2]),
        pltpu.make_async_copy(
            out.at[pl.ds(rim, rim)], whole_hbm.at[pl.ds(rows - rim, rim)], sems.at[3]
        ),
    ]
    side = core_side()
    own_rows = pl.ds(pl.multiple_of(side * half, half), half)
    other_rows = pl.ds(pl.multiple_of((1 - side) * half, half), half)
    sums[own_rows] = own_ref[:half] * scale
    sums[other_rows] = other_ref[:half] * scale
    copies[0].start()
    first = jnp.where(side == 0, own_ref[half : half + 1], other_ref[half : half + 1])
    bias[...] = first * scale
    copies[1].start()
    odd = place_in_mesh() & 1
    for base, spill_ref in (((1 - odd) * rim, first_ref), (odd * rim, second_ref)):
        here = pl.ds(pl.multiple_of(base, rim), rim)
        out[here] = (edge_ref[here] + spill_ref[...].astype(jnp.float32)).astype(jnp.bfloat16)
    for copy in copies[2:]:
        copy.start()
    for copy in copies:
        copy.wait()


def add(values, dtype, after=()):
    size = values[0].size
    return pl.pallas_call(
        functools.partial(add_kernel, len(values)),
        out_shape=jax.ShapeDtypeStruct(values[0].shape, dtype),
        in_specs=[pl.BlockSpec(memory_space=pltpu.VMEM)] * len(values)
        + [pl.BlockSpec(memory_space=pl.ANY)] * len(after),
        compiler_params=pltpu.CompilerParams(vmem_limit_bytes=2 * MIB),
        cost_estimate=pl.CostEstimate(
            flops=size * len(values), bytes_accessed=8 * size, transcendentals=0
        ),
        name="add_halves",
    )(*values, *after)


def swap(value, masks):
    pairs = [(i, i ^ mask) for i, mask in enumerate(masks) if mask]
    return lax.ppermute(value, AXES, pairs)


def with_next(value, count):
    pairs = [(0, 0), (count - 1, count - 1)]
    pairs += [(i, i + 1 if i & 1 else i - 1) for i in range(1, count - 1)]
    return lax.ppermute(value, AXES, pairs)


def sum_halves(send, keep, count, core_bit, marks):
    others = [bit for bit in range(count.bit_length() - 1) if bit != core_bit]
    groups = [others[i : i + 2] for i in range(0, len(others), 2)]
    total = add([keep, swap(send, [1 << core_bit] * count)], jnp.bfloat16, marks.get("core", ()))
    for step in range(len(groups)):
        masks = []
        for group in (groups[step], groups[len(groups) - 1 - step]):
            if len(groups[0]) != len(groups[-1]):
                group = groups[step]
            low = 1 << group[0]
            masks.append((low, 1 << group[1], low | 1 << group[1]) if group[1:] else (low,))
        parts = [total] + [
            swap(total, [masks[(i >> core_bit) & 1][k] for i in range(count)])
            for k in range(len(masks[0]))
        ]
        last = step == len(groups) - 1
        name = "last" if last else step
        total = add(parts, jnp.float32 if last else jnp.bfloat16, marks.get(name, ()))
    return total


def on_device(features, adj_values, adj_offset, adj_count, weight, bias_vector, cotangent):
    blocks, slots = adj_offset.shape
    block_rows = adj_values.shape[2]
    rows, width = features.shape
    rim = BAND * block_rows
    inner = rows - 2 * rim
    cols = lax.axis_size("cols")
    count = lax.axis_size("rows") * cols
    vmem = pl.BlockSpec(memory_space=pltpu.VMEM)
    hbm = pl.BlockSpec(memory_space=pltpu.HBM)
    anywhere = pl.BlockSpec(memory_space=pl.ANY)
    place_scratch = pltpu.SMEM((blocks * slots,), jnp.int32)
    bias_row = bias_vector.reshape(1, width)

    def in_hbm(value):
        return pltpu.with_memory_space_constraint(value, pltpu.HBM)

    def shape(*sizes, dtype=jnp.bfloat16):
        return jax.ShapeDtypeStruct(sizes, dtype)

    def params(mib):
        return pltpu.CompilerParams(vmem_limit_bytes=mib * MIB)

    def cost(share):
        return pl.CostEstimate(
            flops=int(1.2e9 * share), bytes_accessed=int(6e6 * share),
            transcendentals=int(8e5 * share),
        )

    offsets = in_hbm(adj_offset.T)
    counts = in_hbm(adj_count)
    core_bit = cols.bit_length() - 1
    first_rim, second_rim = pl.pallas_call(
        halo_kernel,
        out_shape=(shape(rim, width), shape(rim, width)),
        in_specs=[hbm],
        out_specs=(vmem, vmem),
        scratch_shapes=[pltpu.SemaphoreType.DMA((2,))],
        compiler_params=params(2),
        cost_estimate=cost(0.05),
        name="halo_rows",
    )(in_hbm(features))
    first_halo = swap(first_rim, [1] * count)
    second_halo = with_next(second_rim, count)
    (
        activated, places, grad_inner, partial, sums, weight_near, bias_near, feat_rim, adj_rim,
        cot_rim, adj_inner,
    ) = pl.pallas_call(
        inner_kernel,
        out_shape=(
            shape(rows, width),
            shape(blocks * slots, dtype=jnp.int32),
            shape(inner, width),
            shape(width, width, dtype=jnp.float32),
            shape(8, width, dtype=jnp.float32),
            shape(width, width),
            shape(1, width, dtype=jnp.float32),
            shape(4 * rim, width),
            shape(2 * BAND, slots, block_rows, block_rows),
            shape(2 * rim, width),
            shape(blocks - 2 * BAND, slots, block_rows, block_rows),
        ),
        in_specs=[hbm] * 7,
        out_specs=(hbm, anywhere) + (vmem,) * 9,
        scratch_shapes=[
            pltpu.SMEM((slots, blocks), jnp.int32),
            pltpu.SMEM((blocks,), jnp.int32),
            place_scratch,
            pltpu.VMEM((rows + block_rows, width), jnp.bfloat16),
            pltpu.VMEM((inner, width), jnp.bfloat16),
            pltpu.VMEM((inner, width), jnp.bfloat16),
            pltpu.VMEM((inner, width), jnp.bfloat16),
            pltpu.SemaphoreType.DMA((15,)),
        ],
        compiler_params=params(20),
        cost_estimate=cost(0.5),
        name="inner_rows",
    )(
        offsets, counts,
        *(in_hbm(x) for x in (weight, bias_row, features, adj_values, cotangent)),
    )
    half_shape = (width // 2 + TAIL, width)
    act_rim, grad_rim, send, keep = pl.pallas_call(
        rim_kernel,
        out_shape=(
            shape(2 * rim, width),
            shape(2 * rim, width),
            shape(*half_shape, dtype=jnp.float32),
            shape(*half_shape, dtype=jnp.float32),
        ),
        in_specs=[anywhere] + [vmem] * 9,
        out_specs=(vmem,) * 4,
        scratch_shapes=[
            place_scratch,
            pltpu.VMEM((6 * rim + block_rows, width), jnp.bfloat16),
            pltpu.VMEM((2 * rim, width), jnp.bfloat16),
            pltpu.VMEM((2,) + half_shape, jnp.float32),
            pltpu.SemaphoreType.DMA((1,)),
        ],
        compiler_params=params(12),
        cost_estimate=cost(0.2),
        name="rim_rows",
    )(
        places, weight_near, bias_near, feat_rim, first_halo, second_halo, adj_rim, cot_rim,
        partial, sums,
    )
    mark = shape(8, 128, dtype=jnp.float32)
    activated, rim_spread, first_spill, second_spill, first_mark = pl.pallas_call(
        rim_back_kernel,
        out_shape=(
            shape(rows, width),
            shape(6 * BAND + 1, width, block_rows, dtype=jnp.float32),
            shape(rim, width),
            shape(rim, width),
            mark,
        ),
        in_specs=[anywhere] + [vmem] * 4 + [hbm],
        out_specs=(hbm,) + (vmem,) * 4,
        scratch_shapes=[place_scratch, pltpu.SemaphoreType.DMA((3,))],
        input_output_aliases={5: 0},
        compiler_params=params(12),
        cost_estimate=cost(0.2),
        name="rim_rows_back",
    )(places, weight_near, adj_rim, grad_rim, act_rim, activated)
    first_part = swap(first_spill, [1] * count)
    second_part = with_next(second_spill, count)
    grad_whole, edges, second_mark = pl.pallas_call(
        inner_back_kernel,
        out_shape=(shape(rows, width), shape(2 * rim, width, dtype=jnp.float32), mark),
        in_specs=[anywhere] + [vmem] * 4,
        out_specs=(hbm, vmem, vmem),
        scratch_shapes=[
            place_scratch,
            pltpu.VMEM((blocks + 1, width, block_rows), jnp.float32),
            pltpu.VMEM((inner, width), jnp.bfloat16),
            pltpu.SemaphoreType.DMA((2,)),
        ],
        compiler_params=params(12),
        cost_estimate=cost(0.3),
        name="inner_rows_back",
    )(places, weight_near, adj_inner, grad_inner, rim_spread)
    marks = {"core": (first_mark,), "last": (second_mark, first_part, second_part)}
    own_half = sum_halves(send, keep, count, core_bit, marks)
    other_half = swap(own_half, [1 << core_bit] * count)
    norm_scale = 1.0 / math.sqrt(rows * count)
    grad_weight, grad_bias, grad_features = pl.pallas_call(
        functools.partial(last_kernel, norm_scale),
        out_shape=(
            shape(width, width, dtype=jnp.float32),
            shape(1, width, dtype=jnp.float32),
            shape(rows, width),
        ),
        in_specs=[vmem] * 5 + [hbm],
        out_specs=(hbm, hbm, hbm),
        scratch_shapes=[
            pltpu.VMEM((2 * rim, width), jnp.bfloat16),
            pltpu.VMEM((width, width), jnp.float32),
            pltpu.VMEM((1, width), jnp.float32),
            pltpu.SemaphoreType.DMA((4,)),
        ],
        input_output_aliases={5: 2},
        compiler_params=params(8),
        name="last_step",
    )(own_half, other_half, edges, first_part, second_part, grad_whole)
    return (activated, grad_features, grad_weight, grad_bias.reshape(width))


def solution(mesh):
    return jax.shard_map(
        on_device,
        mesh=mesh,
        in_specs=(
            P(AXES, None),
            P(AXES, None, None, None),
            P(AXES, None),
            P(AXES),
            P(),
            P(),
            P(AXES, None),
        ),
        out_specs=(P(AXES, None), P(AXES, None), P(), P()),
        check_vma=False,
    )
```

```python
import functools
import math

import jax
import jax.numpy as jnp
from jax import lax
from jax.experimental import pallas as pl
from jax.experimental.pallas import tpu as pltpu
from jax.sharding import PartitionSpec as P

BAND = 2
TAIL = 16
AXES = ("rows", "cols")
MIB = 1024 * 1024


def row_of(adj_ref, block, slots):
    return jnp.concatenate([adj_ref[block, slot] for slot in range(slots)], 1)


def pick(source, places, block_rows):
    return jnp.concatenate(
        [
            source[pl.ds(pl.multiple_of(place * block_rows, block_rows), block_rows)]
            for place in places
        ],
        0,
    )


def write_places(off_ref, cnt_ref, place_ref, blocks, slots):
    for block in range(blocks):
        if block < BAND:
            shift, dump = BAND, 6 * BAND
        elif block < blocks - BAND:
            shift, dump = 0, blocks
        else:
            shift, dump = 5 * BAND - blocks, 6 * BAND
        for slot in range(slots):
            place_ref[block * slots + slot] = jnp.where(
                slot < cnt_ref[block], block + shift + off_ref[slot, block], dump
            )


def places_of(place_ref, block, slots):
    return [place_ref[block * slots + slot] for slot in range(slots)]


def rim_block(step, blocks):
    return step if step < BAND else blocks - 2 * BAND + step


def place_in_mesh():
    return lax.axis_index("rows") * lax.axis_size("cols") + lax.axis_index("cols")


def core_side():
    return lax.axis_index("rows") & 1


def halo_kernel(feat_hbm, first_ref, second_ref, sems):
    rows = feat_hbm.shape[0]
    rim = first_ref.shape[0]
    odd = place_in_mesh() & 1
    last = rows - rim
    starts = ((1 - odd) * last, odd * last)
    copies = [
        pltpu.make_async_copy(
            feat_hbm.at[pl.ds(pl.multiple_of(start, rim), rim)], out_ref, sems.at[i]
        )
        for i, (start, out_ref) in enumerate(zip(starts, (first_ref, second_ref)))
    ]
    for copy in copies:
        copy.start()
    for copy in copies:
        copy.wait()


def activate(preact, cotangent):
    gate = 1.0 / (1.0 + jnp.exp(-preact))
    grad = cotangent.astype(jnp.float32) * gate * (1.0 + preact * (1.0 - gate))
    return (preact * gate).astype(jnp.bfloat16), grad.astype(jnp.bfloat16)


def column_sums(grad):
    rows, width = grad.shape
    return jnp.sum(grad.astype(jnp.float32).reshape(rows // 8, 8, width), axis=0)


def to_upstream(weight, grad):
    return lax.dot_general(
        weight, grad, (((1,), (1,)), ((), ())), preferred_element_type=jnp.float32
    ).astype(jnp.bfloat16)


def weight_terms(agg, grad):
    return lax.dot_general(
        agg, grad, (((0,), (0,)), ((), ())), preferred_element_type=jnp.float32
    )


def inner_kernel(
    off_hbm, cnt_hbm, weight_hbm, bias_hbm, feat_hbm, adj_hbm, cot_hbm,
    act_hbm, place_out, grad_ref, partial_ref, sums_ref, weight_ref, bias_ref, feat_rim, adj_rim,
    cot_rim, adj,
    off_ref, cnt_ref, place_ref, feat, cot, act, agg_all, sems,
):
    blocks, slots, block_rows, _ = adj_hbm.shape
    rows, width = feat_hbm.shape
    count = blocks - 2 * BAND
    rim = BAND * block_rows
    half = 2 * rim
    inner = count * block_rows
    scalars = [
        pltpu.make_async_copy(off_hbm, off_ref, sems.at[12]),
        pltpu.make_async_copy(cnt_hbm, cnt_ref, sems.at[13]),
    ]
    copies = [
        pltpu.make_async_copy(feat_hbm, feat.at[pl.ds(0, rows)], sems.at[0]),
        pltpu.make_async_copy(adj_hbm.at[pl.ds(BAND, count)], adj, sems.at[1]),
        pltpu.make_async_copy(weight_hbm, weight_ref, sems.at[2]),
        pltpu.make_async_copy(bias_hbm, bias_ref, sems.at[3]),
        pltpu.make_async_copy(cot_hbm.at[pl.ds(rim, inner)], cot, sems.at[4]),
        pltpu.make_async_copy(feat_hbm.at[pl.ds(0, half)], feat_rim.at[pl.ds(0, half)], sems.at[5]),
        pltpu.make_async_copy(
            feat_hbm.at[pl.ds(rows - half, half)], feat_rim.at[pl.ds(half, half)], sems.at[6]
        ),
        pltpu.make_async_copy(adj_hbm.at[pl.ds(0, BAND)], adj_rim.at[pl.ds(0, BAND)], sems.at[7]),
        pltpu.make_async_copy(
            adj_hbm.at[pl.ds(blocks - BAND, BAND)], adj_rim.at[pl.ds(BAND, BAND)], sems.at[8]
        ),
        pltpu.make_async_copy(cot_hbm.at[pl.ds(0, rim)], cot_rim.at[pl.ds(0, rim)], sems.at[9]),
        pltpu.make_async_copy(
            cot_hbm.at[pl.ds(rows - rim, rim)], cot_rim.at[pl.ds(rim, rim)], sems.at[10]
        ),
    ]
    for copy in scalars + copies:
        copy.start()
    feat[rows:] = jnp.zeros((block_rows, width), jnp.bfloat16)
    for copy in scalars:
        copy.wait()
    write_places(off_ref, cnt_ref, place_ref, blocks, slots)
    place_copy = pltpu.make_async_copy(place_ref, place_out, sems.at[14])
    place_copy.start()
    for copy in copies[:5]:
        copy.wait()
    weight = weight_ref[...]
    bias = bias_ref[...]
    sums = jnp.zeros((8, width), jnp.float32)
    for step in range(0, count, 2):
        for block in (step, step + 1):
            places = places_of(place_ref, block + BAND, slots)
            agg_all[block * block_rows : (block + 1) * block_rows] = jnp.dot(
                row_of(adj, block, slots), pick(feat, places, block_rows),
                preferred_element_type=jnp.float32,
            ).astype(jnp.bfloat16)
        here = pl.ds(step * block_rows, 2 * block_rows)
        preact = jnp.dot(agg_all[here], weight, preferred_element_type=jnp.float32) + bias
        act[here], grad = activate(preact, cot[here])
        grad_ref[here] = grad
        sums = sums + column_sums(grad)
    act_out = pltpu.make_async_copy(act, act_hbm.at[pl.ds(rim, inner)], sems.at[11])
    act_out.start()
    sums_ref[...] = sums
    partial_ref[...] = weight_terms(agg_all[...], grad_ref[...])
    for copy in copies[5:]:
        copy.wait()
    act_out.wait()
    place_copy.wait()


def rim_kernel(
    place_in, weight_ref, bias_ref, feat_ref, first_ref, second_ref, adj_ref, cot_ref,
    partial_ref, sums_ref,
    act_ref, grad_ref, send_ref, keep_ref,
    place_ref, window, agg_all, payload, sems,
):
    fetch = pltpu.make_async_copy(place_in, place_ref, sems.at[0])
    fetch.start()
    steps, slots, block_rows, _ = adj_ref.shape
    blocks = place_ref.shape[0] // slots
    width = feat_ref.shape[1]
    rim = BAND * block_rows
    odd = place_in_mesh() & 1
    window[pl.ds(pl.multiple_of((1 - odd) * 5 * rim, rim), rim)] = first_ref[...]
    window[pl.ds(pl.multiple_of(odd * 5 * rim, rim), rim)] = second_ref[...]
    window[rim : 5 * rim] = feat_ref[...]
    window[6 * rim :] = jnp.zeros((block_rows, width), jnp.bfloat16)
    weight = weight_ref[...]
    bias = bias_ref[...]
    sums = sums_ref[...]
    fetch.wait()
    for step in range(0, steps, 2):
        for block in (step, step + 1):
            places = places_of(place_ref, rim_block(block, blocks), slots)
            agg_all[block * block_rows : (block + 1) * block_rows] = jnp.dot(
                row_of(adj_ref, block, slots), pick(window, places, block_rows),
                preferred_element_type=jnp.float32,
            ).astype(jnp.bfloat16)
        here = pl.ds(step * block_rows, 2 * block_rows)
        preact = jnp.dot(agg_all[here], weight, preferred_element_type=jnp.float32) + bias
        act_ref[here], grad = activate(preact, cot_ref[here])
        grad_ref[here] = grad
        sums = sums + column_sums(grad)
    half = width // 2
    partial = partial_ref[...] + weight_terms(agg_all[...], grad_ref[...])
    payload[0, :half] = partial[:half]
    payload[1, :half] = partial[half:]
    tail = jnp.zeros((TAIL, width), jnp.float32)
    payload[0, half:] = jnp.broadcast_to(jnp.sum(sums, axis=0, keepdims=True), tail.shape)
    payload[1, half:] = tail
    side = core_side()
    keep_ref[...] = payload[side]
    send_ref[...] = payload[1 - side]


def scatter_rows(places, upstream, adj_ref, spread):
    _, slots, block_rows, _ = adj_ref.shape
    for step, targets in enumerate(places):
        terms = jnp.dot(
            upstream[:, step * block_rows : (step + 1) * block_rows],
            row_of(adj_ref, step, slots),
            preferred_element_type=jnp.float32,
        )
        for slot, target in enumerate(targets):
            spread[target] += terms[:, slot * block_rows : (slot + 1) * block_rows]


def rim_back_kernel(
    place_in, weight_ref, adj_ref, grad_ref, act_ref, act_in,
    act_hbm, spread, first_ref, second_ref, mark_ref,
    place_ref, sems,
):
    fetch = pltpu.make_async_copy(place_in, place_ref, sems.at[2])
    fetch.start()
    steps, slots, block_rows, _ = adj_ref.shape
    blocks = place_ref.shape[0] // slots
    rim = BAND * block_rows
    rows = blocks * block_rows
    copies = [
        pltpu.make_async_copy(act_ref.at[pl.ds(0, rim)], act_hbm.at[pl.ds(0, rim)], sems.at[0]),
        pltpu.make_async_copy(
            act_ref.at[pl.ds(rim, rim)], act_hbm.at[pl.ds(rows - rim, rim)], sems.at[1]
        ),
    ]
    for copy in copies:
        copy.start()
    spread[...] = jnp.zeros_like(spread)
    upstream = to_upstream(weight_ref[...], grad_ref[...])
    fetch.wait()
    scatter_rows(
        [places_of(place_ref, rim_block(step, blocks), slots) for step in range(steps)],
        upstream, adj_ref, spread,
    )
    odd = place_in_mesh() & 1
    for block in range(BAND):
        here = pl.ds(block * block_rows, block_rows)
        first_ref[here] = spread[(1 - odd) * 5 * BAND + block].T.astype(jnp.bfloat16)
        second_ref[here] = spread[odd * 5 * BAND + block].T.astype(jnp.bfloat16)
    mark_ref[...] = jnp.zeros_like(mark_ref)
    for copy in copies:
        copy.wait()


def inner_back_kernel(
    place_in, weight_ref, adj_ref, grad_ref, rim_spread,
    whole_hbm, edge_ref, mark_ref,
    place_ref, spread, out, sems,
):
    fetch = pltpu.make_async_copy(place_in, place_ref, sems.at[1])
    fetch.start()
    count, slots, block_rows, _ = adj_ref.shape
    blocks = place_ref.shape[0] // slots
    rim = BAND * block_rows
    spread[: 2 * BAND] = rim_spread[BAND : 3 * BAND]
    spread[2 * BAND :] = jnp.zeros_like(spread[2 * BAND :])
    spread[blocks - 2 * BAND : blocks] = rim_spread[3 * BAND : 5 * BAND]
    upstream = to_upstream(weight_ref[...], grad_ref[...])
    fetch.wait()
    scatter_rows(
        [places_of(place_ref, step + BAND, slots) for step in range(count)],
        upstream, adj_ref, spread,
    )
    for step in range(count):
        here = pl.ds(step * block_rows, block_rows)
        out[here] = spread[BAND + step].T.astype(jnp.bfloat16)
    finish = pltpu.make_async_copy(out, whole_hbm.at[pl.ds(rim, count * block_rows)], sems.at[0])
    finish.start()
    mark_ref[...] = jnp.zeros_like(mark_ref)
    for block in range(BAND):
        edge_ref[block * block_rows : (block + 1) * block_rows] = spread[block].T
        after = BAND + block
        edge_ref[after * block_rows : (after + 1) * block_rows] = spread[blocks - BAND + block].T
    finish.wait()


def add_kernel(parts, *refs):
    values = [ref[...].astype(jnp.float32) for ref in refs[:parts]]
    total = values[0] + values[1]
    if parts == 4:
        total = total + (values[2] + values[3])
    refs[-1][...] = total.astype(refs[-1].dtype)


def last_kernel(
    scale, own_ref, other_ref, edge_ref, first_ref, second_ref, whole_in,
    weight_out, bias_out, whole_hbm,
    out, sums, bias, sems,
):
    half = sums.shape[0] // 2
    rim = first_ref.shape[0]
    rows = whole_hbm.shape[0]
    copies = [
        pltpu.make_async_copy(sums, weight_out, sems.at[0]),
        pltpu.make_async_copy(bias, bias_out, sems.at[1]),
        pltpu.make_async_copy(out.at[pl.ds(0, rim)], whole_hbm.at[pl.ds(0, rim)], sems.at[2]),
        pltpu.make_async_copy(
            out.at[pl.ds(rim, rim)], whole_hbm.at[pl.ds(rows - rim, rim)], sems.at[3]
        ),
    ]
    side = core_side()
    own_rows = pl.ds(pl.multiple_of(side * half, half), half)
    other_rows = pl.ds(pl.multiple_of((1 - side) * half, half), half)
    sums[own_rows] = own_ref[:half] * scale
    sums[other_rows] = other_ref[:half] * scale
    copies[0].start()
    first = jnp.where(side == 0, own_ref[half : half + 1], other_ref[half : half + 1])
    bias[...] = first * scale
    copies[1].start()
    odd = place_in_mesh() & 1
    for base, spill_ref in (((1 - odd) * rim, first_ref), (odd * rim, second_ref)):
        here = pl.ds(pl.multiple_of(base, rim), rim)
        out[here] = (edge_ref[here] + spill_ref[...].astype(jnp.float32)).astype(jnp.bfloat16)
    for copy in copies[2:]:
        copy.start()
    for copy in copies:
        copy.wait()


def add(values, dtype, after=()):
    size = values[0].size
    return pl.pallas_call(
        functools.partial(add_kernel, len(values)),
        out_shape=jax.ShapeDtypeStruct(values[0].shape, dtype),
        in_specs=[pl.BlockSpec(memory_space=pltpu.VMEM)] * len(values)
        + [pl.BlockSpec(memory_space=pl.ANY)] * len(after),
        compiler_params=pltpu.CompilerParams(vmem_limit_bytes=2 * MIB),
        cost_estimate=pl.CostEstimate(
            flops=size * len(values), bytes_accessed=8 * size, transcendentals=0
        ),
        name="add_halves",
    )(*values, *after)


def swap(value, masks):
    pairs = [(i, i ^ mask) for i, mask in enumerate(masks) if mask]
    return lax.ppermute(value, AXES, pairs)


def with_next(value, count):
    pairs = [(i, (i + 1 if i & 1 else i - 1) % count) for i in range(count)]
    return lax.ppermute(value, AXES, pairs)


def sum_halves(send, keep, count, core_bit, marks):
    others = [bit for bit in range(count.bit_length() - 1) if bit != core_bit]
    groups = [others[i : i + 2] for i in range(0, len(others), 2)]
    total = add([keep, swap(send, [1 << core_bit] * count)], jnp.bfloat16, marks.get("core", ()))
    for step in range(len(groups)):
        masks = []
        for group in (groups[step], groups[len(groups) - 1 - step]):
            if len(groups[0]) != len(groups[-1]):
                group = groups[step]
            low = 1 << group[0]
            masks.append((low, 1 << group[1], low | 1 << group[1]) if group[1:] else (low,))
        parts = [total] + [
            swap(total, [masks[(i >> core_bit) & 1][k] for i in range(count)])
            for k in range(len(masks[0]))
        ]
        last = step == len(groups) - 1
        name = "last" if last else step
        total = add(parts, jnp.float32 if last else jnp.bfloat16, marks.get(name, ()))
    return total


def on_device(features, adj_values, adj_offset, adj_count, weight, bias_vector, cotangent):
    blocks, slots = adj_offset.shape
    block_rows = adj_values.shape[2]
    rows, width = features.shape
    rim = BAND * block_rows
    inner = rows - 2 * rim
    cols = lax.axis_size("cols")
    count = lax.axis_size("rows") * cols
    vmem = pl.BlockSpec(memory_space=pltpu.VMEM)
    hbm = pl.BlockSpec(memory_space=pltpu.HBM)
    anywhere = pl.BlockSpec(memory_space=pl.ANY)
    place_scratch = pltpu.SMEM((blocks * slots,), jnp.int32)
    bias_row = bias_vector.reshape(1, width)

    def in_hbm(value):
        return pltpu.with_memory_space_constraint(value, pltpu.HBM)

    def shape(*sizes, dtype=jnp.bfloat16):
        return jax.ShapeDtypeStruct(sizes, dtype)

    def params(mib):
        return pltpu.CompilerParams(vmem_limit_bytes=mib * MIB)

    def cost(share):
        return pl.CostEstimate(
            flops=int(1.2e9 * share), bytes_accessed=int(6e6 * share),
            transcendentals=int(8e5 * share),
        )

    offsets = in_hbm(adj_offset.T)
    counts = in_hbm(adj_count)
    core_bit = cols.bit_length() - 1
    first_rim, second_rim = pl.pallas_call(
        halo_kernel,
        out_shape=(shape(rim, width), shape(rim, width)),
        in_specs=[hbm],
        out_specs=(vmem, vmem),
        scratch_shapes=[pltpu.SemaphoreType.DMA((2,))],
        compiler_params=params(2),
        cost_estimate=cost(0.05),
        name="halo_rows",
    )(in_hbm(features))
    first_halo = swap(first_rim, [1] * count)
    second_halo = with_next(second_rim, count)
    (
        activated, places, grad_inner, partial, sums, weight_near, bias_near, feat_rim, adj_rim,
        cot_rim, adj_inner,
    ) = pl.pallas_call(
        inner_kernel,
        out_shape=(
            shape(rows, width),
            shape(blocks * slots, dtype=jnp.int32),
            shape(inner, width),
            shape(width, width, dtype=jnp.float32),
            shape(8, width, dtype=jnp.float32),
            shape(width, width),
            shape(1, width, dtype=jnp.float32),
            shape(4 * rim, width),
            shape(2 * BAND, slots, block_rows, block_rows),
            shape(2 * rim, width),
            shape(blocks - 2 * BAND, slots, block_rows, block_rows),
        ),
        in_specs=[hbm] * 7,
        out_specs=(hbm, anywhere) + (vmem,) * 9,
        scratch_shapes=[
            pltpu.SMEM((slots, blocks), jnp.int32),
            pltpu.SMEM((blocks,), jnp.int32),
            place_scratch,
            pltpu.VMEM((rows + block_rows, width), jnp.bfloat16),
            pltpu.VMEM((inner, width), jnp.bfloat16),
            pltpu.VMEM((inner, width), jnp.bfloat16),
            pltpu.VMEM((inner, width), jnp.bfloat16),
            pltpu.SemaphoreType.DMA((15,)),
        ],
        compiler_params=params(20),
        cost_estimate=cost(0.5),
        name="inner_rows",
    )(
        offsets, counts,
        *(in_hbm(x) for x in (weight, bias_row, features, adj_values, cotangent)),
    )
    half_shape = (width // 2 + TAIL, width)
    act_rim, grad_rim, send, keep = pl.pallas_call(
        rim_kernel,
        out_shape=(
            shape(2 * rim, width),
            shape(2 * rim, width),
            shape(*half_shape, dtype=jnp.float32),
            shape(*half_shape, dtype=jnp.float32),
        ),
        in_specs=[anywhere] + [vmem] * 9,
        out_specs=(vmem,) * 4,
        scratch_shapes=[
            place_scratch,
            pltpu.VMEM((6 * rim + block_rows, width), jnp.bfloat16),
            pltpu.VMEM((2 * rim, width), jnp.bfloat16),
            pltpu.VMEM((2,) + half_shape, jnp.float32),
            pltpu.SemaphoreType.DMA((1,)),
        ],
        compiler_params=params(12),
        cost_estimate=cost(0.2),
        name="rim_rows",
    )(
        places, weight_near, bias_near, feat_rim, first_halo, second_halo, adj_rim, cot_rim,
        partial, sums,
    )
    mark = shape(8, 128, dtype=jnp.float32)
    activated, rim_spread, first_spill, second_spill, first_mark = pl.pallas_call(
        rim_back_kernel,
        out_shape=(
            shape(rows, width),
            shape(6 * BAND + 1, width, block_rows, dtype=jnp.float32),
            shape(rim, width),
            shape(rim, width),
            mark,
        ),
        in_specs=[anywhere] + [vmem] * 4 + [hbm],
        out_specs=(hbm,) + (vmem,) * 4,
        scratch_shapes=[place_scratch, pltpu.SemaphoreType.DMA((3,))],
        input_output_aliases={5: 0},
        compiler_params=params(12),
        cost_estimate=cost(0.2),
        name="rim_rows_back",
    )(places, weight_near, adj_rim, grad_rim, act_rim, activated)
    first_part = swap(first_spill, [1] * count)
    second_part = with_next(second_spill, count)
    grad_whole, edges, second_mark = pl.pallas_call(
        inner_back_kernel,
        out_shape=(shape(rows, width), shape(2 * rim, width, dtype=jnp.float32), mark),
        in_specs=[anywhere] + [vmem] * 4,
        out_specs=(hbm, vmem, vmem),
        scratch_shapes=[
            place_scratch,
            pltpu.VMEM((blocks + 1, width, block_rows), jnp.float32),
            pltpu.VMEM((inner, width), jnp.bfloat16),
            pltpu.SemaphoreType.DMA((2,)),
        ],
        compiler_params=params(12),
        cost_estimate=cost(0.3),
        name="inner_rows_back",
    )(places, weight_near, adj_inner, grad_inner, rim_spread)
    marks = {"core": (first_mark,), "last": (second_mark, first_part, second_part)}
    own_half = sum_halves(send, keep, count, core_bit, marks)
    other_half = swap(own_half, [1 << core_bit] * count)
    norm_scale = 1.0 / math.sqrt(rows * count)
    grad_weight, grad_bias, grad_features = pl.pallas_call(
        functools.partial(last_kernel, norm_scale),
        out_shape=(
            shape(width, width, dtype=jnp.float32),
            shape(1, width, dtype=jnp.float32),
            shape(rows, width),
        ),
        in_specs=[vmem] * 5 + [hbm],
        out_specs=(hbm, hbm, hbm),
        scratch_shapes=[
            pltpu.VMEM((2 * rim, width), jnp.bfloat16),
            pltpu.VMEM((width, width), jnp.float32),
            pltpu.VMEM((1, width), jnp.float32),
            pltpu.SemaphoreType.DMA((4,)),
        ],
        input_output_aliases={5: 2},
        compiler_params=params(8),
        name="last_step",
    )(own_half, other_half, edges, first_part, second_part, grad_whole)
    return (activated, grad_features, grad_weight, grad_bias.reshape(width))


def solution(mesh):
    return jax.shard_map(
        on_device,
        mesh=mesh,
        in_specs=(
            P(AXES, None),
            P(AXES, None, None, None),
            P(AXES, None),
            P(AXES),
            P(),
            P(),
            P(AXES, None),
        ),
        out_specs=(P(AXES, None), P(AXES, None), P(), P()),
        check_vma=False,
    )
```

```python
import functools
import math

import jax
import jax.numpy as jnp
from jax import lax
from jax.experimental import pallas as pl
from jax.experimental.pallas import tpu as pltpu
from jax.sharding import PartitionSpec as P

BAND = 2
TAIL = 8
AXES = ("rows", "cols")
MIB = 1024 * 1024


def row_of(adj_ref, block, slots):
    return jnp.concatenate([adj_ref[block, slot] for slot in range(slots)], 1)


def pick(source, places, block_rows):
    return jnp.concatenate(
        [
            source[pl.ds(pl.multiple_of(place * block_rows, block_rows), block_rows)]
            for place in places
        ],
        0,
    )


def write_places(off_ref, cnt_ref, place_ref, blocks, slots):
    for block in range(blocks):
        if block < BAND:
            shift, dump = BAND, 6 * BAND
        elif block < blocks - BAND:
            shift, dump = 0, blocks
        else:
            shift, dump = 5 * BAND - blocks, 6 * BAND
        for slot in range(slots):
            place_ref[block * slots + slot] = jnp.where(
                slot < cnt_ref[block], block + shift + off_ref[slot, block], dump
            )


def places_of(place_ref, block, slots):
    return [place_ref[block * slots + slot] for slot in range(slots)]


def rim_block(step, blocks):
    return step if step < BAND else blocks - 2 * BAND + step


def place_in_mesh():
    return lax.axis_index("rows") * lax.axis_size("cols") + lax.axis_index("cols")


def core_side():
    return lax.axis_index("rows") & 1


def halo_kernel(feat_hbm, first_ref, second_ref, sems):
    rows = feat_hbm.shape[0]
    rim = first_ref.shape[0]
    odd = place_in_mesh() & 1
    last = rows - rim
    starts = ((1 - odd) * last, odd * last)
    copies = [
        pltpu.make_async_copy(
            feat_hbm.at[pl.ds(pl.multiple_of(start, rim), rim)], out_ref, sems.at[i]
        )
        for i, (start, out_ref) in enumerate(zip(starts, (first_ref, second_ref)))
    ]
    for copy in copies:
        copy.start()
    for copy in copies:
        copy.wait()


def activate(preact, cotangent):
    gate = 1.0 / (1.0 + jnp.exp(-preact))
    grad = cotangent.astype(jnp.float32) * gate * (1.0 + preact * (1.0 - gate))
    return (preact * gate).astype(jnp.bfloat16), grad.astype(jnp.bfloat16)


def column_sums(grad):
    rows, width = grad.shape
    return jnp.sum(grad.astype(jnp.float32).reshape(rows // 8, 8, width), axis=0)


def to_upstream(weight, grad):
    return lax.dot_general(
        weight, grad, (((1,), (1,)), ((), ())), preferred_element_type=jnp.float32
    ).astype(jnp.bfloat16)


def weight_terms(agg, grad):
    return lax.dot_general(
        agg, grad, (((0,), (0,)), ((), ())), preferred_element_type=jnp.float32
    )


def inner_kernel(
    off_hbm, cnt_hbm, weight_hbm, bias_hbm, feat_hbm, adj_hbm, cot_hbm,
    act_hbm, place_out, grad_ref, partial_ref, sums_ref, weight_ref, bias_ref, feat_rim, adj_rim,
    cot_rim, adj,
    off_ref, cnt_ref, place_ref, feat, cot, act, agg_all, sems,
):
    blocks, slots, block_rows, _ = adj_hbm.shape
    rows, width = feat_hbm.shape
    count = blocks - 2 * BAND
    rim = BAND * block_rows
    half = 2 * rim
    inner = count * block_rows
    scalars = [
        pltpu.make_async_copy(off_hbm, off_ref, sems.at[12]),
        pltpu.make_async_copy(cnt_hbm, cnt_ref, sems.at[13]),
    ]
    copies = [
        pltpu.make_async_copy(feat_hbm, feat.at[pl.ds(0, rows)], sems.at[0]),
        pltpu.make_async_copy(adj_hbm.at[pl.ds(BAND, count)], adj, sems.at[1]),
        pltpu.make_async_copy(weight_hbm, weight_ref, sems.at[2]),
        pltpu.make_async_copy(bias_hbm, bias_ref, sems.at[3]),
        pltpu.make_async_copy(cot_hbm.at[pl.ds(rim, inner)], cot, sems.at[4]),
        pltpu.make_async_copy(feat_hbm.at[pl.ds(0, half)], feat_rim.at[pl.ds(0, half)], sems.at[5]),
        pltpu.make_async_copy(
            feat_hbm.at[pl.ds(rows - half, half)], feat_rim.at[pl.ds(half, half)], sems.at[6]
        ),
        pltpu.make_async_copy(adj_hbm.at[pl.ds(0, BAND)], adj_rim.at[pl.ds(0, BAND)], sems.at[7]),
        pltpu.make_async_copy(
            adj_hbm.at[pl.ds(blocks - BAND, BAND)], adj_rim.at[pl.ds(BAND, BAND)], sems.at[8]
        ),
        pltpu.make_async_copy(cot_hbm.at[pl.ds(0, rim)], cot_rim.at[pl.ds(0, rim)], sems.at[9]),
        pltpu.make_async_copy(
            cot_hbm.at[pl.ds(rows - rim, rim)], cot_rim.at[pl.ds(rim, rim)], sems.at[10]
        ),
    ]
    for copy in scalars + copies:
        copy.start()
    feat[rows:] = jnp.zeros((block_rows, width), jnp.bfloat16)
    for copy in scalars:
        copy.wait()
    write_places(off_ref, cnt_ref, place_ref, blocks, slots)
    place_copy = pltpu.make_async_copy(place_ref, place_out, sems.at[14])
    place_copy.start()
    for copy in copies[:5]:
        copy.wait()
    weight = weight_ref[...]
    bias = bias_ref[...]
    sums = jnp.zeros((8, width), jnp.float32)
    for step in range(0, count, 2):
        for block in (step, step + 1):
            places = places_of(place_ref, block + BAND, slots)
            agg_all[block * block_rows : (block + 1) * block_rows] = jnp.dot(
                row_of(adj, block, slots), pick(feat, places, block_rows),
                preferred_element_type=jnp.float32,
            ).astype(jnp.bfloat16)
        here = pl.ds(step * block_rows, 2 * block_rows)
        preact = jnp.dot(agg_all[here], weight, preferred_element_type=jnp.float32) + bias
        act[here], grad = activate(preact, cot[here])
        grad_ref[here] = grad
        sums = sums + column_sums(grad)
    act_out = pltpu.make_async_copy(act, act_hbm.at[pl.ds(rim, inner)], sems.at[11])
    act_out.start()
    sums_ref[...] = sums
    partial_ref[...] = weight_terms(agg_all[...], grad_ref[...])
    for copy in copies[5:]:
        copy.wait()
    act_out.wait()
    place_copy.wait()


def rim_kernel(
    place_in, weight_ref, bias_ref, feat_ref, first_ref, second_ref, adj_ref, cot_ref,
    partial_ref, sums_ref,
    act_ref, grad_ref, send_ref, keep_ref,
    place_ref, window, agg_all, payload, sems,
):
    fetch = pltpu.make_async_copy(place_in, place_ref, sems.at[0])
    fetch.start()
    steps, slots, block_rows, _ = adj_ref.shape
    blocks = place_ref.shape[0] // slots
    width = feat_ref.shape[1]
    rim = BAND * block_rows
    odd = place_in_mesh() & 1
    window[pl.ds(pl.multiple_of((1 - odd) * 5 * rim, rim), rim)] = first_ref[...]
    window[pl.ds(pl.multiple_of(odd * 5 * rim, rim), rim)] = second_ref[...]
    window[rim : 5 * rim] = feat_ref[...]
    window[6 * rim :] = jnp.zeros((block_rows, width), jnp.bfloat16)
    weight = weight_ref[...]
    bias = bias_ref[...]
    sums = sums_ref[...]
    fetch.wait()
    for step in range(0, steps, 2):
        for block in (step, step + 1):
            places = places_of(place_ref, rim_block(block, blocks), slots)
            agg_all[block * block_rows : (block + 1) * block_rows] = jnp.dot(
                row_of(adj_ref, block, slots), pick(window, places, block_rows),
                preferred_element_type=jnp.float32,
            ).astype(jnp.bfloat16)
        here = pl.ds(step * block_rows, 2 * block_rows)
        preact = jnp.dot(agg_all[here], weight, preferred_element_type=jnp.float32) + bias
        act_ref[here], grad = activate(preact, cot_ref[here])
        grad_ref[here] = grad
        sums = sums + column_sums(grad)
    half = width // 2
    partial = partial_ref[...] + weight_terms(agg_all[...], grad_ref[...])
    payload[0, :half] = partial[:half]
    payload[1, :half] = partial[half:]
    tail = jnp.zeros((TAIL, width), jnp.float32)
    payload[0, half:] = jnp.broadcast_to(jnp.sum(sums, axis=0, keepdims=True), tail.shape)
    payload[1, half:] = tail
    side = core_side()
    keep_ref[...] = payload[side]
    send_ref[...] = payload[1 - side]


def scatter_rows(places, upstream, adj_ref, spread):
    _, slots, block_rows, _ = adj_ref.shape
    for step, targets in enumerate(places):
        terms = jnp.dot(
            upstream[:, step * block_rows : (step + 1) * block_rows],
            row_of(adj_ref, step, slots),
            preferred_element_type=jnp.float32,
        )
        for slot, target in enumerate(targets):
            spread[target] += terms[:, slot * block_rows : (slot + 1) * block_rows]


def rim_back_kernel(
    place_in, weight_ref, adj_ref, grad_ref, act_ref, act_in,
    act_hbm, spread, first_ref, second_ref, mark_ref,
    place_ref, sems,
):
    fetch = pltpu.make_async_copy(place_in, place_ref, sems.at[2])
    fetch.start()
    steps, slots, block_rows, _ = adj_ref.shape
    blocks = place_ref.shape[0] // slots
    rim = BAND * block_rows
    rows = blocks * block_rows
    copies = [
        pltpu.make_async_copy(act_ref.at[pl.ds(0, rim)], act_hbm.at[pl.ds(0, rim)], sems.at[0]),
        pltpu.make_async_copy(
            act_ref.at[pl.ds(rim, rim)], act_hbm.at[pl.ds(rows - rim, rim)], sems.at[1]
        ),
    ]
    for copy in copies:
        copy.start()
    spread[...] = jnp.zeros_like(spread)
    upstream = to_upstream(weight_ref[...], grad_ref[...])
    fetch.wait()
    scatter_rows(
        [places_of(place_ref, rim_block(step, blocks), slots) for step in range(steps)],
        upstream, adj_ref, spread,
    )
    odd = place_in_mesh() & 1
    for block in range(BAND):
        here = pl.ds(block * block_rows, block_rows)
        first_ref[here] = spread[(1 - odd) * 5 * BAND + block].T.astype(jnp.bfloat16)
        second_ref[here] = spread[odd * 5 * BAND + block].T.astype(jnp.bfloat16)
    mark_ref[...] = jnp.zeros_like(mark_ref)
    for copy in copies:
        copy.wait()


def inner_back_kernel(
    place_in, weight_ref, adj_ref, grad_ref, rim_spread,
    whole_hbm, edge_ref, mark_ref,
    place_ref, spread, out, sems,
):
    fetch = pltpu.make_async_copy(place_in, place_ref, sems.at[1])
    fetch.start()
    count, slots, block_rows, _ = adj_ref.shape
    blocks = place_ref.shape[0] // slots
    rim = BAND * block_rows
    spread[: 2 * BAND] = rim_spread[BAND : 3 * BAND]
    spread[2 * BAND :] = jnp.zeros_like(spread[2 * BAND :])
    spread[blocks - 2 * BAND : blocks] = rim_spread[3 * BAND : 5 * BAND]
    upstream = to_upstream(weight_ref[...], grad_ref[...])
    fetch.wait()
    scatter_rows(
        [places_of(place_ref, step + BAND, slots) for step in range(count)],
        upstream, adj_ref, spread,
    )
    for step in range(count):
        here = pl.ds(step * block_rows, block_rows)
        out[here] = spread[BAND + step].T.astype(jnp.bfloat16)
    finish = pltpu.make_async_copy(out, whole_hbm.at[pl.ds(rim, count * block_rows)], sems.at[0])
    finish.start()
    mark_ref[...] = jnp.zeros_like(mark_ref)
    for block in range(BAND):
        edge_ref[block * block_rows : (block + 1) * block_rows] = spread[block].T
        after = BAND + block
        edge_ref[after * block_rows : (after + 1) * block_rows] = spread[blocks - BAND + block].T
    finish.wait()


def add_kernel(parts, *refs):
    values = [ref[...].astype(jnp.float32) for ref in refs[:parts]]
    total = values[0] + values[1]
    if parts == 4:
        total = total + (values[2] + values[3])
    refs[-1][...] = total.astype(refs[-1].dtype)


def last_kernel(
    scale, own_ref, other_ref, edge_ref, first_ref, second_ref, whole_in,
    weight_out, bias_out, whole_hbm,
    out, sums, bias, sems,
):
    half = sums.shape[0] // 2
    rim = first_ref.shape[0]
    rows = whole_hbm.shape[0]
    copies = [
        pltpu.make_async_copy(sums, weight_out, sems.at[0]),
        pltpu.make_async_copy(bias, bias_out, sems.at[1]),
        pltpu.make_async_copy(out.at[pl.ds(0, rim)], whole_hbm.at[pl.ds(0, rim)], sems.at[2]),
        pltpu.make_async_copy(
            out.at[pl.ds(rim, rim)], whole_hbm.at[pl.ds(rows - rim, rim)], sems.at[3]
        ),
    ]
    side = core_side()
    own_rows = pl.ds(pl.multiple_of(side * half, half), half)
    other_rows = pl.ds(pl.multiple_of((1 - side) * half, half), half)
    sums[own_rows] = own_ref[:half] * scale
    sums[other_rows] = other_ref[:half] * scale
    copies[0].start()
    first = jnp.where(side == 0, own_ref[half : half + 1], other_ref[half : half + 1])
    bias[...] = first * scale
    copies[1].start()
    odd = place_in_mesh() & 1
    for base, spill_ref in (((1 - odd) * rim, first_ref), (odd * rim, second_ref)):
        here = pl.ds(pl.multiple_of(base, rim), rim)
        out[here] = (edge_ref[here] + spill_ref[...].astype(jnp.float32)).astype(jnp.bfloat16)
    for copy in copies[2:]:
        copy.start()
    for copy in copies:
        copy.wait()


def add(values, dtype, after=()):
    size = values[0].size
    return pl.pallas_call(
        functools.partial(add_kernel, len(values)),
        out_shape=jax.ShapeDtypeStruct(values[0].shape, dtype),
        in_specs=[pl.BlockSpec(memory_space=pltpu.VMEM)] * len(values)
        + [pl.BlockSpec(memory_space=pl.ANY)] * len(after),
        compiler_params=pltpu.CompilerParams(vmem_limit_bytes=2 * MIB),
        cost_estimate=pl.CostEstimate(
            flops=size * len(values), bytes_accessed=8 * size, transcendentals=0
        ),
        name="add_halves",
    )(*values, *after)


def swap(value, masks):
    pairs = [(i, i ^ mask) for i, mask in enumerate(masks) if mask]
    return lax.ppermute(value, AXES, pairs)


def with_next(value, count):
    pairs = [(i, (i + 1 if i & 1 else i - 1) % count) for i in range(count)]
    return lax.ppermute(value, AXES, pairs)


def sum_halves(send, keep, count, core_bit, marks):
    others = [bit for bit in range(count.bit_length() - 1) if bit != core_bit]
    groups = [others[i : i + 2] for i in range(0, len(others), 2)]
    groups[0] = groups[0][::-1]
    total = add([keep, swap(send, [1 << core_bit] * count)], jnp.bfloat16, marks.get("core", ()))
    for step in range(len(groups)):
        masks = []
        for group in (groups[step], groups[len(groups) - 1 - step]):
            if len(groups[0]) != len(groups[-1]):
                group = groups[step]
            low = 1 << group[0]
            masks.append((low, 1 << group[1], low | 1 << group[1]) if group[1:] else (low,))
        parts = [total] + [
            swap(total, [masks[(i >> core_bit) & 1][k] for i in range(count)])
            for k in range(len(masks[0]))
        ]
        last = step == len(groups) - 1
        name = "last" if last else step
        total = add(parts, jnp.float32 if last else jnp.bfloat16, marks.get(name, ()))
    return total


def on_device(features, adj_values, adj_offset, adj_count, weight, bias_vector, cotangent):
    blocks, slots = adj_offset.shape
    block_rows = adj_values.shape[2]
    rows, width = features.shape
    rim = BAND * block_rows
    inner = rows - 2 * rim
    cols = lax.axis_size("cols")
    count = lax.axis_size("rows") * cols
    vmem = pl.BlockSpec(memory_space=pltpu.VMEM)
    hbm = pl.BlockSpec(memory_space=pltpu.HBM)
    anywhere = pl.BlockSpec(memory_space=pl.ANY)
    place_scratch = pltpu.SMEM((blocks * slots,), jnp.int32)
    bias_row = bias_vector.reshape(1, width)

    def in_hbm(value):
        return pltpu.with_memory_space_constraint(value, pltpu.HBM)

    def shape(*sizes, dtype=jnp.bfloat16):
        return jax.ShapeDtypeStruct(sizes, dtype)

    def params(mib):
        return pltpu.CompilerParams(vmem_limit_bytes=mib * MIB)

    def cost(share):
        return pl.CostEstimate(
            flops=int(1.2e9 * share), bytes_accessed=int(6e6 * share),
            transcendentals=int(8e5 * share),
        )

    offsets = in_hbm(adj_offset.T)
    counts = in_hbm(adj_count)
    core_bit = cols.bit_length() - 1
    first_rim, second_rim = pl.pallas_call(
        halo_kernel,
        out_shape=(shape(rim, width), shape(rim, width)),
        in_specs=[hbm],
        out_specs=(vmem, vmem),
        scratch_shapes=[pltpu.SemaphoreType.DMA((2,))],
        compiler_params=params(2),
        cost_estimate=cost(0.05),
        name="halo_rows",
    )(in_hbm(features))
    first_halo = swap(first_rim, [1] * count)
    second_halo = with_next(second_rim, count)
    (
        activated, places, grad_inner, partial, sums, weight_near, bias_near, feat_rim, adj_rim,
        cot_rim, adj_inner,
    ) = pl.pallas_call(
        inner_kernel,
        out_shape=(
            shape(rows, width),
            shape(blocks * slots, dtype=jnp.int32),
            shape(inner, width),
            shape(width, width, dtype=jnp.float32),
            shape(8, width, dtype=jnp.float32),
            shape(width, width),
            shape(1, width, dtype=jnp.float32),
            shape(4 * rim, width),
            shape(2 * BAND, slots, block_rows, block_rows),
            shape(2 * rim, width),
            shape(blocks - 2 * BAND, slots, block_rows, block_rows),
        ),
        in_specs=[hbm] * 7,
        out_specs=(hbm, anywhere) + (vmem,) * 9,
        scratch_shapes=[
            pltpu.SMEM((slots, blocks), jnp.int32),
            pltpu.SMEM((blocks,), jnp.int32),
            place_scratch,
            pltpu.VMEM((rows + block_rows, width), jnp.bfloat16),
            pltpu.VMEM((inner, width), jnp.bfloat16),
            pltpu.VMEM((inner, width), jnp.bfloat16),
            pltpu.VMEM((inner, width), jnp.bfloat16),
            pltpu.SemaphoreType.DMA((15,)),
        ],
        compiler_params=params(20),
        cost_estimate=cost(0.5),
        name="inner_rows",
    )(
        offsets, counts,
        *(in_hbm(x) for x in (weight, bias_row, features, adj_values, cotangent)),
    )
    half_shape = (width // 2 + TAIL, width)
    act_rim, grad_rim, send, keep = pl.pallas_call(
        rim_kernel,
        out_shape=(
            shape(2 * rim, width),
            shape(2 * rim, width),
            shape(*half_shape, dtype=jnp.float32),
            shape(*half_shape, dtype=jnp.float32),
        ),
        in_specs=[anywhere] + [vmem] * 9,
        out_specs=(vmem,) * 4,
        scratch_shapes=[
            place_scratch,
            pltpu.VMEM((6 * rim + block_rows, width), jnp.bfloat16),
            pltpu.VMEM((2 * rim, width), jnp.bfloat16),
            pltpu.VMEM((2,) + half_shape, jnp.float32),
            pltpu.SemaphoreType.DMA((1,)),
        ],
        compiler_params=params(12),
        cost_estimate=cost(0.2),
        name="rim_rows",
    )(
        places, weight_near, bias_near, feat_rim, first_halo, second_halo, adj_rim, cot_rim,
        partial, sums,
    )
    mark = shape(8, 128, dtype=jnp.float32)
    activated, rim_spread, first_spill, second_spill, first_mark = pl.pallas_call(
        rim_back_kernel,
        out_shape=(
            shape(rows, width),
            shape(6 * BAND + 1, width, block_rows, dtype=jnp.float32),
            shape(rim, width),
            shape(rim, width),
            mark,
        ),
        in_specs=[anywhere] + [vmem] * 4 + [hbm],
        out_specs=(hbm,) + (vmem,) * 4,
        scratch_shapes=[place_scratch, pltpu.SemaphoreType.DMA((3,))],
        input_output_aliases={5: 0},
        compiler_params=params(12),
        cost_estimate=cost(0.2),
        name="rim_rows_back",
    )(places, weight_near, adj_rim, grad_rim, act_rim, activated)
    first_part = swap(first_spill, [1] * count)
    second_part = with_next(second_spill, count)
    grad_whole, edges, second_mark = pl.pallas_call(
        inner_back_kernel,
        out_shape=(shape(rows, width), shape(2 * rim, width, dtype=jnp.float32), mark),
        in_specs=[anywhere] + [vmem] * 4,
        out_specs=(hbm, vmem, vmem),
        scratch_shapes=[
            place_scratch,
            pltpu.VMEM((blocks + 1, width, block_rows), jnp.float32),
            pltpu.VMEM((inner, width), jnp.bfloat16),
            pltpu.SemaphoreType.DMA((2,)),
        ],
        compiler_params=params(12),
        cost_estimate=cost(0.3),
        name="inner_rows_back",
    )(places, weight_near, adj_inner, grad_inner, rim_spread)
    marks = {"core": (first_mark,), "last": (second_mark, first_part, second_part)}
    own_half = sum_halves(send, keep, count, core_bit, marks)
    other_half = swap(own_half, [1 << core_bit] * count)
    norm_scale = 1.0 / math.sqrt(rows * count)
    grad_weight, grad_bias, grad_features = pl.pallas_call(
        functools.partial(last_kernel, norm_scale),
        out_shape=(
            shape(width, width, dtype=jnp.float32),
            shape(1, width, dtype=jnp.float32),
            shape(rows, width),
        ),
        in_specs=[vmem] * 5 + [hbm],
        out_specs=(hbm, hbm, hbm),
        scratch_shapes=[
            pltpu.VMEM((2 * rim, width), jnp.bfloat16),
            pltpu.VMEM((width, width), jnp.float32),
            pltpu.VMEM((1, width), jnp.float32),
            pltpu.SemaphoreType.DMA((4,)),
        ],
        input_output_aliases={5: 2},
        compiler_params=params(8),
        name="last_step",
    )(own_half, other_half, edges, first_part, second_part, grad_whole)
    return (activated, grad_features, grad_weight, grad_bias.reshape(width))


def solution(mesh):
    return jax.shard_map(
        on_device,
        mesh=mesh,
        in_specs=(
            P(AXES, None),
            P(AXES, None, None, None),
            P(AXES, None),
            P(AXES),
            P(),
            P(),
            P(AXES, None),
        ),
        out_specs=(P(AXES, None), P(AXES, None), P(), P()),
        check_vma=False,
    )
```

```python
import functools
import math

import jax
import jax.numpy as jnp
from jax import lax
from jax.experimental import pallas as pl
from jax.experimental.pallas import tpu as pltpu
from jax.sharding import PartitionSpec as P

BAND = 2
TAIL = 8
AXES = ("rows", "cols")
MIB = 1024 * 1024


def row_of(adj_ref, block, slots):
    return jnp.concatenate([adj_ref[block, slot] for slot in range(slots)], 1)


def pick(source, places, block_rows):
    return jnp.concatenate(
        [
            source[pl.ds(pl.multiple_of(place * block_rows, block_rows), block_rows)]
            for place in places
        ],
        0,
    )


def write_places(off_ref, cnt_ref, place_ref, blocks, slots):
    for block in range(blocks):
        if block < BAND:
            shift, dump = BAND, 6 * BAND
        elif block < blocks - BAND:
            shift, dump = 0, blocks
        else:
            shift, dump = 5 * BAND - blocks, 6 * BAND
        for slot in range(slots):
            place_ref[block * slots + slot] = jnp.where(
                slot < cnt_ref[block], block + shift + off_ref[slot, block], dump
            )


def places_of(place_ref, block, slots):
    return [place_ref[block * slots + slot] for slot in range(slots)]


def rim_block(step, blocks):
    return step if step < BAND else blocks - 2 * BAND + step


def place_in_mesh():
    return lax.axis_index("rows") * lax.axis_size("cols") + lax.axis_index("cols")


def core_side():
    return lax.axis_index("rows") & 1


def halo_kernel(feat_hbm, first_ref, second_ref, sems):
    rows = feat_hbm.shape[0]
    rim = first_ref.shape[0]
    odd = place_in_mesh() & 1
    last = rows - rim
    starts = ((1 - odd) * last, odd * last)
    copies = [
        pltpu.make_async_copy(
            feat_hbm.at[pl.ds(pl.multiple_of(start, rim), rim)], out_ref, sems.at[i]
        )
        for i, (start, out_ref) in enumerate(zip(starts, (first_ref, second_ref)))
    ]
    for copy in copies:
        copy.start()
    for copy in copies:
        copy.wait()


def activate(preact, cotangent):
    gate = 1.0 / (1.0 + jnp.exp(-preact))
    grad = cotangent.astype(jnp.float32) * gate * (1.0 + preact * (1.0 - gate))
    return (preact * gate).astype(jnp.bfloat16), grad.astype(jnp.bfloat16)


def column_sums(grad):
    rows, width = grad.shape
    return jnp.sum(grad.astype(jnp.float32).reshape(rows // 8, 8, width), axis=0)


def to_upstream(weight, grad):
    return lax.dot_general(
        weight, grad, (((1,), (1,)), ((), ())), preferred_element_type=jnp.float32
    ).astype(jnp.bfloat16)


def weight_terms(agg, grad):
    return lax.dot_general(
        agg, grad, (((0,), (0,)), ((), ())), preferred_element_type=jnp.float32
    )


def inner_kernel(
    off_hbm, cnt_hbm, weight_hbm, bias_hbm, feat_hbm, adj_hbm, cot_hbm,
    act_hbm, place_out, grad_ref, partial_ref, sums_ref, weight_ref, bias_ref, feat_rim, adj_rim,
    cot_rim, adj,
    off_ref, cnt_ref, place_ref, feat, cot, act, agg_all, sems,
):
    blocks, slots, block_rows, _ = adj_hbm.shape
    rows, width = feat_hbm.shape
    count = blocks - 2 * BAND
    rim = BAND * block_rows
    half = 2 * rim
    inner = count * block_rows
    scalars = [
        pltpu.make_async_copy(off_hbm, off_ref, sems.at[12]),
        pltpu.make_async_copy(cnt_hbm, cnt_ref, sems.at[13]),
    ]
    copies = [
        pltpu.make_async_copy(feat_hbm, feat.at[pl.ds(0, rows)], sems.at[0]),
        pltpu.make_async_copy(adj_hbm.at[pl.ds(BAND, count)], adj, sems.at[1]),
        pltpu.make_async_copy(weight_hbm, weight_ref, sems.at[2]),
        pltpu.make_async_copy(bias_hbm, bias_ref, sems.at[3]),
        pltpu.make_async_copy(cot_hbm.at[pl.ds(rim, inner)], cot, sems.at[4]),
        pltpu.make_async_copy(feat_hbm.at[pl.ds(0, half)], feat_rim.at[pl.ds(0, half)], sems.at[5]),
        pltpu.make_async_copy(
            feat_hbm.at[pl.ds(rows - half, half)], feat_rim.at[pl.ds(half, half)], sems.at[6]
        ),
        pltpu.make_async_copy(adj_hbm.at[pl.ds(0, BAND)], adj_rim.at[pl.ds(0, BAND)], sems.at[7]),
        pltpu.make_async_copy(
            adj_hbm.at[pl.ds(blocks - BAND, BAND)], adj_rim.at[pl.ds(BAND, BAND)], sems.at[8]
        ),
        pltpu.make_async_copy(cot_hbm.at[pl.ds(0, rim)], cot_rim.at[pl.ds(0, rim)], sems.at[9]),
        pltpu.make_async_copy(
            cot_hbm.at[pl.ds(rows - rim, rim)], cot_rim.at[pl.ds(rim, rim)], sems.at[10]
        ),
    ]
    for copy in scalars + copies:
        copy.start()
    feat[rows:] = jnp.zeros((block_rows, width), jnp.bfloat16)
    for copy in scalars:
        copy.wait()
    write_places(off_ref, cnt_ref, place_ref, blocks, slots)
    place_copy = pltpu.make_async_copy(place_ref, place_out, sems.at[14])
    place_copy.start()
    for copy in copies[:5]:
        copy.wait()
    weight = weight_ref[...]
    bias = bias_ref[...]
    sums = jnp.zeros((8, width), jnp.float32)
    for step in range(0, count, 2):
        for block in (step, step + 1):
            places = places_of(place_ref, block + BAND, slots)
            agg_all[block * block_rows : (block + 1) * block_rows] = jnp.dot(
                row_of(adj, block, slots), pick(feat, places, block_rows),
                preferred_element_type=jnp.float32,
            ).astype(jnp.bfloat16)
        here = pl.ds(step * block_rows, 2 * block_rows)
        preact = jnp.dot(agg_all[here], weight, preferred_element_type=jnp.float32) + bias
        act[here], grad = activate(preact, cot[here])
        grad_ref[here] = grad
        sums = sums + column_sums(grad)
    act_out = pltpu.make_async_copy(act, act_hbm.at[pl.ds(rim, inner)], sems.at[11])
    act_out.start()
    sums_ref[...] = sums
    partial_ref[...] = weight_terms(agg_all[...], grad_ref[...])
    for copy in copies[5:]:
        copy.wait()
    act_out.wait()
    place_copy.wait()


def rim_kernel(
    place_in, weight_ref, bias_ref, feat_ref, first_ref, second_ref, adj_ref, cot_ref,
    partial_ref, sums_ref,
    act_ref, grad_ref, send_ref, keep_ref,
    place_ref, window, agg_all, payload, sems,
):
    fetch = pltpu.make_async_copy(place_in, place_ref, sems.at[0])
    fetch.start()
    steps, slots, block_rows, _ = adj_ref.shape
    blocks = place_ref.shape[0] // slots
    width = feat_ref.shape[1]
    rim = BAND * block_rows
    odd = place_in_mesh() & 1
    window[pl.ds(pl.multiple_of((1 - odd) * 5 * rim, rim), rim)] = first_ref[...]
    window[pl.ds(pl.multiple_of(odd * 5 * rim, rim), rim)] = second_ref[...]
    window[rim : 5 * rim] = feat_ref[...]
    window[6 * rim :] = jnp.zeros((block_rows, width), jnp.bfloat16)
    weight = weight_ref[...]
    bias = bias_ref[...]
    sums = sums_ref[...]
    fetch.wait()
    for step in range(0, steps, 2):
        for block in (step, step + 1):
            places = places_of(place_ref, rim_block(block, blocks), slots)
            agg_all[block * block_rows : (block + 1) * block_rows] = jnp.dot(
                row_of(adj_ref, block, slots), pick(window, places, block_rows),
                preferred_element_type=jnp.float32,
            ).astype(jnp.bfloat16)
        here = pl.ds(step * block_rows, 2 * block_rows)
        preact = jnp.dot(agg_all[here], weight, preferred_element_type=jnp.float32) + bias
        act_ref[here], grad = activate(preact, cot_ref[here])
        grad_ref[here] = grad
        sums = sums + column_sums(grad)
    half = width // 2
    partial = partial_ref[...] + weight_terms(agg_all[...], grad_ref[...])
    payload[0, :half] = partial[:half]
    payload[1, :half] = partial[half:]
    tail = jnp.zeros((TAIL, width), jnp.float32)
    payload[0, half:] = jnp.broadcast_to(jnp.sum(sums, axis=0, keepdims=True), tail.shape)
    payload[1, half:] = tail
    side = core_side()
    keep_ref[...] = payload[side]
    send_ref[...] = payload[1 - side]


def scatter_rows(places, upstream, adj_ref, spread):
    _, slots, block_rows, _ = adj_ref.shape
    for step, targets in enumerate(places):
        terms = jnp.dot(
            upstream[:, step * block_rows : (step + 1) * block_rows],
            row_of(adj_ref, step, slots),
            preferred_element_type=jnp.float32,
        )
        for slot, target in enumerate(targets):
            spread[target] += terms[:, slot * block_rows : (slot + 1) * block_rows]


def rim_back_kernel(
    place_in, weight_ref, adj_ref, grad_ref, act_ref, act_in,
    act_hbm, spread, first_ref, second_ref, mark_ref,
    place_ref, sems,
):
    fetch = pltpu.make_async_copy(place_in, place_ref, sems.at[2])
    fetch.start()
    steps, slots, block_rows, _ = adj_ref.shape
    blocks = place_ref.shape[0] // slots
    rim = BAND * block_rows
    rows = blocks * block_rows
    copies = [
        pltpu.make_async_copy(act_ref.at[pl.ds(0, rim)], act_hbm.at[pl.ds(0, rim)], sems.at[0]),
        pltpu.make_async_copy(
            act_ref.at[pl.ds(rim, rim)], act_hbm.at[pl.ds(rows - rim, rim)], sems.at[1]
        ),
    ]
    for copy in copies:
        copy.start()
    spread[...] = jnp.zeros_like(spread)
    upstream = to_upstream(weight_ref[...], grad_ref[...])
    fetch.wait()
    scatter_rows(
        [places_of(place_ref, rim_block(step, blocks), slots) for step in range(steps)],
        upstream, adj_ref, spread,
    )
    odd = place_in_mesh() & 1
    for block in range(BAND):
        here = pl.ds(block * block_rows, block_rows)
        first_ref[here] = spread[(1 - odd) * 5 * BAND + block].T.astype(jnp.bfloat16)
        second_ref[here] = spread[odd * 5 * BAND + block].T.astype(jnp.bfloat16)
    mark_ref[...] = jnp.zeros_like(mark_ref)
    for copy in copies:
        copy.wait()


def inner_back_kernel(
    place_in, weight_ref, adj_ref, grad_ref, rim_spread,
    whole_hbm, edge_ref, mark_ref,
    place_ref, spread, out, sems,
):
    fetch = pltpu.make_async_copy(place_in, place_ref, sems.at[1])
    fetch.start()
    count, slots, block_rows, _ = adj_ref.shape
    blocks = place_ref.shape[0] // slots
    rim = BAND * block_rows
    spread[: 2 * BAND] = rim_spread[BAND : 3 * BAND]
    spread[2 * BAND :] = jnp.zeros_like(spread[2 * BAND :])
    spread[blocks - 2 * BAND : blocks] = rim_spread[3 * BAND : 5 * BAND]
    upstream = to_upstream(weight_ref[...], grad_ref[...])
    fetch.wait()
    scatter_rows(
        [places_of(place_ref, step + BAND, slots) for step in range(count)],
        upstream, adj_ref, spread,
    )
    for step in range(count):
        here = pl.ds(step * block_rows, block_rows)
        out[here] = spread[BAND + step].T.astype(jnp.bfloat16)
    finish = pltpu.make_async_copy(out, whole_hbm.at[pl.ds(rim, count * block_rows)], sems.at[0])
    finish.start()
    mark_ref[...] = jnp.zeros_like(mark_ref)
    for block in range(BAND):
        edge_ref[block * block_rows : (block + 1) * block_rows] = spread[block].T
        after = BAND + block
        edge_ref[after * block_rows : (after + 1) * block_rows] = spread[blocks - BAND + block].T
    finish.wait()


def add_kernel(parts, *refs):
    values = [ref[...].astype(jnp.float32) for ref in refs[:parts]]
    total = values[0] + values[1]
    if parts == 4:
        total = total + (values[2] + values[3])
    refs[-1][...] = total.astype(refs[-1].dtype)


def last_kernel(
    scale, own_ref, other_ref, edge_ref, first_ref, second_ref, whole_in,
    weight_out, bias_out, whole_hbm,
    out, sums, bias, sems,
):
    half = sums.shape[0] // 2
    rim = first_ref.shape[0]
    rows = whole_hbm.shape[0]
    copies = [
        pltpu.make_async_copy(sums, weight_out, sems.at[0]),
        pltpu.make_async_copy(bias, bias_out, sems.at[1]),
        pltpu.make_async_copy(out.at[pl.ds(0, rim)], whole_hbm.at[pl.ds(0, rim)], sems.at[2]),
        pltpu.make_async_copy(
            out.at[pl.ds(rim, rim)], whole_hbm.at[pl.ds(rows - rim, rim)], sems.at[3]
        ),
    ]
    side = core_side()
    own_rows = pl.ds(pl.multiple_of(side * half, half), half)
    other_rows = pl.ds(pl.multiple_of((1 - side) * half, half), half)
    sums[own_rows] = own_ref[:half] * scale
    sums[other_rows] = other_ref[:half] * scale
    copies[0].start()
    first = jnp.where(side == 0, own_ref[half : half + 1], other_ref[half : half + 1])
    bias[...] = first * scale
    copies[1].start()
    odd = place_in_mesh() & 1
    for base, spill_ref in (((1 - odd) * rim, first_ref), (odd * rim, second_ref)):
        here = pl.ds(pl.multiple_of(base, rim), rim)
        out[here] = (edge_ref[here] + spill_ref[...].astype(jnp.float32)).astype(jnp.bfloat16)
    for copy in copies[2:]:
        copy.start()
    for copy in copies:
        copy.wait()


def add(values, dtype, after=()):
    size = values[0].size
    return pl.pallas_call(
        functools.partial(add_kernel, len(values)),
        out_shape=jax.ShapeDtypeStruct(values[0].shape, dtype),
        in_specs=[pl.BlockSpec(memory_space=pltpu.VMEM)] * len(values)
        + [pl.BlockSpec(memory_space=pl.ANY)] * len(after),
        compiler_params=pltpu.CompilerParams(vmem_limit_bytes=2 * MIB),
        cost_estimate=pl.CostEstimate(
            flops=size * len(values), bytes_accessed=8 * size, transcendentals=0
        ),
        name="add_halves",
    )(*values, *after)


def swap(value, masks):
    pairs = [(i, i ^ mask) for i, mask in enumerate(masks) if mask]
    return lax.ppermute(value, AXES, pairs)


def with_next(value, count):
    pairs = [(i, (i + 1 if i & 1 else i - 1) % count) for i in range(count)]
    return lax.ppermute(value, AXES, pairs)


def sum_halves(send, keep, count, core_bit, marks):
    others = [bit for bit in range(count.bit_length() - 1) if bit != core_bit]
    groups = [others[i : i + 2] for i in range(0, len(others), 2)]
    groups[0] = groups[0][::-1]
    total = add([keep, swap(send, [1 << core_bit] * count)], jnp.bfloat16, marks.get("core", ()))
    for step in range(len(groups)):
        masks = []
        for group in (groups[step], groups[len(groups) - 1 - step]):
            if len(groups[0]) != len(groups[-1]):
                group = groups[step]
            low = 1 << group[0]
            masks.append((low, 1 << group[1], low | 1 << group[1]) if group[1:] else (low,))
        parts = [total] + [
            swap(total, [masks[(i >> core_bit) & 1][k] for i in range(count)])
            for k in range(len(masks[0]))
        ]
        last = step == len(groups) - 1
        name = "last" if last else step
        total = add(parts, jnp.float32 if last else jnp.bfloat16, marks.get(name, ()))
    return total


def on_device(features, adj_values, adj_offset, adj_count, weight, bias_vector, cotangent):
    blocks, slots = adj_offset.shape
    block_rows = adj_values.shape[2]
    rows, width = features.shape
    rim = BAND * block_rows
    inner = rows - 2 * rim
    cols = lax.axis_size("cols")
    count = lax.axis_size("rows") * cols
    vmem = pl.BlockSpec(memory_space=pltpu.VMEM)
    hbm = pl.BlockSpec(memory_space=pltpu.HBM)
    anywhere = pl.BlockSpec(memory_space=pl.ANY)
    place_scratch = pltpu.SMEM((blocks * slots,), jnp.int32)
    bias_row = bias_vector.reshape(1, width)

    def in_hbm(value):
        return pltpu.with_memory_space_constraint(value, pltpu.HBM)

    def shape(*sizes, dtype=jnp.bfloat16):
        return jax.ShapeDtypeStruct(sizes, dtype)

    def params(mib):
        return pltpu.CompilerParams(vmem_limit_bytes=mib * MIB)

    def cost(share):
        return pl.CostEstimate(
            flops=int(1.2e9 * share), bytes_accessed=int(6e6 * share),
            transcendentals=int(8e5 * share),
        )

    offsets = in_hbm(adj_offset.T)
    counts = in_hbm(adj_count)
    core_bit = cols.bit_length() - 1
    first_rim, second_rim = pl.pallas_call(
        halo_kernel,
        out_shape=(shape(rim, width), shape(rim, width)),
        in_specs=[hbm],
        out_specs=(vmem, vmem),
        scratch_shapes=[pltpu.SemaphoreType.DMA((2,))],
        compiler_params=params(2),
        cost_estimate=cost(0.05),
        name="halo_rows",
    )(in_hbm(features))
    first_halo = swap(first_rim, [1] * count)
    second_halo = with_next(second_rim, count)
    (
        activated, places, grad_inner, partial, sums, weight_near, bias_near, feat_rim, adj_rim,
        cot_rim, adj_inner,
    ) = pl.pallas_call(
        inner_kernel,
        out_shape=(
            shape(rows, width),
            shape(blocks * slots, dtype=jnp.int32),
            shape(inner, width),
            shape(width, width, dtype=jnp.float32),
            shape(8, width, dtype=jnp.float32),
            shape(width, width),
            shape(1, width, dtype=jnp.float32),
            shape(4 * rim, width),
            shape(2 * BAND, slots, block_rows, block_rows),
            shape(2 * rim, width),
            shape(blocks - 2 * BAND, slots, block_rows, block_rows),
        ),
        in_specs=[hbm] * 7,
        out_specs=(hbm, anywhere) + (vmem,) * 9,
        scratch_shapes=[
            pltpu.SMEM((slots, blocks), jnp.int32),
            pltpu.SMEM((blocks,), jnp.int32),
            place_scratch,
            pltpu.VMEM((rows + block_rows, width), jnp.bfloat16),
            pltpu.VMEM((inner, width), jnp.bfloat16),
            pltpu.VMEM((inner, width), jnp.bfloat16),
            pltpu.VMEM((inner, width), jnp.bfloat16),
            pltpu.SemaphoreType.DMA((15,)),
        ],
        compiler_params=params(20),
        cost_estimate=cost(0.5),
        name="inner_rows",
    )(
        offsets, counts,
        *(in_hbm(x) for x in (weight, bias_row, features, adj_values, cotangent)),
    )
    half_shape = (width // 2 + TAIL, width)
    act_rim, grad_rim, send, keep = pl.pallas_call(
        rim_kernel,
        out_shape=(
            shape(2 * rim, width),
            shape(2 * rim, width),
            shape(*half_shape, dtype=jnp.float32),
            shape(*half_shape, dtype=jnp.float32),
        ),
        in_specs=[anywhere] + [vmem] * 9,
        out_specs=(vmem,) * 4,
        scratch_shapes=[
            place_scratch,
            pltpu.VMEM((6 * rim + block_rows, width), jnp.bfloat16),
            pltpu.VMEM((2 * rim, width), jnp.bfloat16),
            pltpu.VMEM((2,) + half_shape, jnp.float32),
            pltpu.SemaphoreType.DMA((1,)),
        ],
        compiler_params=params(12),
        cost_estimate=cost(0.2),
        name="rim_rows",
    )(
        places, weight_near, bias_near, feat_rim, first_halo, second_halo, adj_rim, cot_rim,
        partial, sums,
    )
    mark = shape(8, 128, dtype=jnp.float32)
    activated, rim_spread, first_spill, second_spill, first_mark = pl.pallas_call(
        rim_back_kernel,
        out_shape=(
            shape(rows, width),
            shape(6 * BAND + 1, width, block_rows, dtype=jnp.float32),
            shape(rim, width),
            shape(rim, width),
            mark,
        ),
        in_specs=[anywhere] + [vmem] * 4 + [hbm],
        out_specs=(hbm,) + (vmem,) * 4,
        scratch_shapes=[place_scratch, pltpu.SemaphoreType.DMA((3,))],
        input_output_aliases={5: 0},
        compiler_params=params(12),
        cost_estimate=cost(0.2),
        name="rim_rows_back",
    )(places, weight_near, adj_rim, grad_rim, act_rim, activated)
    first_part = swap(first_spill, [1] * count)
    second_part = with_next(second_spill, count)
    grad_whole, edges, second_mark = pl.pallas_call(
        inner_back_kernel,
        out_shape=(shape(rows, width), shape(2 * rim, width, dtype=jnp.float32), mark),
        in_specs=[anywhere] + [vmem] * 4,
        out_specs=(hbm, vmem, vmem),
        scratch_shapes=[
            place_scratch,
            pltpu.VMEM((blocks + 1, width, block_rows), jnp.float32),
            pltpu.VMEM((inner, width), jnp.bfloat16),
            pltpu.SemaphoreType.DMA((2,)),
        ],
        compiler_params=params(12),
        cost_estimate=cost(0.3),
        name="inner_rows_back",
    )(places, weight_near, adj_inner, grad_inner, rim_spread)
    marks = {0: (first_mark,), "last": (second_mark, first_part, second_part)}
    own_half = sum_halves(send, keep, count, core_bit, marks)
    other_half = swap(own_half, [1 << core_bit] * count)
    norm_scale = 1.0 / math.sqrt(rows * count)
    grad_weight, grad_bias, grad_features = pl.pallas_call(
        functools.partial(last_kernel, norm_scale),
        out_shape=(
            shape(width, width, dtype=jnp.float32),
            shape(1, width, dtype=jnp.float32),
            shape(rows, width),
        ),
        in_specs=[vmem] * 5 + [hbm],
        out_specs=(hbm, hbm, hbm),
        scratch_shapes=[
            pltpu.VMEM((2 * rim, width), jnp.bfloat16),
            pltpu.VMEM((width, width), jnp.float32),
            pltpu.VMEM((1, width), jnp.float32),
            pltpu.SemaphoreType.DMA((4,)),
        ],
        input_output_aliases={5: 2},
        compiler_params=params(8),
        name="last_step",
    )(own_half, other_half, edges, first_part, second_part, grad_whole)
    return (activated, grad_features, grad_weight, grad_bias.reshape(width))


def solution(mesh):
    return jax.shard_map(
        on_device,
        mesh=mesh,
        in_specs=(
            P(AXES, None),
            P(AXES, None, None, None),
            P(AXES, None),
            P(AXES),
            P(),
            P(),
            P(AXES, None),
        ),
        out_specs=(P(AXES, None), P(AXES, None), P(), P()),
        check_vma=False,
    )
```

```python
import functools
import math

import jax
import jax.numpy as jnp
from jax import lax
from jax.experimental import pallas as pl
from jax.experimental.pallas import tpu as pltpu
from jax.sharding import PartitionSpec as P

BAND = 2
TAIL = 8
AXES = ("rows", "cols")
MIB = 1024 * 1024


def row_of(adj_ref, block, slots):
    return jnp.concatenate([adj_ref[block, slot] for slot in range(slots)], 1)


def pick(source, places, block_rows):
    return jnp.concatenate(
        [
            source[pl.ds(pl.multiple_of(place * block_rows, block_rows), block_rows)]
            for place in places
        ],
        0,
    )


def write_places(off_ref, cnt_ref, place_ref, blocks, slots):
    for block in range(blocks):
        if block < BAND:
            shift, dump = BAND, 3 * BAND
        elif block < blocks - BAND:
            shift, dump = 0, blocks
        else:
            shift, dump = 2 * BAND - blocks, 3 * BAND
        for slot in range(slots):
            place_ref[block * slots + slot] = jnp.where(
                slot < cnt_ref[block], block + shift + off_ref[slot, block], dump
            )


def places_of(place_ref, block, slots):
    return [place_ref[block * slots + slot] for slot in range(slots)]


def side_by_side(dense, side, first, last):
    return jnp.concatenate([dense[side, place] for place in range(first, last)], 1)


def place_in_mesh():
    return lax.axis_index("rows") * lax.axis_size("cols") + lax.axis_index("cols")


def core_side():
    return lax.axis_index("rows") & 1


def halo_kernel(feat_hbm, first_ref, second_ref, sems):
    rows = feat_hbm.shape[0]
    rim = first_ref.shape[0]
    odd = place_in_mesh() & 1
    last = rows - rim
    starts = ((1 - odd) * last, odd * last)
    copies = [
        pltpu.make_async_copy(
            feat_hbm.at[pl.ds(pl.multiple_of(start, rim), rim)], out_ref, sems.at[i]
        )
        for i, (start, out_ref) in enumerate(zip(starts, (first_ref, second_ref)))
    ]
    for copy in copies:
        copy.start()
    for copy in copies:
        copy.wait()


def activate(preact, cotangent):
    gate = 1.0 / (1.0 + jnp.exp(-preact))
    grad = cotangent.astype(jnp.float32) * gate * (1.0 + preact * (1.0 - gate))
    return (preact * gate).astype(jnp.bfloat16), grad.astype(jnp.bfloat16)


def column_sums(grad):
    rows, width = grad.shape
    return jnp.sum(grad.astype(jnp.float32).reshape(rows // 8, 8, width), axis=0)


def to_upstream(weight, grad):
    return lax.dot_general(
        weight, grad, (((1,), (1,)), ((), ())), preferred_element_type=jnp.float32
    ).astype(jnp.bfloat16)


def weight_terms(agg, grad):
    return lax.dot_general(
        agg, grad, (((0,), (0,)), ((), ())), preferred_element_type=jnp.float32
    )


def inner_kernel(
    off_hbm, cnt_hbm, weight_hbm, bias_hbm, feat_hbm, adj_hbm, cot_hbm,
    act_hbm, place_out, grad_ref, partial_ref, sums_ref, weight_ref, bias_ref, dense, own_ref,
    cot_rim, adj,
    off_ref, cnt_ref, place_ref, feat, adj_rim, cot, act, agg_all, sems,
):
    blocks, slots, block_rows, _ = adj_hbm.shape
    rows, width = feat_hbm.shape
    count = blocks - 2 * BAND
    rim = BAND * block_rows
    inner = count * block_rows
    scalars = [
        pltpu.make_async_copy(off_hbm, off_ref, sems.at[12]),
        pltpu.make_async_copy(cnt_hbm, cnt_ref, sems.at[13]),
    ]
    copies = [
        pltpu.make_async_copy(feat_hbm, feat.at[pl.ds(0, rows)], sems.at[0]),
        pltpu.make_async_copy(adj_hbm.at[pl.ds(BAND, count)], adj, sems.at[1]),
        pltpu.make_async_copy(weight_hbm, weight_ref, sems.at[2]),
        pltpu.make_async_copy(bias_hbm, bias_ref, sems.at[3]),
        pltpu.make_async_copy(cot_hbm.at[pl.ds(rim, inner)], cot, sems.at[4]),
        pltpu.make_async_copy(adj_hbm.at[pl.ds(0, BAND)], adj_rim.at[pl.ds(0, BAND)], sems.at[5]),
        pltpu.make_async_copy(
            adj_hbm.at[pl.ds(blocks - BAND, BAND)], adj_rim.at[pl.ds(BAND, BAND)], sems.at[6]
        ),
        pltpu.make_async_copy(cot_hbm.at[pl.ds(0, rim)], cot_rim.at[pl.ds(0, rim)], sems.at[7]),
        pltpu.make_async_copy(
            cot_hbm.at[pl.ds(rows - rim, rim)], cot_rim.at[pl.ds(rim, rim)], sems.at[8]
        ),
    ]
    for copy in scalars + copies:
        copy.start()
    feat[rows:] = jnp.zeros((block_rows, width), jnp.bfloat16)
    dense[...] = jnp.zeros_like(dense)
    for copy in scalars:
        copy.wait()
    write_places(off_ref, cnt_ref, place_ref, blocks, slots)
    place_copy = pltpu.make_async_copy(place_ref, place_out, sems.at[14])
    place_copy.start()
    for copy in copies[:5]:
        copy.wait()
    weight = weight_ref[...]
    bias = bias_ref[...]
    sums = jnp.zeros((8, width), jnp.float32)
    for step in range(0, count, 2):
        for block in (step, step + 1):
            places = places_of(place_ref, block + BAND, slots)
            agg_all[block * block_rows : (block + 1) * block_rows] = jnp.dot(
                row_of(adj, block, slots), pick(feat, places, block_rows),
                preferred_element_type=jnp.float32,
            ).astype(jnp.bfloat16)
        here = pl.ds(step * block_rows, 2 * block_rows)
        preact = jnp.dot(agg_all[here], weight, preferred_element_type=jnp.float32) + bias
        act[here], grad = activate(preact, cot[here])
        grad_ref[here] = grad
        sums = sums + column_sums(grad)
    act_out = pltpu.make_async_copy(act, act_hbm.at[pl.ds(rim, inner)], sems.at[11])
    act_out.start()
    sums_ref[...] = sums
    partial_ref[...] = weight_terms(agg_all[...], grad_ref[...])
    for copy in copies[5:]:
        copy.wait()
    for side, first in enumerate((0, blocks - BAND)):
        for row in range(BAND):
            here = pl.ds(row * block_rows, block_rows)
            for slot, place in enumerate(places_of(place_ref, first + row, slots)):
                dense[side, place, here] = adj_rim[side * BAND + row, slot]
    own_ref[:rim] = jnp.dot(
        side_by_side(dense, 0, BAND, 3 * BAND), feat[: 2 * rim],
        preferred_element_type=jnp.float32,
    )
    own_ref[rim:] = jnp.dot(
        side_by_side(dense, 1, 0, 2 * BAND), feat[rows - 2 * rim : rows],
        preferred_element_type=jnp.float32,
    )
    act_out.wait()
    place_copy.wait()


def rim_kernel(
    weight_ref, bias_ref, own_ref, first_ref, second_ref, dense, cot_ref, partial_ref, sums_ref,
    act_ref, grad_ref, send_ref, keep_ref,
    halo, agg_all, payload,
):
    rim, width = first_ref.shape
    odd = place_in_mesh() & 1
    halo[pl.ds(pl.multiple_of((1 - odd) * rim, rim), rim)] = first_ref[...]
    halo[pl.ds(pl.multiple_of(odd * rim, rim), rim)] = second_ref[...]
    weight = weight_ref[...]
    bias = bias_ref[...]
    sums = sums_ref[...]
    for side, first in enumerate((0, 2 * BAND)):
        here = pl.ds(side * rim, rim)
        agg = own_ref[here] + jnp.dot(
            side_by_side(dense, side, first, first + BAND), halo[here],
            preferred_element_type=jnp.float32,
        )
        agg = agg.astype(jnp.bfloat16)
        agg_all[here] = agg
        preact = jnp.dot(agg, weight, preferred_element_type=jnp.float32) + bias
        act_ref[here], grad = activate(preact, cot_ref[here])
        grad_ref[here] = grad
        sums = sums + column_sums(grad)
    half = width // 2
    partial = partial_ref[...] + weight_terms(agg_all[...], grad_ref[...])
    payload[0, :half] = partial[:half]
    payload[1, :half] = partial[half:]
    tail = jnp.zeros((TAIL, width), jnp.float32)
    payload[0, half:] = jnp.broadcast_to(jnp.sum(sums, axis=0, keepdims=True), tail.shape)
    payload[1, half:] = tail
    side = core_side()
    keep_ref[...] = payload[side]
    send_ref[...] = payload[1 - side]


def scatter_rows(places, upstream, adj_ref, spread):
    _, slots, block_rows, _ = adj_ref.shape
    for step, targets in enumerate(places):
        terms = jnp.dot(
            upstream[:, step * block_rows : (step + 1) * block_rows],
            row_of(adj_ref, step, slots),
            preferred_element_type=jnp.float32,
        )
        for slot, target in enumerate(targets):
            spread[target] += terms[:, slot * block_rows : (slot + 1) * block_rows]


def rim_back_kernel(
    weight_ref, dense, grad_ref, act_ref, act_in,
    act_hbm, spread, first_ref, second_ref, mark_ref,
    spill, sems,
):
    block_rows = dense.shape[3]
    rim = BAND * block_rows
    rows = act_hbm.shape[0]
    copies = [
        pltpu.make_async_copy(act_ref.at[pl.ds(0, rim)], act_hbm.at[pl.ds(0, rim)], sems.at[0]),
        pltpu.make_async_copy(
            act_ref.at[pl.ds(rim, rim)], act_hbm.at[pl.ds(rows - rim, rim)], sems.at[1]
        ),
    ]
    for copy in copies:
        copy.start()
    weight = weight_ref[...]
    for side, (inside, outside) in enumerate(((BAND, 0), (0, 2 * BAND))):
        terms = jnp.dot(
            to_upstream(weight, grad_ref[side * rim : (side + 1) * rim]),
            side_by_side(dense, side, 0, 3 * BAND),
            preferred_element_type=jnp.float32,
        )
        for block in range(2 * BAND):
            lane = (inside + block) * block_rows
            spread[side * 2 * BAND + block] = terms[:, lane : lane + block_rows]
        for block in range(BAND):
            lane = (outside + block) * block_rows
            here = pl.ds(side * rim + block * block_rows, block_rows)
            spill[here] = terms[:, lane : lane + block_rows].T.astype(jnp.bfloat16)
    odd = place_in_mesh() & 1
    first_ref[...] = spill[pl.ds(pl.multiple_of((1 - odd) * rim, rim), rim)]
    second_ref[...] = spill[pl.ds(pl.multiple_of(odd * rim, rim), rim)]
    mark_ref[...] = jnp.zeros_like(mark_ref)
    for copy in copies:
        copy.wait()


def inner_back_kernel(
    place_in, weight_ref, adj_ref, grad_ref, rim_spread,
    whole_hbm, edge_ref, mark_ref,
    place_ref, spread, out, sems,
):
    fetch = pltpu.make_async_copy(place_in, place_ref, sems.at[1])
    fetch.start()
    count, slots, block_rows, _ = adj_ref.shape
    blocks = place_ref.shape[0] // slots
    rim = BAND * block_rows
    spread[: 2 * BAND] = rim_spread[: 2 * BAND]
    spread[2 * BAND :] = jnp.zeros_like(spread[2 * BAND :])
    spread[blocks - 2 * BAND : blocks] = rim_spread[2 * BAND :]
    upstream = to_upstream(weight_ref[...], grad_ref[...])
    fetch.wait()
    scatter_rows(
        [places_of(place_ref, step + BAND, slots) for step in range(count)],
        upstream, adj_ref, spread,
    )
    for step in range(count):
        here = pl.ds(step * block_rows, block_rows)
        out[here] = spread[BAND + step].T.astype(jnp.bfloat16)
    finish = pltpu.make_async_copy(out, whole_hbm.at[pl.ds(rim, count * block_rows)], sems.at[0])
    finish.start()
    mark_ref[...] = jnp.zeros_like(mark_ref)
    for block in range(BAND):
        edge_ref[block * block_rows : (block + 1) * block_rows] = spread[block].T
        after = BAND + block
        edge_ref[after * block_rows : (after + 1) * block_rows] = spread[blocks - BAND + block].T
    finish.wait()


def add_kernel(parts, *refs):
    values = [ref[...].astype(jnp.float32) for ref in refs[:parts]]
    total = values[0] + values[1]
    if parts == 4:
        total = total + (values[2] + values[3])
    refs[-1][...] = total.astype(refs[-1].dtype)


def last_kernel(
    scale, own_ref, other_ref, edge_ref, first_ref, second_ref, whole_in,
    weight_out, bias_out, whole_hbm,
    out, sums, bias, sems,
):
    half = sums.shape[0] // 2
    rim = first_ref.shape[0]
    rows = whole_hbm.shape[0]
    copies = [
        pltpu.make_async_copy(sums, weight_out, sems.at[0]),
        pltpu.make_async_copy(bias, bias_out, sems.at[1]),
        pltpu.make_async_copy(out.at[pl.ds(0, rim)], whole_hbm.at[pl.ds(0, rim)], sems.at[2]),
        pltpu.make_async_copy(
            out.at[pl.ds(rim, rim)], whole_hbm.at[pl.ds(rows - rim, rim)], sems.at[3]
        ),
    ]
    side = core_side()
    own_rows = pl.ds(pl.multiple_of(side * half, half), half)
    other_rows = pl.ds(pl.multiple_of((1 - side) * half, half), half)
    sums[own_rows] = own_ref[:half] * scale
    sums[other_rows] = other_ref[:half] * scale
    copies[0].start()
    first = jnp.where(side == 0, own_ref[half : half + 1], other_ref[half : half + 1])
    bias[...] = first * scale
    copies[1].start()
    odd = place_in_mesh() & 1
    for base, spill_ref in (((1 - odd) * rim, first_ref), (odd * rim, second_ref)):
        here = pl.ds(pl.multiple_of(base, rim), rim)
        out[here] = (edge_ref[here] + spill_ref[...].astype(jnp.float32)).astype(jnp.bfloat16)
    for copy in copies[2:]:
        copy.start()
    for copy in copies:
        copy.wait()


def add(values, dtype, after=()):
    size = values[0].size
    return pl.pallas_call(
        functools.partial(add_kernel, len(values)),
        out_shape=jax.ShapeDtypeStruct(values[0].shape, dtype),
        in_specs=[pl.BlockSpec(memory_space=pltpu.VMEM)] * len(values)
        + [pl.BlockSpec(memory_space=pl.ANY)] * len(after),
        compiler_params=pltpu.CompilerParams(vmem_limit_bytes=2 * MIB),
        cost_estimate=pl.CostEstimate(
            flops=size * len(values), bytes_accessed=8 * size, transcendentals=0
        ),
        name="add_halves",
    )(*values, *after)


def swap(value, masks):
    pairs = [(i, i ^ mask) for i, mask in enumerate(masks) if mask]
    return lax.ppermute(value, AXES, pairs)


def with_next(value, count):
    pairs = [(i, (i + 1 if i & 1 else i - 1) % count) for i in range(count)]
    return lax.ppermute(value, AXES, pairs)


def sum_halves(send, keep, count, core_bit, marks):
    others = [bit for bit in range(count.bit_length() - 1) if bit != core_bit]
    groups = [others[i : i + 2] for i in range(0, len(others), 2)]
    groups[0] = groups[0][::-1]
    total = add([keep, swap(send, [1 << core_bit] * count)], jnp.bfloat16, marks.get("core", ()))
    for step in range(len(groups)):
        masks = []
        for group in (groups[step], groups[len(groups) - 1 - step]):
            if len(groups[0]) != len(groups[-1]):
                group = groups[step]
            low = 1 << group[0]
            masks.append((low, 1 << group[1], low | 1 << group[1]) if group[1:] else (low,))
        parts = [total] + [
            swap(total, [masks[(i >> core_bit) & 1][k] for i in range(count)])
            for k in range(len(masks[0]))
        ]
        last = step == len(groups) - 1
        name = "last" if last else step
        total = add(parts, jnp.float32 if last else jnp.bfloat16, marks.get(name, ()))
    return total


def on_device(features, adj_values, adj_offset, adj_count, weight, bias_vector, cotangent):
    blocks, slots = adj_offset.shape
    block_rows = adj_values.shape[2]
    rows, width = features.shape
    rim = BAND * block_rows
    inner = rows - 2 * rim
    cols = lax.axis_size("cols")
    count = lax.axis_size("rows") * cols
    vmem = pl.BlockSpec(memory_space=pltpu.VMEM)
    hbm = pl.BlockSpec(memory_space=pltpu.HBM)
    anywhere = pl.BlockSpec(memory_space=pl.ANY)
    place_scratch = pltpu.SMEM((blocks * slots,), jnp.int32)
    bias_row = bias_vector.reshape(1, width)

    def in_hbm(value):
        return pltpu.with_memory_space_constraint(value, pltpu.HBM)

    def shape(*sizes, dtype=jnp.bfloat16):
        return jax.ShapeDtypeStruct(sizes, dtype)

    def params(mib):
        return pltpu.CompilerParams(vmem_limit_bytes=mib * MIB)

    def cost(share):
        return pl.CostEstimate(
            flops=int(1.2e9 * share), bytes_accessed=int(6e6 * share),
            transcendentals=int(8e5 * share),
        )

    offsets = in_hbm(adj_offset.T)
    counts = in_hbm(adj_count)
    core_bit = cols.bit_length() - 1
    first_rim, second_rim = pl.pallas_call(
        halo_kernel,
        out_shape=(shape(rim, width), shape(rim, width)),
        in_specs=[hbm],
        out_specs=(vmem, vmem),
        scratch_shapes=[pltpu.SemaphoreType.DMA((2,))],
        compiler_params=params(2),
        cost_estimate=cost(0.05),
        name="halo_rows",
    )(in_hbm(features))
    first_halo = swap(first_rim, [1] * count)
    second_halo = with_next(second_rim, count)
    (
        activated, places, grad_inner, partial, sums, weight_near, bias_near, dense, own_part,
        cot_rim, adj_inner,
    ) = pl.pallas_call(
        inner_kernel,
        out_shape=(
            shape(rows, width),
            shape(blocks * slots, dtype=jnp.int32),
            shape(inner, width),
            shape(width, width, dtype=jnp.float32),
            shape(8, width, dtype=jnp.float32),
            shape(width, width),
            shape(1, width, dtype=jnp.float32),
            shape(2, 3 * BAND + 1, rim, block_rows),
            shape(2 * rim, width, dtype=jnp.float32),
            shape(2 * rim, width),
            shape(blocks - 2 * BAND, slots, block_rows, block_rows),
        ),
        in_specs=[hbm] * 7,
        out_specs=(hbm, anywhere) + (vmem,) * 9,
        scratch_shapes=[
            pltpu.SMEM((slots, blocks), jnp.int32),
            pltpu.SMEM((blocks,), jnp.int32),
            place_scratch,
            pltpu.VMEM((rows + block_rows, width), jnp.bfloat16),
            pltpu.VMEM((2 * BAND, slots, block_rows, block_rows), jnp.bfloat16),
            pltpu.VMEM((inner, width), jnp.bfloat16),
            pltpu.VMEM((inner, width), jnp.bfloat16),
            pltpu.VMEM((inner, width), jnp.bfloat16),
            pltpu.SemaphoreType.DMA((15,)),
        ],
        compiler_params=params(20),
        cost_estimate=cost(0.5),
        name="inner_rows",
    )(
        offsets, counts,
        *(in_hbm(x) for x in (weight, bias_row, features, adj_values, cotangent)),
    )
    half_shape = (width // 2 + TAIL, width)
    act_rim, grad_rim, send, keep = pl.pallas_call(
        rim_kernel,
        out_shape=(
            shape(2 * rim, width),
            shape(2 * rim, width),
            shape(*half_shape, dtype=jnp.float32),
            shape(*half_shape, dtype=jnp.float32),
        ),
        in_specs=[vmem] * 9,
        out_specs=(vmem,) * 4,
        scratch_shapes=[
            pltpu.VMEM((2 * rim, width), jnp.bfloat16),
            pltpu.VMEM((2 * rim, width), jnp.bfloat16),
            pltpu.VMEM((2,) + half_shape, jnp.float32),
        ],
        compiler_params=params(12),
        cost_estimate=cost(0.2),
        name="rim_rows",
    )(
        weight_near, bias_near, own_part, first_halo, second_halo, dense, cot_rim, partial, sums,
    )
    mark = shape(8, 128, dtype=jnp.float32)
    activated, rim_spread, first_spill, second_spill, first_mark = pl.pallas_call(
        rim_back_kernel,
        out_shape=(
            shape(rows, width),
            shape(4 * BAND, width, block_rows, dtype=jnp.float32),
            shape(rim, width),
            shape(rim, width),
            mark,
        ),
        in_specs=[vmem] * 4 + [hbm],
        out_specs=(hbm,) + (vmem,) * 4,
        scratch_shapes=[
            pltpu.VMEM((2 * rim, width), jnp.bfloat16),
            pltpu.SemaphoreType.DMA((2,)),
        ],
        input_output_aliases={4: 0},
        compiler_params=params(12),
        cost_estimate=cost(0.2),
        name="rim_rows_back",
    )(weight_near, dense, grad_rim, act_rim, activated)
    first_part = swap(first_spill, [1] * count)
    second_part = with_next(second_spill, count)
    grad_whole, edges, second_mark = pl.pallas_call(
        inner_back_kernel,
        out_shape=(shape(rows, width), shape(2 * rim, width, dtype=jnp.float32), mark),
        in_specs=[anywhere] + [vmem] * 4,
        out_specs=(hbm, vmem, vmem),
        scratch_shapes=[
            place_scratch,
            pltpu.VMEM((blocks + 1, width, block_rows), jnp.float32),
            pltpu.VMEM((inner, width), jnp.bfloat16),
            pltpu.SemaphoreType.DMA((2,)),
        ],
        compiler_params=params(12),
        cost_estimate=cost(0.3),
        name="inner_rows_back",
    )(places, weight_near, adj_inner, grad_inner, rim_spread)
    marks = {"core": (first_mark,), "last": (second_mark, first_part, second_part)}
    own_half = sum_halves(send, keep, count, core_bit, marks)
    other_half = swap(own_half, [1 << core_bit] * count)
    norm_scale = 1.0 / math.sqrt(rows * count)
    grad_weight, grad_bias, grad_features = pl.pallas_call(
        functools.partial(last_kernel, norm_scale),
        out_shape=(
            shape(width, width, dtype=jnp.float32),
            shape(1, width, dtype=jnp.float32),
            shape(rows, width),
        ),
        in_specs=[vmem] * 5 + [hbm],
        out_specs=(hbm, hbm, hbm),
        scratch_shapes=[
            pltpu.VMEM((2 * rim, width), jnp.bfloat16),
            pltpu.VMEM((width, width), jnp.float32),
            pltpu.VMEM((1, width), jnp.float32),
            pltpu.SemaphoreType.DMA((4,)),
        ],
        input_output_aliases={5: 2},
        compiler_params=params(8),
        name="last_step",
    )(own_half, other_half, edges, first_part, second_part, grad_whole)
    return (activated, grad_features, grad_weight, grad_bias.reshape(width))


def solution(mesh):
    return jax.shard_map(
        on_device,
        mesh=mesh,
        in_specs=(
            P(AXES, None),
            P(AXES, None, None, None),
            P(AXES, None),
            P(AXES),
            P(),
            P(),
            P(AXES, None),
        ),
        out_specs=(P(AXES, None), P(AXES, None), P(), P()),
        check_vma=False,
    )
```

```python
import functools
import math

import jax
import jax.numpy as jnp
from jax import lax
from jax.experimental import pallas as pl
from jax.experimental.pallas import tpu as pltpu
from jax.sharding import PartitionSpec as P

BAND = 2
TAIL = 8
AXES = ("rows", "cols")
MIB = 1024 * 1024


def row_of(adj_ref, block, slots):
    return jnp.concatenate([adj_ref[block, slot] for slot in range(slots)], 1)


def pick(source, places, block_rows):
    return jnp.concatenate(
        [
            source[pl.ds(pl.multiple_of(place * block_rows, block_rows), block_rows)]
            for place in places
        ],
        0,
    )


def write_places(off_ref, cnt_ref, place_ref, blocks, slots):
    for block in range(blocks):
        if block < BAND:
            shift, dump = BAND, 3 * BAND
        elif block < blocks - BAND:
            shift, dump = 0, blocks
        else:
            shift, dump = 2 * BAND - blocks, 3 * BAND
        for slot in range(slots):
            place_ref[block * slots + slot] = jnp.where(
                slot < cnt_ref[block], block + shift + off_ref[slot, block], dump
            )


def places_of(place_ref, block, slots):
    return [place_ref[block * slots + slot] for slot in range(slots)]


def side_by_side(dense, side, first, last):
    return jnp.concatenate([dense[side, place] for place in range(first, last)], 1)


def place_in_mesh():
    return lax.axis_index("rows") * lax.axis_size("cols") + lax.axis_index("cols")


def core_side():
    return lax.axis_index("rows") & 1


def halo_kernel(feat_hbm, first_ref, second_ref, sems):
    rows = feat_hbm.shape[0]
    rim = first_ref.shape[0]
    odd = place_in_mesh() & 1
    last = rows - rim
    starts = ((1 - odd) * last, odd * last)
    copies = [
        pltpu.make_async_copy(
            feat_hbm.at[pl.ds(pl.multiple_of(start, rim), rim)], out_ref, sems.at[i]
        )
        for i, (start, out_ref) in enumerate(zip(starts, (first_ref, second_ref)))
    ]
    for copy in copies:
        copy.start()
    for copy in copies:
        copy.wait()


def activate(preact, cotangent):
    gate = 1.0 / (1.0 + jnp.exp(-preact))
    grad = cotangent.astype(jnp.float32) * gate * (1.0 + preact * (1.0 - gate))
    return (preact * gate).astype(jnp.bfloat16), grad.astype(jnp.bfloat16)


def column_sums(grad):
    rows, width = grad.shape
    return jnp.sum(grad.astype(jnp.float32).reshape(rows // 8, 8, width), axis=0)


def to_upstream(weight, grad):
    return lax.dot_general(
        weight, grad, (((1,), (1,)), ((), ())), preferred_element_type=jnp.float32
    ).astype(jnp.bfloat16)


def weight_terms(agg, grad):
    return lax.dot_general(
        agg, grad, (((0,), (0,)), ((), ())), preferred_element_type=jnp.float32
    )


def inner_kernel(
    off_hbm, cnt_hbm, weight_hbm, bias_hbm, feat_hbm, adj_hbm, cot_hbm,
    act_hbm, place_out, grad_ref, partial_ref, sums_ref, weight_ref, bias_ref, dense, own_ref,
    cot_rim, adj,
    off_ref, cnt_ref, place_ref, feat, adj_rim, cot, act, agg_all, sems,
):
    blocks, slots, block_rows, _ = adj_hbm.shape
    rows, width = feat_hbm.shape
    count = blocks - 2 * BAND
    rim = BAND * block_rows
    inner = count * block_rows
    scalars = [
        pltpu.make_async_copy(off_hbm, off_ref, sems.at[12]),
        pltpu.make_async_copy(cnt_hbm, cnt_ref, sems.at[13]),
    ]
    copies = [
        pltpu.make_async_copy(feat_hbm, feat.at[pl.ds(0, rows)], sems.at[0]),
        pltpu.make_async_copy(adj_hbm.at[pl.ds(BAND, count)], adj, sems.at[1]),
        pltpu.make_async_copy(weight_hbm, weight_ref, sems.at[2]),
        pltpu.make_async_copy(bias_hbm, bias_ref, sems.at[3]),
        pltpu.make_async_copy(cot_hbm.at[pl.ds(rim, inner)], cot, sems.at[4]),
        pltpu.make_async_copy(adj_hbm.at[pl.ds(0, BAND)], adj_rim.at[pl.ds(0, BAND)], sems.at[5]),
        pltpu.make_async_copy(
            adj_hbm.at[pl.ds(blocks - BAND, BAND)], adj_rim.at[pl.ds(BAND, BAND)], sems.at[6]
        ),
        pltpu.make_async_copy(cot_hbm.at[pl.ds(0, rim)], cot_rim.at[pl.ds(0, rim)], sems.at[7]),
        pltpu.make_async_copy(
            cot_hbm.at[pl.ds(rows - rim, rim)], cot_rim.at[pl.ds(rim, rim)], sems.at[8]
        ),
    ]
    for copy in scalars + copies:
        copy.start()
    feat[rows:] = jnp.zeros((block_rows, width), jnp.bfloat16)
    dense[...] = jnp.zeros_like(dense)
    for copy in scalars:
        copy.wait()
    write_places(off_ref, cnt_ref, place_ref, blocks, slots)
    place_copy = pltpu.make_async_copy(place_ref, place_out, sems.at[14])
    place_copy.start()
    for copy in copies[:5]:
        copy.wait()
    weight = weight_ref[...]
    bias = bias_ref[...]
    sums = jnp.zeros((8, width), jnp.float32)
    for step in range(0, count, 2):
        for block in (step, step + 1):
            places = places_of(place_ref, block + BAND, slots)
            agg_all[block * block_rows : (block + 1) * block_rows] = jnp.dot(
                row_of(adj, block, slots), pick(feat, places, block_rows),
                preferred_element_type=jnp.float32,
            ).astype(jnp.bfloat16)
        here = pl.ds(step * block_rows, 2 * block_rows)
        preact = jnp.dot(agg_all[here], weight, preferred_element_type=jnp.float32) + bias
        act[here], grad = activate(preact, cot[here])
        grad_ref[here] = grad
        sums = sums + column_sums(grad)
    act_out = pltpu.make_async_copy(act, act_hbm.at[pl.ds(rim, inner)], sems.at[11])
    act_out.start()
    sums_ref[...] = sums
    partial_ref[...] = weight_terms(agg_all[...], grad_ref[...])
    for copy in copies[5:]:
        copy.wait()
    for side, first in enumerate((0, blocks - BAND)):
        for row in range(BAND):
            here = pl.ds(row * block_rows, block_rows)
            for slot, place in enumerate(places_of(place_ref, first + row, slots)):
                dense[side, place, here] = adj_rim[side * BAND + row, slot]
    own_ref[:rim] = jnp.dot(
        side_by_side(dense, 0, BAND, 3 * BAND), feat[: 2 * rim],
        preferred_element_type=jnp.float32,
    )
    own_ref[rim:] = jnp.dot(
        side_by_side(dense, 1, 0, 2 * BAND), feat[rows - 2 * rim : rows],
        preferred_element_type=jnp.float32,
    )
    act_out.wait()
    place_copy.wait()


def rim_kernel(
    weight_ref, bias_ref, own_ref, first_ref, second_ref, dense, cot_ref, partial_ref, sums_ref,
    act_ref, grad_ref, send_ref, keep_ref,
    halo, agg_all, payload,
):
    rim, width = first_ref.shape
    odd = place_in_mesh() & 1
    halo[pl.ds(pl.multiple_of((1 - odd) * rim, rim), rim)] = first_ref[...]
    halo[pl.ds(pl.multiple_of(odd * rim, rim), rim)] = second_ref[...]
    weight = weight_ref[...]
    bias = bias_ref[...]
    sums = sums_ref[...]
    for side, first in enumerate((0, 2 * BAND)):
        here = pl.ds(side * rim, rim)
        agg = own_ref[here] + jnp.dot(
            side_by_side(dense, side, first, first + BAND), halo[here],
            preferred_element_type=jnp.float32,
        )
        agg = agg.astype(jnp.bfloat16)
        agg_all[here] = agg
        preact = jnp.dot(agg, weight, preferred_element_type=jnp.float32) + bias
        act_ref[here], grad = activate(preact, cot_ref[here])
        grad_ref[here] = grad
        sums = sums + column_sums(grad)
    half = width // 2
    partial = partial_ref[...] + weight_terms(agg_all[...], grad_ref[...])
    payload[0, :half] = partial[:half]
    payload[1, :half] = partial[half:]
    tail = jnp.zeros((TAIL, width), jnp.float32)
    payload[0, half:] = jnp.broadcast_to(jnp.sum(sums, axis=0, keepdims=True), tail.shape)
    payload[1, half:] = tail
    side = core_side()
    keep_ref[...] = payload[side]
    send_ref[...] = payload[1 - side].astype(send_ref.dtype)


def scatter_rows(places, upstream, adj_ref, spread):
    _, slots, block_rows, _ = adj_ref.shape
    for step, targets in enumerate(places):
        terms = jnp.dot(
            upstream[:, step * block_rows : (step + 1) * block_rows],
            row_of(adj_ref, step, slots),
            preferred_element_type=jnp.float32,
        )
        for slot, target in enumerate(targets):
            spread[target] += terms[:, slot * block_rows : (slot + 1) * block_rows]


def rim_back_kernel(
    weight_ref, dense, grad_ref, act_ref, act_in,
    act_hbm, spread, first_ref, second_ref, mark_ref,
    spill, sems,
):
    block_rows = dense.shape[3]
    rim = BAND * block_rows
    rows = act_hbm.shape[0]
    copies = [
        pltpu.make_async_copy(act_ref.at[pl.ds(0, rim)], act_hbm.at[pl.ds(0, rim)], sems.at[0]),
        pltpu.make_async_copy(
            act_ref.at[pl.ds(rim, rim)], act_hbm.at[pl.ds(rows - rim, rim)], sems.at[1]
        ),
    ]
    for copy in copies:
        copy.start()
    weight = weight_ref[...]
    for side, (inside, outside) in enumerate(((BAND, 0), (0, 2 * BAND))):
        terms = jnp.dot(
            to_upstream(weight, grad_ref[side * rim : (side + 1) * rim]),
            side_by_side(dense, side, 0, 3 * BAND),
            preferred_element_type=jnp.float32,
        )
        for block in range(2 * BAND):
            lane = (inside + block) * block_rows
            spread[side * 2 * BAND + block] = terms[:, lane : lane + block_rows]
        for block in range(BAND):
            lane = (outside + block) * block_rows
            here = pl.ds(side * rim + block * block_rows, block_rows)
            spill[here] = terms[:, lane : lane + block_rows].T.astype(jnp.bfloat16)
    odd = place_in_mesh() & 1
    first_ref[...] = spill[pl.ds(pl.multiple_of((1 - odd) * rim, rim), rim)]
    second_ref[...] = spill[pl.ds(pl.multiple_of(odd * rim, rim), rim)]
    mark_ref[...] = jnp.zeros_like(mark_ref)
    for copy in copies:
        copy.wait()


def inner_back_kernel(
    place_in, weight_ref, adj_ref, grad_ref, rim_spread,
    whole_hbm, edge_ref, mark_ref,
    place_ref, spread, out, sems,
):
    fetch = pltpu.make_async_copy(place_in, place_ref, sems.at[1])
    fetch.start()
    count, slots, block_rows, _ = adj_ref.shape
    blocks = place_ref.shape[0] // slots
    rim = BAND * block_rows
    spread[: 2 * BAND] = rim_spread[: 2 * BAND]
    spread[2 * BAND :] = jnp.zeros_like(spread[2 * BAND :])
    spread[blocks - 2 * BAND : blocks] = rim_spread[2 * BAND :]
    upstream = to_upstream(weight_ref[...], grad_ref[...])
    fetch.wait()
    scatter_rows(
        [places_of(place_ref, step + BAND, slots) for step in range(count)],
        upstream, adj_ref, spread,
    )
    for step in range(count):
        here = pl.ds(step * block_rows, block_rows)
        out[here] = spread[BAND + step].T.astype(jnp.bfloat16)
    finish = pltpu.make_async_copy(out, whole_hbm.at[pl.ds(rim, count * block_rows)], sems.at[0])
    finish.start()
    mark_ref[...] = jnp.zeros_like(mark_ref)
    for block in range(BAND):
        edge_ref[block * block_rows : (block + 1) * block_rows] = spread[block].T
        after = BAND + block
        edge_ref[after * block_rows : (after + 1) * block_rows] = spread[blocks - BAND + block].T
    finish.wait()


def add_kernel(parts, *refs):
    values = [ref[...].astype(jnp.float32) for ref in refs[:parts]]
    total = values[0] + values[1]
    if parts == 4:
        total = total + (values[2] + values[3])
    refs[-1][...] = total.astype(refs[-1].dtype)


def last_kernel(
    scale, own_ref, other_ref, edge_ref, first_ref, second_ref, whole_in,
    weight_out, bias_out, whole_hbm,
    out, sums, bias, sems,
):
    half = sums.shape[0] // 2
    rim = first_ref.shape[0]
    rows = whole_hbm.shape[0]
    copies = [
        pltpu.make_async_copy(sums, weight_out, sems.at[0]),
        pltpu.make_async_copy(bias, bias_out, sems.at[1]),
        pltpu.make_async_copy(out.at[pl.ds(0, rim)], whole_hbm.at[pl.ds(0, rim)], sems.at[2]),
        pltpu.make_async_copy(
            out.at[pl.ds(rim, rim)], whole_hbm.at[pl.ds(rows - rim, rim)], sems.at[3]
        ),
    ]
    side = core_side()
    own_rows = pl.ds(pl.multiple_of(side * half, half), half)
    other_rows = pl.ds(pl.multiple_of((1 - side) * half, half), half)
    own = own_ref[...].astype(jnp.float32) * scale
    other = other_ref[...].astype(jnp.float32) * scale
    sums[own_rows] = own[:half]
    sums[other_rows] = other[:half]
    copies[0].start()
    bias[...] = jnp.where(side == 0, own[half : half + 1], other[half : half + 1])
    copies[1].start()
    odd = place_in_mesh() & 1
    for base, spill_ref in (((1 - odd) * rim, first_ref), (odd * rim, second_ref)):
        here = pl.ds(pl.multiple_of(base, rim), rim)
        out[here] = (edge_ref[here] + spill_ref[...].astype(jnp.float32)).astype(jnp.bfloat16)
    for copy in copies[2:]:
        copy.start()
    for copy in copies:
        copy.wait()


def add(values, dtype, after=()):
    size = values[0].size
    return pl.pallas_call(
        functools.partial(add_kernel, len(values)),
        out_shape=jax.ShapeDtypeStruct(values[0].shape, dtype),
        in_specs=[pl.BlockSpec(memory_space=pltpu.VMEM)] * len(values)
        + [pl.BlockSpec(memory_space=pl.ANY)] * len(after),
        compiler_params=pltpu.CompilerParams(vmem_limit_bytes=2 * MIB),
        cost_estimate=pl.CostEstimate(
            flops=size * len(values), bytes_accessed=8 * size, transcendentals=0
        ),
        name="add_halves",
    )(*values, *after)


def swap(value, masks):
    pairs = [(i, i ^ mask) for i, mask in enumerate(masks) if mask]
    return lax.ppermute(value, AXES, pairs)


def with_next(value, count):
    pairs = [(i, (i + 1 if i & 1 else i - 1) % count) for i in range(count)]
    return lax.ppermute(value, AXES, pairs)


def sum_halves(send, keep, count, core_bit, marks):
    others = [bit for bit in range(count.bit_length() - 1) if bit != core_bit]
    groups = [others[i : i + 2] for i in range(0, len(others), 2)]
    groups[0] = groups[0][::-1]
    total = add([keep, swap(send, [1 << core_bit] * count)], jnp.bfloat16, marks.get("core", ()))
    for step in range(len(groups)):
        masks = []
        for group in (groups[step], groups[len(groups) - 1 - step]):
            if len(groups[0]) != len(groups[-1]):
                group = groups[step]
            low = 1 << group[0]
            masks.append((low, 1 << group[1], low | 1 << group[1]) if group[1:] else (low,))
        parts = [total] + [
            swap(total, [masks[(i >> core_bit) & 1][k] for i in range(count)])
            for k in range(len(masks[0]))
        ]
        last = step == len(groups) - 1
        name = "last" if last else step
        total = add(parts, jnp.bfloat16, marks.get(name, ()))
    return total


def on_device(features, adj_values, adj_offset, adj_count, weight, bias_vector, cotangent):
    blocks, slots = adj_offset.shape
    block_rows = adj_values.shape[2]
    rows, width = features.shape
    rim = BAND * block_rows
    inner = rows - 2 * rim
    cols = lax.axis_size("cols")
    count = lax.axis_size("rows") * cols
    vmem = pl.BlockSpec(memory_space=pltpu.VMEM)
    hbm = pl.BlockSpec(memory_space=pltpu.HBM)
    anywhere = pl.BlockSpec(memory_space=pl.ANY)
    place_scratch = pltpu.SMEM((blocks * slots,), jnp.int32)
    bias_row = bias_vector.reshape(1, width)

    def in_hbm(value):
        return pltpu.with_memory_space_constraint(value, pltpu.HBM)

    def shape(*sizes, dtype=jnp.bfloat16):
        return jax.ShapeDtypeStruct(sizes, dtype)

    def params(mib):
        return pltpu.CompilerParams(vmem_limit_bytes=mib * MIB)

    def cost(share):
        return pl.CostEstimate(
            flops=int(1.2e9 * share), bytes_accessed=int(6e6 * share),
            transcendentals=int(8e5 * share),
        )

    offsets = in_hbm(adj_offset.T)
    counts = in_hbm(adj_count)
    core_bit = cols.bit_length() - 1
    first_rim, second_rim = pl.pallas_call(
        halo_kernel,
        out_shape=(shape(rim, width), shape(rim, width)),
        in_specs=[hbm],
        out_specs=(vmem, vmem),
        scratch_shapes=[pltpu.SemaphoreType.DMA((2,))],
        compiler_params=params(2),
        cost_estimate=cost(0.05),
        name="halo_rows",
    )(in_hbm(features))
    first_halo = swap(first_rim, [1] * count)
    second_halo = with_next(second_rim, count)
    (
        activated, places, grad_inner, partial, sums, weight_near, bias_near, dense, own_part,
        cot_rim, adj_inner,
    ) = pl.pallas_call(
        inner_kernel,
        out_shape=(
            shape(rows, width),
            shape(blocks * slots, dtype=jnp.int32),
            shape(inner, width),
            shape(width, width, dtype=jnp.float32),
            shape(8, width, dtype=jnp.float32),
            shape(width, width),
            shape(1, width, dtype=jnp.float32),
            shape(2, 3 * BAND + 1, rim, block_rows),
            shape(2 * rim, width, dtype=jnp.float32),
            shape(2 * rim, width),
            shape(blocks - 2 * BAND, slots, block_rows, block_rows),
        ),
        in_specs=[hbm] * 7,
        out_specs=(hbm, anywhere) + (vmem,) * 9,
        scratch_shapes=[
            pltpu.SMEM((slots, blocks), jnp.int32),
            pltpu.SMEM((blocks,), jnp.int32),
            place_scratch,
            pltpu.VMEM((rows + block_rows, width), jnp.bfloat16),
            pltpu.VMEM((2 * BAND, slots, block_rows, block_rows), jnp.bfloat16),
            pltpu.VMEM((inner, width), jnp.bfloat16),
            pltpu.VMEM((inner, width), jnp.bfloat16),
            pltpu.VMEM((inner, width), jnp.bfloat16),
            pltpu.SemaphoreType.DMA((15,)),
        ],
        compiler_params=params(20),
        cost_estimate=cost(0.5),
        name="inner_rows",
    )(
        offsets, counts,
        *(in_hbm(x) for x in (weight, bias_row, features, adj_values, cotangent)),
    )
    half_shape = (width // 2 + TAIL, width)
    act_rim, grad_rim, send, keep = pl.pallas_call(
        rim_kernel,
        out_shape=(
            shape(2 * rim, width),
            shape(2 * rim, width),
            shape(*half_shape),
            shape(*half_shape, dtype=jnp.float32),
        ),
        in_specs=[vmem] * 9,
        out_specs=(vmem,) * 4,
        scratch_shapes=[
            pltpu.VMEM((2 * rim, width), jnp.bfloat16),
            pltpu.VMEM((2 * rim, width), jnp.bfloat16),
            pltpu.VMEM((2,) + half_shape, jnp.float32),
        ],
        compiler_params=params(12),
        cost_estimate=cost(0.2),
        name="rim_rows",
    )(
        weight_near, bias_near, own_part, first_halo, second_halo, dense, cot_rim, partial, sums,
    )
    mark = shape(8, 128, dtype=jnp.float32)
    activated, rim_spread, first_spill, second_spill, first_mark = pl.pallas_call(
        rim_back_kernel,
        out_shape=(
            shape(rows, width),
            shape(4 * BAND, width, block_rows, dtype=jnp.float32),
            shape(rim, width),
            shape(rim, width),
            mark,
        ),
        in_specs=[vmem] * 4 + [hbm],
        out_specs=(hbm,) + (vmem,) * 4,
        scratch_shapes=[
            pltpu.VMEM((2 * rim, width), jnp.bfloat16),
            pltpu.SemaphoreType.DMA((2,)),
        ],
        input_output_aliases={4: 0},
        compiler_params=params(12),
        cost_estimate=cost(0.2),
        name="rim_rows_back",
    )(weight_near, dense, grad_rim, act_rim, activated)
    first_part = swap(first_spill, [1] * count)
    second_part = with_next(second_spill, count)
    grad_whole, edges, second_mark = pl.pallas_call(
        inner_back_kernel,
        out_shape=(shape(rows, width), shape(2 * rim, width, dtype=jnp.float32), mark),
        in_specs=[anywhere] + [vmem] * 4,
        out_specs=(hbm, vmem, vmem),
        scratch_shapes=[
            place_scratch,
            pltpu.VMEM((blocks + 1, width, block_rows), jnp.float32),
            pltpu.VMEM((inner, width), jnp.bfloat16),
            pltpu.SemaphoreType.DMA((2,)),
        ],
        compiler_params=params(12),
        cost_estimate=cost(0.3),
        name="inner_rows_back",
    )(places, weight_near, adj_inner, grad_inner, rim_spread)
    marks = {"core": (first_mark,), "last": (second_mark, first_part, second_part)}
    own_half = sum_halves(send, keep, count, core_bit, marks)
    other_half = swap(own_half, [1 << core_bit] * count)
    norm_scale = 1.0 / math.sqrt(rows * count)
    grad_weight, grad_bias, grad_features = pl.pallas_call(
        functools.partial(last_kernel, norm_scale),
        out_shape=(
            shape(width, width, dtype=jnp.float32),
            shape(1, width, dtype=jnp.float32),
            shape(rows, width),
        ),
        in_specs=[vmem] * 5 + [hbm],
        out_specs=(hbm, hbm, hbm),
        scratch_shapes=[
            pltpu.VMEM((2 * rim, width), jnp.bfloat16),
            pltpu.VMEM((width, width), jnp.float32),
            pltpu.VMEM((1, width), jnp.float32),
            pltpu.SemaphoreType.DMA((4,)),
        ],
        input_output_aliases={5: 2},
        compiler_params=params(8),
        name="last_step",
    )(own_half, other_half, edges, first_part, second_part, grad_whole)
    return (activated, grad_features, grad_weight, grad_bias.reshape(width))


def solution(mesh):
    return jax.shard_map(
        on_device,
        mesh=mesh,
        in_specs=(
            P(AXES, None),
            P(AXES, None, None, None),
            P(AXES, None),
            P(AXES),
            P(),
            P(),
            P(AXES, None),
        ),
        out_specs=(P(AXES, None), P(AXES, None), P(), P()),
        check_vma=False,
    )
```

```python
import functools
import math

import jax
import jax.numpy as jnp
from jax import lax
from jax.experimental import pallas as pl
from jax.experimental.pallas import tpu as pltpu
from jax.sharding import PartitionSpec as P

BAND = 2
TAIL = 8
AXES = ("rows", "cols")
MIB = 1024 * 1024


def row_of(adj_ref, block, slots):
    return jnp.concatenate([adj_ref[block, slot] for slot in range(slots)], 1)


def pick(source, places, block_rows):
    return jnp.concatenate(
        [
            source[pl.ds(pl.multiple_of(place * block_rows, block_rows), block_rows)]
            for place in places
        ],
        0,
    )


def write_places(off_ref, cnt_ref, place_ref, blocks, slots):
    for block in range(blocks):
        if block < BAND:
            shift, dump = BAND, 3 * BAND
        elif block < blocks - BAND:
            shift, dump = 0, blocks
        else:
            shift, dump = 2 * BAND - blocks, 3 * BAND
        for slot in range(slots):
            place_ref[block * slots + slot] = jnp.where(
                slot < cnt_ref[block], block + shift + off_ref[slot, block], dump
            )


def places_of(place_ref, block, slots):
    return [place_ref[block * slots + slot] for slot in range(slots)]


def side_by_side(dense, side, first, last):
    return jnp.concatenate([dense[side, place] for place in range(first, last)], 1)


def place_in_mesh():
    return lax.axis_index("rows") * lax.axis_size("cols") + lax.axis_index("cols")


def core_side():
    return lax.axis_index("rows") & 1


def halo_kernel(feat_hbm, first_ref, second_ref, sems):
    rows = feat_hbm.shape[0]
    rim = first_ref.shape[0]
    odd = place_in_mesh() & 1
    last = rows - rim
    starts = ((1 - odd) * last, odd * last)
    copies = [
        pltpu.make_async_copy(
            feat_hbm.at[pl.ds(pl.multiple_of(start, rim), rim)], out_ref, sems.at[i]
        )
        for i, (start, out_ref) in enumerate(zip(starts, (first_ref, second_ref)))
    ]
    for copy in copies:
        copy.start()
    for copy in copies:
        copy.wait()


def activate(preact, cotangent):
    gate = 1.0 / (1.0 + jnp.exp(-preact))
    grad = cotangent.astype(jnp.float32) * gate * (1.0 + preact * (1.0 - gate))
    return (preact * gate).astype(jnp.bfloat16), grad.astype(jnp.bfloat16)


def column_sums(grad):
    rows, width = grad.shape
    return jnp.sum(grad.astype(jnp.float32).reshape(rows // 8, 8, width), axis=0)


def to_upstream(weight, grad):
    return lax.dot_general(
        weight, grad, (((1,), (1,)), ((), ())), preferred_element_type=jnp.float32
    ).astype(jnp.bfloat16)


def weight_terms(agg, grad):
    return lax.dot_general(
        agg, grad, (((0,), (0,)), ((), ())), preferred_element_type=jnp.float32
    )


def inner_kernel(
    off_hbm, cnt_hbm, weight_hbm, bias_hbm, feat_hbm, adj_hbm, cot_hbm,
    act_hbm, place_out, grad_ref, partial_ref, sums_ref, weight_ref, bias_ref, dense, own_ref,
    cot_rim, adj,
    off_ref, cnt_ref, place_ref, feat, adj_rim, cot, act, agg_all, sems,
):
    blocks, slots, block_rows, _ = adj_hbm.shape
    rows, width = feat_hbm.shape
    count = blocks - 2 * BAND
    rim = BAND * block_rows
    inner = count * block_rows
    scalars = [
        pltpu.make_async_copy(off_hbm, off_ref, sems.at[12]),
        pltpu.make_async_copy(cnt_hbm, cnt_ref, sems.at[13]),
    ]
    copies = [
        pltpu.make_async_copy(feat_hbm, feat.at[pl.ds(0, rows)], sems.at[0]),
        pltpu.make_async_copy(adj_hbm.at[pl.ds(BAND, count)], adj, sems.at[1]),
        pltpu.make_async_copy(weight_hbm, weight_ref, sems.at[2]),
        pltpu.make_async_copy(bias_hbm, bias_ref, sems.at[3]),
        pltpu.make_async_copy(cot_hbm.at[pl.ds(rim, inner)], cot, sems.at[4]),
        pltpu.make_async_copy(adj_hbm.at[pl.ds(0, BAND)], adj_rim.at[pl.ds(0, BAND)], sems.at[5]),
        pltpu.make_async_copy(
            adj_hbm.at[pl.ds(blocks - BAND, BAND)], adj_rim.at[pl.ds(BAND, BAND)], sems.at[6]
        ),
        pltpu.make_async_copy(cot_hbm.at[pl.ds(0, rim)], cot_rim.at[pl.ds(0, rim)], sems.at[7]),
        pltpu.make_async_copy(
            cot_hbm.at[pl.ds(rows - rim, rim)], cot_rim.at[pl.ds(rim, rim)], sems.at[8]
        ),
    ]
    for copy in scalars + copies:
        copy.start()
    feat[rows:] = jnp.zeros((block_rows, width), jnp.bfloat16)
    dense[...] = jnp.zeros_like(dense)
    for copy in scalars:
        copy.wait()
    write_places(off_ref, cnt_ref, place_ref, blocks, slots)
    place_copy = pltpu.make_async_copy(place_ref, place_out, sems.at[14])
    place_copy.start()
    for copy in copies[:5]:
        copy.wait()
    weight = weight_ref[...]
    bias = bias_ref[...]
    sums = jnp.zeros((8, width), jnp.float32)
    for step in range(0, count, 2):
        for block in (step, step + 1):
            places = places_of(place_ref, block + BAND, slots)
            agg_all[block * block_rows : (block + 1) * block_rows] = jnp.dot(
                row_of(adj, block, slots), pick(feat, places, block_rows),
                preferred_element_type=jnp.float32,
            ).astype(jnp.bfloat16)
        here = pl.ds(step * block_rows, 2 * block_rows)
        preact = jnp.dot(agg_all[here], weight, preferred_element_type=jnp.float32) + bias
        act[here], grad = activate(preact, cot[here])
        grad_ref[here] = grad
        sums = sums + column_sums(grad)
    act_out = pltpu.make_async_copy(act, act_hbm.at[pl.ds(rim, inner)], sems.at[11])
    act_out.start()
    sums_ref[...] = sums
    partial_ref[...] = weight_terms(agg_all[...], grad_ref[...])
    for copy in copies[5:]:
        copy.wait()
    for side, first in enumerate((0, blocks - BAND)):
        for row in range(BAND):
            here = pl.ds(row * block_rows, block_rows)
            for slot, place in enumerate(places_of(place_ref, first + row, slots)):
                dense[side, place, here] = adj_rim[side * BAND + row, slot]
    own_ref[:rim] = jnp.dot(
        side_by_side(dense, 0, BAND, 3 * BAND), feat[: 2 * rim],
        preferred_element_type=jnp.float32,
    )
    own_ref[rim:] = jnp.dot(
        side_by_side(dense, 1, 0, 2 * BAND), feat[rows - 2 * rim : rows],
        preferred_element_type=jnp.float32,
    )
    act_out.wait()
    place_copy.wait()


def rim_kernel(
    weight_ref, bias_ref, own_ref, first_ref, second_ref, dense, cot_ref, partial_ref, sums_ref,
    act_ref, grad_ref, send_ref, keep_ref,
    halo, agg_all, payload,
):
    rim, width = first_ref.shape
    odd = place_in_mesh() & 1
    halo[pl.ds(pl.multiple_of((1 - odd) * rim, rim), rim)] = first_ref[...]
    halo[pl.ds(pl.multiple_of(odd * rim, rim), rim)] = second_ref[...]
    weight = weight_ref[...]
    bias = bias_ref[...]
    sums = sums_ref[...]
    for side, first in enumerate((0, 2 * BAND)):
        here = pl.ds(side * rim, rim)
        agg = own_ref[here] + jnp.dot(
            side_by_side(dense, side, first, first + BAND), halo[here],
            preferred_element_type=jnp.float32,
        )
        agg = agg.astype(jnp.bfloat16)
        agg_all[here] = agg
        preact = jnp.dot(agg, weight, preferred_element_type=jnp.float32) + bias
        act_ref[here], grad = activate(preact, cot_ref[here])
        grad_ref[here] = grad
        sums = sums + column_sums(grad)
    half = width // 2
    partial = partial_ref[...] + weight_terms(agg_all[...], grad_ref[...])
    payload[0, :half] = partial[:half]
    payload[1, :half] = partial[half:]
    tail = jnp.zeros((TAIL, width), jnp.float32)
    payload[0, half:] = jnp.broadcast_to(jnp.sum(sums, axis=0, keepdims=True), tail.shape)
    payload[1, half:] = tail
    side = core_side()
    keep_ref[...] = payload[side]
    send_ref[...] = payload[1 - side].astype(send_ref.dtype)


def scatter_rows(places, upstream, adj_ref, spread):
    _, slots, block_rows, _ = adj_ref.shape
    for step, targets in enumerate(places):
        terms = jnp.dot(
            upstream[:, step * block_rows : (step + 1) * block_rows],
            row_of(adj_ref, step, slots),
            preferred_element_type=jnp.float32,
        )
        for slot, target in enumerate(targets):
            spread[target] += terms[:, slot * block_rows : (slot + 1) * block_rows]


def rim_back_kernel(
    weight_ref, dense, grad_ref, act_ref, act_in,
    act_hbm, spread, first_ref, second_ref, mark_ref,
    spill, sems,
):
    block_rows = dense.shape[3]
    rim = BAND * block_rows
    rows = act_hbm.shape[0]
    copies = [
        pltpu.make_async_copy(act_ref.at[pl.ds(0, rim)], act_hbm.at[pl.ds(0, rim)], sems.at[0]),
        pltpu.make_async_copy(
            act_ref.at[pl.ds(rim, rim)], act_hbm.at[pl.ds(rows - rim, rim)], sems.at[1]
        ),
    ]
    for copy in copies:
        copy.start()
    weight = weight_ref[...]
    for side, (inside, outside) in enumerate(((BAND, 0), (0, 2 * BAND))):
        terms = jnp.dot(
            to_upstream(weight, grad_ref[side * rim : (side + 1) * rim]),
            side_by_side(dense, side, 0, 3 * BAND),
            preferred_element_type=jnp.float32,
        )
        for block in range(2 * BAND):
            lane = (inside + block) * block_rows
            spread[side * 2 * BAND + block] = terms[:, lane : lane + block_rows]
        for block in range(BAND):
            lane = (outside + block) * block_rows
            here = pl.ds(side * rim + block * block_rows, block_rows)
            spill[here] = terms[:, lane : lane + block_rows].T.astype(jnp.bfloat16)
    odd = place_in_mesh() & 1
    first_ref[...] = spill[pl.ds(pl.multiple_of((1 - odd) * rim, rim), rim)]
    second_ref[...] = spill[pl.ds(pl.multiple_of(odd * rim, rim), rim)]
    mark_ref[...] = jnp.zeros_like(mark_ref)
    for copy in copies:
        copy.wait()


def inner_back_kernel(
    place_in, weight_ref, adj_ref, grad_ref, rim_spread,
    whole_hbm, edge_ref, mark_ref,
    place_ref, spread, out, sems,
):
    fetch = pltpu.make_async_copy(place_in, place_ref, sems.at[1])
    fetch.start()
    count, slots, block_rows, _ = adj_ref.shape
    blocks = place_ref.shape[0] // slots
    rim = BAND * block_rows
    spread[: 2 * BAND] = rim_spread[: 2 * BAND]
    spread[2 * BAND :] = jnp.zeros_like(spread[2 * BAND :])
    spread[blocks - 2 * BAND : blocks] = rim_spread[2 * BAND :]
    upstream = to_upstream(weight_ref[...], grad_ref[...])
    fetch.wait()
    scatter_rows(
        [places_of(place_ref, step + BAND, slots) for step in range(count)],
        upstream, adj_ref, spread,
    )
    for step in range(count):
        here = pl.ds(step * block_rows, block_rows)
        out[here] = spread[BAND + step].T.astype(jnp.bfloat16)
    finish = pltpu.make_async_copy(out, whole_hbm.at[pl.ds(rim, count * block_rows)], sems.at[0])
    finish.start()
    mark_ref[...] = jnp.zeros_like(mark_ref)
    for block in range(BAND):
        edge_ref[block * block_rows : (block + 1) * block_rows] = spread[block].T
        after = BAND + block
        edge_ref[after * block_rows : (after + 1) * block_rows] = spread[blocks - BAND + block].T
    finish.wait()


def add_kernel(parts, *refs):
    values = [ref[...].astype(jnp.float32) for ref in refs[:parts]]
    total = values[0] + values[1]
    if parts == 4:
        total = total + (values[2] + values[3])
    refs[-1][...] = total.astype(refs[-1].dtype)


def last_kernel(
    scale, own_ref, other_ref, edge_ref, first_ref, second_ref, whole_in,
    weight_out, bias_out, whole_hbm,
    out, sums, bias, sems,
):
    half = sums.shape[0] // 2
    rim = first_ref.shape[0]
    rows = whole_hbm.shape[0]
    copies = [
        pltpu.make_async_copy(sums, weight_out, sems.at[0]),
        pltpu.make_async_copy(bias, bias_out, sems.at[1]),
        pltpu.make_async_copy(out.at[pl.ds(0, rim)], whole_hbm.at[pl.ds(0, rim)], sems.at[2]),
        pltpu.make_async_copy(
            out.at[pl.ds(rim, rim)], whole_hbm.at[pl.ds(rows - rim, rim)], sems.at[3]
        ),
    ]
    side = core_side()
    own_rows = pl.ds(pl.multiple_of(side * half, half), half)
    other_rows = pl.ds(pl.multiple_of((1 - side) * half, half), half)
    own = own_ref[...].astype(jnp.float32) * scale
    other = other_ref[...].astype(jnp.float32) * scale
    sums[own_rows] = own[:half]
    sums[other_rows] = other[:half]
    copies[0].start()
    bias[...] = jnp.where(side == 0, own[half : half + 1], other[half : half + 1])
    copies[1].start()
    odd = place_in_mesh() & 1
    for base, spill_ref in (((1 - odd) * rim, first_ref), (odd * rim, second_ref)):
        here = pl.ds(pl.multiple_of(base, rim), rim)
        out[here] = (edge_ref[here] + spill_ref[...].astype(jnp.float32)).astype(jnp.bfloat16)
    for copy in copies[2:]:
        copy.start()
    for copy in copies:
        copy.wait()


def add(values, dtype, after=()):
    size = values[0].size
    return pl.pallas_call(
        functools.partial(add_kernel, len(values)),
        out_shape=jax.ShapeDtypeStruct(values[0].shape, dtype),
        in_specs=[pl.BlockSpec(memory_space=pltpu.VMEM)] * len(values)
        + [pl.BlockSpec(memory_space=pl.ANY)] * len(after),
        compiler_params=pltpu.CompilerParams(vmem_limit_bytes=2 * MIB),
        cost_estimate=pl.CostEstimate(
            flops=size * len(values), bytes_accessed=8 * size, transcendentals=0
        ),
        name="add_halves",
    )(*values, *after)


def swap(value, masks):
    pairs = [(i, i ^ mask) for i, mask in enumerate(masks) if mask]
    return lax.ppermute(value, AXES, pairs)


def with_next(value, count):
    pairs = [(i, (i + 1 if i & 1 else i - 1) % count) for i in range(count)]
    return lax.ppermute(value, AXES, pairs)


def sum_halves(send, keep, count, core_bit, marks):
    others = [bit for bit in range(count.bit_length() - 1) if bit != core_bit]
    groups = [others[i : i + 2] for i in range(0, len(others), 2)]
    groups[0] = groups[0][::-1]
    total = add([keep, swap(send, [1 << core_bit] * count)], jnp.bfloat16, marks.get("core", ()))
    for step in range(len(groups)):
        masks = []
        for group in (groups[step], groups[len(groups) - 1 - step]):
            if len(groups[0]) != len(groups[-1]):
                group = groups[step]
            bits = [1 << bit for bit in group]
            if group[1:]:
                both = bits[0] | bits[1]
                near = group is groups[0]
                bits = [bits[0], both, bits[1]] if near else [*bits, both]
            masks.append(bits)
        parts = [total] + [
            swap(total, [masks[(i >> core_bit) & 1][k] for i in range(count)])
            for k in range(len(masks[0]))
        ]
        last = step == len(groups) - 1
        name = "last" if last else step
        total = add(parts, jnp.bfloat16, marks.get(name, ()))
    return total


def on_device(features, adj_values, adj_offset, adj_count, weight, bias_vector, cotangent):
    blocks, slots = adj_offset.shape
    block_rows = adj_values.shape[2]
    rows, width = features.shape
    rim = BAND * block_rows
    inner = rows - 2 * rim
    cols = lax.axis_size("cols")
    count = lax.axis_size("rows") * cols
    vmem = pl.BlockSpec(memory_space=pltpu.VMEM)
    hbm = pl.BlockSpec(memory_space=pltpu.HBM)
    anywhere = pl.BlockSpec(memory_space=pl.ANY)
    place_scratch = pltpu.SMEM((blocks * slots,), jnp.int32)
    bias_row = bias_vector.reshape(1, width)

    def in_hbm(value):
        return pltpu.with_memory_space_constraint(value, pltpu.HBM)

    def shape(*sizes, dtype=jnp.bfloat16):
        return jax.ShapeDtypeStruct(sizes, dtype)

    def params(mib):
        return pltpu.CompilerParams(vmem_limit_bytes=mib * MIB)

    def cost(share):
        return pl.CostEstimate(
            flops=int(1.2e9 * share), bytes_accessed=int(6e6 * share),
            transcendentals=int(8e5 * share),
        )

    offsets = in_hbm(adj_offset.T)
    counts = in_hbm(adj_count)
    core_bit = cols.bit_length() - 1
    first_rim, second_rim = pl.pallas_call(
        halo_kernel,
        out_shape=(shape(rim, width), shape(rim, width)),
        in_specs=[hbm],
        out_specs=(vmem, vmem),
        scratch_shapes=[pltpu.SemaphoreType.DMA((2,))],
        compiler_params=params(2),
        cost_estimate=cost(0.05),
        name="halo_rows",
    )(in_hbm(features))
    first_halo = swap(first_rim, [1] * count)
    second_halo = with_next(second_rim, count)
    (
        activated, places, grad_inner, partial, sums, weight_near, bias_near, dense, own_part,
        cot_rim, adj_inner,
    ) = pl.pallas_call(
        inner_kernel,
        out_shape=(
            shape(rows, width),
            shape(blocks * slots, dtype=jnp.int32),
            shape(inner, width),
            shape(width, width, dtype=jnp.float32),
            shape(8, width, dtype=jnp.float32),
            shape(width, width),
            shape(1, width, dtype=jnp.float32),
            shape(2, 3 * BAND + 1, rim, block_rows),
            shape(2 * rim, width, dtype=jnp.float32),
            shape(2 * rim, width),
            shape(blocks - 2 * BAND, slots, block_rows, block_rows),
        ),
        in_specs=[hbm] * 7,
        out_specs=(hbm, anywhere) + (vmem,) * 9,
        scratch_shapes=[
            pltpu.SMEM((slots, blocks), jnp.int32),
            pltpu.SMEM((blocks,), jnp.int32),
            place_scratch,
            pltpu.VMEM((rows + block_rows, width), jnp.bfloat16),
            pltpu.VMEM((2 * BAND, slots, block_rows, block_rows), jnp.bfloat16),
            pltpu.VMEM((inner, width), jnp.bfloat16),
            pltpu.VMEM((inner, width), jnp.bfloat16),
            pltpu.VMEM((inner, width), jnp.bfloat16),
            pltpu.SemaphoreType.DMA((15,)),
        ],
        compiler_params=params(20),
        cost_estimate=cost(0.5),
        name="inner_rows",
    )(
        offsets, counts,
        *(in_hbm(x) for x in (weight, bias_row, features, adj_values, cotangent)),
    )
    half_shape = (width // 2 + TAIL, width)
    act_rim, grad_rim, send, keep = pl.pallas_call(
        rim_kernel,
        out_shape=(
            shape(2 * rim, width),
            shape(2 * rim, width),
            shape(*half_shape),
            shape(*half_shape, dtype=jnp.float32),
        ),
        in_specs=[vmem] * 9,
        out_specs=(vmem,) * 4,
        scratch_shapes=[
            pltpu.VMEM((2 * rim, width), jnp.bfloat16),
            pltpu.VMEM((2 * rim, width), jnp.bfloat16),
            pltpu.VMEM((2,) + half_shape, jnp.float32),
        ],
        compiler_params=params(12),
        cost_estimate=cost(0.2),
        name="rim_rows",
    )(
        weight_near, bias_near, own_part, first_halo, second_halo, dense, cot_rim, partial, sums,
    )
    mark = shape(8, 128, dtype=jnp.float32)
    activated, rim_spread, first_spill, second_spill, first_mark = pl.pallas_call(
        rim_back_kernel,
        out_shape=(
            shape(rows, width),
            shape(4 * BAND, width, block_rows, dtype=jnp.float32),
            shape(rim, width),
            shape(rim, width),
            mark,
        ),
        in_specs=[vmem] * 4 + [hbm],
        out_specs=(hbm,) + (vmem,) * 4,
        scratch_shapes=[
            pltpu.VMEM((2 * rim, width), jnp.bfloat16),
            pltpu.SemaphoreType.DMA((2,)),
        ],
        input_output_aliases={4: 0},
        compiler_params=params(12),
        cost_estimate=cost(0.2),
        name="rim_rows_back",
    )(weight_near, dense, grad_rim, act_rim, activated)
    first_part = swap(first_spill, [1] * count)
    second_part = with_next(second_spill, count)
    grad_whole, edges, second_mark = pl.pallas_call(
        inner_back_kernel,
        out_shape=(shape(rows, width), shape(2 * rim, width, dtype=jnp.float32), mark),
        in_specs=[anywhere] + [vmem] * 4,
        out_specs=(hbm, vmem, vmem),
        scratch_shapes=[
            place_scratch,
            pltpu.VMEM((blocks + 1, width, block_rows), jnp.float32),
            pltpu.VMEM((inner, width), jnp.bfloat16),
            pltpu.SemaphoreType.DMA((2,)),
        ],
        compiler_params=params(12),
        cost_estimate=cost(0.3),
        name="inner_rows_back",
    )(places, weight_near, adj_inner, grad_inner, rim_spread)
    marks = {"core": (first_mark,), "last": (second_mark, first_part, second_part)}
    own_half = sum_halves(send, keep, count, core_bit, marks)
    other_half = swap(own_half, [1 << core_bit] * count)
    norm_scale = 1.0 / math.sqrt(rows * count)
    grad_weight, grad_bias, grad_features = pl.pallas_call(
        functools.partial(last_kernel, norm_scale),
        out_shape=(
            shape(width, width, dtype=jnp.float32),
            shape(1, width, dtype=jnp.float32),
            shape(rows, width),
        ),
        in_specs=[vmem] * 5 + [hbm],
        out_specs=(hbm, hbm, hbm),
        scratch_shapes=[
            pltpu.VMEM((2 * rim, width), jnp.bfloat16),
            pltpu.VMEM((width, width), jnp.float32),
            pltpu.VMEM((1, width), jnp.float32),
            pltpu.SemaphoreType.DMA((4,)),
        ],
        input_output_aliases={5: 2},
        compiler_params=params(8),
        name="last_step",
    )(own_half, other_half, edges, first_part, second_part, grad_whole)
    return (activated, grad_features, grad_weight, grad_bias.reshape(width))


def solution(mesh):
    return jax.shard_map(
        on_device,
        mesh=mesh,
        in_specs=(
            P(AXES, None),
            P(AXES, None, None, None),
            P(AXES, None),
            P(AXES),
            P(),
            P(),
            P(AXES, None),
        ),
        out_specs=(P(AXES, None), P(AXES, None), P(), P()),
        check_vma=False,
    )
```

```python
import functools
import math

import jax
import jax.numpy as jnp
from jax import lax
from jax.experimental import pallas as pl
from jax.experimental.pallas import tpu as pltpu
from jax.sharding import PartitionSpec as P

BAND = 2
TAIL = 8
AXES = ("rows", "cols")
MIB = 1024 * 1024


def row_of(adj_ref, block, slots):
    return jnp.concatenate([adj_ref[block, slot] for slot in range(slots)], 1)


def pick(source, places, block_rows):
    return jnp.concatenate(
        [
            source[pl.ds(pl.multiple_of(place * block_rows, block_rows), block_rows)]
            for place in places
        ],
        0,
    )


def write_places(off_ref, cnt_ref, place_ref, blocks, slots):
    for block in range(blocks):
        if block < BAND:
            shift, dump = BAND, 3 * BAND
        elif block < blocks - BAND:
            shift, dump = 0, blocks
        else:
            shift, dump = 2 * BAND - blocks, 3 * BAND
        for slot in range(slots):
            place_ref[block * slots + slot] = jnp.where(
                slot < cnt_ref[block], block + shift + off_ref[slot, block], dump
            )


def places_of(place_ref, block, slots):
    return [place_ref[block * slots + slot] for slot in range(slots)]


def side_by_side(dense, side, first, last):
    return jnp.concatenate([dense[side, place] for place in range(first, last)], 1)


def place_in_mesh():
    return lax.axis_index("rows") * lax.axis_size("cols") + lax.axis_index("cols")


def core_side():
    return lax.axis_index("rows") & 1


def halo_kernel(feat_hbm, first_ref, second_ref, sems):
    rows = feat_hbm.shape[0]
    rim = first_ref.shape[0]
    odd = place_in_mesh() & 1
    last = rows - rim
    starts = ((1 - odd) * last, odd * last)
    copies = [
        pltpu.make_async_copy(
            feat_hbm.at[pl.ds(pl.multiple_of(start, rim), rim)], out_ref, sems.at[i]
        )
        for i, (start, out_ref) in enumerate(zip(starts, (first_ref, second_ref)))
    ]
    for copy in copies:
        copy.start()
    for copy in copies:
        copy.wait()


def activate(preact, cotangent):
    gate = 1.0 / (1.0 + jnp.exp(-preact))
    grad = cotangent.astype(jnp.float32) * gate * (1.0 + preact * (1.0 - gate))
    return (preact * gate).astype(jnp.bfloat16), grad.astype(jnp.bfloat16)


def column_sums(grad):
    rows, width = grad.shape
    return jnp.sum(grad.astype(jnp.float32).reshape(rows // 8, 8, width), axis=0)


def to_upstream(weight, grad):
    return lax.dot_general(
        weight, grad, (((1,), (1,)), ((), ())), preferred_element_type=jnp.float32
    ).astype(jnp.bfloat16)


def weight_terms(agg, grad):
    return lax.dot_general(
        agg, grad, (((0,), (0,)), ((), ())), preferred_element_type=jnp.float32
    )


def inner_kernel(
    off_hbm, cnt_hbm, weight_hbm, bias_hbm, feat_hbm, adj_hbm, cot_hbm,
    act_hbm, place_out, grad_ref, partial_ref, sums_ref, weight_ref, bias_ref, dense, own_ref,
    cot_rim, adj,
    off_ref, cnt_ref, place_ref, feat, adj_rim, cot, act, agg_all, sems,
):
    blocks, slots, block_rows, _ = adj_hbm.shape
    rows, width = feat_hbm.shape
    count = blocks - 2 * BAND
    rim = BAND * block_rows
    inner = count * block_rows
    scalars = [
        pltpu.make_async_copy(off_hbm, off_ref, sems.at[12]),
        pltpu.make_async_copy(cnt_hbm, cnt_ref, sems.at[13]),
    ]
    copies = [
        pltpu.make_async_copy(feat_hbm, feat.at[pl.ds(0, rows)], sems.at[0]),
        pltpu.make_async_copy(adj_hbm.at[pl.ds(BAND, count)], adj, sems.at[1]),
        pltpu.make_async_copy(weight_hbm, weight_ref, sems.at[2]),
        pltpu.make_async_copy(bias_hbm, bias_ref, sems.at[3]),
        pltpu.make_async_copy(cot_hbm.at[pl.ds(rim, inner)], cot, sems.at[4]),
        pltpu.make_async_copy(adj_hbm.at[pl.ds(0, BAND)], adj_rim.at[pl.ds(0, BAND)], sems.at[5]),
        pltpu.make_async_copy(
            adj_hbm.at[pl.ds(blocks - BAND, BAND)], adj_rim.at[pl.ds(BAND, BAND)], sems.at[6]
        ),
        pltpu.make_async_copy(cot_hbm.at[pl.ds(0, rim)], cot_rim.at[pl.ds(0, rim)], sems.at[7]),
        pltpu.make_async_copy(
            cot_hbm.at[pl.ds(rows - rim, rim)], cot_rim.at[pl.ds(rim, rim)], sems.at[8]
        ),
    ]
    for copy in scalars + copies:
        copy.start()
    feat[rows:] = jnp.zeros((block_rows, width), jnp.bfloat16)
    dense[...] = jnp.zeros_like(dense)
    for copy in scalars:
        copy.wait()
    write_places(off_ref, cnt_ref, place_ref, blocks, slots)
    place_copy = pltpu.make_async_copy(place_ref, place_out, sems.at[14])
    place_copy.start()
    for copy in copies[:5]:
        copy.wait()
    weight = weight_ref[...]
    bias = bias_ref[...]
    sums = jnp.zeros((8, width), jnp.float32)
    for step in range(0, count, 2):
        for block in (step, step + 1):
            places = places_of(place_ref, block + BAND, slots)
            agg_all[block * block_rows : (block + 1) * block_rows] = jnp.dot(
                row_of(adj, block, slots), pick(feat, places, block_rows),
                preferred_element_type=jnp.float32,
            ).astype(jnp.bfloat16)
        here = pl.ds(step * block_rows, 2 * block_rows)
        preact = jnp.dot(agg_all[here], weight, preferred_element_type=jnp.float32) + bias
        act[here], grad = activate(preact, cot[here])
        grad_ref[here] = grad
        sums = sums + column_sums(grad)
    act_out = pltpu.make_async_copy(act, act_hbm.at[pl.ds(rim, inner)], sems.at[11])
    act_out.start()
    sums_ref[...] = sums
    partial_ref[...] = weight_terms(agg_all[...], grad_ref[...])
    for copy in copies[5:]:
        copy.wait()
    for side, first in enumerate((0, blocks - BAND)):
        for row in range(BAND):
            here = pl.ds(row * block_rows, block_rows)
            for slot, place in enumerate(places_of(place_ref, first + row, slots)):
                dense[side, place, here] = adj_rim[side * BAND + row, slot]
    own_ref[:rim] = jnp.dot(
        side_by_side(dense, 0, BAND, 3 * BAND), feat[: 2 * rim],
        preferred_element_type=jnp.float32,
    )
    own_ref[rim:] = jnp.dot(
        side_by_side(dense, 1, 0, 2 * BAND), feat[rows - 2 * rim : rows],
        preferred_element_type=jnp.float32,
    )
    act_out.wait()
    place_copy.wait()


def rim_kernel(
    weight_ref, bias_ref, own_ref, first_ref, second_ref, dense, cot_ref, partial_ref, sums_ref,
    act_ref, grad_ref, send_ref, keep_ref,
    halo, agg_all, payload,
):
    rim, width = first_ref.shape
    odd = place_in_mesh() & 1
    halo[pl.ds(pl.multiple_of((1 - odd) * rim, rim), rim)] = first_ref[...]
    halo[pl.ds(pl.multiple_of(odd * rim, rim), rim)] = second_ref[...]
    weight = weight_ref[...]
    bias = bias_ref[...]
    sums = sums_ref[...]
    for side, first in enumerate((0, 2 * BAND)):
        here = pl.ds(side * rim, rim)
        agg = own_ref[here] + jnp.dot(
            side_by_side(dense, side, first, first + BAND), halo[here],
            preferred_element_type=jnp.float32,
        )
        agg = agg.astype(jnp.bfloat16)
        agg_all[here] = agg
        preact = jnp.dot(agg, weight, preferred_element_type=jnp.float32) + bias
        act_ref[here], grad = activate(preact, cot_ref[here])
        grad_ref[here] = grad
        sums = sums + column_sums(grad)
    half = width // 2
    partial = partial_ref[...] + weight_terms(agg_all[...], grad_ref[...])
    payload[0, :half] = partial[:half]
    payload[1, :half] = partial[half:]
    tail = jnp.zeros((TAIL, width), jnp.float32)
    payload[0, half:] = jnp.broadcast_to(jnp.sum(sums, axis=0, keepdims=True), tail.shape)
    payload[1, half:] = tail
    side = core_side()
    keep_ref[...] = payload[side]
    send_ref[...] = payload[1 - side].astype(send_ref.dtype)


def scatter_rows(places, upstream, adj_ref, spread):
    _, slots, block_rows, _ = adj_ref.shape
    for step, targets in enumerate(places):
        terms = jnp.dot(
            upstream[:, step * block_rows : (step + 1) * block_rows],
            row_of(adj_ref, step, slots),
            preferred_element_type=jnp.float32,
        )
        for slot, target in enumerate(targets):
            spread[target] += terms[:, slot * block_rows : (slot + 1) * block_rows]


def rim_back_kernel(
    weight_ref, dense, grad_ref, act_ref, act_in,
    act_hbm, spread, first_ref, second_ref, mark_ref,
    spill, sems,
):
    block_rows = dense.shape[3]
    rim = BAND * block_rows
    rows = act_hbm.shape[0]
    copies = [
        pltpu.make_async_copy(act_ref.at[pl.ds(0, rim)], act_hbm.at[pl.ds(0, rim)], sems.at[0]),
        pltpu.make_async_copy(
            act_ref.at[pl.ds(rim, rim)], act_hbm.at[pl.ds(rows - rim, rim)], sems.at[1]
        ),
    ]
    for copy in copies:
        copy.start()
    weight = weight_ref[...]
    for side, (inside, outside) in enumerate(((BAND, 0), (0, 2 * BAND))):
        terms = jnp.dot(
            to_upstream(weight, grad_ref[side * rim : (side + 1) * rim]),
            side_by_side(dense, side, 0, 3 * BAND),
            preferred_element_type=jnp.float32,
        )
        for block in range(2 * BAND):
            lane = (inside + block) * block_rows
            spread[side * 2 * BAND + block] = terms[:, lane : lane + block_rows]
        for block in range(BAND):
            lane = (outside + block) * block_rows
            here = pl.ds(side * rim + block * block_rows, block_rows)
            spill[here] = terms[:, lane : lane + block_rows].T.astype(jnp.bfloat16)
    odd = place_in_mesh() & 1
    first_ref[...] = spill[pl.ds(pl.multiple_of((1 - odd) * rim, rim), rim)]
    second_ref[...] = spill[pl.ds(pl.multiple_of(odd * rim, rim), rim)]
    mark_ref[...] = jnp.zeros_like(mark_ref)
    for copy in copies:
        copy.wait()


def inner_back_kernel(
    place_in, weight_ref, adj_ref, grad_ref, rim_spread,
    whole_hbm, edge_ref, mark_ref,
    place_ref, spread, out, sems,
):
    fetch = pltpu.make_async_copy(place_in, place_ref, sems.at[1])
    fetch.start()
    count, slots, block_rows, _ = adj_ref.shape
    blocks = place_ref.shape[0] // slots
    rim = BAND * block_rows
    spread[: 2 * BAND] = rim_spread[: 2 * BAND]
    spread[2 * BAND :] = jnp.zeros_like(spread[2 * BAND :])
    spread[blocks - 2 * BAND : blocks] = rim_spread[2 * BAND :]
    upstream = to_upstream(weight_ref[...], grad_ref[...])
    fetch.wait()
    scatter_rows(
        [places_of(place_ref, step + BAND, slots) for step in range(count)],
        upstream, adj_ref, spread,
    )
    for step in range(count):
        here = pl.ds(step * block_rows, block_rows)
        out[here] = spread[BAND + step].T.astype(jnp.bfloat16)
    finish = pltpu.make_async_copy(out, whole_hbm.at[pl.ds(rim, count * block_rows)], sems.at[0])
    finish.start()
    mark_ref[...] = jnp.zeros_like(mark_ref)
    for block in range(BAND):
        edge_ref[block * block_rows : (block + 1) * block_rows] = spread[block].T
        after = BAND + block
        edge_ref[after * block_rows : (after + 1) * block_rows] = spread[blocks - BAND + block].T
    finish.wait()


def add_kernel(parts, *refs):
    values = [ref[...].astype(jnp.float32) for ref in refs[:parts]]
    total = values[0] + values[1]
    if parts == 4:
        total = total + (values[2] + values[3])
    refs[-1][...] = total.astype(refs[-1].dtype)


def last_kernel(
    scale, own_ref, other_ref, edge_ref, first_ref, second_ref, whole_in,
    weight_out, bias_out, whole_hbm,
    out, sums, bias, sems,
):
    half = sums.shape[0] // 2
    rim = first_ref.shape[0]
    rows = whole_hbm.shape[0]
    copies = [
        pltpu.make_async_copy(sums, weight_out, sems.at[0]),
        pltpu.make_async_copy(bias, bias_out, sems.at[1]),
        pltpu.make_async_copy(out.at[pl.ds(0, rim)], whole_hbm.at[pl.ds(0, rim)], sems.at[2]),
        pltpu.make_async_copy(
            out.at[pl.ds(rim, rim)], whole_hbm.at[pl.ds(rows - rim, rim)], sems.at[3]
        ),
    ]
    side = core_side()
    own_rows = pl.ds(pl.multiple_of(side * half, half), half)
    other_rows = pl.ds(pl.multiple_of((1 - side) * half, half), half)
    own = own_ref[...].astype(jnp.float32) * scale
    other = other_ref[...].astype(jnp.float32) * scale
    sums[own_rows] = own[:half]
    sums[other_rows] = other[:half]
    copies[0].start()
    bias[...] = jnp.where(side == 0, own[half : half + 1], other[half : half + 1])
    copies[1].start()
    odd = place_in_mesh() & 1
    for base, spill_ref in (((1 - odd) * rim, first_ref), (odd * rim, second_ref)):
        here = pl.ds(pl.multiple_of(base, rim), rim)
        out[here] = (edge_ref[here] + spill_ref[...].astype(jnp.float32)).astype(jnp.bfloat16)
    for copy in copies[2:]:
        copy.start()
    for copy in copies:
        copy.wait()


def add(values, dtype, after=()):
    size = values[0].size
    return pl.pallas_call(
        functools.partial(add_kernel, len(values)),
        out_shape=jax.ShapeDtypeStruct(values[0].shape, dtype),
        in_specs=[pl.BlockSpec(memory_space=pltpu.VMEM)] * len(values)
        + [pl.BlockSpec(memory_space=pl.ANY)] * len(after),
        compiler_params=pltpu.CompilerParams(vmem_limit_bytes=2 * MIB),
        cost_estimate=pl.CostEstimate(
            flops=size * len(values), bytes_accessed=8 * size, transcendentals=0
        ),
        name="add_halves",
    )(*values, *after)


def swap(value, masks):
    pairs = [(i, i ^ mask) for i, mask in enumerate(masks) if mask]
    return lax.ppermute(value, AXES, pairs)


def with_next(value, count):
    pairs = [(i, (i + 1 if i & 1 else i - 1) % count) for i in range(count)]
    return lax.ppermute(value, AXES, pairs)


def sum_halves(send, keep, count, core_bit, marks):
    others = [bit for bit in range(count.bit_length() - 1) if bit != core_bit]
    groups = [others[i : i + 2] for i in range(0, len(others), 2)]
    groups[0] = groups[0][::-1]
    total = add([keep, swap(send, [1 << core_bit] * count)], jnp.bfloat16, marks.get("core", ()))
    for step in range(len(groups)):
        masks = []
        for group in (groups[step], groups[len(groups) - 1 - step]):
            if len(groups[0]) != len(groups[-1]):
                group = groups[step]
            bits = [1 << bit for bit in group]
            if group[1:]:
                both = bits[0] | bits[1]
                near = group is groups[0]
                bits = [bits[0], both, bits[1]] if near else [*bits, both]
            masks.append(bits)
        parts = [total] + [
            swap(total, [masks[(i >> core_bit) & 1][k] for i in range(count)])
            for k in range(len(masks[0]))
        ]
        last = step == len(groups) - 1
        name = "last" if last else step
        total = add(parts, jnp.bfloat16, marks.get(name, ()))
    return total


def on_device(features, adj_values, adj_offset, adj_count, weight, bias_vector, cotangent):
    blocks, slots = adj_offset.shape
    block_rows = adj_values.shape[2]
    rows, width = features.shape
    rim = BAND * block_rows
    inner = rows - 2 * rim
    cols = lax.axis_size("cols")
    count = lax.axis_size("rows") * cols
    vmem = pl.BlockSpec(memory_space=pltpu.VMEM)
    hbm = pl.BlockSpec(memory_space=pltpu.HBM)
    anywhere = pl.BlockSpec(memory_space=pl.ANY)
    place_scratch = pltpu.SMEM((blocks * slots,), jnp.int32)
    bias_row = bias_vector.reshape(1, width)

    def in_hbm(value):
        return pltpu.with_memory_space_constraint(value, pltpu.HBM)

    def shape(*sizes, dtype=jnp.bfloat16):
        return jax.ShapeDtypeStruct(sizes, dtype)

    def params(mib):
        return pltpu.CompilerParams(vmem_limit_bytes=mib * MIB)

    def cost(share):
        return pl.CostEstimate(
            flops=int(1.2e9 * share), bytes_accessed=int(6e6 * share),
            transcendentals=int(8e5 * share),
        )

    offsets = in_hbm(adj_offset.T)
    counts = in_hbm(adj_count)
    core_bit = cols.bit_length() - 1
    first_rim, second_rim = pl.pallas_call(
        halo_kernel,
        out_shape=(shape(rim, width), shape(rim, width)),
        in_specs=[hbm],
        out_specs=(vmem, vmem),
        scratch_shapes=[pltpu.SemaphoreType.DMA((2,))],
        compiler_params=params(2),
        cost_estimate=cost(0.05),
        name="halo_rows",
    )(in_hbm(features))
    first_halo = swap(first_rim, [1] * count)
    second_halo = with_next(second_rim, count)
    (
        activated, places, grad_inner, partial, sums, weight_near, bias_near, dense, own_part,
        cot_rim, adj_inner,
    ) = pl.pallas_call(
        inner_kernel,
        out_shape=(
            shape(rows, width),
            shape(blocks * slots, dtype=jnp.int32),
            shape(inner, width),
            shape(width, width, dtype=jnp.float32),
            shape(8, width, dtype=jnp.float32),
            shape(width, width),
            shape(1, width, dtype=jnp.float32),
            shape(2, 3 * BAND + 1, rim, block_rows),
            shape(2 * rim, width, dtype=jnp.float32),
            shape(2 * rim, width),
            shape(blocks - 2 * BAND, slots, block_rows, block_rows),
        ),
        in_specs=[hbm] * 7,
        out_specs=(hbm, anywhere) + (vmem,) * 9,
        scratch_shapes=[
            pltpu.SMEM((slots, blocks), jnp.int32),
            pltpu.SMEM((blocks,), jnp.int32),
            place_scratch,
            pltpu.VMEM((rows + block_rows, width), jnp.bfloat16),
            pltpu.VMEM((2 * BAND, slots, block_rows, block_rows), jnp.bfloat16),
            pltpu.VMEM((inner, width), jnp.bfloat16),
            pltpu.VMEM((inner, width), jnp.bfloat16),
            pltpu.VMEM((inner, width), jnp.bfloat16),
            pltpu.SemaphoreType.DMA((15,)),
        ],
        compiler_params=params(20),
        cost_estimate=cost(0.5),
        name="inner_rows",
    )(
        offsets, counts,
        *(in_hbm(x) for x in (weight, bias_row, features, adj_values, cotangent)),
    )
    half_shape = (width // 2 + TAIL, width)
    act_rim, grad_rim, send, keep = pl.pallas_call(
        rim_kernel,
        out_shape=(
            shape(2 * rim, width),
            shape(2 * rim, width),
            shape(*half_shape),
            shape(*half_shape, dtype=jnp.float32),
        ),
        in_specs=[vmem] * 9,
        out_specs=(vmem,) * 4,
        scratch_shapes=[
            pltpu.VMEM((2 * rim, width), jnp.bfloat16),
            pltpu.VMEM((2 * rim, width), jnp.bfloat16),
            pltpu.VMEM((2,) + half_shape, jnp.float32),
        ],
        compiler_params=params(12),
        cost_estimate=cost(0.2),
        name="rim_rows",
    )(
        weight_near, bias_near, own_part, first_halo, second_halo, dense, cot_rim, partial, sums,
    )
    mark = shape(8, 128, dtype=jnp.float32)
    activated, rim_spread, first_spill, second_spill, first_mark = pl.pallas_call(
        rim_back_kernel,
        out_shape=(
            shape(rows, width),
            shape(4 * BAND, width, block_rows, dtype=jnp.float32),
            shape(rim, width),
            shape(rim, width),
            mark,
        ),
        in_specs=[vmem] * 4 + [hbm],
        out_specs=(hbm,) + (vmem,) * 4,
        scratch_shapes=[
            pltpu.VMEM((2 * rim, width), jnp.bfloat16),
            pltpu.SemaphoreType.DMA((2,)),
        ],
        input_output_aliases={4: 0},
        compiler_params=params(12),
        cost_estimate=cost(0.2),
        name="rim_rows_back",
    )(weight_near, dense, grad_rim, act_rim, activated)
    first_part = swap(first_spill, [1] * count)
    second_part = with_next(second_spill, count)
    grad_whole, edges, second_mark = pl.pallas_call(
        inner_back_kernel,
        out_shape=(shape(rows, width), shape(2 * rim, width, dtype=jnp.float32), mark),
        in_specs=[anywhere] + [vmem] * 4,
        out_specs=(hbm, vmem, vmem),
        scratch_shapes=[
            place_scratch,
            pltpu.VMEM((blocks + 1, width, block_rows), jnp.float32),
            pltpu.VMEM((inner, width), jnp.bfloat16),
            pltpu.SemaphoreType.DMA((2,)),
        ],
        compiler_params=params(12),
        cost_estimate=cost(0.3),
        name="inner_rows_back",
    )(places, weight_near, adj_inner, grad_inner, rim_spread)
    marks = {"core": (first_mark,), "last": (second_mark, first_part)}
    own_half = sum_halves(send, keep, count, core_bit, marks)
    other_half = swap(own_half, [1 << core_bit] * count)
    norm_scale = 1.0 / math.sqrt(rows * count)
    grad_weight, grad_bias, grad_features = pl.pallas_call(
        functools.partial(last_kernel, norm_scale),
        out_shape=(
            shape(width, width, dtype=jnp.float32),
            shape(1, width, dtype=jnp.float32),
            shape(rows, width),
        ),
        in_specs=[vmem] * 5 + [hbm],
        out_specs=(hbm, hbm, hbm),
        scratch_shapes=[
            pltpu.VMEM((2 * rim, width), jnp.bfloat16),
            pltpu.VMEM((width, width), jnp.float32),
            pltpu.VMEM((1, width), jnp.float32),
            pltpu.SemaphoreType.DMA((4,)),
        ],
        input_output_aliases={5: 2},
        compiler_params=params(8),
        name="last_step",
    )(own_half, other_half, edges, first_part, second_part, grad_whole)
    return (activated, grad_features, grad_weight, grad_bias.reshape(width))


def solution(mesh):
    return jax.shard_map(
        on_device,
        mesh=mesh,
        in_specs=(
            P(AXES, None),
            P(AXES, None, None, None),
            P(AXES, None),
            P(AXES),
            P(),
            P(),
            P(AXES, None),
        ),
        out_specs=(P(AXES, None), P(AXES, None), P(), P()),
        check_vma=False,
    )
```

```python
import functools
import math

import jax
import jax.numpy as jnp
from jax import lax
from jax.experimental import pallas as pl
from jax.experimental.pallas import tpu as pltpu
from jax.sharding import PartitionSpec as P

BAND = 2
TAIL = 8
AXES = ("rows", "cols")
MIB = 1024 * 1024


def row_of(adj_ref, block, slots):
    return jnp.concatenate([adj_ref[block, slot] for slot in range(slots)], 1)


def pick(source, places, block_rows):
    return jnp.concatenate(
        [
            source[pl.ds(pl.multiple_of(place * block_rows, block_rows), block_rows)]
            for place in places
        ],
        0,
    )


def write_places(off_ref, cnt_ref, place_ref, blocks, slots):
    for block in range(blocks):
        if block < BAND:
            shift, dump = BAND, 3 * BAND
        elif block < blocks - BAND:
            shift, dump = 0, blocks
        else:
            shift, dump = 2 * BAND - blocks, 3 * BAND
        for slot in range(slots):
            place_ref[block * slots + slot] = jnp.where(
                slot < cnt_ref[block], block + shift + off_ref[slot, block], dump
            )


def places_of(place_ref, block, slots):
    return [place_ref[block * slots + slot] for slot in range(slots)]


def side_by_side(dense, side, first, last):
    return jnp.concatenate([dense[side, place] for place in range(first, last)], 1)


def place_in_mesh():
    return lax.axis_index("rows") * lax.axis_size("cols") + lax.axis_index("cols")


def core_side():
    return lax.axis_index("rows") & 1


def halo_kernel(feat_hbm, first_ref, second_ref, sems):
    rows = feat_hbm.shape[0]
    rim = first_ref.shape[0]
    odd = place_in_mesh() & 1
    last = rows - rim
    starts = ((1 - odd) * last, odd * last)
    copies = [
        pltpu.make_async_copy(
            feat_hbm.at[pl.ds(pl.multiple_of(start, rim), rim)], out_ref, sems.at[i]
        )
        for i, (start, out_ref) in enumerate(zip(starts, (first_ref, second_ref)))
    ]
    for copy in copies:
        copy.start()
    for copy in copies:
        copy.wait()


def activate(preact, cotangent):
    gate = 1.0 / (1.0 + jnp.exp(-preact))
    grad = cotangent.astype(jnp.float32) * gate * (1.0 + preact * (1.0 - gate))
    return (preact * gate).astype(jnp.bfloat16), grad.astype(jnp.bfloat16)


def column_sums(grad):
    rows, width = grad.shape
    return jnp.sum(grad.astype(jnp.float32).reshape(rows // 8, 8, width), axis=0)


def to_upstream(weight, grad):
    return lax.dot_general(
        weight, grad, (((1,), (1,)), ((), ())), preferred_element_type=jnp.float32
    ).astype(jnp.bfloat16)


def weight_terms(agg, grad):
    return lax.dot_general(
        agg, grad, (((0,), (0,)), ((), ())), preferred_element_type=jnp.float32
    )


def inner_kernel(
    off_hbm, cnt_hbm, weight_hbm, bias_hbm, feat_hbm, adj_hbm, cot_hbm,
    act_hbm, place_out, grad_ref, partial_ref, sums_ref, weight_ref, bias_ref, dense, own_ref,
    cot_rim, adj,
    off_ref, cnt_ref, place_ref, feat, adj_rim, cot, act, agg_all, sems,
):
    blocks, slots, block_rows, _ = adj_hbm.shape
    rows, width = feat_hbm.shape
    count = blocks - 2 * BAND
    rim = BAND * block_rows
    inner = count * block_rows
    scalars = [
        pltpu.make_async_copy(off_hbm, off_ref, sems.at[12]),
        pltpu.make_async_copy(cnt_hbm, cnt_ref, sems.at[13]),
    ]
    copies = [
        pltpu.make_async_copy(feat_hbm, feat.at[pl.ds(0, rows)], sems.at[0]),
        pltpu.make_async_copy(adj_hbm.at[pl.ds(BAND, count)], adj, sems.at[1]),
        pltpu.make_async_copy(weight_hbm, weight_ref, sems.at[2]),
        pltpu.make_async_copy(bias_hbm, bias_ref, sems.at[3]),
        pltpu.make_async_copy(cot_hbm.at[pl.ds(rim, inner)], cot, sems.at[4]),
        pltpu.make_async_copy(adj_hbm.at[pl.ds(0, BAND)], adj_rim.at[pl.ds(0, BAND)], sems.at[5]),
        pltpu.make_async_copy(
            adj_hbm.at[pl.ds(blocks - BAND, BAND)], adj_rim.at[pl.ds(BAND, BAND)], sems.at[6]
        ),
        pltpu.make_async_copy(cot_hbm.at[pl.ds(0, rim)], cot_rim.at[pl.ds(0, rim)], sems.at[7]),
        pltpu.make_async_copy(
            cot_hbm.at[pl.ds(rows - rim, rim)], cot_rim.at[pl.ds(rim, rim)], sems.at[8]
        ),
    ]
    for copy in scalars + copies:
        copy.start()
    feat[rows:] = jnp.zeros((block_rows, width), jnp.bfloat16)
    dense[...] = jnp.zeros_like(dense)
    for copy in scalars:
        copy.wait()
    write_places(off_ref, cnt_ref, place_ref, blocks, slots)
    place_copy = pltpu.make_async_copy(place_ref, place_out, sems.at[14])
    place_copy.start()
    for copy in copies[:5]:
        copy.wait()
    weight = weight_ref[...]
    bias = bias_ref[...]
    sums = jnp.zeros((8, width), jnp.float32)
    for step in range(0, count, 2):
        for block in (step, step + 1):
            places = places_of(place_ref, block + BAND, slots)
            agg_all[block * block_rows : (block + 1) * block_rows] = jnp.dot(
                row_of(adj, block, slots), pick(feat, places, block_rows),
                preferred_element_type=jnp.float32,
            ).astype(jnp.bfloat16)
        here = pl.ds(step * block_rows, 2 * block_rows)
        preact = jnp.dot(agg_all[here], weight, preferred_element_type=jnp.float32) + bias
        act[here], grad = activate(preact, cot[here])
        grad_ref[here] = grad
        sums = sums + column_sums(grad)
    act_out = pltpu.make_async_copy(act, act_hbm.at[pl.ds(rim, inner)], sems.at[11])
    act_out.start()
    sums_ref[...] = sums
    partial_ref[...] = weight_terms(agg_all[...], grad_ref[...])
    for copy in copies[5:]:
        copy.wait()
    for side, first in enumerate((0, blocks - BAND)):
        for row in range(BAND):
            here = pl.ds(row * block_rows, block_rows)
            for slot, place in enumerate(places_of(place_ref, first + row, slots)):
                dense[side, place, here] = adj_rim[side * BAND + row, slot]
    own_ref[:rim] = jnp.dot(
        side_by_side(dense, 0, BAND, 3 * BAND), feat[: 2 * rim],
        preferred_element_type=jnp.float32,
    )
    own_ref[rim:] = jnp.dot(
        side_by_side(dense, 1, 0, 2 * BAND), feat[rows - 2 * rim : rows],
        preferred_element_type=jnp.float32,
    )
    act_out.wait()
    place_copy.wait()


def rim_kernel(
    weight_ref, bias_ref, own_ref, first_ref, second_ref, dense, cot_ref, partial_ref, sums_ref,
    act_ref, grad_ref, send_ref, keep_ref,
    halo, agg_all, payload,
):
    rim, width = first_ref.shape
    odd = place_in_mesh() & 1
    halo[pl.ds(pl.multiple_of((1 - odd) * rim, rim), rim)] = first_ref[...]
    halo[pl.ds(pl.multiple_of(odd * rim, rim), rim)] = second_ref[...]
    weight = weight_ref[...]
    bias = bias_ref[...]
    sums = sums_ref[...]
    for side, first in enumerate((0, 2 * BAND)):
        here = pl.ds(side * rim, rim)
        agg = own_ref[here] + jnp.dot(
            side_by_side(dense, side, first, first + BAND), halo[here],
            preferred_element_type=jnp.float32,
        )
        agg = agg.astype(jnp.bfloat16)
        agg_all[here] = agg
        preact = jnp.dot(agg, weight, preferred_element_type=jnp.float32) + bias
        act_ref[here], grad = activate(preact, cot_ref[here])
        grad_ref[here] = grad
        sums = sums + column_sums(grad)
    half = width // 2
    partial = partial_ref[...] + weight_terms(agg_all[...], grad_ref[...])
    payload[0, :half] = partial[:half]
    payload[1, :half] = partial[half:]
    tail = jnp.zeros((TAIL, width), jnp.float32)
    payload[0, half:] = jnp.broadcast_to(jnp.sum(sums, axis=0, keepdims=True), tail.shape)
    payload[1, half:] = tail
    side = core_side()
    keep_ref[...] = payload[side]
    send_ref[...] = payload[1 - side].astype(send_ref.dtype)


def scatter_rows(places, upstream, adj_ref, spread):
    _, slots, block_rows, _ = adj_ref.shape
    for step, targets in enumerate(places):
        terms = jnp.dot(
            upstream[:, step * block_rows : (step + 1) * block_rows],
            row_of(adj_ref, step, slots),
            preferred_element_type=jnp.float32,
        )
        for slot, target in enumerate(targets):
            spread[target] += terms[:, slot * block_rows : (slot + 1) * block_rows]


def rim_back_kernel(
    weight_ref, dense, grad_ref, act_ref, act_in,
    act_hbm, spread, first_ref, second_ref, mark_ref,
    spill, sems,
):
    block_rows = dense.shape[3]
    rim = BAND * block_rows
    rows = act_hbm.shape[0]
    copies = [
        pltpu.make_async_copy(act_ref.at[pl.ds(0, rim)], act_hbm.at[pl.ds(0, rim)], sems.at[0]),
        pltpu.make_async_copy(
            act_ref.at[pl.ds(rim, rim)], act_hbm.at[pl.ds(rows - rim, rim)], sems.at[1]
        ),
    ]
    for copy in copies:
        copy.start()
    weight = weight_ref[...]
    for side, (inside, outside) in enumerate(((BAND, 0), (0, 2 * BAND))):
        terms = jnp.dot(
            to_upstream(weight, grad_ref[side * rim : (side + 1) * rim]),
            side_by_side(dense, side, 0, 3 * BAND),
            preferred_element_type=jnp.float32,
        )
        for block in range(2 * BAND):
            lane = (inside + block) * block_rows
            spread[side * 2 * BAND + block] = terms[:, lane : lane + block_rows]
        for block in range(BAND):
            lane = (outside + block) * block_rows
            here = pl.ds(side * rim + block * block_rows, block_rows)
            spill[here] = terms[:, lane : lane + block_rows].T.astype(jnp.bfloat16)
    odd = place_in_mesh() & 1
    first_ref[...] = spill[pl.ds(pl.multiple_of((1 - odd) * rim, rim), rim)]
    second_ref[...] = spill[pl.ds(pl.multiple_of(odd * rim, rim), rim)]
    mark_ref[...] = jnp.zeros_like(mark_ref)
    for copy in copies:
        copy.wait()


def inner_back_kernel(
    place_in, weight_ref, adj_ref, grad_ref, rim_spread,
    whole_hbm, edge_ref, mark_ref,
    place_ref, spread, out, sems,
):
    fetch = pltpu.make_async_copy(place_in, place_ref, sems.at[1])
    fetch.start()
    count, slots, block_rows, _ = adj_ref.shape
    blocks = place_ref.shape[0] // slots
    rim = BAND * block_rows
    spread[: 2 * BAND] = rim_spread[: 2 * BAND]
    spread[2 * BAND :] = jnp.zeros_like(spread[2 * BAND :])
    spread[blocks - 2 * BAND : blocks] = rim_spread[2 * BAND :]
    upstream = to_upstream(weight_ref[...], grad_ref[...])
    fetch.wait()
    scatter_rows(
        [places_of(place_ref, step + BAND, slots) for step in range(count)],
        upstream, adj_ref, spread,
    )
    for step in range(count):
        here = pl.ds(step * block_rows, block_rows)
        out[here] = spread[BAND + step].T.astype(jnp.bfloat16)
    finish = pltpu.make_async_copy(out, whole_hbm.at[pl.ds(rim, count * block_rows)], sems.at[0])
    finish.start()
    mark_ref[...] = jnp.zeros_like(mark_ref)
    for block in range(BAND):
        edge_ref[block * block_rows : (block + 1) * block_rows] = spread[block].T
        after = BAND + block
        edge_ref[after * block_rows : (after + 1) * block_rows] = spread[blocks - BAND + block].T
    finish.wait()


def add_kernel(parts, *refs):
    values = [ref[...].astype(jnp.float32) for ref in refs[:parts]]
    total = values[0] + values[1]
    if parts == 4:
        total = total + (values[2] + values[3])
    refs[-1][...] = total.astype(refs[-1].dtype)


def last_kernel(
    scale, own_ref, other_ref, edge_ref, first_ref, second_ref, whole_in,
    weight_out, bias_out, whole_hbm,
    out, sums, bias, sems,
):
    half = sums.shape[0] // 2
    rim = first_ref.shape[0]
    rows = whole_hbm.shape[0]
    copies = [
        pltpu.make_async_copy(sums, weight_out, sems.at[0]),
        pltpu.make_async_copy(bias, bias_out, sems.at[1]),
        pltpu.make_async_copy(out.at[pl.ds(0, rim)], whole_hbm.at[pl.ds(0, rim)], sems.at[2]),
        pltpu.make_async_copy(
            out.at[pl.ds(rim, rim)], whole_hbm.at[pl.ds(rows - rim, rim)], sems.at[3]
        ),
    ]
    side = core_side()
    own_rows = pl.ds(pl.multiple_of(side * half, half), half)
    other_rows = pl.ds(pl.multiple_of((1 - side) * half, half), half)
    own = own_ref[...].astype(jnp.float32) * scale
    other = other_ref[...].astype(jnp.float32) * scale
    sums[own_rows] = own[:half]
    sums[other_rows] = other[:half]
    copies[0].start()
    bias[...] = jnp.where(side == 0, own[half : half + 1], other[half : half + 1])
    copies[1].start()
    odd = place_in_mesh() & 1
    for base, spill_ref in (((1 - odd) * rim, first_ref), (odd * rim, second_ref)):
        here = pl.ds(pl.multiple_of(base, rim), rim)
        out[here] = (edge_ref[here] + spill_ref[...].astype(jnp.float32)).astype(jnp.bfloat16)
    for copy in copies[2:]:
        copy.start()
    for copy in copies:
        copy.wait()


def add(values, dtype, after=()):
    size = values[0].size
    return pl.pallas_call(
        functools.partial(add_kernel, len(values)),
        out_shape=jax.ShapeDtypeStruct(values[0].shape, dtype),
        in_specs=[pl.BlockSpec(memory_space=pltpu.VMEM)] * len(values)
        + [pl.BlockSpec(memory_space=pl.ANY)] * len(after),
        compiler_params=pltpu.CompilerParams(vmem_limit_bytes=2 * MIB),
        cost_estimate=pl.CostEstimate(
            flops=size * len(values), bytes_accessed=8 * size, transcendentals=0
        ),
        name="add_halves",
    )(*values, *after)


def swap(value, masks):
    pairs = [(i, i ^ mask) for i, mask in enumerate(masks) if mask]
    return lax.ppermute(value, AXES, pairs)


def with_next(value, count, closed):
    pairs = [(i, (i + 1 if i & 1 else i - 1) % count) for i in range(count)]
    return lax.ppermute(value, AXES, pairs if closed else pairs[1:-1])


def sum_halves(send, keep, count, core_bit, marks):
    others = [bit for bit in range(count.bit_length() - 1) if bit != core_bit]
    groups = [others[i : i + 2] for i in range(0, len(others), 2)]
    groups[0] = groups[0][::-1]
    total = add([keep, swap(send, [1 << core_bit] * count)], jnp.bfloat16, marks.get("core", ()))
    for step in range(len(groups)):
        masks = []
        for group in (groups[step], groups[len(groups) - 1 - step]):
            if len(groups[0]) != len(groups[-1]):
                group = groups[step]
            bits = [1 << bit for bit in group]
            if group[1:]:
                both = bits[0] | bits[1]
                near = group is groups[0]
                bits = [bits[0], both, bits[1]] if near else [*bits, both]
            masks.append(bits)
        parts = [total] + [
            swap(total, [masks[(i >> core_bit) & 1][k] for i in range(count)])
            for k in range(len(masks[0]))
        ]
        last = step == len(groups) - 1
        name = "last" if last else step
        total = add(parts, jnp.bfloat16, marks.get(name, ()))
    return total


def on_device(features, adj_values, adj_offset, adj_count, weight, bias_vector, cotangent):
    blocks, slots = adj_offset.shape
    block_rows = adj_values.shape[2]
    rows, width = features.shape
    rim = BAND * block_rows
    inner = rows - 2 * rim
    cols = lax.axis_size("cols")
    count = lax.axis_size("rows") * cols
    vmem = pl.BlockSpec(memory_space=pltpu.VMEM)
    hbm = pl.BlockSpec(memory_space=pltpu.HBM)
    anywhere = pl.BlockSpec(memory_space=pl.ANY)
    place_scratch = pltpu.SMEM((blocks * slots,), jnp.int32)
    bias_row = bias_vector.reshape(1, width)

    def in_hbm(value):
        return pltpu.with_memory_space_constraint(value, pltpu.HBM)

    def shape(*sizes, dtype=jnp.bfloat16):
        return jax.ShapeDtypeStruct(sizes, dtype)

    def params(mib):
        return pltpu.CompilerParams(vmem_limit_bytes=mib * MIB)

    def cost(share):
        return pl.CostEstimate(
            flops=int(1.2e9 * share), bytes_accessed=int(6e6 * share),
            transcendentals=int(8e5 * share),
        )

    offsets = in_hbm(adj_offset.T)
    counts = in_hbm(adj_count)
    core_bit = cols.bit_length() - 1
    first_rim, second_rim = pl.pallas_call(
        halo_kernel,
        out_shape=(shape(rim, width), shape(rim, width)),
        in_specs=[hbm],
        out_specs=(vmem, vmem),
        scratch_shapes=[pltpu.SemaphoreType.DMA((2,))],
        compiler_params=params(2),
        cost_estimate=cost(0.05),
        name="halo_rows",
    )(in_hbm(features))
    first_halo = swap(first_rim, [1] * count)
    second_halo = with_next(second_rim, count, True)
    (
        activated, places, grad_inner, partial, sums, weight_near, bias_near, dense, own_part,
        cot_rim, adj_inner,
    ) = pl.pallas_call(
        inner_kernel,
        out_shape=(
            shape(rows, width),
            shape(blocks * slots, dtype=jnp.int32),
            shape(inner, width),
            shape(width, width, dtype=jnp.float32),
            shape(8, width, dtype=jnp.float32),
            shape(width, width),
            shape(1, width, dtype=jnp.float32),
            shape(2, 3 * BAND + 1, rim, block_rows),
            shape(2 * rim, width, dtype=jnp.float32),
            shape(2 * rim, width),
            shape(blocks - 2 * BAND, slots, block_rows, block_rows),
        ),
        in_specs=[hbm] * 7,
        out_specs=(hbm, anywhere) + (vmem,) * 9,
        scratch_shapes=[
            pltpu.SMEM((slots, blocks), jnp.int32),
            pltpu.SMEM((blocks,), jnp.int32),
            place_scratch,
            pltpu.VMEM((rows + block_rows, width), jnp.bfloat16),
            pltpu.VMEM((2 * BAND, slots, block_rows, block_rows), jnp.bfloat16),
            pltpu.VMEM((inner, width), jnp.bfloat16),
            pltpu.VMEM((inner, width), jnp.bfloat16),
            pltpu.VMEM((inner, width), jnp.bfloat16),
            pltpu.SemaphoreType.DMA((15,)),
        ],
        compiler_params=params(20),
        cost_estimate=cost(0.5),
        name="inner_rows",
    )(
        offsets, counts,
        *(in_hbm(x) for x in (weight, bias_row, features, adj_values, cotangent)),
    )
    half_shape = (width // 2 + TAIL, width)
    act_rim, grad_rim, send, keep = pl.pallas_call(
        rim_kernel,
        out_shape=(
            shape(2 * rim, width),
            shape(2 * rim, width),
            shape(*half_shape),
            shape(*half_shape, dtype=jnp.float32),
        ),
        in_specs=[vmem] * 9,
        out_specs=(vmem,) * 4,
        scratch_shapes=[
            pltpu.VMEM((2 * rim, width), jnp.bfloat16),
            pltpu.VMEM((2 * rim, width), jnp.bfloat16),
            pltpu.VMEM((2,) + half_shape, jnp.float32),
        ],
        compiler_params=params(12),
        cost_estimate=cost(0.2),
        name="rim_rows",
    )(
        weight_near, bias_near, own_part, first_halo, second_halo, dense, cot_rim, partial, sums,
    )
    mark = shape(8, 128, dtype=jnp.float32)
    activated, rim_spread, first_spill, second_spill, first_mark = pl.pallas_call(
        rim_back_kernel,
        out_shape=(
            shape(rows, width),
            shape(4 * BAND, width, block_rows, dtype=jnp.float32),
            shape(rim, width),
            shape(rim, width),
            mark,
        ),
        in_specs=[vmem] * 4 + [hbm],
        out_specs=(hbm,) + (vmem,) * 4,
        scratch_shapes=[
            pltpu.VMEM((2 * rim, width), jnp.bfloat16),
            pltpu.SemaphoreType.DMA((2,)),
        ],
        input_output_aliases={4: 0},
        compiler_params=params(12),
        cost_estimate=cost(0.2),
        name="rim_rows_back",
    )(weight_near, dense, grad_rim, act_rim, activated)
    first_part = swap(first_spill, [1] * count)
    second_part = with_next(second_spill, count, False)
    grad_whole, edges, second_mark = pl.pallas_call(
        inner_back_kernel,
        out_shape=(shape(rows, width), shape(2 * rim, width, dtype=jnp.float32), mark),
        in_specs=[anywhere] + [vmem] * 4,
        out_specs=(hbm, vmem, vmem),
        scratch_shapes=[
            place_scratch,
            pltpu.VMEM((blocks + 1, width, block_rows), jnp.float32),
            pltpu.VMEM((inner, width), jnp.bfloat16),
            pltpu.SemaphoreType.DMA((2,)),
        ],
        compiler_params=params(12),
        cost_estimate=cost(0.3),
        name="inner_rows_back",
    )(places, weight_near, adj_inner, grad_inner, rim_spread)
    marks = {"core": (first_mark,), "last": (second_mark, second_part)}
    own_half = sum_halves(send, keep, count, core_bit, marks)
    other_half = swap(own_half, [1 << core_bit] * count)
    norm_scale = 1.0 / math.sqrt(rows * count)
    grad_weight, grad_bias, grad_features = pl.pallas_call(
        functools.partial(last_kernel, norm_scale),
        out_shape=(
            shape(width, width, dtype=jnp.float32),
            shape(1, width, dtype=jnp.float32),
            shape(rows, width),
        ),
        in_specs=[vmem] * 5 + [hbm],
        out_specs=(hbm, hbm, hbm),
        scratch_shapes=[
            pltpu.VMEM((2 * rim, width), jnp.bfloat16),
            pltpu.VMEM((width, width), jnp.float32),
            pltpu.VMEM((1, width), jnp.float32),
            pltpu.SemaphoreType.DMA((4,)),
        ],
        input_output_aliases={5: 2},
        compiler_params=params(8),
        name="last_step",
    )(own_half, other_half, edges, first_part, second_part, grad_whole)
    return (activated, grad_features, grad_weight, grad_bias.reshape(width))


def solution(mesh):
    return jax.shard_map(
        on_device,
        mesh=mesh,
        in_specs=(
            P(AXES, None),
            P(AXES, None, None, None),
            P(AXES, None),
            P(AXES),
            P(),
            P(),
            P(AXES, None),
        ),
        out_specs=(P(AXES, None), P(AXES, None), P(), P()),
        check_vma=False,
    )
```

```python
import functools
import math

import jax
import jax.numpy as jnp
from jax import lax
from jax.experimental import pallas as pl
from jax.experimental.pallas import tpu as pltpu
from jax.sharding import PartitionSpec as P

BAND = 2
TAIL = 8
AXES = ("rows", "cols")
MIB = 1024 * 1024


def row_of(adj_ref, block, slots):
    return jnp.concatenate([adj_ref[block, slot] for slot in range(slots)], 1)


def pick(source, places, block_rows):
    return jnp.concatenate(
        [
            source[pl.ds(pl.multiple_of(place * block_rows, block_rows), block_rows)]
            for place in places
        ],
        0,
    )


def write_places(off_ref, cnt_ref, place_ref, blocks, slots):
    for block in range(blocks):
        if block < BAND:
            shift, dump = BAND, 3 * BAND
        elif block < blocks - BAND:
            shift, dump = 0, blocks
        else:
            shift, dump = 2 * BAND - blocks, 3 * BAND
        for slot in range(slots):
            place_ref[block * slots + slot] = jnp.where(
                slot < cnt_ref[block], block + shift + off_ref[slot, block], dump
            )


def places_of(place_ref, block, slots):
    return [place_ref[block * slots + slot] for slot in range(slots)]


def side_by_side(dense, side, first, last):
    return jnp.concatenate([dense[side, place] for place in range(first, last)], 1)


def place_in_mesh():
    return lax.axis_index("rows") * lax.axis_size("cols") + lax.axis_index("cols")


def core_side():
    return lax.axis_index("rows") & 1


def halo_kernel(feat_hbm, first_ref, second_ref, sems):
    rows = feat_hbm.shape[0]
    rim = first_ref.shape[0]
    odd = place_in_mesh() & 1
    last = rows - rim
    starts = ((1 - odd) * last, odd * last)
    copies = [
        pltpu.make_async_copy(
            feat_hbm.at[pl.ds(pl.multiple_of(start, rim), rim)], out_ref, sems.at[i]
        )
        for i, (start, out_ref) in enumerate(zip(starts, (first_ref, second_ref)))
    ]
    for copy in copies:
        copy.start()
    for copy in copies:
        copy.wait()


def activate(preact, cotangent):
    gate = 1.0 / (1.0 + jnp.exp(-preact))
    grad = cotangent.astype(jnp.float32) * gate * (1.0 + preact * (1.0 - gate))
    return (preact * gate).astype(jnp.bfloat16), grad.astype(jnp.bfloat16)


def column_sums(grad):
    rows, width = grad.shape
    return jnp.sum(grad.astype(jnp.float32).reshape(rows // 8, 8, width), axis=0)


def to_upstream(weight, grad):
    return lax.dot_general(
        weight, grad, (((1,), (1,)), ((), ())), preferred_element_type=jnp.float32
    ).astype(jnp.bfloat16)


def weight_terms(agg, grad):
    return lax.dot_general(
        agg, grad, (((0,), (0,)), ((), ())), preferred_element_type=jnp.float32
    )


def inner_kernel(
    off_hbm, cnt_hbm, weight_hbm, bias_hbm, feat_hbm, adj_hbm, cot_hbm,
    act_hbm, place_out, grad_ref, partial_ref, sums_ref, weight_ref, bias_ref, dense, own_ref,
    cot_rim, adj,
    off_ref, cnt_ref, place_ref, feat, adj_rim, cot, act, agg_all, sems,
):
    blocks, slots, block_rows, _ = adj_hbm.shape
    rows, width = feat_hbm.shape
    count = blocks - 2 * BAND
    rim = BAND * block_rows
    inner = count * block_rows
    scalars = [
        pltpu.make_async_copy(off_hbm, off_ref, sems.at[12]),
        pltpu.make_async_copy(cnt_hbm, cnt_ref, sems.at[13]),
    ]
    copies = [
        pltpu.make_async_copy(feat_hbm, feat.at[pl.ds(0, rows)], sems.at[0]),
        pltpu.make_async_copy(adj_hbm.at[pl.ds(BAND, count)], adj, sems.at[1]),
        pltpu.make_async_copy(weight_hbm, weight_ref, sems.at[2]),
        pltpu.make_async_copy(bias_hbm, bias_ref, sems.at[3]),
        pltpu.make_async_copy(cot_hbm.at[pl.ds(rim, inner)], cot, sems.at[4]),
        pltpu.make_async_copy(adj_hbm.at[pl.ds(0, BAND)], adj_rim.at[pl.ds(0, BAND)], sems.at[5]),
        pltpu.make_async_copy(
            adj_hbm.at[pl.ds(blocks - BAND, BAND)], adj_rim.at[pl.ds(BAND, BAND)], sems.at[6]
        ),
        pltpu.make_async_copy(cot_hbm.at[pl.ds(0, rim)], cot_rim.at[pl.ds(0, rim)], sems.at[7]),
        pltpu.make_async_copy(
            cot_hbm.at[pl.ds(rows - rim, rim)], cot_rim.at[pl.ds(rim, rim)], sems.at[8]
        ),
    ]
    for copy in scalars + copies:
        copy.start()
    feat[rows:] = jnp.zeros((block_rows, width), jnp.bfloat16)
    dense[...] = jnp.zeros_like(dense)
    for copy in scalars:
        copy.wait()
    write_places(off_ref, cnt_ref, place_ref, blocks, slots)
    place_copy = pltpu.make_async_copy(place_ref, place_out, sems.at[14])
    place_copy.start()
    for copy in copies[:5]:
        copy.wait()
    weight = weight_ref[...]
    bias = bias_ref[...]
    sums = jnp.zeros((8, width), jnp.float32)
    for step in range(0, count, 2):
        for block in (step, step + 1):
            places = places_of(place_ref, block + BAND, slots)
            agg_all[block * block_rows : (block + 1) * block_rows] = jnp.dot(
                row_of(adj, block, slots), pick(feat, places, block_rows),
                preferred_element_type=jnp.float32,
            ).astype(jnp.bfloat16)
        here = pl.ds(step * block_rows, 2 * block_rows)
        preact = jnp.dot(agg_all[here], weight, preferred_element_type=jnp.float32) + bias
        act[here], grad = activate(preact, cot[here])
        grad_ref[here] = grad
        sums = sums + column_sums(grad)
    act_out = pltpu.make_async_copy(act, act_hbm.at[pl.ds(rim, inner)], sems.at[11])
    act_out.start()
    sums_ref[...] = sums
    partial_ref[...] = weight_terms(agg_all[...], grad_ref[...])
    for copy in copies[5:]:
        copy.wait()
    for side, first in enumerate((0, blocks - BAND)):
        for row in range(BAND):
            here = pl.ds(row * block_rows, block_rows)
            for slot, place in enumerate(places_of(place_ref, first + row, slots)):
                dense[side, place, here] = adj_rim[side * BAND + row, slot]
    own_ref[:rim] = jnp.dot(
        side_by_side(dense, 0, BAND, 3 * BAND), feat[: 2 * rim],
        preferred_element_type=jnp.float32,
    )
    own_ref[rim:] = jnp.dot(
        side_by_side(dense, 1, 0, 2 * BAND), feat[rows - 2 * rim : rows],
        preferred_element_type=jnp.float32,
    )
    act_out.wait()
    place_copy.wait()


def rim_kernel(
    weight_ref, bias_ref, own_ref, first_ref, second_ref, dense, cot_ref, partial_ref, sums_ref,
    act_ref, grad_ref, send_ref, keep_ref,
    halo, agg_all,
):
    rim, width = first_ref.shape
    odd = place_in_mesh() & 1
    halo[pl.ds(pl.multiple_of((1 - odd) * rim, rim), rim)] = first_ref[...]
    halo[pl.ds(pl.multiple_of(odd * rim, rim), rim)] = second_ref[...]
    weight = weight_ref[...]
    bias = bias_ref[...]
    sums = sums_ref[...]
    for side, first in enumerate((0, 2 * BAND)):
        here = pl.ds(side * rim, rim)
        agg = own_ref[here] + jnp.dot(
            side_by_side(dense, side, first, first + BAND), halo[here],
            preferred_element_type=jnp.float32,
        )
        agg = agg.astype(jnp.bfloat16)
        agg_all[here] = agg
        preact = jnp.dot(agg, weight, preferred_element_type=jnp.float32) + bias
        act_ref[here], grad = activate(preact, cot_ref[here])
        grad_ref[here] = grad
        sums = sums + column_sums(grad)
    half = width // 2
    partial = partial_ref[...] + weight_terms(agg_all[...], grad_ref[...])
    bias_tail = jnp.broadcast_to(jnp.sum(sums, axis=0, keepdims=True), (TAIL, width))
    upper = jnp.concatenate([partial[:half], bias_tail], 0)
    lower = jnp.concatenate([partial[half:], jnp.zeros_like(bias_tail)], 0)
    first = core_side() == 0
    keep_ref[...] = jnp.where(first, upper, lower)
    send_ref[...] = jnp.where(first, lower, upper).astype(send_ref.dtype)


def scatter_rows(places, upstream, adj_ref, spread):
    _, slots, block_rows, _ = adj_ref.shape
    for step, targets in enumerate(places):
        terms = jnp.dot(
            upstream[:, step * block_rows : (step + 1) * block_rows],
            row_of(adj_ref, step, slots),
            preferred_element_type=jnp.float32,
        )
        for slot, target in enumerate(targets):
            spread[target] += terms[:, slot * block_rows : (slot + 1) * block_rows]


def rim_back_kernel(
    weight_ref, dense, grad_ref, act_ref, act_in,
    act_hbm, spread, first_ref, second_ref, mark_ref,
    spill, sems,
):
    block_rows = dense.shape[3]
    rim = BAND * block_rows
    rows = act_hbm.shape[0]
    copies = [
        pltpu.make_async_copy(act_ref.at[pl.ds(0, rim)], act_hbm.at[pl.ds(0, rim)], sems.at[0]),
        pltpu.make_async_copy(
            act_ref.at[pl.ds(rim, rim)], act_hbm.at[pl.ds(rows - rim, rim)], sems.at[1]
        ),
    ]
    for copy in copies:
        copy.start()
    weight = weight_ref[...]
    for side, (inside, outside) in enumerate(((BAND, 0), (0, 2 * BAND))):
        terms = jnp.dot(
            to_upstream(weight, grad_ref[side * rim : (side + 1) * rim]),
            side_by_side(dense, side, 0, 3 * BAND),
            preferred_element_type=jnp.float32,
        )
        for block in range(2 * BAND):
            lane = (inside + block) * block_rows
            spread[side * 2 * BAND + block] = terms[:, lane : lane + block_rows]
        for block in range(BAND):
            lane = (outside + block) * block_rows
            here = pl.ds(side * rim + block * block_rows, block_rows)
            spill[here] = terms[:, lane : lane + block_rows].T.astype(jnp.bfloat16)
    odd = place_in_mesh() & 1
    first_ref[...] = spill[pl.ds(pl.multiple_of((1 - odd) * rim, rim), rim)]
    second_ref[...] = spill[pl.ds(pl.multiple_of(odd * rim, rim), rim)]
    mark_ref[...] = jnp.zeros_like(mark_ref)
    for copy in copies:
        copy.wait()


def inner_back_kernel(
    place_in, weight_ref, adj_ref, grad_ref, rim_spread,
    whole_hbm, edge_ref, mark_ref,
    place_ref, spread, out, sems,
):
    fetch = pltpu.make_async_copy(place_in, place_ref, sems.at[1])
    fetch.start()
    count, slots, block_rows, _ = adj_ref.shape
    blocks = place_ref.shape[0] // slots
    rim = BAND * block_rows
    spread[: 2 * BAND] = rim_spread[: 2 * BAND]
    spread[2 * BAND :] = jnp.zeros_like(spread[2 * BAND :])
    spread[blocks - 2 * BAND : blocks] = rim_spread[2 * BAND :]
    upstream = to_upstream(weight_ref[...], grad_ref[...])
    fetch.wait()
    scatter_rows(
        [places_of(place_ref, step + BAND, slots) for step in range(count)],
        upstream, adj_ref, spread,
    )
    for step in range(count):
        here = pl.ds(step * block_rows, block_rows)
        out[here] = spread[BAND + step].T.astype(jnp.bfloat16)
    finish = pltpu.make_async_copy(out, whole_hbm.at[pl.ds(rim, count * block_rows)], sems.at[0])
    finish.start()
    mark_ref[...] = jnp.zeros_like(mark_ref)
    for block in range(BAND):
        edge_ref[block * block_rows : (block + 1) * block_rows] = spread[block].T
        after = BAND + block
        edge_ref[after * block_rows : (after + 1) * block_rows] = spread[blocks - BAND + block].T
    finish.wait()


def add_kernel(parts, *refs):
    values = [ref[...].astype(jnp.float32) for ref in refs[:parts]]
    total = values[0] + values[1]
    if parts == 4:
        total = total + (values[2] + values[3])
    refs[-1][...] = total.astype(refs[-1].dtype)


def last_kernel(
    scale, own_ref, other_ref, edge_ref, first_ref, second_ref, whole_in,
    weight_out, bias_out, whole_hbm,
    out, sums, bias, sems,
):
    half = sums.shape[0] // 2
    rim = first_ref.shape[0]
    rows = whole_hbm.shape[0]
    copies = [
        pltpu.make_async_copy(sums, weight_out, sems.at[0]),
        pltpu.make_async_copy(bias, bias_out, sems.at[1]),
        pltpu.make_async_copy(out.at[pl.ds(0, rim)], whole_hbm.at[pl.ds(0, rim)], sems.at[2]),
        pltpu.make_async_copy(
            out.at[pl.ds(rim, rim)], whole_hbm.at[pl.ds(rows - rim, rim)], sems.at[3]
        ),
    ]
    side = core_side()
    own_rows = pl.ds(pl.multiple_of(side * half, half), half)
    other_rows = pl.ds(pl.multiple_of((1 - side) * half, half), half)
    own = own_ref[...].astype(jnp.float32) * scale
    other = other_ref[...].astype(jnp.float32) * scale
    sums[own_rows] = own[:half]
    sums[other_rows] = other[:half]
    copies[0].start()
    bias[...] = jnp.where(side == 0, own[half : half + 1], other[half : half + 1])
    copies[1].start()
    odd = place_in_mesh() & 1
    for base, spill_ref in (((1 - odd) * rim, first_ref), (odd * rim, second_ref)):
        here = pl.ds(pl.multiple_of(base, rim), rim)
        out[here] = (edge_ref[here] + spill_ref[...].astype(jnp.float32)).astype(jnp.bfloat16)
    for copy in copies[2:]:
        copy.start()
    for copy in copies:
        copy.wait()


def add(values, dtype, after=()):
    size = values[0].size
    return pl.pallas_call(
        functools.partial(add_kernel, len(values)),
        out_shape=jax.ShapeDtypeStruct(values[0].shape, dtype),
        in_specs=[pl.BlockSpec(memory_space=pltpu.VMEM)] * len(values)
        + [pl.BlockSpec(memory_space=pl.ANY)] * len(after),
        compiler_params=pltpu.CompilerParams(vmem_limit_bytes=2 * MIB),
        cost_estimate=pl.CostEstimate(
            flops=size * len(values), bytes_accessed=8 * size, transcendentals=0
        ),
        name="add_halves",
    )(*values, *after)


def swap(value, masks):
    pairs = [(i, i ^ mask) for i, mask in enumerate(masks) if mask]
    return lax.ppermute(value, AXES, pairs)


def with_next(value, count, closed):
    pairs = [(i, (i + 1 if i & 1 else i - 1) % count) for i in range(count)]
    return lax.ppermute(value, AXES, pairs if closed else pairs[1:-1])


def sum_halves(send, keep, count, core_bit, marks):
    others = [bit for bit in range(count.bit_length() - 1) if bit != core_bit]
    groups = [others[i : i + 2] for i in range(0, len(others), 2)]
    groups[0] = groups[0][::-1]
    total = add([keep, swap(send, [1 << core_bit] * count)], jnp.bfloat16, marks.get("core", ()))
    for step in range(len(groups)):
        masks = []
        for group in (groups[len(groups) - 1 - step], groups[step]):
            if len(groups[0]) != len(groups[-1]):
                group = groups[step]
            bits = [1 << bit for bit in group]
            if group[1:]:
                both = bits[0] | bits[1]
                near = group is groups[0]
                bits = [bits[0], both, bits[1]] if near else [*bits, both]
            masks.append(bits)
        parts = [total] + [
            swap(total, [masks[(i >> core_bit) & 1][k] for i in range(count)])
            for k in range(len(masks[0]))
        ]
        last = step == len(groups) - 1
        name = "last" if last else step
        total = add(parts, jnp.bfloat16, marks.get(name, ()))
    return total


def on_device(features, adj_values, adj_offset, adj_count, weight, bias_vector, cotangent):
    blocks, slots = adj_offset.shape
    block_rows = adj_values.shape[2]
    rows, width = features.shape
    rim = BAND * block_rows
    inner = rows - 2 * rim
    cols = lax.axis_size("cols")
    count = lax.axis_size("rows") * cols
    vmem = pl.BlockSpec(memory_space=pltpu.VMEM)
    hbm = pl.BlockSpec(memory_space=pltpu.HBM)
    anywhere = pl.BlockSpec(memory_space=pl.ANY)
    place_scratch = pltpu.SMEM((blocks * slots,), jnp.int32)
    bias_row = bias_vector.reshape(1, width)

    def in_hbm(value):
        return pltpu.with_memory_space_constraint(value, pltpu.HBM)

    def shape(*sizes, dtype=jnp.bfloat16):
        return jax.ShapeDtypeStruct(sizes, dtype)

    def params(mib):
        return pltpu.CompilerParams(vmem_limit_bytes=mib * MIB)

    def cost(share):
        return pl.CostEstimate(
            flops=int(1.2e9 * share), bytes_accessed=int(6e6 * share),
            transcendentals=int(8e5 * share),
        )

    offsets = in_hbm(adj_offset.T)
    counts = in_hbm(adj_count)
    core_bit = cols.bit_length() - 1
    first_rim, second_rim = pl.pallas_call(
        halo_kernel,
        out_shape=(shape(rim, width), shape(rim, width)),
        in_specs=[hbm],
        out_specs=(vmem, vmem),
        scratch_shapes=[pltpu.SemaphoreType.DMA((2,))],
        compiler_params=params(2),
        cost_estimate=cost(0.05),
        name="halo_rows",
    )(in_hbm(features))
    first_halo = swap(first_rim, [1] * count)
    second_halo = with_next(second_rim, count, True)
    (
        activated, places, grad_inner, partial, sums, weight_near, bias_near, dense, own_part,
        cot_rim, adj_inner,
    ) = pl.pallas_call(
        inner_kernel,
        out_shape=(
            shape(rows, width),
            shape(blocks * slots, dtype=jnp.int32),
            shape(inner, width),
            shape(width, width, dtype=jnp.float32),
            shape(8, width, dtype=jnp.float32),
            shape(width, width),
            shape(1, width, dtype=jnp.float32),
            shape(2, 3 * BAND + 1, rim, block_rows),
            shape(2 * rim, width, dtype=jnp.float32),
            shape(2 * rim, width),
            shape(blocks - 2 * BAND, slots, block_rows, block_rows),
        ),
        in_specs=[hbm] * 7,
        out_specs=(hbm, anywhere) + (vmem,) * 9,
        scratch_shapes=[
            pltpu.SMEM((slots, blocks), jnp.int32),
            pltpu.SMEM((blocks,), jnp.int32),
            place_scratch,
            pltpu.VMEM((rows + block_rows, width), jnp.bfloat16),
            pltpu.VMEM((2 * BAND, slots, block_rows, block_rows), jnp.bfloat16),
            pltpu.VMEM((inner, width), jnp.bfloat16),
            pltpu.VMEM((inner, width), jnp.bfloat16),
            pltpu.VMEM((inner, width), jnp.bfloat16),
            pltpu.SemaphoreType.DMA((15,)),
        ],
        compiler_params=params(20),
        cost_estimate=cost(0.5),
        name="inner_rows",
    )(
        offsets, counts,
        *(in_hbm(x) for x in (weight, bias_row, features, adj_values, cotangent)),
    )
    half_shape = (width // 2 + TAIL, width)
    act_rim, grad_rim, send, keep = pl.pallas_call(
        rim_kernel,
        out_shape=(
            shape(2 * rim, width),
            shape(2 * rim, width),
            shape(*half_shape),
            shape(*half_shape, dtype=jnp.float32),
        ),
        in_specs=[vmem] * 9,
        out_specs=(vmem,) * 4,
        scratch_shapes=[
            pltpu.VMEM((2 * rim, width), jnp.bfloat16),
            pltpu.VMEM((2 * rim, width), jnp.bfloat16),
        ],
        compiler_params=params(12),
        cost_estimate=cost(0.2),
        name="rim_rows",
    )(
        weight_near, bias_near, own_part, first_halo, second_halo, dense, cot_rim, partial, sums,
    )
    mark = shape(8, 128, dtype=jnp.float32)
    activated, rim_spread, first_spill, second_spill, first_mark = pl.pallas_call(
        rim_back_kernel,
        out_shape=(
            shape(rows, width),
            shape(4 * BAND, width, block_rows, dtype=jnp.float32),
            shape(rim, width),
            shape(rim, width),
            mark,
        ),
        in_specs=[vmem] * 4 + [hbm],
        out_specs=(hbm,) + (vmem,) * 4,
        scratch_shapes=[
            pltpu.VMEM((2 * rim, width), jnp.bfloat16),
            pltpu.SemaphoreType.DMA((2,)),
        ],
        input_output_aliases={4: 0},
        compiler_params=params(12),
        cost_estimate=cost(0.2),
        name="rim_rows_back",
    )(weight_near, dense, grad_rim, act_rim, activated)
    first_part = swap(first_spill, [1] * count)
    second_part = with_next(second_spill, count, False)
    grad_whole, edges, second_mark = pl.pallas_call(
        inner_back_kernel,
        out_shape=(shape(rows, width), shape(2 * rim, width, dtype=jnp.float32), mark),
        in_specs=[anywhere] + [vmem] * 4,
        out_specs=(hbm, vmem, vmem),
        scratch_shapes=[
            place_scratch,
            pltpu.VMEM((blocks + 1, width, block_rows), jnp.float32),
            pltpu.VMEM((inner, width), jnp.bfloat16),
            pltpu.SemaphoreType.DMA((2,)),
        ],
        compiler_params=params(12),
        cost_estimate=cost(0.3),
        name="inner_rows_back",
    )(places, weight_near, adj_inner, grad_inner, rim_spread)
    marks = {"core": (first_mark,), "last": (second_mark, second_part)}
    own_half = sum_halves(send, keep, count, core_bit, marks)
    other_half = swap(own_half, [1 << core_bit] * count)
    norm_scale = 1.0 / math.sqrt(rows * count)
    grad_weight, grad_bias, grad_features = pl.pallas_call(
        functools.partial(last_kernel, norm_scale),
        out_shape=(
            shape(width, width, dtype=jnp.float32),
            shape(1, width, dtype=jnp.float32),
            shape(rows, width),
        ),
        in_specs=[vmem] * 5 + [hbm],
        out_specs=(hbm, hbm, hbm),
        scratch_shapes=[
            pltpu.VMEM((2 * rim, width), jnp.bfloat16),
            pltpu.VMEM((width, width), jnp.float32),
            pltpu.VMEM((1, width), jnp.float32),
            pltpu.SemaphoreType.DMA((4,)),
        ],
        input_output_aliases={5: 2},
        compiler_params=params(8),
        name="last_step",
    )(own_half, other_half, edges, first_part, second_part, grad_whole)
    return (activated, grad_features, grad_weight, grad_bias.reshape(width))


def solution(mesh):
    return jax.shard_map(
        on_device,
        mesh=mesh,
        in_specs=(
            P(AXES, None),
            P(AXES, None, None, None),
            P(AXES, None),
            P(AXES),
            P(),
            P(),
            P(AXES, None),
        ),
        out_specs=(P(AXES, None), P(AXES, None), P(), P()),
        check_vma=False,
    )
```

```python
import functools
import math

import jax
import jax.numpy as jnp
from jax import lax
from jax.experimental import pallas as pl
from jax.experimental.pallas import tpu as pltpu
from jax.sharding import PartitionSpec as P

BAND = 2
TAIL = 8
AXES = ("rows", "cols")
MIB = 1024 * 1024


def row_of(adj_ref, block, slots):
    return jnp.concatenate([adj_ref[block, slot] for slot in range(slots)], 1)


def pick(source, places, block_rows):
    return jnp.concatenate(
        [
            source[pl.ds(pl.multiple_of(place * block_rows, block_rows), block_rows)]
            for place in places
        ],
        0,
    )


def write_places(off_ref, cnt_ref, place_ref, blocks, slots):
    for block in range(blocks):
        if block < BAND:
            shift, dump = BAND, 3 * BAND
        elif block < blocks - BAND:
            shift, dump = 0, blocks
        else:
            shift, dump = 2 * BAND - blocks, 3 * BAND
        for slot in range(slots):
            place_ref[block * slots + slot] = jnp.where(
                slot < cnt_ref[block], block + shift + off_ref[slot, block], dump
            )


def places_of(place_ref, block, slots):
    return [place_ref[block * slots + slot] for slot in range(slots)]


def side_by_side(dense, side, first, last):
    return jnp.concatenate([dense[side, place] for place in range(first, last)], 1)


def place_in_mesh():
    return lax.axis_index("rows") * lax.axis_size("cols") + lax.axis_index("cols")


def core_side():
    return lax.axis_index("rows") & 1


def halo_kernel(feat_hbm, first_ref, second_ref, sems):
    rows = feat_hbm.shape[0]
    rim = first_ref.shape[0]
    odd = place_in_mesh() & 1
    last = rows - rim
    starts = ((1 - odd) * last, odd * last)
    copies = [
        pltpu.make_async_copy(
            feat_hbm.at[pl.ds(pl.multiple_of(start, rim), rim)], out_ref, sems.at[i]
        )
        for i, (start, out_ref) in enumerate(zip(starts, (first_ref, second_ref)))
    ]
    for copy in copies:
        copy.start()
    for copy in copies:
        copy.wait()


def activate(preact, cotangent):
    gate = 1.0 / (1.0 + jnp.exp(-preact))
    grad = cotangent.astype(jnp.float32) * gate * (1.0 + preact * (1.0 - gate))
    return (preact * gate).astype(jnp.bfloat16), grad.astype(jnp.bfloat16)


def column_sums(grad):
    rows, width = grad.shape
    return jnp.sum(grad.astype(jnp.float32).reshape(rows // 8, 8, width), axis=0)


def to_upstream(weight, grad):
    return lax.dot_general(
        weight, grad, (((1,), (1,)), ((), ())), preferred_element_type=jnp.float32
    ).astype(jnp.bfloat16)


def weight_terms(agg, grad):
    return lax.dot_general(
        agg, grad, (((0,), (0,)), ((), ())), preferred_element_type=jnp.float32
    )


def inner_kernel(
    off_hbm, cnt_hbm, weight_hbm, bias_hbm, feat_hbm, adj_hbm, cot_hbm,
    act_hbm, place_out, grad_ref, partial_ref, sums_ref, weight_ref, bias_ref, dense, own_ref,
    cot_rim, adj,
    off_ref, cnt_ref, place_ref, feat, adj_rim, cot, act, agg_all, sems,
):
    blocks, slots, block_rows, _ = adj_hbm.shape
    rows, width = feat_hbm.shape
    count = blocks - 2 * BAND
    rim = BAND * block_rows
    inner = count * block_rows
    scalars = [
        pltpu.make_async_copy(off_hbm, off_ref, sems.at[12]),
        pltpu.make_async_copy(cnt_hbm, cnt_ref, sems.at[13]),
    ]
    copies = [
        pltpu.make_async_copy(feat_hbm, feat.at[pl.ds(0, rows)], sems.at[0]),
        pltpu.make_async_copy(adj_hbm.at[pl.ds(BAND, count)], adj, sems.at[1]),
        pltpu.make_async_copy(weight_hbm, weight_ref, sems.at[2]),
        pltpu.make_async_copy(bias_hbm, bias_ref, sems.at[3]),
        pltpu.make_async_copy(cot_hbm.at[pl.ds(rim, inner)], cot, sems.at[4]),
        pltpu.make_async_copy(adj_hbm.at[pl.ds(0, BAND)], adj_rim.at[pl.ds(0, BAND)], sems.at[5]),
        pltpu.make_async_copy(
            adj_hbm.at[pl.ds(blocks - BAND, BAND)], adj_rim.at[pl.ds(BAND, BAND)], sems.at[6]
        ),
        pltpu.make_async_copy(cot_hbm.at[pl.ds(0, rim)], cot_rim.at[pl.ds(0, rim)], sems.at[7]),
        pltpu.make_async_copy(
            cot_hbm.at[pl.ds(rows - rim, rim)], cot_rim.at[pl.ds(rim, rim)], sems.at[8]
        ),
    ]
    for copy in scalars + copies:
        copy.start()
    feat[rows:] = jnp.zeros((block_rows, width), jnp.bfloat16)
    dense[...] = jnp.zeros_like(dense)
    for copy in scalars:
        copy.wait()
    write_places(off_ref, cnt_ref, place_ref, blocks, slots)
    place_copy = pltpu.make_async_copy(place_ref, place_out, sems.at[14])
    place_copy.start()
    for copy in copies[:5]:
        copy.wait()
    weight = weight_ref[...]
    bias = bias_ref[...]
    sums = jnp.zeros((8, width), jnp.float32)
    for step in range(0, count, 2):
        for block in (step, step + 1):
            places = places_of(place_ref, block + BAND, slots)
            agg_all[block * block_rows : (block + 1) * block_rows] = jnp.dot(
                row_of(adj, block, slots), pick(feat, places, block_rows),
                preferred_element_type=jnp.float32,
            ).astype(jnp.bfloat16)
        here = pl.ds(step * block_rows, 2 * block_rows)
        preact = jnp.dot(agg_all[here], weight, preferred_element_type=jnp.float32) + bias
        act[here], grad = activate(preact, cot[here])
        grad_ref[here] = grad
        sums = sums + column_sums(grad)
    act_out = pltpu.make_async_copy(act, act_hbm.at[pl.ds(rim, inner)], sems.at[11])
    act_out.start()
    sums_ref[...] = sums
    partial_ref[...] = weight_terms(agg_all[...], grad_ref[...])
    for copy in copies[5:]:
        copy.wait()
    for side, first in enumerate((0, blocks - BAND)):
        for row in range(BAND):
            here = pl.ds(row * block_rows, block_rows)
            for slot, place in enumerate(places_of(place_ref, first + row, slots)):
                dense[side, place, here] = adj_rim[side * BAND + row, slot]
    own_ref[:rim] = jnp.dot(
        side_by_side(dense, 0, BAND, 3 * BAND), feat[: 2 * rim],
        preferred_element_type=jnp.float32,
    )
    own_ref[rim:] = jnp.dot(
        side_by_side(dense, 1, 0, 2 * BAND), feat[rows - 2 * rim : rows],
        preferred_element_type=jnp.float32,
    )
    act_out.wait()
    place_copy.wait()


def rim_kernel(
    weight_ref, bias_ref, own_ref, first_ref, second_ref, dense, cot_ref, partial_ref, sums_ref,
    act_ref, grad_ref, send_ref, keep_ref,
    halo, agg_all,
):
    rim, width = first_ref.shape
    odd = place_in_mesh() & 1
    halo[pl.ds(pl.multiple_of((1 - odd) * rim, rim), rim)] = first_ref[...]
    halo[pl.ds(pl.multiple_of(odd * rim, rim), rim)] = second_ref[...]
    weight = weight_ref[...]
    bias = bias_ref[...]
    sums = sums_ref[...]
    for side, first in enumerate((0, 2 * BAND)):
        here = pl.ds(side * rim, rim)
        agg = own_ref[here] + jnp.dot(
            side_by_side(dense, side, first, first + BAND), halo[here],
            preferred_element_type=jnp.float32,
        )
        agg = agg.astype(jnp.bfloat16)
        agg_all[here] = agg
        preact = jnp.dot(agg, weight, preferred_element_type=jnp.float32) + bias
        act_ref[here], grad = activate(preact, cot_ref[here])
        grad_ref[here] = grad
        sums = sums + column_sums(grad)
    half = width // 2
    partial = partial_ref[...] + weight_terms(agg_all[...], grad_ref[...])
    bias_tail = jnp.broadcast_to(jnp.sum(sums, axis=0, keepdims=True), (TAIL, width))
    upper = jnp.concatenate([partial[:half], bias_tail], 0)
    lower = jnp.concatenate([partial[half:], jnp.zeros_like(bias_tail)], 0)
    first = core_side() == 0
    keep_ref[...] = jnp.where(first, upper, lower)
    send_ref[...] = jnp.where(first, lower, upper).astype(send_ref.dtype)


def scatter_rows(places, upstream, adj_ref, spread):
    _, slots, block_rows, _ = adj_ref.shape
    for step, targets in enumerate(places):
        terms = jnp.dot(
            upstream[:, step * block_rows : (step + 1) * block_rows],
            row_of(adj_ref, step, slots),
            preferred_element_type=jnp.float32,
        )
        for slot, target in enumerate(targets):
            spread[target] += terms[:, slot * block_rows : (slot + 1) * block_rows]


def rim_back_kernel(
    weight_ref, dense, grad_ref, act_ref, act_in,
    act_hbm, spread, first_ref, second_ref, mark_ref,
    spill, sems,
):
    block_rows = dense.shape[3]
    rim = BAND * block_rows
    rows = act_hbm.shape[0]
    copies = [
        pltpu.make_async_copy(act_ref.at[pl.ds(0, rim)], act_hbm.at[pl.ds(0, rim)], sems.at[0]),
        pltpu.make_async_copy(
            act_ref.at[pl.ds(rim, rim)], act_hbm.at[pl.ds(rows - rim, rim)], sems.at[1]
        ),
    ]
    for copy in copies:
        copy.start()
    weight = weight_ref[...]
    for side, (inside, outside) in enumerate(((BAND, 0), (0, 2 * BAND))):
        terms = jnp.dot(
            to_upstream(weight, grad_ref[side * rim : (side + 1) * rim]),
            side_by_side(dense, side, 0, 3 * BAND),
            preferred_element_type=jnp.float32,
        )
        for block in range(2 * BAND):
            lane = (inside + block) * block_rows
            spread[side * 2 * BAND + block] = terms[:, lane : lane + block_rows]
        for block in range(BAND):
            lane = (outside + block) * block_rows
            here = pl.ds(side * rim + block * block_rows, block_rows)
            spill[here] = terms[:, lane : lane + block_rows].T.astype(jnp.bfloat16)
    odd = place_in_mesh() & 1
    first_ref[...] = spill[pl.ds(pl.multiple_of((1 - odd) * rim, rim), rim)]
    second_ref[...] = spill[pl.ds(pl.multiple_of(odd * rim, rim), rim)]
    mark_ref[...] = jnp.zeros_like(mark_ref)
    for copy in copies:
        copy.wait()


def inner_back_kernel(
    place_in, weight_ref, adj_ref, grad_ref, rim_spread,
    whole_hbm, edge_ref, mark_ref,
    place_ref, spread, out, sems,
):
    fetch = pltpu.make_async_copy(place_in, place_ref, sems.at[1])
    fetch.start()
    count, slots, block_rows, _ = adj_ref.shape
    blocks = place_ref.shape[0] // slots
    rim = BAND * block_rows
    spread[: 2 * BAND] = rim_spread[: 2 * BAND]
    spread[2 * BAND :] = jnp.zeros_like(spread[2 * BAND :])
    spread[blocks - 2 * BAND : blocks] = rim_spread[2 * BAND :]
    upstream = to_upstream(weight_ref[...], grad_ref[...])
    fetch.wait()
    scatter_rows(
        [places_of(place_ref, step + BAND, slots) for step in range(count)],
        upstream, adj_ref, spread,
    )
    for step in range(count):
        here = pl.ds(step * block_rows, block_rows)
        out[here] = spread[BAND + step].T.astype(jnp.bfloat16)
    finish = pltpu.make_async_copy(out, whole_hbm.at[pl.ds(rim, count * block_rows)], sems.at[0])
    finish.start()
    mark_ref[...] = jnp.zeros_like(mark_ref)
    for block in range(BAND):
        edge_ref[block * block_rows : (block + 1) * block_rows] = spread[block].T
        after = BAND + block
        edge_ref[after * block_rows : (after + 1) * block_rows] = spread[blocks - BAND + block].T
    finish.wait()


def add_kernel(parts, *refs):
    values = [ref[...].astype(jnp.float32) for ref in refs[:parts]]
    total = values[0] + values[1]
    if parts == 4:
        total = total + (values[2] + values[3])
    refs[-1][...] = total.astype(refs[-1].dtype)


def last_kernel(
    scale, own_ref, other_ref, edge_ref, first_ref, second_ref, whole_in,
    weight_out, bias_out, whole_hbm,
    out, sums, bias, sems,
):
    half = sums.shape[0] // 2
    rim = first_ref.shape[0]
    rows = whole_hbm.shape[0]
    copies = [
        pltpu.make_async_copy(sums, weight_out, sems.at[0]),
        pltpu.make_async_copy(bias, bias_out, sems.at[1]),
        pltpu.make_async_copy(out.at[pl.ds(0, rim)], whole_hbm.at[pl.ds(0, rim)], sems.at[2]),
        pltpu.make_async_copy(
            out.at[pl.ds(rim, rim)], whole_hbm.at[pl.ds(rows - rim, rim)], sems.at[3]
        ),
    ]
    side = core_side()
    own_rows = pl.ds(pl.multiple_of(side * half, half), half)
    other_rows = pl.ds(pl.multiple_of((1 - side) * half, half), half)
    own = own_ref[...].astype(jnp.float32) * scale
    other = other_ref[...].astype(jnp.float32) * scale
    sums[own_rows] = own[:half]
    sums[other_rows] = other[:half]
    copies[0].start()
    bias[...] = jnp.where(side == 0, own[half : half + 1], other[half : half + 1])
    copies[1].start()
    odd = place_in_mesh() & 1
    for base, spill_ref in (((1 - odd) * rim, first_ref), (odd * rim, second_ref)):
        here = pl.ds(pl.multiple_of(base, rim), rim)
        out[here] = (edge_ref[here] + spill_ref[...].astype(jnp.float32)).astype(jnp.bfloat16)
    for copy in copies[2:]:
        copy.start()
    for copy in copies:
        copy.wait()


def add(values, dtype, after=()):
    size = values[0].size
    return pl.pallas_call(
        functools.partial(add_kernel, len(values)),
        out_shape=jax.ShapeDtypeStruct(values[0].shape, dtype),
        in_specs=[pl.BlockSpec(memory_space=pltpu.VMEM)] * len(values)
        + [pl.BlockSpec(memory_space=pl.ANY)] * len(after),
        compiler_params=pltpu.CompilerParams(vmem_limit_bytes=2 * MIB),
        cost_estimate=pl.CostEstimate(
            flops=size * len(values), bytes_accessed=8 * size, transcendentals=0
        ),
        name="add_halves",
    )(*values, *after)


def swap(value, masks):
    pairs = [(i, i ^ mask) for i, mask in enumerate(masks) if mask]
    return lax.ppermute(value, AXES, pairs)


def with_next(value, count, closed):
    pairs = [(i, (i + 1 if i & 1 else i - 1) % count) for i in range(count)]
    return lax.ppermute(value, AXES, pairs if closed else pairs[1:-1])


def sum_halves(send, keep, count, core_bit, marks):
    others = [bit for bit in range(count.bit_length() - 1) if bit != core_bit]
    groups = [others[i : i + 2] for i in range(0, len(others), 2)]
    groups[0] = groups[0][::-1]
    total = add([keep, swap(send, [1 << core_bit] * count)], jnp.bfloat16, marks.get("core", ()))
    for step in range(len(groups)):
        masks = []
        for group in (groups[step], groups[len(groups) - 1 - step]):
            if len(groups[0]) != len(groups[-1]):
                group = groups[step]
            bits = [1 << bit for bit in group]
            if group[1:]:
                both = bits[0] | bits[1]
                near = group is groups[0]
                bits = [bits[0], both, bits[1]] if near else [*bits, both]
            masks.append(bits)
        parts = [total] + [
            swap(total, [masks[(i >> core_bit) & 1][k] for i in range(count)])
            for k in range(len(masks[0]))
        ]
        last = step == len(groups) - 1
        name = "last" if last else step
        total = add(parts, jnp.bfloat16, marks.get(name, ()))
    return total


def on_device(features, adj_values, adj_offset, adj_count, weight, bias_vector, cotangent):
    blocks, slots = adj_offset.shape
    block_rows = adj_values.shape[2]
    rows, width = features.shape
    rim = BAND * block_rows
    inner = rows - 2 * rim
    cols = lax.axis_size("cols")
    count = lax.axis_size("rows") * cols
    vmem = pl.BlockSpec(memory_space=pltpu.VMEM)
    hbm = pl.BlockSpec(memory_space=pltpu.HBM)
    anywhere = pl.BlockSpec(memory_space=pl.ANY)
    place_scratch = pltpu.SMEM((blocks * slots,), jnp.int32)
    bias_row = bias_vector.reshape(1, width)

    def in_hbm(value):
        return pltpu.with_memory_space_constraint(value, pltpu.HBM)

    def shape(*sizes, dtype=jnp.bfloat16):
        return jax.ShapeDtypeStruct(sizes, dtype)

    def params(mib):
        return pltpu.CompilerParams(vmem_limit_bytes=mib * MIB)

    def cost(share):
        return pl.CostEstimate(
            flops=int(1.2e9 * share), bytes_accessed=int(6e6 * share),
            transcendentals=int(8e5 * share),
        )

    offsets = in_hbm(adj_offset.T)
    counts = in_hbm(adj_count)
    core_bit = cols.bit_length() - 1
    first_rim, second_rim = pl.pallas_call(
        halo_kernel,
        out_shape=(shape(rim, width), shape(rim, width)),
        in_specs=[hbm],
        out_specs=(vmem, vmem),
        scratch_shapes=[pltpu.SemaphoreType.DMA((2,))],
        compiler_params=params(2),
        cost_estimate=cost(0.05),
        name="halo_rows",
    )(in_hbm(features))
    first_halo = swap(first_rim, [1] * count)
    second_halo = with_next(second_rim, count, True)
    (
        activated, places, grad_inner, partial, sums, weight_near, bias_near, dense, own_part,
        cot_rim, adj_inner,
    ) = pl.pallas_call(
        inner_kernel,
        out_shape=(
            shape(rows, width),
            shape(blocks * slots, dtype=jnp.int32),
            shape(inner, width),
            shape(width, width, dtype=jnp.float32),
            shape(8, width, dtype=jnp.float32),
            shape(width, width),
            shape(1, width, dtype=jnp.float32),
            shape(2, 3 * BAND + 1, rim, block_rows),
            shape(2 * rim, width, dtype=jnp.float32),
            shape(2 * rim, width),
            shape(blocks - 2 * BAND, slots, block_rows, block_rows),
        ),
        in_specs=[hbm] * 7,
        out_specs=(hbm, anywhere) + (vmem,) * 9,
        scratch_shapes=[
            pltpu.SMEM((slots, blocks), jnp.int32),
            pltpu.SMEM((blocks,), jnp.int32),
            place_scratch,
            pltpu.VMEM((rows + block_rows, width), jnp.bfloat16),
            pltpu.VMEM((2 * BAND, slots, block_rows, block_rows), jnp.bfloat16),
            pltpu.VMEM((inner, width), jnp.bfloat16),
            pltpu.VMEM((inner, width), jnp.bfloat16),
            pltpu.VMEM((inner, width), jnp.bfloat16),
            pltpu.SemaphoreType.DMA((15,)),
        ],
        compiler_params=params(20),
        cost_estimate=cost(0.5),
        name="inner_rows",
    )(
        offsets, counts,
        *(in_hbm(x) for x in (weight, bias_row, features, adj_values, cotangent)),
    )
    half_shape = (width // 2 + TAIL, width)
    act_rim, grad_rim, send, keep = pl.pallas_call(
        rim_kernel,
        out_shape=(
            shape(2 * rim, width),
            shape(2 * rim, width),
            shape(*half_shape),
            shape(*half_shape, dtype=jnp.float32),
        ),
        in_specs=[vmem] * 9,
        out_specs=(vmem,) * 4,
        scratch_shapes=[
            pltpu.VMEM((2 * rim, width), jnp.bfloat16),
            pltpu.VMEM((2 * rim, width), jnp.bfloat16),
        ],
        compiler_params=params(12),
        cost_estimate=cost(0.2),
        name="rim_rows",
    )(
        weight_near, bias_near, own_part, first_halo, second_halo, dense, cot_rim, partial, sums,
    )
    mark = shape(8, 128, dtype=jnp.float32)
    activated, rim_spread, first_spill, second_spill, first_mark = pl.pallas_call(
        rim_back_kernel,
        out_shape=(
            shape(rows, width),
            shape(4 * BAND, width, block_rows, dtype=jnp.float32),
            shape(rim, width),
            shape(rim, width),
            mark,
        ),
        in_specs=[vmem] * 4 + [hbm],
        out_specs=(hbm,) + (vmem,) * 4,
        scratch_shapes=[
            pltpu.VMEM((2 * rim, width), jnp.bfloat16),
            pltpu.SemaphoreType.DMA((2,)),
        ],
        input_output_aliases={4: 0},
        compiler_params=params(12),
        cost_estimate=cost(0.2),
        name="rim_rows_back",
    )(weight_near, dense, grad_rim, act_rim, activated)
    first_part = swap(first_spill, [1] * count)
    second_part = with_next(second_spill, count, False)
    grad_whole, edges, second_mark = pl.pallas_call(
        inner_back_kernel,
        out_shape=(shape(rows, width), shape(2 * rim, width, dtype=jnp.float32), mark),
        in_specs=[anywhere] + [vmem] * 4,
        out_specs=(hbm, vmem, vmem),
        scratch_shapes=[
            place_scratch,
            pltpu.VMEM((blocks + 1, width, block_rows), jnp.float32),
            pltpu.VMEM((inner, width), jnp.bfloat16),
            pltpu.SemaphoreType.DMA((2,)),
        ],
        compiler_params=params(12),
        cost_estimate=cost(0.3),
        name="inner_rows_back",
    )(places, weight_near, adj_inner, grad_inner, rim_spread)
    marks = {"core": (first_mark,), "last": (second_mark, second_part)}
    own_half = sum_halves(send, keep, count, core_bit, marks)
    other_half = swap(own_half, [1 << core_bit] * count)
    norm_scale = 1.0 / math.sqrt(rows * count)
    grad_weight, grad_bias, grad_features = pl.pallas_call(
        functools.partial(last_kernel, norm_scale),
        out_shape=(
            shape(width, width, dtype=jnp.float32),
            shape(1, width, dtype=jnp.float32),
            shape(rows, width),
        ),
        in_specs=[vmem] * 5 + [hbm],
        out_specs=(hbm, hbm, hbm),
        scratch_shapes=[
            pltpu.VMEM((2 * rim, width), jnp.bfloat16),
            pltpu.VMEM((width, width), jnp.float32),
            pltpu.VMEM((1, width), jnp.float32),
            pltpu.SemaphoreType.DMA((4,)),
        ],
        input_output_aliases={5: 2},
        compiler_params=params(8),
        name="last_step",
    )(own_half, other_half, edges, first_part, second_part, grad_whole)
    return (activated, grad_features, grad_weight, grad_bias.reshape(width))


def solution(mesh):
    return jax.shard_map(
        on_device,
        mesh=mesh,
        in_specs=(
            P(AXES, None),
            P(AXES, None, None, None),
            P(AXES, None),
            P(AXES),
            P(),
            P(),
            P(AXES, None),
        ),
        out_specs=(P(AXES, None), P(AXES, None), P(), P()),
        check_vma=False,
    )
```

```python
import functools
import math

import jax
import jax.numpy as jnp
from jax import lax
from jax.experimental import pallas as pl
from jax.experimental.pallas import tpu as pltpu
from jax.sharding import PartitionSpec as P

BAND = 2
TAIL = 8
AXES = ("rows", "cols")
MIB = 1024 * 1024


def row_of(adj_ref, block, slots):
    return jnp.concatenate([adj_ref[block, slot] for slot in range(slots)], 1)


def pick(source, places, block_rows):
    return jnp.concatenate(
        [
            source[pl.ds(pl.multiple_of(place * block_rows, block_rows), block_rows)]
            for place in places
        ],
        0,
    )


def write_places(off_ref, cnt_ref, place_ref, blocks, slots):
    for block in range(blocks):
        if block < BAND:
            shift, dump = BAND, 3 * BAND
        elif block < blocks - BAND:
            shift, dump = 0, blocks
        else:
            shift, dump = 2 * BAND - blocks, 3 * BAND
        for slot in range(slots):
            place_ref[block * slots + slot] = jnp.where(
                slot < cnt_ref[block], block + shift + off_ref[slot, block], dump
            )


def places_of(place_ref, block, slots):
    return [place_ref[block * slots + slot] for slot in range(slots)]


def side_by_side(dense, side, first, last):
    return jnp.concatenate([dense[side, place] for place in range(first, last)], 1)


def place_in_mesh():
    return lax.axis_index("rows") * lax.axis_size("cols") + lax.axis_index("cols")


def core_side():
    return lax.axis_index("rows") & 1


def halo_kernel(feat_hbm, first_ref, second_ref, sems):
    rows = feat_hbm.shape[0]
    rim = first_ref.shape[0]
    odd = place_in_mesh() & 1
    last = rows - rim
    starts = ((1 - odd) * last, odd * last)
    copies = [
        pltpu.make_async_copy(
            feat_hbm.at[pl.ds(pl.multiple_of(start, rim), rim)], out_ref, sems.at[i]
        )
        for i, (start, out_ref) in enumerate(zip(starts, (first_ref, second_ref)))
    ]
    for copy in copies:
        copy.start()
    for copy in copies:
        copy.wait()


def activate(preact, cotangent):
    gate = 1.0 / (1.0 + jnp.exp(-preact))
    grad = cotangent.astype(jnp.float32) * gate * (1.0 + preact * (1.0 - gate))
    return (preact * gate).astype(jnp.bfloat16), grad.astype(jnp.bfloat16)


def column_sums(grad):
    rows, width = grad.shape
    return jnp.sum(grad.astype(jnp.float32).reshape(rows // 8, 8, width), axis=0)


def to_upstream(weight, grad):
    return lax.dot_general(
        weight, grad, (((1,), (1,)), ((), ())), preferred_element_type=jnp.float32
    ).astype(jnp.bfloat16)


def weight_terms(agg, grad):
    return lax.dot_general(
        agg, grad, (((0,), (0,)), ((), ())), preferred_element_type=jnp.float32
    )


def inner_kernel(
    off_hbm, cnt_hbm, weight_hbm, bias_hbm, feat_hbm, adj_hbm, cot_hbm,
    act_hbm, place_out, grad_ref, partial_ref, sums_ref, weight_ref, bias_ref, dense, own_ref,
    cot_rim, adj,
    off_ref, cnt_ref, place_ref, feat, adj_rim, cot, act, agg_all, sems,
):
    blocks, slots, block_rows, _ = adj_hbm.shape
    rows, width = feat_hbm.shape
    count = blocks - 2 * BAND
    rim = BAND * block_rows
    inner = count * block_rows
    scalars = [
        pltpu.make_async_copy(off_hbm, off_ref, sems.at[12]),
        pltpu.make_async_copy(cnt_hbm, cnt_ref, sems.at[13]),
    ]
    copies = [
        pltpu.make_async_copy(feat_hbm, feat.at[pl.ds(0, rows)], sems.at[0]),
        pltpu.make_async_copy(adj_hbm.at[pl.ds(BAND, count)], adj, sems.at[1]),
        pltpu.make_async_copy(weight_hbm, weight_ref, sems.at[2]),
        pltpu.make_async_copy(bias_hbm, bias_ref, sems.at[3]),
        pltpu.make_async_copy(cot_hbm.at[pl.ds(rim, inner)], cot, sems.at[4]),
        pltpu.make_async_copy(adj_hbm.at[pl.ds(0, BAND)], adj_rim.at[pl.ds(0, BAND)], sems.at[5]),
        pltpu.make_async_copy(
            adj_hbm.at[pl.ds(blocks - BAND, BAND)], adj_rim.at[pl.ds(BAND, BAND)], sems.at[6]
        ),
        pltpu.make_async_copy(cot_hbm.at[pl.ds(0, rim)], cot_rim.at[pl.ds(0, rim)], sems.at[7]),
        pltpu.make_async_copy(
            cot_hbm.at[pl.ds(rows - rim, rim)], cot_rim.at[pl.ds(rim, rim)], sems.at[8]
        ),
    ]
    for copy in scalars + copies:
        copy.start()
    feat[rows:] = jnp.zeros((block_rows, width), jnp.bfloat16)
    dense[...] = jnp.zeros_like(dense)
    for copy in scalars:
        copy.wait()
    write_places(off_ref, cnt_ref, place_ref, blocks, slots)
    place_copy = pltpu.make_async_copy(place_ref, place_out, sems.at[14])
    place_copy.start()
    for copy in copies[:5]:
        copy.wait()
    weight = weight_ref[...]
    bias = bias_ref[...]
    sums = jnp.zeros((8, width), jnp.float32)
    for step in range(0, count, 2):
        for block in (step, step + 1):
            places = places_of(place_ref, block + BAND, slots)
            agg_all[block * block_rows : (block + 1) * block_rows] = jnp.dot(
                row_of(adj, block, slots), pick(feat, places, block_rows),
                preferred_element_type=jnp.float32,
            ).astype(jnp.bfloat16)
        here = pl.ds(step * block_rows, 2 * block_rows)
        preact = jnp.dot(agg_all[here], weight, preferred_element_type=jnp.float32) + bias
        act[here], grad = activate(preact, cot[here])
        grad_ref[here] = grad
        sums = sums + column_sums(grad)
    act_out = pltpu.make_async_copy(act, act_hbm.at[pl.ds(rim, inner)], sems.at[11])
    act_out.start()
    sums_ref[...] = sums
    partial_ref[...] = weight_terms(agg_all[...], grad_ref[...])
    for copy in copies[5:]:
        copy.wait()
    for side, first in enumerate((0, blocks - BAND)):
        for row in range(BAND):
            here = pl.ds(row * block_rows, block_rows)
            for slot, place in enumerate(places_of(place_ref, first + row, slots)):
                dense[side, place, here] = adj_rim[side * BAND + row, slot]
    own_ref[:rim] = jnp.dot(
        side_by_side(dense, 0, BAND, 3 * BAND), feat[: 2 * rim],
        preferred_element_type=jnp.float32,
    )
    own_ref[rim:] = jnp.dot(
        side_by_side(dense, 1, 0, 2 * BAND), feat[rows - 2 * rim : rows],
        preferred_element_type=jnp.float32,
    )
    act_out.wait()
    place_copy.wait()


def rim_side(order):
    odd = place_in_mesh() & 1
    return odd if order else 1 - odd


def rim_kernel(
    order, weight_ref, bias_ref, own_ref, halo_ref, dense, cot_ref, partial_ref, sums_ref,
    act_ref, grad_ref, *outs,
):
    rim = halo_ref.shape[0]
    side = rim_side(order)
    here = pl.ds(pl.multiple_of(side * rim, rim), rim)
    beyond = side * 2 * BAND
    row = jnp.concatenate([dense[side, beyond + block] for block in range(BAND)], 1)
    agg = own_ref[here] + jnp.dot(row, halo_ref[...], preferred_element_type=jnp.float32)
    agg = agg.astype(jnp.bfloat16)
    preact = jnp.dot(agg, weight_ref[...], preferred_element_type=jnp.float32) + bias_ref[...]
    act_ref[...], grad = activate(preact, cot_ref[here])
    grad_ref[...] = grad
    sums = sums_ref[...] + column_sums(grad)
    partial = partial_ref[...] + weight_terms(agg, grad)
    if order == 0:
        partial_out, sums_out = outs
        partial_out[...] = partial
        sums_out[...] = sums
        return
    send_ref, keep_ref = outs
    half, width = partial.shape[0] // 2, partial.shape[1]
    bias_tail = jnp.broadcast_to(jnp.sum(sums, axis=0, keepdims=True), (TAIL, width))
    upper = jnp.concatenate([partial[:half], bias_tail], 0)
    lower = jnp.concatenate([partial[half:], jnp.zeros_like(bias_tail)], 0)
    first = core_side() == 0
    keep_ref[...] = jnp.where(first, upper, lower)
    send_ref[...] = jnp.where(first, lower, upper).astype(send_ref.dtype)


def scatter_rows(places, upstream, adj_ref, spread):
    _, slots, block_rows, _ = adj_ref.shape
    for step, targets in enumerate(places):
        terms = jnp.dot(
            upstream[:, step * block_rows : (step + 1) * block_rows],
            row_of(adj_ref, step, slots),
            preferred_element_type=jnp.float32,
        )
        for slot, target in enumerate(targets):
            spread[target] += terms[:, slot * block_rows : (slot + 1) * block_rows]


def rim_back_kernel(
    weight_ref, dense, grad_first, grad_second, act_first, act_second, act_in,
    act_hbm, spread, first_ref, second_ref, mark_ref,
    grad_ref, spill, sems,
):
    block_rows = dense.shape[3]
    rim = BAND * block_rows
    rows = act_hbm.shape[0]
    copies = [
        pltpu.make_async_copy(
            act_ref,
            act_hbm.at[pl.ds(pl.multiple_of(rim_side(order) * (rows - rim), rim), rim)],
            sems.at[order],
        )
        for order, act_ref in enumerate((act_first, act_second))
    ]
    for copy in copies:
        copy.start()
    for order, grad in enumerate((grad_first, grad_second)):
        grad_ref[pl.ds(pl.multiple_of(rim_side(order) * rim, rim), rim)] = grad[...]
    weight = weight_ref[...]
    for side, (inside, outside) in enumerate(((BAND, 0), (0, 2 * BAND))):
        terms = jnp.dot(
            to_upstream(weight, grad_ref[side * rim : (side + 1) * rim]),
            side_by_side(dense, side, 0, 3 * BAND),
            preferred_element_type=jnp.float32,
        )
        for block in range(2 * BAND):
            lane = (inside + block) * block_rows
            spread[side * 2 * BAND + block] = terms[:, lane : lane + block_rows]
        for block in range(BAND):
            lane = (outside + block) * block_rows
            here = pl.ds(side * rim + block * block_rows, block_rows)
            spill[here] = terms[:, lane : lane + block_rows].T.astype(jnp.bfloat16)
    odd = place_in_mesh() & 1
    first_ref[...] = spill[pl.ds(pl.multiple_of((1 - odd) * rim, rim), rim)]
    second_ref[...] = spill[pl.ds(pl.multiple_of(odd * rim, rim), rim)]
    mark_ref[...] = jnp.zeros_like(mark_ref)
    for copy in copies:
        copy.wait()


def inner_back_kernel(
    place_in, weight_ref, adj_ref, grad_ref, rim_spread,
    whole_hbm, edge_ref, mark_ref,
    place_ref, spread, out, sems,
):
    fetch = pltpu.make_async_copy(place_in, place_ref, sems.at[1])
    fetch.start()
    count, slots, block_rows, _ = adj_ref.shape
    blocks = place_ref.shape[0] // slots
    rim = BAND * block_rows
    spread[: 2 * BAND] = rim_spread[: 2 * BAND]
    spread[2 * BAND :] = jnp.zeros_like(spread[2 * BAND :])
    spread[blocks - 2 * BAND : blocks] = rim_spread[2 * BAND :]
    upstream = to_upstream(weight_ref[...], grad_ref[...])
    fetch.wait()
    scatter_rows(
        [places_of(place_ref, step + BAND, slots) for step in range(count)],
        upstream, adj_ref, spread,
    )
    for step in range(count):
        here = pl.ds(step * block_rows, block_rows)
        out[here] = spread[BAND + step].T.astype(jnp.bfloat16)
    finish = pltpu.make_async_copy(out, whole_hbm.at[pl.ds(rim, count * block_rows)], sems.at[0])
    finish.start()
    mark_ref[...] = jnp.zeros_like(mark_ref)
    for block in range(BAND):
        edge_ref[block * block_rows : (block + 1) * block_rows] = spread[block].T
        after = BAND + block
        edge_ref[after * block_rows : (after + 1) * block_rows] = spread[blocks - BAND + block].T
    finish.wait()


def add_kernel(parts, *refs):
    values = [ref[...].astype(jnp.float32) for ref in refs[:parts]]
    total = values[0] + values[1]
    if parts == 4:
        total = total + (values[2] + values[3])
    refs[-1][...] = total.astype(refs[-1].dtype)


def last_kernel(
    scale, own_ref, other_ref, edge_ref, first_ref, second_ref, whole_in,
    weight_out, bias_out, whole_hbm,
    out, sums, bias, sems,
):
    half = sums.shape[0] // 2
    rim = first_ref.shape[0]
    rows = whole_hbm.shape[0]
    copies = [
        pltpu.make_async_copy(sums, weight_out, sems.at[0]),
        pltpu.make_async_copy(bias, bias_out, sems.at[1]),
        pltpu.make_async_copy(out.at[pl.ds(0, rim)], whole_hbm.at[pl.ds(0, rim)], sems.at[2]),
        pltpu.make_async_copy(
            out.at[pl.ds(rim, rim)], whole_hbm.at[pl.ds(rows - rim, rim)], sems.at[3]
        ),
    ]
    side = core_side()
    own_rows = pl.ds(pl.multiple_of(side * half, half), half)
    other_rows = pl.ds(pl.multiple_of((1 - side) * half, half), half)
    own = own_ref[...].astype(jnp.float32) * scale
    other = other_ref[...].astype(jnp.float32) * scale
    sums[own_rows] = own[:half]
    sums[other_rows] = other[:half]
    copies[0].start()
    bias[...] = jnp.where(side == 0, own[half : half + 1], other[half : half + 1])
    copies[1].start()
    odd = place_in_mesh() & 1
    for base, spill_ref in (((1 - odd) * rim, first_ref), (odd * rim, second_ref)):
        here = pl.ds(pl.multiple_of(base, rim), rim)
        out[here] = (edge_ref[here] + spill_ref[...].astype(jnp.float32)).astype(jnp.bfloat16)
    for copy in copies[2:]:
        copy.start()
    for copy in copies:
        copy.wait()


def add(values, dtype, after=()):
    size = values[0].size
    return pl.pallas_call(
        functools.partial(add_kernel, len(values)),
        out_shape=jax.ShapeDtypeStruct(values[0].shape, dtype),
        in_specs=[pl.BlockSpec(memory_space=pltpu.VMEM)] * len(values)
        + [pl.BlockSpec(memory_space=pl.ANY)] * len(after),
        compiler_params=pltpu.CompilerParams(vmem_limit_bytes=2 * MIB),
        cost_estimate=pl.CostEstimate(
            flops=size * len(values), bytes_accessed=8 * size, transcendentals=0
        ),
        name="add_halves",
    )(*values, *after)


def swap(value, masks):
    pairs = [(i, i ^ mask) for i, mask in enumerate(masks) if mask]
    return lax.ppermute(value, AXES, pairs)


def with_next(value, count, closed):
    pairs = [(i, (i + 1 if i & 1 else i - 1) % count) for i in range(count)]
    return lax.ppermute(value, AXES, pairs if closed else pairs[1:-1])


def sum_halves(send, keep, count, core_bit, marks):
    others = [bit for bit in range(count.bit_length() - 1) if bit != core_bit]
    groups = [others[i : i + 2] for i in range(0, len(others), 2)]
    groups[0] = groups[0][::-1]
    total = add([keep, swap(send, [1 << core_bit] * count)], jnp.bfloat16, marks.get("core", ()))
    for step in range(len(groups)):
        masks = []
        for group in (groups[step], groups[len(groups) - 1 - step]):
            if len(groups[0]) != len(groups[-1]):
                group = groups[step]
            bits = [1 << bit for bit in group]
            if group[1:]:
                both = bits[0] | bits[1]
                near = group is groups[0]
                bits = [bits[0], both, bits[1]] if near else [*bits, both]
            masks.append(bits)
        parts = [total] + [
            swap(total, [masks[(i >> core_bit) & 1][k] for i in range(count)])
            for k in range(len(masks[0]))
        ]
        last = step == len(groups) - 1
        name = "last" if last else step
        total = add(parts, jnp.bfloat16, marks.get(name, ()))
    return total


def on_device(features, adj_values, adj_offset, adj_count, weight, bias_vector, cotangent):
    blocks, slots = adj_offset.shape
    block_rows = adj_values.shape[2]
    rows, width = features.shape
    rim = BAND * block_rows
    inner = rows - 2 * rim
    cols = lax.axis_size("cols")
    count = lax.axis_size("rows") * cols
    vmem = pl.BlockSpec(memory_space=pltpu.VMEM)
    hbm = pl.BlockSpec(memory_space=pltpu.HBM)
    anywhere = pl.BlockSpec(memory_space=pl.ANY)
    place_scratch = pltpu.SMEM((blocks * slots,), jnp.int32)
    bias_row = bias_vector.reshape(1, width)

    def in_hbm(value):
        return pltpu.with_memory_space_constraint(value, pltpu.HBM)

    def shape(*sizes, dtype=jnp.bfloat16):
        return jax.ShapeDtypeStruct(sizes, dtype)

    def params(mib):
        return pltpu.CompilerParams(vmem_limit_bytes=mib * MIB)

    def cost(share):
        return pl.CostEstimate(
            flops=int(1.2e9 * share), bytes_accessed=int(6e6 * share),
            transcendentals=int(8e5 * share),
        )

    offsets = in_hbm(adj_offset.T)
    counts = in_hbm(adj_count)
    core_bit = cols.bit_length() - 1
    first_rim, second_rim = pl.pallas_call(
        halo_kernel,
        out_shape=(shape(rim, width), shape(rim, width)),
        in_specs=[hbm],
        out_specs=(vmem, vmem),
        scratch_shapes=[pltpu.SemaphoreType.DMA((2,))],
        compiler_params=params(2),
        cost_estimate=cost(0.05),
        name="halo_rows",
    )(in_hbm(features))
    first_halo = swap(first_rim, [1] * count)
    second_halo = with_next(second_rim, count, True)
    (
        activated, places, grad_inner, partial, sums, weight_near, bias_near, dense, own_part,
        cot_rim, adj_inner,
    ) = pl.pallas_call(
        inner_kernel,
        out_shape=(
            shape(rows, width),
            shape(blocks * slots, dtype=jnp.int32),
            shape(inner, width),
            shape(width, width, dtype=jnp.float32),
            shape(8, width, dtype=jnp.float32),
            shape(width, width),
            shape(1, width, dtype=jnp.float32),
            shape(2, 3 * BAND + 1, rim, block_rows),
            shape(2 * rim, width, dtype=jnp.float32),
            shape(2 * rim, width),
            shape(blocks - 2 * BAND, slots, block_rows, block_rows),
        ),
        in_specs=[hbm] * 7,
        out_specs=(hbm, anywhere) + (vmem,) * 9,
        scratch_shapes=[
            pltpu.SMEM((slots, blocks), jnp.int32),
            pltpu.SMEM((blocks,), jnp.int32),
            place_scratch,
            pltpu.VMEM((rows + block_rows, width), jnp.bfloat16),
            pltpu.VMEM((2 * BAND, slots, block_rows, block_rows), jnp.bfloat16),
            pltpu.VMEM((inner, width), jnp.bfloat16),
            pltpu.VMEM((inner, width), jnp.bfloat16),
            pltpu.VMEM((inner, width), jnp.bfloat16),
            pltpu.SemaphoreType.DMA((15,)),
        ],
        compiler_params=params(20),
        cost_estimate=cost(0.5),
        name="inner_rows",
    )(
        offsets, counts,
        *(in_hbm(x) for x in (weight, bias_row, features, adj_values, cotangent)),
    )
    half_shape = (width // 2 + TAIL, width)
    def rim_rows(order, halo, partial, sums, *outs):
        return pl.pallas_call(
            functools.partial(rim_kernel, order),
            out_shape=(shape(rim, width), shape(rim, width)) + outs,
            in_specs=[vmem] * 8,
            out_specs=(vmem,) * 4,
            compiler_params=params(12),
            cost_estimate=cost(0.1),
            name="rim_rows",
        )(weight_near, bias_near, own_part, halo, dense, cot_rim, partial, sums)

    act_first, grad_first, partial, sums = rim_rows(
        0, first_halo, partial, sums,
        shape(width, width, dtype=jnp.float32), shape(8, width, dtype=jnp.float32),
    )
    act_second, grad_second, send, keep = rim_rows(
        1, second_halo, partial, sums,
        shape(*half_shape), shape(*half_shape, dtype=jnp.float32),
    )
    mark = shape(8, 128, dtype=jnp.float32)
    activated, rim_spread, first_spill, second_spill, first_mark = pl.pallas_call(
        rim_back_kernel,
        out_shape=(
            shape(rows, width),
            shape(4 * BAND, width, block_rows, dtype=jnp.float32),
            shape(rim, width),
            shape(rim, width),
            mark,
        ),
        in_specs=[vmem] * 6 + [hbm],
        out_specs=(hbm,) + (vmem,) * 4,
        scratch_shapes=[
            pltpu.VMEM((2 * rim, width), jnp.bfloat16),
            pltpu.VMEM((2 * rim, width), jnp.bfloat16),
            pltpu.SemaphoreType.DMA((2,)),
        ],
        input_output_aliases={6: 0},
        compiler_params=params(12),
        cost_estimate=cost(0.2),
        name="rim_rows_back",
    )(
        weight_near, dense, grad_first, grad_second, act_first, act_second, activated
    )
    first_part = swap(first_spill, [1] * count)
    second_part = with_next(second_spill, count, False)
    grad_whole, edges, second_mark = pl.pallas_call(
        inner_back_kernel,
        out_shape=(shape(rows, width), shape(2 * rim, width, dtype=jnp.float32), mark),
        in_specs=[anywhere] + [vmem] * 4,
        out_specs=(hbm, vmem, vmem),
        scratch_shapes=[
            place_scratch,
            pltpu.VMEM((blocks + 1, width, block_rows), jnp.float32),
            pltpu.VMEM((inner, width), jnp.bfloat16),
            pltpu.SemaphoreType.DMA((2,)),
        ],
        compiler_params=params(12),
        cost_estimate=cost(0.3),
        name="inner_rows_back",
    )(places, weight_near, adj_inner, grad_inner, rim_spread)
    marks = {"core": (first_mark,), "last": (second_mark, second_part)}
    own_half = sum_halves(send, keep, count, core_bit, marks)
    other_half = swap(own_half, [1 << core_bit] * count)
    norm_scale = 1.0 / math.sqrt(rows * count)
    grad_weight, grad_bias, grad_features = pl.pallas_call(
        functools.partial(last_kernel, norm_scale),
        out_shape=(
            shape(width, width, dtype=jnp.float32),
            shape(1, width, dtype=jnp.float32),
            shape(rows, width),
        ),
        in_specs=[vmem] * 5 + [hbm],
        out_specs=(hbm, hbm, hbm),
        scratch_shapes=[
            pltpu.VMEM((2 * rim, width), jnp.bfloat16),
            pltpu.VMEM((width, width), jnp.float32),
            pltpu.VMEM((1, width), jnp.float32),
            pltpu.SemaphoreType.DMA((4,)),
        ],
        input_output_aliases={5: 2},
        compiler_params=params(8),
        name="last_step",
    )(own_half, other_half, edges, first_part, second_part, grad_whole)
    return (activated, grad_features, grad_weight, grad_bias.reshape(width))


def solution(mesh):
    return jax.shard_map(
        on_device,
        mesh=mesh,
        in_specs=(
            P(AXES, None),
            P(AXES, None, None, None),
            P(AXES, None),
            P(AXES),
            P(),
            P(),
            P(AXES, None),
        ),
        out_specs=(P(AXES, None), P(AXES, None), P(), P()),
        check_vma=False,
    )
```

```python
import functools
import math

import jax
import jax.numpy as jnp
from jax import lax
from jax.experimental import pallas as pl
from jax.experimental.pallas import tpu as pltpu
from jax.sharding import PartitionSpec as P

BAND = 2
TAIL = 8
AXES = ("rows", "cols")
MIB = 1024 * 1024


def row_of(adj_ref, block, slots):
    return jnp.concatenate([adj_ref[block, slot] for slot in range(slots)], 1)


def pick(source, places, block_rows):
    return jnp.concatenate(
        [
            source[pl.ds(pl.multiple_of(place * block_rows, block_rows), block_rows)]
            for place in places
        ],
        0,
    )


def write_places(off_ref, cnt_ref, place_ref, blocks, slots):
    for block in range(blocks):
        if block < BAND:
            shift, dump = BAND, 3 * BAND
        elif block < blocks - BAND:
            shift, dump = 0, blocks
        else:
            shift, dump = 2 * BAND - blocks, 3 * BAND
        for slot in range(slots):
            place_ref[block * slots + slot] = jnp.where(
                slot < cnt_ref[block], block + shift + off_ref[slot, block], dump
            )


def places_of(place_ref, block, slots):
    return [place_ref[block * slots + slot] for slot in range(slots)]


def side_by_side(dense, side, first, last):
    return jnp.concatenate([dense[side, place] for place in range(first, last)], 1)


def place_in_mesh():
    return lax.axis_index("rows") * lax.axis_size("cols") + lax.axis_index("cols")


def core_side():
    return lax.axis_index("rows") & 1


def halo_kernel(feat_hbm, first_ref, second_ref, sems):
    rows = feat_hbm.shape[0]
    rim = first_ref.shape[0]
    odd = place_in_mesh() & 1
    last = rows - rim
    starts = ((1 - odd) * last, odd * last)
    copies = [
        pltpu.make_async_copy(
            feat_hbm.at[pl.ds(pl.multiple_of(start, rim), rim)], out_ref, sems.at[i]
        )
        for i, (start, out_ref) in enumerate(zip(starts, (first_ref, second_ref)))
    ]
    for copy in copies:
        copy.start()
    for copy in copies:
        copy.wait()


def activate(preact, cotangent):
    gate = 1.0 / (1.0 + jnp.exp(-preact))
    grad = cotangent.astype(jnp.float32) * gate * (1.0 + preact * (1.0 - gate))
    return (preact * gate).astype(jnp.bfloat16), grad.astype(jnp.bfloat16)


def column_sums(grad):
    rows, width = grad.shape
    return jnp.sum(grad.astype(jnp.float32).reshape(rows // 8, 8, width), axis=0)


def to_upstream(weight, grad):
    return lax.dot_general(
        weight, grad, (((1,), (1,)), ((), ())), preferred_element_type=jnp.float32
    ).astype(jnp.bfloat16)


def weight_terms(agg, grad):
    return lax.dot_general(
        agg, grad, (((0,), (0,)), ((), ())), preferred_element_type=jnp.float32
    )


def inner_kernel(
    off_hbm, cnt_hbm, weight_hbm, bias_hbm, feat_hbm, adj_hbm, cot_hbm,
    act_hbm, place_out, grad_ref, partial_ref, sums_ref, weight_ref, bias_ref, dense, own_ref,
    cot_rim, adj,
    off_ref, cnt_ref, place_ref, feat, adj_rim, cot, act, agg_all, sems,
):
    blocks, slots, block_rows, _ = adj_hbm.shape
    rows, width = feat_hbm.shape
    count = blocks - 2 * BAND
    rim = BAND * block_rows
    inner = count * block_rows
    scalars = [
        pltpu.make_async_copy(off_hbm, off_ref, sems.at[12]),
        pltpu.make_async_copy(cnt_hbm, cnt_ref, sems.at[13]),
    ]
    copies = [
        pltpu.make_async_copy(feat_hbm, feat.at[pl.ds(0, rows)], sems.at[0]),
        pltpu.make_async_copy(adj_hbm.at[pl.ds(BAND, count)], adj, sems.at[1]),
        pltpu.make_async_copy(weight_hbm, weight_ref, sems.at[2]),
        pltpu.make_async_copy(bias_hbm, bias_ref, sems.at[3]),
        pltpu.make_async_copy(cot_hbm.at[pl.ds(rim, inner)], cot, sems.at[4]),
        pltpu.make_async_copy(adj_hbm.at[pl.ds(0, BAND)], adj_rim.at[pl.ds(0, BAND)], sems.at[5]),
        pltpu.make_async_copy(
            adj_hbm.at[pl.ds(blocks - BAND, BAND)], adj_rim.at[pl.ds(BAND, BAND)], sems.at[6]
        ),
        pltpu.make_async_copy(cot_hbm.at[pl.ds(0, rim)], cot_rim.at[pl.ds(0, rim)], sems.at[7]),
        pltpu.make_async_copy(
            cot_hbm.at[pl.ds(rows - rim, rim)], cot_rim.at[pl.ds(rim, rim)], sems.at[8]
        ),
    ]
    for copy in scalars + copies:
        copy.start()
    feat[rows:] = jnp.zeros((block_rows, width), jnp.bfloat16)
    dense[...] = jnp.zeros_like(dense)
    for copy in scalars:
        copy.wait()
    write_places(off_ref, cnt_ref, place_ref, blocks, slots)
    place_copy = pltpu.make_async_copy(place_ref, place_out, sems.at[14])
    place_copy.start()
    for copy in copies[:5]:
        copy.wait()
    weight = weight_ref[...]
    bias = bias_ref[...]
    sums = jnp.zeros((8, width), jnp.float32)
    for step in range(0, count, 2):
        for block in (step, step + 1):
            places = places_of(place_ref, block + BAND, slots)
            agg_all[block * block_rows : (block + 1) * block_rows] = jnp.dot(
                row_of(adj, block, slots), pick(feat, places, block_rows),
                preferred_element_type=jnp.float32,
            ).astype(jnp.bfloat16)
        here = pl.ds(step * block_rows, 2 * block_rows)
        preact = jnp.dot(agg_all[here], weight, preferred_element_type=jnp.float32) + bias
        act[here], grad = activate(preact, cot[here])
        grad_ref[here] = grad
        sums = sums + column_sums(grad)
    act_out = pltpu.make_async_copy(act, act_hbm.at[pl.ds(rim, inner)], sems.at[11])
    act_out.start()
    sums_ref[...] = sums
    partial_ref[...] = weight_terms(agg_all[...], grad_ref[...])
    for copy in copies[5:]:
        copy.wait()
    for side, first in enumerate((0, blocks - BAND)):
        for row in range(BAND):
            here = pl.ds(row * block_rows, block_rows)
            for slot, place in enumerate(places_of(place_ref, first + row, slots)):
                dense[side, place, here] = adj_rim[side * BAND + row, slot]
    own_ref[:rim] = jnp.dot(
        side_by_side(dense, 0, BAND, 3 * BAND), feat[: 2 * rim],
        preferred_element_type=jnp.float32,
    )
    own_ref[rim:] = jnp.dot(
        side_by_side(dense, 1, 0, 2 * BAND), feat[rows - 2 * rim : rows],
        preferred_element_type=jnp.float32,
    )
    act_out.wait()
    place_copy.wait()


def rim_side(order):
    odd = place_in_mesh() & 1
    return odd if order else 1 - odd


def rim_kernel(
    order, weight_ref, bias_ref, own_ref, halo_ref, dense, cot_ref, partial_ref, sums_ref,
    act_ref, grad_ref, *outs,
):
    rim = halo_ref.shape[0]
    side = rim_side(order)
    here = pl.ds(pl.multiple_of(side * rim, rim), rim)
    beyond = side * 2 * BAND
    row = jnp.concatenate([dense[side, beyond + block] for block in range(BAND)], 1)
    agg = own_ref[here] + jnp.dot(row, halo_ref[...], preferred_element_type=jnp.float32)
    agg = agg.astype(jnp.bfloat16)
    preact = jnp.dot(agg, weight_ref[...], preferred_element_type=jnp.float32) + bias_ref[...]
    act_ref[...], grad = activate(preact, cot_ref[here])
    grad_ref[...] = grad
    sums = sums_ref[...] + column_sums(grad)
    partial = partial_ref[...] + weight_terms(agg, grad)
    if order == 0:
        partial_out, sums_out = outs
        partial_out[...] = partial
        sums_out[...] = sums
        return
    send_ref, keep_ref = outs
    half, width = partial.shape[0] // 2, partial.shape[1]
    bias_tail = jnp.broadcast_to(jnp.sum(sums, axis=0, keepdims=True), (TAIL, width))
    upper = jnp.concatenate([partial[:half], bias_tail], 0)
    lower = jnp.concatenate([partial[half:], jnp.zeros_like(bias_tail)], 0)
    first = core_side() == 0
    keep_ref[...] = jnp.where(first, upper, lower)
    send_ref[...] = jnp.where(first, lower, upper).astype(send_ref.dtype)


def scatter_rows(places, upstream, adj_ref, spread):
    _, slots, block_rows, _ = adj_ref.shape
    for step, targets in enumerate(places):
        terms = jnp.dot(
            upstream[:, step * block_rows : (step + 1) * block_rows],
            row_of(adj_ref, step, slots),
            preferred_element_type=jnp.float32,
        )
        for slot, target in enumerate(targets):
            spread[target] += terms[:, slot * block_rows : (slot + 1) * block_rows]


def rim_back_kernel(
    weight_ref, dense, grad_first, grad_second, act_first, act_second, act_in,
    act_hbm, spread, first_ref, second_ref, mark_ref,
    sems,
):
    block_rows = dense.shape[3]
    rim = BAND * block_rows
    rows = act_hbm.shape[0]
    copies = [
        pltpu.make_async_copy(
            act_ref,
            act_hbm.at[pl.ds(pl.multiple_of(rim_side(order) * (rows - rim), rim), rim)],
            sems.at[order],
        )
        for order, act_ref in enumerate((act_first, act_second))
    ]
    for copy in copies:
        copy.start()
    weight = weight_ref[...]
    exchanges = ((grad_first, first_ref), (grad_second, second_ref))
    for order, (grad_ref, spill_ref) in enumerate(exchanges):
        side = rim_side(order)
        terms = jnp.dot(
            to_upstream(weight, grad_ref[...]), side_by_side(dense, side, 0, 3 * BAND),
            preferred_element_type=jnp.float32,
        )
        for block in range(3 * BAND):
            lane = block * block_rows
            spread[order, block] = terms[:, lane : lane + block_rows]
        for block in range(BAND):
            here = pl.ds(block * block_rows, block_rows)
            spill_ref[here] = spread[order, side * 2 * BAND + block].T.astype(jnp.bfloat16)
    mark_ref[...] = jnp.zeros_like(mark_ref)
    for copy in copies:
        copy.wait()


def inner_back_kernel(
    place_in, weight_ref, adj_ref, grad_ref, rim_spread,
    whole_hbm, edge_ref, mark_ref,
    place_ref, spread, out, sems,
):
    fetch = pltpu.make_async_copy(place_in, place_ref, sems.at[1])
    fetch.start()
    count, slots, block_rows, _ = adj_ref.shape
    blocks = place_ref.shape[0] // slots
    rim = BAND * block_rows
    odd = place_in_mesh() & 1
    spread[: 2 * BAND] = rim_spread[1 - odd, BAND:]
    spread[2 * BAND :] = jnp.zeros_like(spread[2 * BAND :])
    spread[blocks - 2 * BAND : blocks] = rim_spread[odd, : 2 * BAND]
    upstream = to_upstream(weight_ref[...], grad_ref[...])
    fetch.wait()
    scatter_rows(
        [places_of(place_ref, step + BAND, slots) for step in range(count)],
        upstream, adj_ref, spread,
    )
    for step in range(count):
        here = pl.ds(step * block_rows, block_rows)
        out[here] = spread[BAND + step].T.astype(jnp.bfloat16)
    finish = pltpu.make_async_copy(out, whole_hbm.at[pl.ds(rim, count * block_rows)], sems.at[0])
    finish.start()
    mark_ref[...] = jnp.zeros_like(mark_ref)
    for block in range(BAND):
        edge_ref[block * block_rows : (block + 1) * block_rows] = spread[block].T
        after = BAND + block
        edge_ref[after * block_rows : (after + 1) * block_rows] = spread[blocks - BAND + block].T
    finish.wait()


def add_kernel(parts, *refs):
    values = [ref[...].astype(jnp.float32) for ref in refs[:parts]]
    total = values[0] + values[1]
    if parts == 4:
        total = total + (values[2] + values[3])
    refs[-1][...] = total.astype(refs[-1].dtype)


def last_kernel(
    scale, own_ref, other_ref, edge_ref, first_ref, second_ref, whole_in,
    weight_out, bias_out, whole_hbm,
    out, sums, bias, sems,
):
    half = sums.shape[0] // 2
    rim = first_ref.shape[0]
    rows = whole_hbm.shape[0]
    copies = [
        pltpu.make_async_copy(sums, weight_out, sems.at[0]),
        pltpu.make_async_copy(bias, bias_out, sems.at[1]),
        pltpu.make_async_copy(out.at[pl.ds(0, rim)], whole_hbm.at[pl.ds(0, rim)], sems.at[2]),
        pltpu.make_async_copy(
            out.at[pl.ds(rim, rim)], whole_hbm.at[pl.ds(rows - rim, rim)], sems.at[3]
        ),
    ]
    side = core_side()
    own_rows = pl.ds(pl.multiple_of(side * half, half), half)
    other_rows = pl.ds(pl.multiple_of((1 - side) * half, half), half)
    own = own_ref[...].astype(jnp.float32) * scale
    other = other_ref[...].astype(jnp.float32) * scale
    sums[own_rows] = own[:half]
    sums[other_rows] = other[:half]
    copies[0].start()
    bias[...] = jnp.where(side == 0, own[half : half + 1], other[half : half + 1])
    copies[1].start()
    odd = place_in_mesh() & 1
    for base, spill_ref in (((1 - odd) * rim, first_ref), (odd * rim, second_ref)):
        here = pl.ds(pl.multiple_of(base, rim), rim)
        out[here] = (edge_ref[here] + spill_ref[...].astype(jnp.float32)).astype(jnp.bfloat16)
    for copy in copies[2:]:
        copy.start()
    for copy in copies:
        copy.wait()


def add(values, dtype, after=()):
    size = values[0].size
    return pl.pallas_call(
        functools.partial(add_kernel, len(values)),
        out_shape=jax.ShapeDtypeStruct(values[0].shape, dtype),
        in_specs=[pl.BlockSpec(memory_space=pltpu.VMEM)] * len(values)
        + [pl.BlockSpec(memory_space=pl.ANY)] * len(after),
        compiler_params=pltpu.CompilerParams(vmem_limit_bytes=2 * MIB),
        cost_estimate=pl.CostEstimate(
            flops=size * len(values), bytes_accessed=8 * size, transcendentals=0
        ),
        name="add_halves",
    )(*values, *after)


def swap(value, masks):
    pairs = [(i, i ^ mask) for i, mask in enumerate(masks) if mask]
    return lax.ppermute(value, AXES, pairs)


def with_next(value, count, closed):
    pairs = [(i, (i + 1 if i & 1 else i - 1) % count) for i in range(count)]
    return lax.ppermute(value, AXES, pairs if closed else pairs[1:-1])


def sum_halves(send, keep, count, core_bit, marks):
    others = [bit for bit in range(count.bit_length() - 1) if bit != core_bit]
    groups = [others[i : i + 2] for i in range(0, len(others), 2)]
    groups[0] = groups[0][::-1]
    total = add([keep, swap(send, [1 << core_bit] * count)], jnp.bfloat16, marks.get("core", ()))
    for step in range(len(groups)):
        masks = []
        for group in (groups[step], groups[len(groups) - 1 - step]):
            if len(groups[0]) != len(groups[-1]):
                group = groups[step]
            bits = [1 << bit for bit in group]
            if group[1:]:
                both = bits[0] | bits[1]
                near = group is groups[0]
                bits = [bits[0], both, bits[1]] if near else [*bits, both]
            masks.append(bits)
        parts = [total] + [
            swap(total, [masks[(i >> core_bit) & 1][k] for i in range(count)])
            for k in range(len(masks[0]))
        ]
        last = step == len(groups) - 1
        name = "last" if last else step
        total = add(parts, jnp.bfloat16, marks.get(name, ()))
    return total


def on_device(features, adj_values, adj_offset, adj_count, weight, bias_vector, cotangent):
    blocks, slots = adj_offset.shape
    block_rows = adj_values.shape[2]
    rows, width = features.shape
    rim = BAND * block_rows
    inner = rows - 2 * rim
    cols = lax.axis_size("cols")
    count = lax.axis_size("rows") * cols
    vmem = pl.BlockSpec(memory_space=pltpu.VMEM)
    hbm = pl.BlockSpec(memory_space=pltpu.HBM)
    anywhere = pl.BlockSpec(memory_space=pl.ANY)
    place_scratch = pltpu.SMEM((blocks * slots,), jnp.int32)
    bias_row = bias_vector.reshape(1, width)

    def in_hbm(value):
        return pltpu.with_memory_space_constraint(value, pltpu.HBM)

    def shape(*sizes, dtype=jnp.bfloat16):
        return jax.ShapeDtypeStruct(sizes, dtype)

    def params(mib):
        return pltpu.CompilerParams(vmem_limit_bytes=mib * MIB)

    def cost(share):
        return pl.CostEstimate(
            flops=int(1.2e9 * share), bytes_accessed=int(6e6 * share),
            transcendentals=int(8e5 * share),
        )

    offsets = in_hbm(adj_offset.T)
    counts = in_hbm(adj_count)
    core_bit = cols.bit_length() - 1
    first_rim, second_rim = pl.pallas_call(
        halo_kernel,
        out_shape=(shape(rim, width), shape(rim, width)),
        in_specs=[hbm],
        out_specs=(vmem, vmem),
        scratch_shapes=[pltpu.SemaphoreType.DMA((2,))],
        compiler_params=params(2),
        cost_estimate=cost(0.05),
        name="halo_rows",
    )(in_hbm(features))
    first_halo = swap(first_rim, [1] * count)
    second_halo = with_next(second_rim, count, True)
    (
        activated, places, grad_inner, partial, sums, weight_near, bias_near, dense, own_part,
        cot_rim, adj_inner,
    ) = pl.pallas_call(
        inner_kernel,
        out_shape=(
            shape(rows, width),
            shape(blocks * slots, dtype=jnp.int32),
            shape(inner, width),
            shape(width, width, dtype=jnp.float32),
            shape(8, width, dtype=jnp.float32),
            shape(width, width),
            shape(1, width, dtype=jnp.float32),
            shape(2, 3 * BAND + 1, rim, block_rows),
            shape(2 * rim, width, dtype=jnp.float32),
            shape(2 * rim, width),
            shape(blocks - 2 * BAND, slots, block_rows, block_rows),
        ),
        in_specs=[hbm] * 7,
        out_specs=(hbm, anywhere) + (vmem,) * 9,
        scratch_shapes=[
            pltpu.SMEM((slots, blocks), jnp.int32),
            pltpu.SMEM((blocks,), jnp.int32),
            place_scratch,
            pltpu.VMEM((rows + block_rows, width), jnp.bfloat16),
            pltpu.VMEM((2 * BAND, slots, block_rows, block_rows), jnp.bfloat16),
            pltpu.VMEM((inner, width), jnp.bfloat16),
            pltpu.VMEM((inner, width), jnp.bfloat16),
            pltpu.VMEM((inner, width), jnp.bfloat16),
            pltpu.SemaphoreType.DMA((15,)),
        ],
        compiler_params=params(20),
        cost_estimate=cost(0.5),
        name="inner_rows",
    )(
        offsets, counts,
        *(in_hbm(x) for x in (weight, bias_row, features, adj_values, cotangent)),
    )
    half_shape = (width // 2 + TAIL, width)
    def rim_rows(order, halo, partial, sums, *outs):
        return pl.pallas_call(
            functools.partial(rim_kernel, order),
            out_shape=(shape(rim, width), shape(rim, width)) + outs,
            in_specs=[vmem] * 8,
            out_specs=(vmem,) * 4,
            compiler_params=params(12),
            cost_estimate=cost(0.1),
            name="rim_rows",
        )(weight_near, bias_near, own_part, halo, dense, cot_rim, partial, sums)

    act_first, grad_first, partial, sums = rim_rows(
        0, first_halo, partial, sums,
        shape(width, width, dtype=jnp.float32), shape(8, width, dtype=jnp.float32),
    )
    act_second, grad_second, send, keep = rim_rows(
        1, second_halo, partial, sums,
        shape(*half_shape), shape(*half_shape, dtype=jnp.float32),
    )
    mark = shape(8, 128, dtype=jnp.float32)
    activated, rim_spread, first_spill, second_spill, first_mark = pl.pallas_call(
        rim_back_kernel,
        out_shape=(
            shape(rows, width),
            shape(2, 3 * BAND, width, block_rows, dtype=jnp.float32),
            shape(rim, width),
            shape(rim, width),
            mark,
        ),
        in_specs=[vmem] * 6 + [hbm],
        out_specs=(hbm,) + (vmem,) * 4,
        scratch_shapes=[pltpu.SemaphoreType.DMA((2,))],
        input_output_aliases={6: 0},
        compiler_params=params(12),
        cost_estimate=cost(0.2),
        name="rim_rows_back",
    )(
        weight_near, dense, grad_first, grad_second, act_first, act_second, activated
    )
    first_part = swap(first_spill, [1] * count)
    second_part = with_next(second_spill, count, False)
    grad_whole, edges, second_mark = pl.pallas_call(
        inner_back_kernel,
        out_shape=(shape(rows, width), shape(2 * rim, width, dtype=jnp.float32), mark),
        in_specs=[anywhere] + [vmem] * 4,
        out_specs=(hbm, vmem, vmem),
        scratch_shapes=[
            place_scratch,
            pltpu.VMEM((blocks + 1, width, block_rows), jnp.float32),
            pltpu.VMEM((inner, width), jnp.bfloat16),
            pltpu.SemaphoreType.DMA((2,)),
        ],
        compiler_params=params(12),
        cost_estimate=cost(0.3),
        name="inner_rows_back",
    )(places, weight_near, adj_inner, grad_inner, rim_spread)
    marks = {"core": (first_mark,), "last": (second_mark, second_part)}
    own_half = sum_halves(send, keep, count, core_bit, marks)
    other_half = swap(own_half, [1 << core_bit] * count)
    norm_scale = 1.0 / math.sqrt(rows * count)
    grad_weight, grad_bias, grad_features = pl.pallas_call(
        functools.partial(last_kernel, norm_scale),
        out_shape=(
            shape(width, width, dtype=jnp.float32),
            shape(1, width, dtype=jnp.float32),
            shape(rows, width),
        ),
        in_specs=[vmem] * 5 + [hbm],
        out_specs=(hbm, hbm, hbm),
        scratch_shapes=[
            pltpu.VMEM((2 * rim, width), jnp.bfloat16),
            pltpu.VMEM((width, width), jnp.float32),
            pltpu.VMEM((1, width), jnp.float32),
            pltpu.SemaphoreType.DMA((4,)),
        ],
        input_output_aliases={5: 2},
        compiler_params=params(8),
        name="last_step",
    )(own_half, other_half, edges, first_part, second_part, grad_whole)
    return (activated, grad_features, grad_weight, grad_bias.reshape(width))


def solution(mesh):
    return jax.shard_map(
        on_device,
        mesh=mesh,
        in_specs=(
            P(AXES, None),
            P(AXES, None, None, None),
            P(AXES, None),
            P(AXES),
            P(),
            P(),
            P(AXES, None),
        ),
        out_specs=(P(AXES, None), P(AXES, None), P(), P()),
        check_vma=False,
    )
```

```python
import functools
import math

import jax
import jax.numpy as jnp
from jax import lax
from jax.experimental import pallas as pl
from jax.experimental.pallas import tpu as pltpu
from jax.sharding import PartitionSpec as P

BAND = 2
TAIL = 8
AXES = ("rows", "cols")
MIB = 1024 * 1024


def row_of(adj_ref, block, slots):
    return jnp.concatenate([adj_ref[block, slot] for slot in range(slots)], 1)


def pick(source, places, block_rows):
    return jnp.concatenate(
        [
            source[pl.ds(pl.multiple_of(place * block_rows, block_rows), block_rows)]
            for place in places
        ],
        0,
    )


def write_places(off_ref, cnt_ref, place_ref, blocks, slots):
    for block in range(blocks):
        if block < BAND:
            shift, dump = BAND, 3 * BAND
        elif block < blocks - BAND:
            shift, dump = 0, blocks
        else:
            shift, dump = 2 * BAND - blocks, 3 * BAND
        for slot in range(slots):
            place_ref[block * slots + slot] = jnp.where(
                slot < cnt_ref[block], block + shift + off_ref[slot, block], dump
            )


def places_of(place_ref, block, slots):
    return [place_ref[block * slots + slot] for slot in range(slots)]


def side_by_side(dense, side, first, last):
    return jnp.concatenate([dense[side, place] for place in range(first, last)], 1)


def place_in_mesh():
    return lax.axis_index("rows") * lax.axis_size("cols") + lax.axis_index("cols")


def core_side():
    return lax.axis_index("rows") & 1


def halo_kernel(feat_hbm, first_ref, second_ref, sems):
    rows = feat_hbm.shape[0]
    rim = first_ref.shape[0]
    odd = place_in_mesh() & 1
    last = rows - rim
    starts = ((1 - odd) * last, odd * last)
    copies = [
        pltpu.make_async_copy(
            feat_hbm.at[pl.ds(pl.multiple_of(start, rim), rim)], out_ref, sems.at[i]
        )
        for i, (start, out_ref) in enumerate(zip(starts, (first_ref, second_ref)))
    ]
    for copy in copies:
        copy.start()
    for copy in copies:
        copy.wait()


def activate(preact, cotangent):
    gate = 1.0 / (1.0 + jnp.exp(-preact))
    grad = cotangent.astype(jnp.float32) * gate * (1.0 + preact * (1.0 - gate))
    return (preact * gate).astype(jnp.bfloat16), grad.astype(jnp.bfloat16)


def column_sums(grad):
    rows, width = grad.shape
    return jnp.sum(grad.astype(jnp.float32).reshape(rows // 8, 8, width), axis=0)


def to_upstream(weight, grad):
    return lax.dot_general(
        weight, grad, (((1,), (1,)), ((), ())), preferred_element_type=jnp.float32
    ).astype(jnp.bfloat16)


def weight_terms(agg, grad):
    return lax.dot_general(
        agg, grad, (((0,), (0,)), ((), ())), preferred_element_type=jnp.float32
    )


def inner_kernel(
    off_hbm, cnt_hbm, weight_hbm, bias_hbm, feat_hbm, adj_hbm, cot_hbm,
    act_hbm, place_out, grad_ref, partial_ref, sums_ref, weight_ref, bias_ref, dense, own_ref,
    cot_rim, adj,
    off_ref, cnt_ref, place_ref, feat, adj_rim, cot, act, agg_all, sems,
):
    blocks, slots, block_rows, _ = adj_hbm.shape
    rows, width = feat_hbm.shape
    count = blocks - 2 * BAND
    rim = BAND * block_rows
    inner = count * block_rows
    scalars = [
        pltpu.make_async_copy(off_hbm, off_ref, sems.at[12]),
        pltpu.make_async_copy(cnt_hbm, cnt_ref, sems.at[13]),
    ]
    copies = [
        pltpu.make_async_copy(feat_hbm, feat.at[pl.ds(0, rows)], sems.at[0]),
        pltpu.make_async_copy(adj_hbm.at[pl.ds(BAND, count)], adj, sems.at[1]),
        pltpu.make_async_copy(weight_hbm, weight_ref, sems.at[2]),
        pltpu.make_async_copy(bias_hbm, bias_ref, sems.at[3]),
        pltpu.make_async_copy(cot_hbm.at[pl.ds(rim, inner)], cot, sems.at[4]),
        pltpu.make_async_copy(adj_hbm.at[pl.ds(0, BAND)], adj_rim.at[pl.ds(0, BAND)], sems.at[5]),
        pltpu.make_async_copy(
            adj_hbm.at[pl.ds(blocks - BAND, BAND)], adj_rim.at[pl.ds(BAND, BAND)], sems.at[6]
        ),
        pltpu.make_async_copy(cot_hbm.at[pl.ds(0, rim)], cot_rim.at[pl.ds(0, rim)], sems.at[7]),
        pltpu.make_async_copy(
            cot_hbm.at[pl.ds(rows - rim, rim)], cot_rim.at[pl.ds(rim, rim)], sems.at[8]
        ),
    ]
    for copy in scalars + copies:
        copy.start()
    feat[rows:] = jnp.zeros((block_rows, width), jnp.bfloat16)
    dense[...] = jnp.zeros_like(dense)
    for copy in scalars:
        copy.wait()
    write_places(off_ref, cnt_ref, place_ref, blocks, slots)
    place_copy = pltpu.make_async_copy(place_ref, place_out, sems.at[14])
    place_copy.start()
    for copy in copies[:5]:
        copy.wait()
    weight = weight_ref[...]
    bias = bias_ref[...]
    sums = jnp.zeros((8, width), jnp.float32)
    for step in range(0, count, 2):
        for block in (step, step + 1):
            places = places_of(place_ref, block + BAND, slots)
            agg_all[block * block_rows : (block + 1) * block_rows] = jnp.dot(
                row_of(adj, block, slots), pick(feat, places, block_rows),
                preferred_element_type=jnp.float32,
            ).astype(jnp.bfloat16)
        here = pl.ds(step * block_rows, 2 * block_rows)
        preact = jnp.dot(agg_all[here], weight, preferred_element_type=jnp.float32) + bias
        act[here], grad = activate(preact, cot[here])
        grad_ref[here] = grad
        sums = sums + column_sums(grad)
    act_out = pltpu.make_async_copy(act, act_hbm.at[pl.ds(rim, inner)], sems.at[11])
    act_out.start()
    sums_ref[...] = sums
    partial_ref[...] = weight_terms(agg_all[...], grad_ref[...])
    for copy in copies[5:]:
        copy.wait()
    for side, first in enumerate((0, blocks - BAND)):
        for row in range(BAND):
            here = pl.ds(row * block_rows, block_rows)
            for slot, place in enumerate(places_of(place_ref, first + row, slots)):
                dense[side, place, here] = adj_rim[side * BAND + row, slot]
    own_ref[:rim] = jnp.dot(
        side_by_side(dense, 0, BAND, 3 * BAND), feat[: 2 * rim],
        preferred_element_type=jnp.float32,
    )
    own_ref[rim:] = jnp.dot(
        side_by_side(dense, 1, 0, 2 * BAND), feat[rows - 2 * rim : rows],
        preferred_element_type=jnp.float32,
    )
    act_out.wait()
    place_copy.wait()


def rim_kernel(
    weight_ref, bias_ref, own_ref, first_ref, second_ref, dense, cot_ref, partial_ref, sums_ref,
    act_ref, grad_ref, send_ref, keep_ref,
    halo, agg_all,
):
    rim, width = first_ref.shape
    odd = place_in_mesh() & 1
    halo[pl.ds(pl.multiple_of((1 - odd) * rim, rim), rim)] = first_ref[...]
    halo[pl.ds(pl.multiple_of(odd * rim, rim), rim)] = second_ref[...]
    weight = weight_ref[...]
    bias = bias_ref[...]
    sums = sums_ref[...]
    for side, first in enumerate((0, 2 * BAND)):
        here = pl.ds(side * rim, rim)
        agg = own_ref[here] + jnp.dot(
            side_by_side(dense, side, first, first + BAND), halo[here],
            preferred_element_type=jnp.float32,
        )
        agg = agg.astype(jnp.bfloat16)
        agg_all[here] = agg
        preact = jnp.dot(agg, weight, preferred_element_type=jnp.float32) + bias
        act_ref[here], grad = activate(preact, cot_ref[here])
        grad_ref[here] = grad
        sums = sums + column_sums(grad)
    half = width // 2
    partial = partial_ref[...] + weight_terms(agg_all[...], grad_ref[...])
    bias_tail = jnp.broadcast_to(jnp.sum(sums, axis=0, keepdims=True), (TAIL, width))
    upper = jnp.concatenate([partial[:half], bias_tail], 0)
    lower = jnp.concatenate([partial[half:], jnp.zeros_like(bias_tail)], 0)
    first = core_side() == 0
    keep_ref[...] = jnp.where(first, upper, lower)
    send_ref[...] = jnp.where(first, lower, upper).astype(send_ref.dtype)


def scatter_rows(places, upstream, adj_ref, spread):
    _, slots, block_rows, _ = adj_ref.shape
    for step, targets in enumerate(places):
        terms = jnp.dot(
            upstream[:, step * block_rows : (step + 1) * block_rows],
            row_of(adj_ref, step, slots),
            preferred_element_type=jnp.float32,
        )
        for slot, target in enumerate(targets):
            spread[target] += terms[:, slot * block_rows : (slot + 1) * block_rows]


def rim_back_kernel(
    weight_ref, dense, grad_ref, act_ref, act_in,
    act_hbm, spread, first_ref, second_ref, mark_ref,
    spill, sems,
):
    block_rows = dense.shape[3]
    rim = BAND * block_rows
    rows = act_hbm.shape[0]
    copies = [
        pltpu.make_async_copy(act_ref.at[pl.ds(0, rim)], act_hbm.at[pl.ds(0, rim)], sems.at[0]),
        pltpu.make_async_copy(
            act_ref.at[pl.ds(rim, rim)], act_hbm.at[pl.ds(rows - rim, rim)], sems.at[1]
        ),
    ]
    for copy in copies:
        copy.start()
    weight = weight_ref[...]
    for side, (inside, outside) in enumerate(((BAND, 0), (0, 2 * BAND))):
        terms = jnp.dot(
            to_upstream(weight, grad_ref[side * rim : (side + 1) * rim]),
            side_by_side(dense, side, 0, 3 * BAND),
            preferred_element_type=jnp.float32,
        )
        for block in range(2 * BAND):
            lane = (inside + block) * block_rows
            spread[side * 2 * BAND + block] = terms[:, lane : lane + block_rows]
        for block in range(BAND):
            lane = (outside + block) * block_rows
            here = pl.ds(side * rim + block * block_rows, block_rows)
            spill[here] = terms[:, lane : lane + block_rows].T.astype(jnp.bfloat16)
    odd = place_in_mesh() & 1
    first_ref[...] = spill[pl.ds(pl.multiple_of((1 - odd) * rim, rim), rim)]
    second_ref[...] = spill[pl.ds(pl.multiple_of(odd * rim, rim), rim)]
    mark_ref[...] = jnp.zeros_like(mark_ref)
    for copy in copies:
        copy.wait()


def inner_back_kernel(
    place_in, weight_ref, adj_ref, grad_ref, rim_spread,
    whole_hbm, edge_ref, mark_ref,
    place_ref, spread, out, sems,
):
    fetch = pltpu.make_async_copy(place_in, place_ref, sems.at[1])
    fetch.start()
    count, slots, block_rows, _ = adj_ref.shape
    blocks = place_ref.shape[0] // slots
    rim = BAND * block_rows
    spread[: 2 * BAND] = rim_spread[: 2 * BAND]
    spread[2 * BAND :] = jnp.zeros_like(spread[2 * BAND :])
    spread[blocks - 2 * BAND : blocks] = rim_spread[2 * BAND :]
    upstream = to_upstream(weight_ref[...], grad_ref[...])
    fetch.wait()
    scatter_rows(
        [places_of(place_ref, step + BAND, slots) for step in range(count)],
        upstream, adj_ref, spread,
    )
    for step in range(count):
        here = pl.ds(step * block_rows, block_rows)
        out[here] = spread[BAND + step].T.astype(jnp.bfloat16)
    finish = pltpu.make_async_copy(out, whole_hbm.at[pl.ds(rim, count * block_rows)], sems.at[0])
    finish.start()
    mark_ref[...] = jnp.zeros_like(mark_ref)
    for block in range(BAND):
        edge_ref[block * block_rows : (block + 1) * block_rows] = spread[block].T
        after = BAND + block
        edge_ref[after * block_rows : (after + 1) * block_rows] = spread[blocks - BAND + block].T
    finish.wait()


def add_kernel(parts, *refs):
    values = [ref[...].astype(jnp.float32) for ref in refs[:parts]]
    total = values[0] + values[1]
    if parts == 4:
        total = total + (values[2] + values[3])
    refs[-1][...] = total.astype(refs[-1].dtype)


def last_kernel(
    scale, own_ref, other_ref, edge_ref, first_ref, second_ref, whole_in,
    weight_out, bias_out, whole_hbm,
    out, sums, bias, sems,
):
    half = sums.shape[0] // 2
    rim = first_ref.shape[0]
    rows = whole_hbm.shape[0]
    copies = [
        pltpu.make_async_copy(sums, weight_out, sems.at[0]),
        pltpu.make_async_copy(bias, bias_out, sems.at[1]),
        pltpu.make_async_copy(out.at[pl.ds(0, rim)], whole_hbm.at[pl.ds(0, rim)], sems.at[2]),
        pltpu.make_async_copy(
            out.at[pl.ds(rim, rim)], whole_hbm.at[pl.ds(rows - rim, rim)], sems.at[3]
        ),
    ]
    side = core_side()
    own_rows = pl.ds(pl.multiple_of(side * half, half), half)
    other_rows = pl.ds(pl.multiple_of((1 - side) * half, half), half)
    own = own_ref[...].astype(jnp.float32) * scale
    other = other_ref[...].astype(jnp.float32) * scale
    sums[own_rows] = own[:half]
    sums[other_rows] = other[:half]
    copies[0].start()
    bias[...] = jnp.where(side == 0, own[half : half + 1], other[half : half + 1])
    copies[1].start()
    odd = place_in_mesh() & 1
    for base, spill_ref in (((1 - odd) * rim, first_ref), (odd * rim, second_ref)):
        here = pl.ds(pl.multiple_of(base, rim), rim)
        out[here] = (edge_ref[here] + spill_ref[...].astype(jnp.float32)).astype(jnp.bfloat16)
    for copy in copies[2:]:
        copy.start()
    for copy in copies:
        copy.wait()


def add(values, dtype, after=()):
    size = values[0].size
    return pl.pallas_call(
        functools.partial(add_kernel, len(values)),
        out_shape=jax.ShapeDtypeStruct(values[0].shape, dtype),
        in_specs=[pl.BlockSpec(memory_space=pltpu.VMEM)] * len(values)
        + [pl.BlockSpec(memory_space=pl.ANY)] * len(after),
        compiler_params=pltpu.CompilerParams(vmem_limit_bytes=2 * MIB),
        cost_estimate=pl.CostEstimate(
            flops=size * len(values), bytes_accessed=8 * size, transcendentals=0
        ),
        name="add_halves",
    )(*values, *after)


def swap(value, masks):
    pairs = [(i, i ^ mask) for i, mask in enumerate(masks) if mask]
    return lax.ppermute(value, AXES, pairs)


def with_next(value, count, closed):
    pairs = [(i, (i + 1 if i & 1 else i - 1) % count) for i in range(count)]
    return lax.ppermute(value, AXES, pairs if closed else pairs[1:-1])


def sum_halves(send, keep, count, core_bit, marks):
    others = [bit for bit in range(count.bit_length() - 1) if bit != core_bit]
    groups = [others[i : i + 2] for i in range(0, len(others), 2)]
    groups[0] = groups[0][::-1]
    total = add([keep, swap(send, [1 << core_bit] * count)], jnp.bfloat16, marks.get("core", ()))
    for step in range(len(groups)):
        masks = []
        for group in (groups[step], groups[len(groups) - 1 - step]):
            if len(groups[0]) != len(groups[-1]):
                group = groups[step]
            bits = [1 << bit for bit in group]
            if group[1:]:
                both = bits[0] | bits[1]
                near = group is groups[0]
                bits = [bits[0], both, bits[1]] if near else [*bits, both]
            masks.append(bits)
        parts = [total] + [
            swap(total, [masks[(i >> core_bit) & 1][k] for i in range(count)])
            for k in range(len(masks[0]))
        ]
        last = step == len(groups) - 1
        name = "last" if last else step
        total = add(parts, jnp.bfloat16, marks.get(name, ()))
    return total


def on_device(features, adj_values, adj_offset, adj_count, weight, bias_vector, cotangent):
    blocks, slots = adj_offset.shape
    block_rows = adj_values.shape[2]
    rows, width = features.shape
    rim = BAND * block_rows
    inner = rows - 2 * rim
    cols = lax.axis_size("cols")
    count = lax.axis_size("rows") * cols
    vmem = pl.BlockSpec(memory_space=pltpu.VMEM)
    hbm = pl.BlockSpec(memory_space=pltpu.HBM)
    anywhere = pl.BlockSpec(memory_space=pl.ANY)
    place_scratch = pltpu.SMEM((blocks * slots,), jnp.int32)
    bias_row = bias_vector.reshape(1, width)

    def in_hbm(value):
        return pltpu.with_memory_space_constraint(value, pltpu.HBM)

    def shape(*sizes, dtype=jnp.bfloat16):
        return jax.ShapeDtypeStruct(sizes, dtype)

    def params(mib):
        return pltpu.CompilerParams(vmem_limit_bytes=mib * MIB)

    def cost(share):
        return pl.CostEstimate(
            flops=int(1.2e9 * share), bytes_accessed=int(6e6 * share),
            transcendentals=int(8e5 * share),
        )

    offsets = in_hbm(adj_offset.T)
    counts = in_hbm(adj_count)
    core_bit = cols.bit_length() - 1
    first_rim, second_rim = pl.pallas_call(
        halo_kernel,
        out_shape=(shape(rim, width), shape(rim, width)),
        in_specs=[hbm],
        out_specs=(vmem, vmem),
        scratch_shapes=[pltpu.SemaphoreType.DMA((2,))],
        compiler_params=params(2),
        cost_estimate=cost(0.05),
        name="halo_rows",
    )(in_hbm(features))
    first_halo = swap(first_rim, [1] * count)
    second_halo = with_next(second_rim, count, True)
    (
        activated, places, grad_inner, partial, sums, weight_near, bias_near, dense, own_part,
        cot_rim, adj_inner,
    ) = pl.pallas_call(
        inner_kernel,
        out_shape=(
            shape(rows, width),
            shape(blocks * slots, dtype=jnp.int32),
            shape(inner, width),
            shape(width, width, dtype=jnp.float32),
            shape(8, width, dtype=jnp.float32),
            shape(width, width),
            shape(1, width, dtype=jnp.float32),
            shape(2, 3 * BAND + 1, rim, block_rows),
            shape(2 * rim, width, dtype=jnp.float32),
            shape(2 * rim, width),
            shape(blocks - 2 * BAND, slots, block_rows, block_rows),
        ),
        in_specs=[hbm] * 7,
        out_specs=(hbm, anywhere) + (vmem,) * 9,
        scratch_shapes=[
            pltpu.SMEM((slots, blocks), jnp.int32),
            pltpu.SMEM((blocks,), jnp.int32),
            place_scratch,
            pltpu.VMEM((rows + block_rows, width), jnp.bfloat16),
            pltpu.VMEM((2 * BAND, slots, block_rows, block_rows), jnp.bfloat16),
            pltpu.VMEM((inner, width), jnp.bfloat16),
            pltpu.VMEM((inner, width), jnp.bfloat16),
            pltpu.VMEM((inner, width), jnp.bfloat16),
            pltpu.SemaphoreType.DMA((15,)),
        ],
        compiler_params=params(20),
        cost_estimate=cost(0.5),
        name="inner_rows",
    )(
        offsets, counts,
        *(in_hbm(x) for x in (weight, bias_row, features, adj_values, cotangent)),
    )
    half_shape = (width // 2 + TAIL, width)
    act_rim, grad_rim, send, keep = pl.pallas_call(
        rim_kernel,
        out_shape=(
            shape(2 * rim, width),
            shape(2 * rim, width),
            shape(*half_shape),
            shape(*half_shape, dtype=jnp.float32),
        ),
        in_specs=[vmem] * 9,
        out_specs=(vmem,) * 4,
        scratch_shapes=[
            pltpu.VMEM((2 * rim, width), jnp.bfloat16),
            pltpu.VMEM((2 * rim, width), jnp.bfloat16),
        ],
        compiler_params=params(12),
        cost_estimate=cost(0.2),
        name="rim_rows",
    )(
        weight_near, bias_near, own_part, first_halo, second_halo, dense, cot_rim, partial, sums,
    )
    mark = shape(8, 128, dtype=jnp.float32)
    activated, rim_spread, first_spill, second_spill, first_mark = pl.pallas_call(
        rim_back_kernel,
        out_shape=(
            shape(rows, width),
            shape(4 * BAND, width, block_rows, dtype=jnp.float32),
            shape(rim, width),
            shape(rim, width),
            mark,
        ),
        in_specs=[vmem] * 4 + [hbm],
        out_specs=(hbm,) + (vmem,) * 4,
        scratch_shapes=[
            pltpu.VMEM((2 * rim, width), jnp.bfloat16),
            pltpu.SemaphoreType.DMA((2,)),
        ],
        input_output_aliases={4: 0},
        compiler_params=params(12),
        cost_estimate=cost(0.2),
        name="rim_rows_back",
    )(weight_near, dense, grad_rim, act_rim, activated)
    first_part = swap(first_spill, [1] * count)
    second_part = with_next(second_spill, count, True)
    grad_whole, edges, second_mark = pl.pallas_call(
        inner_back_kernel,
        out_shape=(shape(rows, width), shape(2 * rim, width, dtype=jnp.float32), mark),
        in_specs=[anywhere] + [vmem] * 4,
        out_specs=(hbm, vmem, vmem),
        scratch_shapes=[
            place_scratch,
            pltpu.VMEM((blocks + 1, width, block_rows), jnp.float32),
            pltpu.VMEM((inner, width), jnp.bfloat16),
            pltpu.SemaphoreType.DMA((2,)),
        ],
        compiler_params=params(12),
        cost_estimate=cost(0.3),
        name="inner_rows_back",
    )(places, weight_near, adj_inner, grad_inner, rim_spread)
    marks = {"core": (first_mark,), "last": (second_mark, second_part)}
    own_half = sum_halves(send, keep, count, core_bit, marks)
    other_half = swap(own_half, [1 << core_bit] * count)
    norm_scale = 1.0 / math.sqrt(rows * count)
    grad_weight, grad_bias, grad_features = pl.pallas_call(
        functools.partial(last_kernel, norm_scale),
        out_shape=(
            shape(width, width, dtype=jnp.float32),
            shape(1, width, dtype=jnp.float32),
            shape(rows, width),
        ),
        in_specs=[vmem] * 5 + [hbm],
        out_specs=(hbm, hbm, hbm),
        scratch_shapes=[
            pltpu.VMEM((2 * rim, width), jnp.bfloat16),
            pltpu.VMEM((width, width), jnp.float32),
            pltpu.VMEM((1, width), jnp.float32),
            pltpu.SemaphoreType.DMA((4,)),
        ],
        input_output_aliases={5: 2},
        compiler_params=params(8),
        name="last_step",
    )(own_half, other_half, edges, first_part, second_part, grad_whole)
    return (activated, grad_features, grad_weight, grad_bias.reshape(width))


def solution(mesh):
    return jax.shard_map(
        on_device,
        mesh=mesh,
        in_specs=(
            P(AXES, None),
            P(AXES, None, None, None),
            P(AXES, None),
            P(AXES),
            P(),
            P(),
            P(AXES, None),
        ),
        out_specs=(P(AXES, None), P(AXES, None), P(), P()),
        check_vma=False,
    )
```

```python
import functools
import math

import jax
import jax.numpy as jnp
from jax import lax
from jax.experimental import pallas as pl
from jax.experimental.pallas import tpu as pltpu
from jax.sharding import PartitionSpec as P

BAND = 2
TAIL = 8
AXES = ("rows", "cols")
MIB = 1024 * 1024


def row_of(adj_ref, block, slots):
    return jnp.concatenate([adj_ref[block, slot] for slot in range(slots)], 1)


def pick(source, places, block_rows):
    return jnp.concatenate(
        [
            source[pl.ds(pl.multiple_of(place * block_rows, block_rows), block_rows)]
            for place in places
        ],
        0,
    )


def write_places(off_ref, cnt_ref, place_ref, blocks, slots):
    for block in range(blocks):
        if block < BAND:
            shift, dump = BAND, 3 * BAND
        elif block < blocks - BAND:
            shift, dump = 0, blocks
        else:
            shift, dump = 2 * BAND - blocks, 3 * BAND
        for slot in range(slots):
            place_ref[block * slots + slot] = jnp.where(
                slot < cnt_ref[block], block + shift + off_ref[slot, block], dump
            )


def places_of(place_ref, block, slots):
    return [place_ref[block * slots + slot] for slot in range(slots)]


def side_by_side(dense, side, first, last):
    return jnp.concatenate([dense[side, place] for place in range(first, last)], 1)


def place_in_mesh():
    return lax.axis_index("rows") * lax.axis_size("cols") + lax.axis_index("cols")


def core_side():
    return lax.axis_index("rows") & 1


def halo_kernel(feat_hbm, first_ref, second_ref, sems):
    rows = feat_hbm.shape[0]
    rim = first_ref.shape[0]
    odd = place_in_mesh() & 1
    last = rows - rim
    starts = ((1 - odd) * last, odd * last)
    copies = [
        pltpu.make_async_copy(
            feat_hbm.at[pl.ds(pl.multiple_of(start, rim), rim)], out_ref, sems.at[i]
        )
        for i, (start, out_ref) in enumerate(zip(starts, (first_ref, second_ref)))
    ]
    for copy in copies:
        copy.start()
    for copy in copies:
        copy.wait()


def activate(preact, cotangent):
    gate = 1.0 / (1.0 + jnp.exp(-preact))
    grad = cotangent.astype(jnp.float32) * gate * (1.0 + preact * (1.0 - gate))
    return (preact * gate).astype(jnp.bfloat16), grad.astype(jnp.bfloat16)


def column_sums(grad):
    rows, width = grad.shape
    return jnp.sum(grad.astype(jnp.float32).reshape(rows // 8, 8, width), axis=0)


def to_upstream(weight, grad):
    return lax.dot_general(
        weight, grad, (((1,), (1,)), ((), ())), preferred_element_type=jnp.float32
    ).astype(jnp.bfloat16)


def weight_terms(agg, grad):
    return lax.dot_general(
        agg, grad, (((0,), (0,)), ((), ())), preferred_element_type=jnp.float32
    )


def inner_kernel(
    off_hbm, cnt_hbm, weight_hbm, bias_hbm, feat_hbm, adj_hbm, cot_hbm,
    act_hbm, place_out, grad_ref, partial_ref, sums_ref, weight_ref, bias_ref, dense, own_ref,
    cot_rim, adj,
    off_ref, cnt_ref, place_ref, feat, adj_rim, cot, act, agg_all, sems,
):
    blocks, slots, block_rows, _ = adj_hbm.shape
    rows, width = feat_hbm.shape
    count = blocks - 2 * BAND
    rim = BAND * block_rows
    inner = count * block_rows
    scalars = [
        pltpu.make_async_copy(off_hbm, off_ref, sems.at[12]),
        pltpu.make_async_copy(cnt_hbm, cnt_ref, sems.at[13]),
    ]
    copies = [
        pltpu.make_async_copy(feat_hbm, feat.at[pl.ds(0, rows)], sems.at[0]),
        pltpu.make_async_copy(adj_hbm.at[pl.ds(BAND, count)], adj, sems.at[1]),
        pltpu.make_async_copy(weight_hbm, weight_ref, sems.at[2]),
        pltpu.make_async_copy(bias_hbm, bias_ref, sems.at[3]),
        pltpu.make_async_copy(cot_hbm.at[pl.ds(rim, inner)], cot, sems.at[4]),
        pltpu.make_async_copy(adj_hbm.at[pl.ds(0, BAND)], adj_rim.at[pl.ds(0, BAND)], sems.at[5]),
        pltpu.make_async_copy(
            adj_hbm.at[pl.ds(blocks - BAND, BAND)], adj_rim.at[pl.ds(BAND, BAND)], sems.at[6]
        ),
        pltpu.make_async_copy(cot_hbm.at[pl.ds(0, rim)], cot_rim.at[pl.ds(0, rim)], sems.at[7]),
        pltpu.make_async_copy(
            cot_hbm.at[pl.ds(rows - rim, rim)], cot_rim.at[pl.ds(rim, rim)], sems.at[8]
        ),
    ]
    for copy in scalars + copies:
        copy.start()
    feat[rows:] = jnp.zeros((block_rows, width), jnp.bfloat16)
    dense[...] = jnp.zeros_like(dense)
    for copy in scalars:
        copy.wait()
    write_places(off_ref, cnt_ref, place_ref, blocks, slots)
    place_copy = pltpu.make_async_copy(place_ref, place_out, sems.at[14])
    place_copy.start()
    for copy in copies[:5]:
        copy.wait()
    weight = weight_ref[...]
    bias = bias_ref[...]
    sums = jnp.zeros((8, width), jnp.float32)
    for step in range(0, count, 2):
        for block in (step, step + 1):
            places = places_of(place_ref, block + BAND, slots)
            agg_all[block * block_rows : (block + 1) * block_rows] = jnp.dot(
                row_of(adj, block, slots), pick(feat, places, block_rows),
                preferred_element_type=jnp.float32,
            ).astype(jnp.bfloat16)
        here = pl.ds(step * block_rows, 2 * block_rows)
        preact = jnp.dot(agg_all[here], weight, preferred_element_type=jnp.float32) + bias
        act[here], grad = activate(preact, cot[here])
        grad_ref[here] = grad
        sums = sums + column_sums(grad)
    act_out = pltpu.make_async_copy(act, act_hbm.at[pl.ds(rim, inner)], sems.at[11])
    act_out.start()
    sums_ref[...] = sums
    partial_ref[...] = weight_terms(agg_all[...], grad_ref[...])
    for copy in copies[5:]:
        copy.wait()
    for side, first in enumerate((0, blocks - BAND)):
        for row in range(BAND):
            here = pl.ds(row * block_rows, block_rows)
            for slot, place in enumerate(places_of(place_ref, first + row, slots)):
                dense[side, place, here] = adj_rim[side * BAND + row, slot]
    own_ref[:rim] = jnp.dot(
        side_by_side(dense, 0, BAND, 3 * BAND), feat[: 2 * rim],
        preferred_element_type=jnp.float32,
    )
    own_ref[rim:] = jnp.dot(
        side_by_side(dense, 1, 0, 2 * BAND), feat[rows - 2 * rim : rows],
        preferred_element_type=jnp.float32,
    )
    act_out.wait()
    place_copy.wait()


def rim_kernel(
    weight_ref, bias_ref, own_ref, second_ref, first_ref, dense, cot_ref, partial_ref, sums_ref,
    act_ref, grad_ref, send_ref, keep_ref,
    halo, agg_all,
):
    rim, width = first_ref.shape
    odd = place_in_mesh() & 1
    halo[pl.ds(pl.multiple_of((1 - odd) * rim, rim), rim)] = first_ref[...]
    halo[pl.ds(pl.multiple_of(odd * rim, rim), rim)] = second_ref[...]
    weight = weight_ref[...]
    bias = bias_ref[...]
    sums = sums_ref[...]
    for side, first in enumerate((0, 2 * BAND)):
        here = pl.ds(side * rim, rim)
        agg = own_ref[here] + jnp.dot(
            side_by_side(dense, side, first, first + BAND), halo[here],
            preferred_element_type=jnp.float32,
        )
        agg = agg.astype(jnp.bfloat16)
        agg_all[here] = agg
        preact = jnp.dot(agg, weight, preferred_element_type=jnp.float32) + bias
        act_ref[here], grad = activate(preact, cot_ref[here])
        grad_ref[here] = grad
        sums = sums + column_sums(grad)
    half = width // 2
    partial = partial_ref[...] + weight_terms(agg_all[...], grad_ref[...])
    bias_tail = jnp.broadcast_to(jnp.sum(sums, axis=0, keepdims=True), (TAIL, width))
    upper = jnp.concatenate([partial[:half], bias_tail], 0)
    lower = jnp.concatenate([partial[half:], jnp.zeros_like(bias_tail)], 0)
    first = core_side() == 0
    keep_ref[...] = jnp.where(first, upper, lower)
    send_ref[...] = jnp.where(first, lower, upper).astype(send_ref.dtype)


def scatter_rows(places, upstream, adj_ref, spread):
    _, slots, block_rows, _ = adj_ref.shape
    for step, targets in enumerate(places):
        terms = jnp.dot(
            upstream[:, step * block_rows : (step + 1) * block_rows],
            row_of(adj_ref, step, slots),
            preferred_element_type=jnp.float32,
        )
        for slot, target in enumerate(targets):
            spread[target] += terms[:, slot * block_rows : (slot + 1) * block_rows]


def rim_back_kernel(
    weight_ref, dense, grad_ref, act_ref, act_in,
    act_hbm, spread, first_ref, second_ref, mark_ref,
    spill, sems,
):
    block_rows = dense.shape[3]
    rim = BAND * block_rows
    rows = act_hbm.shape[0]
    copies = [
        pltpu.make_async_copy(act_ref.at[pl.ds(0, rim)], act_hbm.at[pl.ds(0, rim)], sems.at[0]),
        pltpu.make_async_copy(
            act_ref.at[pl.ds(rim, rim)], act_hbm.at[pl.ds(rows - rim, rim)], sems.at[1]
        ),
    ]
    for copy in copies:
        copy.start()
    weight = weight_ref[...]
    for side, (inside, outside) in enumerate(((BAND, 0), (0, 2 * BAND))):
        terms = jnp.dot(
            to_upstream(weight, grad_ref[side * rim : (side + 1) * rim]),
            side_by_side(dense, side, 0, 3 * BAND),
            preferred_element_type=jnp.float32,
        )
        for block in range(2 * BAND):
            lane = (inside + block) * block_rows
            spread[side * 2 * BAND + block] = terms[:, lane : lane + block_rows]
        for block in range(BAND):
            lane = (outside + block) * block_rows
            here = pl.ds(side * rim + block * block_rows, block_rows)
            spill[here] = terms[:, lane : lane + block_rows].T.astype(jnp.bfloat16)
    odd = place_in_mesh() & 1
    first_ref[...] = spill[pl.ds(pl.multiple_of((1 - odd) * rim, rim), rim)]
    second_ref[...] = spill[pl.ds(pl.multiple_of(odd * rim, rim), rim)]
    mark_ref[...] = jnp.zeros_like(mark_ref)
    for copy in copies:
        copy.wait()


def inner_back_kernel(
    place_in, weight_ref, adj_ref, grad_ref, rim_spread,
    whole_hbm, edge_ref, mark_ref,
    place_ref, spread, out, sems,
):
    fetch = pltpu.make_async_copy(place_in, place_ref, sems.at[1])
    fetch.start()
    count, slots, block_rows, _ = adj_ref.shape
    blocks = place_ref.shape[0] // slots
    rim = BAND * block_rows
    spread[: 2 * BAND] = rim_spread[: 2 * BAND]
    spread[2 * BAND :] = jnp.zeros_like(spread[2 * BAND :])
    spread[blocks - 2 * BAND : blocks] = rim_spread[2 * BAND :]
    upstream = to_upstream(weight_ref[...], grad_ref[...])
    fetch.wait()
    scatter_rows(
        [places_of(place_ref, step + BAND, slots) for step in range(count)],
        upstream, adj_ref, spread,
    )
    for step in range(count):
        here = pl.ds(step * block_rows, block_rows)
        out[here] = spread[BAND + step].T.astype(jnp.bfloat16)
    finish = pltpu.make_async_copy(out, whole_hbm.at[pl.ds(rim, count * block_rows)], sems.at[0])
    finish.start()
    mark_ref[...] = jnp.zeros_like(mark_ref)
    for block in range(BAND):
        edge_ref[block * block_rows : (block + 1) * block_rows] = spread[block].T
        after = BAND + block
        edge_ref[after * block_rows : (after + 1) * block_rows] = spread[blocks - BAND + block].T
    finish.wait()


def add_kernel(parts, *refs):
    values = [ref[...].astype(jnp.float32) for ref in refs[:parts]]
    total = values[0] + values[1]
    if parts == 4:
        total = total + (values[2] + values[3])
    refs[-1][...] = total.astype(refs[-1].dtype)


def last_kernel(
    scale, own_ref, other_ref, edge_ref, first_ref, second_ref, whole_in,
    weight_out, bias_out, whole_hbm,
    out, sums, bias, sems,
):
    half = sums.shape[0] // 2
    rim = first_ref.shape[0]
    rows = whole_hbm.shape[0]
    copies = [
        pltpu.make_async_copy(sums, weight_out, sems.at[0]),
        pltpu.make_async_copy(bias, bias_out, sems.at[1]),
        pltpu.make_async_copy(out.at[pl.ds(0, rim)], whole_hbm.at[pl.ds(0, rim)], sems.at[2]),
        pltpu.make_async_copy(
            out.at[pl.ds(rim, rim)], whole_hbm.at[pl.ds(rows - rim, rim)], sems.at[3]
        ),
    ]
    side = core_side()
    own_rows = pl.ds(pl.multiple_of(side * half, half), half)
    other_rows = pl.ds(pl.multiple_of((1 - side) * half, half), half)
    own = own_ref[...].astype(jnp.float32) * scale
    other = other_ref[...].astype(jnp.float32) * scale
    sums[own_rows] = own[:half]
    sums[other_rows] = other[:half]
    copies[0].start()
    bias[...] = jnp.where(side == 0, own[half : half + 1], other[half : half + 1])
    copies[1].start()
    odd = place_in_mesh() & 1
    for base, spill_ref in (((1 - odd) * rim, first_ref), (odd * rim, second_ref)):
        here = pl.ds(pl.multiple_of(base, rim), rim)
        out[here] = (edge_ref[here] + spill_ref[...].astype(jnp.float32)).astype(jnp.bfloat16)
    for copy in copies[2:]:
        copy.start()
    for copy in copies:
        copy.wait()


def add(values, dtype, after=()):
    size = values[0].size
    return pl.pallas_call(
        functools.partial(add_kernel, len(values)),
        out_shape=jax.ShapeDtypeStruct(values[0].shape, dtype),
        in_specs=[pl.BlockSpec(memory_space=pltpu.VMEM)] * len(values)
        + [pl.BlockSpec(memory_space=pl.ANY)] * len(after),
        compiler_params=pltpu.CompilerParams(vmem_limit_bytes=2 * MIB),
        cost_estimate=pl.CostEstimate(
            flops=size * len(values), bytes_accessed=8 * size, transcendentals=0
        ),
        name="add_halves",
    )(*values, *after)


def swap(value, masks):
    pairs = [(i, i ^ mask) for i, mask in enumerate(masks) if mask]
    return lax.ppermute(value, AXES, pairs)


def with_next(value, count, closed):
    pairs = [(i, (i + 1 if i & 1 else i - 1) % count) for i in range(count)]
    return lax.ppermute(value, AXES, pairs if closed else pairs[1:-1])


def sum_halves(send, keep, count, core_bit, marks):
    others = [bit for bit in range(count.bit_length() - 1) if bit != core_bit]
    groups = [others[i : i + 2] for i in range(0, len(others), 2)]
    groups[0] = groups[0][::-1]
    total = add([keep, swap(send, [1 << core_bit] * count)], jnp.bfloat16, marks.get("core", ()))
    for step in range(len(groups)):
        masks = []
        for group in (groups[step], groups[len(groups) - 1 - step]):
            if len(groups[0]) != len(groups[-1]):
                group = groups[step]
            bits = [1 << bit for bit in group]
            if group[1:]:
                both = bits[0] | bits[1]
                near = group is groups[0]
                bits = [bits[0], both, bits[1]] if near else [*bits, both]
            masks.append(bits)
        parts = [total] + [
            swap(total, [masks[(i >> core_bit) & 1][k] for i in range(count)])
            for k in range(len(masks[0]))
        ]
        last = step == len(groups) - 1
        name = "last" if last else step
        total = add(parts, jnp.bfloat16, marks.get(name, ()))
    return total


def on_device(features, adj_values, adj_offset, adj_count, weight, bias_vector, cotangent):
    blocks, slots = adj_offset.shape
    block_rows = adj_values.shape[2]
    rows, width = features.shape
    rim = BAND * block_rows
    inner = rows - 2 * rim
    cols = lax.axis_size("cols")
    count = lax.axis_size("rows") * cols
    vmem = pl.BlockSpec(memory_space=pltpu.VMEM)
    hbm = pl.BlockSpec(memory_space=pltpu.HBM)
    anywhere = pl.BlockSpec(memory_space=pl.ANY)
    place_scratch = pltpu.SMEM((blocks * slots,), jnp.int32)
    bias_row = bias_vector.reshape(1, width)

    def in_hbm(value):
        return pltpu.with_memory_space_constraint(value, pltpu.HBM)

    def shape(*sizes, dtype=jnp.bfloat16):
        return jax.ShapeDtypeStruct(sizes, dtype)

    def params(mib):
        return pltpu.CompilerParams(vmem_limit_bytes=mib * MIB)

    def cost(share):
        return pl.CostEstimate(
            flops=int(1.2e9 * share), bytes_accessed=int(6e6 * share),
            transcendentals=int(8e5 * share),
        )

    offsets = in_hbm(adj_offset.T)
    counts = in_hbm(adj_count)
    core_bit = cols.bit_length() - 1
    first_rim, second_rim = pl.pallas_call(
        halo_kernel,
        out_shape=(shape(rim, width), shape(rim, width)),
        in_specs=[hbm],
        out_specs=(vmem, vmem),
        scratch_shapes=[pltpu.SemaphoreType.DMA((2,))],
        compiler_params=params(2),
        cost_estimate=cost(0.05),
        name="halo_rows",
    )(in_hbm(features))
    second_halo = with_next(second_rim, count, True)
    first_halo = swap(first_rim, [1] * count)
    (
        activated, places, grad_inner, partial, sums, weight_near, bias_near, dense, own_part,
        cot_rim, adj_inner,
    ) = pl.pallas_call(
        inner_kernel,
        out_shape=(
            shape(rows, width),
            shape(blocks * slots, dtype=jnp.int32),
            shape(inner, width),
            shape(width, width, dtype=jnp.float32),
            shape(8, width, dtype=jnp.float32),
            shape(width, width),
            shape(1, width, dtype=jnp.float32),
            shape(2, 3 * BAND + 1, rim, block_rows),
            shape(2 * rim, width, dtype=jnp.float32),
            shape(2 * rim, width),
            shape(blocks - 2 * BAND, slots, block_rows, block_rows),
        ),
        in_specs=[hbm] * 7,
        out_specs=(hbm, anywhere) + (vmem,) * 9,
        scratch_shapes=[
            pltpu.SMEM((slots, blocks), jnp.int32),
            pltpu.SMEM((blocks,), jnp.int32),
            place_scratch,
            pltpu.VMEM((rows + block_rows, width), jnp.bfloat16),
            pltpu.VMEM((2 * BAND, slots, block_rows, block_rows), jnp.bfloat16),
            pltpu.VMEM((inner, width), jnp.bfloat16),
            pltpu.VMEM((inner, width), jnp.bfloat16),
            pltpu.VMEM((inner, width), jnp.bfloat16),
            pltpu.SemaphoreType.DMA((15,)),
        ],
        compiler_params=params(20),
        cost_estimate=cost(0.5),
        name="inner_rows",
    )(
        offsets, counts,
        *(in_hbm(x) for x in (weight, bias_row, features, adj_values, cotangent)),
    )
    half_shape = (width // 2 + TAIL, width)
    act_rim, grad_rim, send, keep = pl.pallas_call(
        rim_kernel,
        out_shape=(
            shape(2 * rim, width),
            shape(2 * rim, width),
            shape(*half_shape),
            shape(*half_shape, dtype=jnp.float32),
        ),
        in_specs=[vmem] * 9,
        out_specs=(vmem,) * 4,
        scratch_shapes=[
            pltpu.VMEM((2 * rim, width), jnp.bfloat16),
            pltpu.VMEM((2 * rim, width), jnp.bfloat16),
        ],
        compiler_params=params(12),
        cost_estimate=cost(0.2),
        name="rim_rows",
    )(
        weight_near, bias_near, own_part, second_halo, first_halo, dense, cot_rim, partial, sums,
    )
    mark = shape(8, 128, dtype=jnp.float32)
    activated, rim_spread, first_spill, second_spill, first_mark = pl.pallas_call(
        rim_back_kernel,
        out_shape=(
            shape(rows, width),
            shape(4 * BAND, width, block_rows, dtype=jnp.float32),
            shape(rim, width),
            shape(rim, width),
            mark,
        ),
        in_specs=[vmem] * 4 + [hbm],
        out_specs=(hbm,) + (vmem,) * 4,
        scratch_shapes=[
            pltpu.VMEM((2 * rim, width), jnp.bfloat16),
            pltpu.SemaphoreType.DMA((2,)),
        ],
        input_output_aliases={4: 0},
        compiler_params=params(12),
        cost_estimate=cost(0.2),
        name="rim_rows_back",
    )(weight_near, dense, grad_rim, act_rim, activated)
    first_part = swap(first_spill, [1] * count)
    second_part = with_next(second_spill, count, False)
    grad_whole, edges, second_mark = pl.pallas_call(
        inner_back_kernel,
        out_shape=(shape(rows, width), shape(2 * rim, width, dtype=jnp.float32), mark),
        in_specs=[anywhere] + [vmem] * 4,
        out_specs=(hbm, vmem, vmem),
        scratch_shapes=[
            place_scratch,
            pltpu.VMEM((blocks + 1, width, block_rows), jnp.float32),
            pltpu.VMEM((inner, width), jnp.bfloat16),
            pltpu.SemaphoreType.DMA((2,)),
        ],
        compiler_params=params(12),
        cost_estimate=cost(0.3),
        name="inner_rows_back",
    )(places, weight_near, adj_inner, grad_inner, rim_spread)
    marks = {"core": (first_mark,), "last": (second_mark, second_part)}
    own_half = sum_halves(send, keep, count, core_bit, marks)
    other_half = swap(own_half, [1 << core_bit] * count)
    norm_scale = 1.0 / math.sqrt(rows * count)
    grad_weight, grad_bias, grad_features = pl.pallas_call(
        functools.partial(last_kernel, norm_scale),
        out_shape=(
            shape(width, width, dtype=jnp.float32),
            shape(1, width, dtype=jnp.float32),
            shape(rows, width),
        ),
        in_specs=[vmem] * 5 + [hbm],
        out_specs=(hbm, hbm, hbm),
        scratch_shapes=[
            pltpu.VMEM((2 * rim, width), jnp.bfloat16),
            pltpu.VMEM((width, width), jnp.float32),
            pltpu.VMEM((1, width), jnp.float32),
            pltpu.SemaphoreType.DMA((4,)),
        ],
        input_output_aliases={5: 2},
        compiler_params=params(8),
        name="last_step",
    )(own_half, other_half, edges, first_part, second_part, grad_whole)
    return (activated, grad_features, grad_weight, grad_bias.reshape(width))


def solution(mesh):
    return jax.shard_map(
        on_device,
        mesh=mesh,
        in_specs=(
            P(AXES, None),
            P(AXES, None, None, None),
            P(AXES, None),
            P(AXES),
            P(),
            P(),
            P(AXES, None),
        ),
        out_specs=(P(AXES, None), P(AXES, None), P(), P()),
        check_vma=False,
    )
```

```python
import functools
import math

import jax
import jax.numpy as jnp
from jax import lax
from jax.experimental import pallas as pl
from jax.experimental.pallas import tpu as pltpu
from jax.sharding import PartitionSpec as P

BAND = 2
TAIL = 8
AXES = ("rows", "cols")
MIB = 1024 * 1024


def row_of(adj_ref, block, slots):
    return jnp.concatenate([adj_ref[block, slot] for slot in range(slots)], 1)


def pick(source, places, block_rows):
    return jnp.concatenate(
        [
            source[pl.ds(pl.multiple_of(place * block_rows, block_rows), block_rows)]
            for place in places
        ],
        0,
    )


def write_places(off_ref, cnt_ref, place_ref, blocks, slots):
    for block in range(blocks):
        if block < BAND:
            shift, dump = BAND, 3 * BAND
        elif block < blocks - BAND:
            shift, dump = 0, blocks
        else:
            shift, dump = 2 * BAND - blocks, 3 * BAND
        for slot in range(slots):
            place_ref[block * slots + slot] = jnp.where(
                slot < cnt_ref[block], block + shift + off_ref[slot, block], dump
            )


def places_of(place_ref, block, slots):
    return [place_ref[block * slots + slot] for slot in range(slots)]


def side_by_side(dense, side, first, last):
    return jnp.concatenate([dense[side, place] for place in range(first, last)], 1)


def place_in_mesh():
    return lax.axis_index("rows") * lax.axis_size("cols") + lax.axis_index("cols")


def core_side():
    return lax.axis_index("rows") & 1


def halo_kernel(feat_hbm, first_ref, second_ref, sems):
    rows = feat_hbm.shape[0]
    rim = first_ref.shape[0]
    odd = place_in_mesh() & 1
    last = rows - rim
    starts = ((1 - odd) * last, odd * last)
    copies = [
        pltpu.make_async_copy(
            feat_hbm.at[pl.ds(pl.multiple_of(start, rim), rim)], out_ref, sems.at[i]
        )
        for i, (start, out_ref) in enumerate(zip(starts, (first_ref, second_ref)))
    ]
    for copy in copies:
        copy.start()
    for copy in copies:
        copy.wait()


def activate(preact, cotangent):
    gate = 1.0 / (1.0 + jnp.exp(-preact))
    grad = cotangent.astype(jnp.float32) * gate * (1.0 + preact * (1.0 - gate))
    return (preact * gate).astype(jnp.bfloat16), grad.astype(jnp.bfloat16)


def column_sums(grad):
    rows, width = grad.shape
    return jnp.sum(grad.astype(jnp.float32).reshape(rows // 8, 8, width), axis=0)


def to_upstream(weight, grad):
    return lax.dot_general(
        weight, grad, (((1,), (1,)), ((), ())), preferred_element_type=jnp.float32
    ).astype(jnp.bfloat16)


def weight_terms(agg, grad):
    return lax.dot_general(
        agg, grad, (((0,), (0,)), ((), ())), preferred_element_type=jnp.float32
    )


def inner_kernel(
    off_hbm, cnt_hbm, weight_hbm, bias_hbm, feat_hbm, adj_hbm, cot_hbm,
    act_hbm, place_out, grad_ref, partial_ref, sums_ref, weight_ref, bias_ref, dense, own_ref,
    cot_rim, adj,
    off_ref, cnt_ref, place_ref, feat, adj_rim, cot, act, agg_all, sems,
):
    blocks, slots, block_rows, _ = adj_hbm.shape
    rows, width = feat_hbm.shape
    count = blocks - 2 * BAND
    rim = BAND * block_rows
    inner = count * block_rows
    scalars = [
        pltpu.make_async_copy(off_hbm, off_ref, sems.at[12]),
        pltpu.make_async_copy(cnt_hbm, cnt_ref, sems.at[13]),
    ]
    copies = [
        pltpu.make_async_copy(feat_hbm, feat.at[pl.ds(0, rows)], sems.at[0]),
        pltpu.make_async_copy(adj_hbm.at[pl.ds(BAND, count)], adj, sems.at[1]),
        pltpu.make_async_copy(weight_hbm, weight_ref, sems.at[2]),
        pltpu.make_async_copy(bias_hbm, bias_ref, sems.at[3]),
        pltpu.make_async_copy(cot_hbm.at[pl.ds(rim, inner)], cot, sems.at[4]),
        pltpu.make_async_copy(adj_hbm.at[pl.ds(0, BAND)], adj_rim.at[pl.ds(0, BAND)], sems.at[5]),
        pltpu.make_async_copy(
            adj_hbm.at[pl.ds(blocks - BAND, BAND)], adj_rim.at[pl.ds(BAND, BAND)], sems.at[6]
        ),
        pltpu.make_async_copy(cot_hbm.at[pl.ds(0, rim)], cot_rim.at[pl.ds(0, rim)], sems.at[7]),
        pltpu.make_async_copy(
            cot_hbm.at[pl.ds(rows - rim, rim)], cot_rim.at[pl.ds(rim, rim)], sems.at[8]
        ),
    ]
    for copy in scalars + copies:
        copy.start()
    feat[rows:] = jnp.zeros((block_rows, width), jnp.bfloat16)
    dense[...] = jnp.zeros_like(dense)
    for copy in scalars:
        copy.wait()
    write_places(off_ref, cnt_ref, place_ref, blocks, slots)
    place_copy = pltpu.make_async_copy(place_ref, place_out, sems.at[14])
    place_copy.start()
    for copy in copies[:5]:
        copy.wait()
    weight = weight_ref[...]
    bias = bias_ref[...]
    sums = jnp.zeros((8, width), jnp.float32)
    for step in range(0, count, 2):
        for block in (step, step + 1):
            places = places_of(place_ref, block + BAND, slots)
            agg_all[block * block_rows : (block + 1) * block_rows] = jnp.dot(
                row_of(adj, block, slots), pick(feat, places, block_rows),
                preferred_element_type=jnp.float32,
            ).astype(jnp.bfloat16)
        here = pl.ds(step * block_rows, 2 * block_rows)
        preact = jnp.dot(agg_all[here], weight, preferred_element_type=jnp.float32) + bias
        act[here], grad = activate(preact, cot[here])
        grad_ref[here] = grad
        sums = sums + column_sums(grad)
    act_out = pltpu.make_async_copy(act, act_hbm.at[pl.ds(rim, inner)], sems.at[11])
    act_out.start()
    sums_ref[...] = sums
    partial_ref[...] = weight_terms(agg_all[...], grad_ref[...])
    for copy in copies[5:]:
        copy.wait()
    for side, first in enumerate((0, blocks - BAND)):
        for row in range(BAND):
            here = pl.ds(row * block_rows, block_rows)
            for slot, place in enumerate(places_of(place_ref, first + row, slots)):
                dense[side, place, here] = adj_rim[side * BAND + row, slot]
    own_ref[:rim] = jnp.dot(
        side_by_side(dense, 0, BAND, 3 * BAND), feat[: 2 * rim],
        preferred_element_type=jnp.float32,
    )
    own_ref[rim:] = jnp.dot(
        side_by_side(dense, 1, 0, 2 * BAND), feat[rows - 2 * rim : rows],
        preferred_element_type=jnp.float32,
    )
    act_out.wait()
    place_copy.wait()


def rim_kernel(
    weight_ref, bias_ref, own_ref, first_ref, second_ref, dense, cot_ref, partial_ref, sums_ref,
    act_ref, grad_ref, send_ref, keep_ref,
    halo, agg_all,
):
    rim, width = first_ref.shape
    odd = place_in_mesh() & 1
    halo[pl.ds(pl.multiple_of((1 - odd) * rim, rim), rim)] = first_ref[...]
    halo[pl.ds(pl.multiple_of(odd * rim, rim), rim)] = second_ref[...]
    weight = weight_ref[...]
    bias = bias_ref[...]
    sums = sums_ref[...]
    for side, first in enumerate((0, 2 * BAND)):
        here = pl.ds(side * rim, rim)
        agg = own_ref[here] + jnp.dot(
            side_by_side(dense, side, first, first + BAND), halo[here],
            preferred_element_type=jnp.float32,
        )
        agg = agg.astype(jnp.bfloat16)
        agg_all[here] = agg
        preact = jnp.dot(agg, weight, preferred_element_type=jnp.float32) + bias
        act_ref[here], grad = activate(preact, cot_ref[here])
        grad_ref[here] = grad
        sums = sums + column_sums(grad)
    half = width // 2
    partial = partial_ref[...] + weight_terms(agg_all[...], grad_ref[...])
    bias_tail = jnp.broadcast_to(jnp.sum(sums, axis=0, keepdims=True), (TAIL, width))
    upper = jnp.concatenate([partial[:half], bias_tail], 0)
    lower = jnp.concatenate([partial[half:], jnp.zeros_like(bias_tail)], 0)
    first = core_side() == 0
    keep_ref[...] = jnp.where(first, upper, lower)
    send_ref[...] = jnp.where(first, lower, upper).astype(send_ref.dtype)


def scatter_rows(places, upstream, adj_ref, spread):
    _, slots, block_rows, _ = adj_ref.shape
    for step, targets in enumerate(places):
        terms = jnp.dot(
            upstream[:, step * block_rows : (step + 1) * block_rows],
            row_of(adj_ref, step, slots),
            preferred_element_type=jnp.float32,
        )
        for slot, target in enumerate(targets):
            spread[target] += terms[:, slot * block_rows : (slot + 1) * block_rows]


def rim_back_kernel(
    weight_ref, dense, grad_ref, act_ref, act_in,
    act_hbm, spread, first_ref, second_ref, mark_ref,
    spill, sems,
):
    block_rows = dense.shape[3]
    rim = BAND * block_rows
    rows = act_hbm.shape[0]
    copies = [
        pltpu.make_async_copy(act_ref.at[pl.ds(0, rim)], act_hbm.at[pl.ds(0, rim)], sems.at[0]),
        pltpu.make_async_copy(
            act_ref.at[pl.ds(rim, rim)], act_hbm.at[pl.ds(rows - rim, rim)], sems.at[1]
        ),
    ]
    for copy in copies:
        copy.start()
    weight = weight_ref[...]
    for side, (inside, outside) in enumerate(((BAND, 0), (0, 2 * BAND))):
        terms = jnp.dot(
            to_upstream(weight, grad_ref[side * rim : (side + 1) * rim]),
            side_by_side(dense, side, 0, 3 * BAND),
            preferred_element_type=jnp.float32,
        )
        for block in range(2 * BAND):
            lane = (inside + block) * block_rows
            spread[side * 2 * BAND + block] = terms[:, lane : lane + block_rows]
        for block in range(BAND):
            lane = (outside + block) * block_rows
            here = pl.ds(side * rim + block * block_rows, block_rows)
            spill[here] = terms[:, lane : lane + block_rows].T.astype(jnp.bfloat16)
    odd = place_in_mesh() & 1
    first_ref[...] = spill[pl.ds(pl.multiple_of((1 - odd) * rim, rim), rim)]
    second_ref[...] = spill[pl.ds(pl.multiple_of(odd * rim, rim), rim)]
    mark_ref[...] = jnp.zeros_like(mark_ref)
    for copy in copies:
        copy.wait()


def inner_back_kernel(
    place_in, weight_ref, adj_ref, grad_ref, rim_spread,
    whole_hbm, edge_ref, mark_ref,
    place_ref, spread, out, sems,
):
    fetch = pltpu.make_async_copy(place_in, place_ref, sems.at[1])
    fetch.start()
    count, slots, block_rows, _ = adj_ref.shape
    blocks = place_ref.shape[0] // slots
    rim = BAND * block_rows
    spread[: 2 * BAND] = rim_spread[: 2 * BAND]
    spread[2 * BAND :] = jnp.zeros_like(spread[2 * BAND :])
    spread[blocks - 2 * BAND : blocks] = rim_spread[2 * BAND :]
    upstream = to_upstream(weight_ref[...], grad_ref[...])
    fetch.wait()
    scatter_rows(
        [places_of(place_ref, step + BAND, slots) for step in range(count)],
        upstream, adj_ref, spread,
    )
    for step in range(count):
        here = pl.ds(step * block_rows, block_rows)
        out[here] = spread[BAND + step].T.astype(jnp.bfloat16)
    finish = pltpu.make_async_copy(out, whole_hbm.at[pl.ds(rim, count * block_rows)], sems.at[0])
    finish.start()
    mark_ref[...] = jnp.zeros_like(mark_ref)
    for block in range(BAND):
        edge_ref[block * block_rows : (block + 1) * block_rows] = spread[block].T
        after = BAND + block
        edge_ref[after * block_rows : (after + 1) * block_rows] = spread[blocks - BAND + block].T
    finish.wait()


def add_kernel(parts, *refs):
    values = [ref[...].astype(jnp.float32) for ref in refs[:parts]]
    total = values[0] + values[1]
    if parts == 4:
        total = total + (values[2] + values[3])
    refs[-1][...] = total.astype(refs[-1].dtype)


def last_kernel(
    scale, own_ref, other_ref, edge_ref, first_ref, second_ref, whole_in,
    weight_out, bias_out, whole_hbm,
    out, sums, bias, sems,
):
    half = sums.shape[0] // 2
    rim = first_ref.shape[0]
    rows = whole_hbm.shape[0]
    copies = [
        pltpu.make_async_copy(sums, weight_out, sems.at[0]),
        pltpu.make_async_copy(bias, bias_out, sems.at[1]),
        pltpu.make_async_copy(out.at[pl.ds(0, rim)], whole_hbm.at[pl.ds(0, rim)], sems.at[2]),
        pltpu.make_async_copy(
            out.at[pl.ds(rim, rim)], whole_hbm.at[pl.ds(rows - rim, rim)], sems.at[3]
        ),
    ]
    side = core_side()
    own_rows = pl.ds(pl.multiple_of(side * half, half), half)
    other_rows = pl.ds(pl.multiple_of((1 - side) * half, half), half)
    own = own_ref[...].astype(jnp.float32) * scale
    other = other_ref[...].astype(jnp.float32) * scale
    sums[own_rows] = own[:half]
    sums[other_rows] = other[:half]
    copies[0].start()
    bias[...] = jnp.where(side == 0, own[half : half + 1], other[half : half + 1])
    copies[1].start()
    odd = place_in_mesh() & 1
    for base, spill_ref in (((1 - odd) * rim, first_ref), (odd * rim, second_ref)):
        here = pl.ds(pl.multiple_of(base, rim), rim)
        out[here] = (edge_ref[here] + spill_ref[...].astype(jnp.float32)).astype(jnp.bfloat16)
    for copy in copies[2:]:
        copy.start()
    for copy in copies:
        copy.wait()


def add(values, dtype, after=()):
    size = values[0].size
    return pl.pallas_call(
        functools.partial(add_kernel, len(values)),
        out_shape=jax.ShapeDtypeStruct(values[0].shape, dtype),
        in_specs=[pl.BlockSpec(memory_space=pltpu.VMEM)] * len(values)
        + [pl.BlockSpec(memory_space=pl.ANY)] * len(after),
        compiler_params=pltpu.CompilerParams(vmem_limit_bytes=2 * MIB),
        cost_estimate=pl.CostEstimate(
            flops=size * len(values), bytes_accessed=8 * size, transcendentals=0
        ),
        name="add_halves",
    )(*values, *after)


def swap(value, masks):
    pairs = [(i, i ^ mask) for i, mask in enumerate(masks) if mask]
    return lax.ppermute(value, AXES, pairs)


def with_next(value, count, closed):
    pairs = [(i, (i + 1 if i & 1 else i - 1) % count) for i in range(count)]
    return lax.ppermute(value, AXES, pairs if closed else pairs[1:-1])


def sum_halves(send, keep, count, core_bit, marks):
    others = [bit for bit in range(count.bit_length() - 1) if bit != core_bit]
    half = (len(others) + 1) // 2
    groups = [others[i::half] for i in range(half)]
    groups[0] = groups[0][::-1]
    total = add([keep, swap(send, [1 << core_bit] * count)], jnp.bfloat16, marks.get("core", ()))
    for step in range(len(groups)):
        masks = []
        for group in (groups[step], groups[len(groups) - 1 - step]):
            if len(groups[0]) != len(groups[-1]):
                group = groups[step]
            bits = [1 << bit for bit in group]
            if group[1:]:
                both = bits[0] | bits[1]
                near = group is groups[0]
                bits = [bits[0], both, bits[1]] if near else [*bits, both]
            masks.append(bits)
        parts = [total] + [
            swap(total, [masks[(i >> core_bit) & 1][k] for i in range(count)])
            for k in range(len(masks[0]))
        ]
        last = step == len(groups) - 1
        name = "last" if last else step
        total = add(parts, jnp.bfloat16, marks.get(name, ()))
    return total


def on_device(features, adj_values, adj_offset, adj_count, weight, bias_vector, cotangent):
    blocks, slots = adj_offset.shape
    block_rows = adj_values.shape[2]
    rows, width = features.shape
    rim = BAND * block_rows
    inner = rows - 2 * rim
    cols = lax.axis_size("cols")
    count = lax.axis_size("rows") * cols
    vmem = pl.BlockSpec(memory_space=pltpu.VMEM)
    hbm = pl.BlockSpec(memory_space=pltpu.HBM)
    anywhere = pl.BlockSpec(memory_space=pl.ANY)
    place_scratch = pltpu.SMEM((blocks * slots,), jnp.int32)
    bias_row = bias_vector.reshape(1, width)

    def in_hbm(value):
        return pltpu.with_memory_space_constraint(value, pltpu.HBM)

    def shape(*sizes, dtype=jnp.bfloat16):
        return jax.ShapeDtypeStruct(sizes, dtype)

    def params(mib):
        return pltpu.CompilerParams(vmem_limit_bytes=mib * MIB)

    def cost(share):
        return pl.CostEstimate(
            flops=int(1.2e9 * share), bytes_accessed=int(6e6 * share),
            transcendentals=int(8e5 * share),
        )

    offsets = in_hbm(adj_offset.T)
    counts = in_hbm(adj_count)
    core_bit = cols.bit_length() - 1
    first_rim, second_rim = pl.pallas_call(
        halo_kernel,
        out_shape=(shape(rim, width), shape(rim, width)),
        in_specs=[hbm],
        out_specs=(vmem, vmem),
        scratch_shapes=[pltpu.SemaphoreType.DMA((2,))],
        compiler_params=params(2),
        cost_estimate=cost(0.05),
        name="halo_rows",
    )(in_hbm(features))
    first_halo = swap(first_rim, [1] * count)
    second_halo = with_next(second_rim, count, True)
    (
        activated, places, grad_inner, partial, sums, weight_near, bias_near, dense, own_part,
        cot_rim, adj_inner,
    ) = pl.pallas_call(
        inner_kernel,
        out_shape=(
            shape(rows, width),
            shape(blocks * slots, dtype=jnp.int32),
            shape(inner, width),
            shape(width, width, dtype=jnp.float32),
            shape(8, width, dtype=jnp.float32),
            shape(width, width),
            shape(1, width, dtype=jnp.float32),
            shape(2, 3 * BAND + 1, rim, block_rows),
            shape(2 * rim, width, dtype=jnp.float32),
            shape(2 * rim, width),
            shape(blocks - 2 * BAND, slots, block_rows, block_rows),
        ),
        in_specs=[hbm] * 7,
        out_specs=(hbm, anywhere) + (vmem,) * 9,
        scratch_shapes=[
            pltpu.SMEM((slots, blocks), jnp.int32),
            pltpu.SMEM((blocks,), jnp.int32),
            place_scratch,
            pltpu.VMEM((rows + block_rows, width), jnp.bfloat16),
            pltpu.VMEM((2 * BAND, slots, block_rows, block_rows), jnp.bfloat16),
            pltpu.VMEM((inner, width), jnp.bfloat16),
            pltpu.VMEM((inner, width), jnp.bfloat16),
            pltpu.VMEM((inner, width), jnp.bfloat16),
            pltpu.SemaphoreType.DMA((15,)),
        ],
        compiler_params=params(20),
        cost_estimate=cost(0.5),
        name="inner_rows",
    )(
        offsets, counts,
        *(in_hbm(x) for x in (weight, bias_row, features, adj_values, cotangent)),
    )
    half_shape = (width // 2 + TAIL, width)
    act_rim, grad_rim, send, keep = pl.pallas_call(
        rim_kernel,
        out_shape=(
            shape(2 * rim, width),
            shape(2 * rim, width),
            shape(*half_shape),
            shape(*half_shape, dtype=jnp.float32),
        ),
        in_specs=[vmem] * 9,
        out_specs=(vmem,) * 4,
        scratch_shapes=[
            pltpu.VMEM((2 * rim, width), jnp.bfloat16),
            pltpu.VMEM((2 * rim, width), jnp.bfloat16),
        ],
        compiler_params=params(12),
        cost_estimate=cost(0.2),
        name="rim_rows",
    )(
        weight_near, bias_near, own_part, first_halo, second_halo, dense, cot_rim, partial, sums,
    )
    mark = shape(8, 128, dtype=jnp.float32)
    activated, rim_spread, first_spill, second_spill, first_mark = pl.pallas_call(
        rim_back_kernel,
        out_shape=(
            shape(rows, width),
            shape(4 * BAND, width, block_rows, dtype=jnp.float32),
            shape(rim, width),
            shape(rim, width),
            mark,
        ),
        in_specs=[vmem] * 4 + [hbm],
        out_specs=(hbm,) + (vmem,) * 4,
        scratch_shapes=[
            pltpu.VMEM((2 * rim, width), jnp.bfloat16),
            pltpu.SemaphoreType.DMA((2,)),
        ],
        input_output_aliases={4: 0},
        compiler_params=params(12),
        cost_estimate=cost(0.2),
        name="rim_rows_back",
    )(weight_near, dense, grad_rim, act_rim, activated)
    first_part = swap(first_spill, [1] * count)
    second_part = with_next(second_spill, count, False)
    grad_whole, edges, second_mark = pl.pallas_call(
        inner_back_kernel,
        out_shape=(shape(rows, width), shape(2 * rim, width, dtype=jnp.float32), mark),
        in_specs=[anywhere] + [vmem] * 4,
        out_specs=(hbm, vmem, vmem),
        scratch_shapes=[
            place_scratch,
            pltpu.VMEM((blocks + 1, width, block_rows), jnp.float32),
            pltpu.VMEM((inner, width), jnp.bfloat16),
            pltpu.SemaphoreType.DMA((2,)),
        ],
        compiler_params=params(12),
        cost_estimate=cost(0.3),
        name="inner_rows_back",
    )(places, weight_near, adj_inner, grad_inner, rim_spread)
    marks = {"core": (first_mark,), "last": (second_mark, second_part)}
    own_half = sum_halves(send, keep, count, core_bit, marks)
    other_half = swap(own_half, [1 << core_bit] * count)
    norm_scale = 1.0 / math.sqrt(rows * count)
    grad_weight, grad_bias, grad_features = pl.pallas_call(
        functools.partial(last_kernel, norm_scale),
        out_shape=(
            shape(width, width, dtype=jnp.float32),
            shape(1, width, dtype=jnp.float32),
            shape(rows, width),
        ),
        in_specs=[vmem] * 5 + [hbm],
        out_specs=(hbm, hbm, hbm),
        scratch_shapes=[
            pltpu.VMEM((2 * rim, width), jnp.bfloat16),
            pltpu.VMEM((width, width), jnp.float32),
            pltpu.VMEM((1, width), jnp.float32),
            pltpu.SemaphoreType.DMA((4,)),
        ],
        input_output_aliases={5: 2},
        compiler_params=params(8),
        name="last_step",
    )(own_half, other_half, edges, first_part, second_part, grad_whole)
    return (activated, grad_features, grad_weight, grad_bias.reshape(width))


def solution(mesh):
    return jax.shard_map(
        on_device,
        mesh=mesh,
        in_specs=(
            P(AXES, None),
            P(AXES, None, None, None),
            P(AXES, None),
            P(AXES),
            P(),
            P(),
            P(AXES, None),
        ),
        out_specs=(P(AXES, None), P(AXES, None), P(), P()),
        check_vma=False,
    )
```

```python
import functools
import math

import jax
import jax.numpy as jnp
from jax import lax
from jax.experimental import pallas as pl
from jax.experimental.pallas import tpu as pltpu
from jax.sharding import PartitionSpec as P

BAND = 2
TAIL = 8
AXES = ("rows", "cols")
MIB = 1024 * 1024


def row_of(adj_ref, block, slots):
    return jnp.concatenate([adj_ref[block, slot] for slot in range(slots)], 1)


def pick(source, places, block_rows):
    return jnp.concatenate(
        [
            source[pl.ds(pl.multiple_of(place * block_rows, block_rows), block_rows)]
            for place in places
        ],
        0,
    )


def write_places(off_ref, cnt_ref, place_ref, blocks, slots):
    for block in range(blocks):
        if block < BAND:
            shift, dump = BAND, 3 * BAND
        elif block < blocks - BAND:
            shift, dump = 0, blocks
        else:
            shift, dump = 2 * BAND - blocks, 3 * BAND
        for slot in range(slots):
            place_ref[block * slots + slot] = jnp.where(
                slot < cnt_ref[block], block + shift + off_ref[slot, block], dump
            )


def places_of(place_ref, block, slots):
    return [place_ref[block * slots + slot] for slot in range(slots)]


def side_by_side(dense, side, first, last):
    return jnp.concatenate([dense[side, place] for place in range(first, last)], 1)


def place_in_mesh():
    return lax.axis_index("rows") * lax.axis_size("cols") + lax.axis_index("cols")


def core_side():
    return lax.axis_index("rows") & 1


def halo_kernel(feat_hbm, first_ref, second_ref, sems):
    rows = feat_hbm.shape[0]
    rim = first_ref.shape[0]
    odd = place_in_mesh() & 1
    last = rows - rim
    piece = rim // 4
    starts = ((1 - odd) * last, odd * last)
    copies = [
        pltpu.make_async_copy(
            feat_hbm.at[pl.ds(pl.multiple_of(start + part * piece, piece), piece)],
            out_ref.at[pl.ds(part * piece, piece)],
            sems.at[4 * i + part],
        )
        for i, (start, out_ref) in enumerate(zip(starts, (first_ref, second_ref)))
        for part in range(4)
    ]
    for copy in copies:
        copy.start()
    for copy in copies:
        copy.wait()


def activate(preact, cotangent):
    gate = 1.0 / (1.0 + jnp.exp(-preact))
    grad = cotangent.astype(jnp.float32) * gate * (1.0 + preact * (1.0 - gate))
    return (preact * gate).astype(jnp.bfloat16), grad.astype(jnp.bfloat16)


def column_sums(grad):
    rows, width = grad.shape
    return jnp.sum(grad.astype(jnp.float32).reshape(rows // 8, 8, width), axis=0)


def to_upstream(weight, grad):
    return lax.dot_general(
        weight, grad, (((1,), (1,)), ((), ())), preferred_element_type=jnp.float32
    ).astype(jnp.bfloat16)


def weight_terms(agg, grad):
    return lax.dot_general(
        agg, grad, (((0,), (0,)), ((), ())), preferred_element_type=jnp.float32
    )


def inner_kernel(
    off_hbm, cnt_hbm, weight_hbm, bias_hbm, feat_hbm, adj_hbm, cot_hbm,
    act_hbm, place_out, grad_ref, partial_ref, sums_ref, weight_ref, bias_ref, dense, own_ref,
    cot_rim, adj,
    off_ref, cnt_ref, place_ref, feat, adj_rim, cot, act, agg_all, sems,
):
    blocks, slots, block_rows, _ = adj_hbm.shape
    rows, width = feat_hbm.shape
    count = blocks - 2 * BAND
    rim = BAND * block_rows
    inner = count * block_rows
    scalars = [
        pltpu.make_async_copy(off_hbm, off_ref, sems.at[12]),
        pltpu.make_async_copy(cnt_hbm, cnt_ref, sems.at[13]),
    ]
    copies = [
        pltpu.make_async_copy(feat_hbm, feat.at[pl.ds(0, rows)], sems.at[0]),
        pltpu.make_async_copy(adj_hbm.at[pl.ds(BAND, count)], adj, sems.at[1]),
        pltpu.make_async_copy(weight_hbm, weight_ref, sems.at[2]),
        pltpu.make_async_copy(bias_hbm, bias_ref, sems.at[3]),
        pltpu.make_async_copy(cot_hbm.at[pl.ds(rim, inner)], cot, sems.at[4]),
        pltpu.make_async_copy(adj_hbm.at[pl.ds(0, BAND)], adj_rim.at[pl.ds(0, BAND)], sems.at[5]),
        pltpu.make_async_copy(
            adj_hbm.at[pl.ds(blocks - BAND, BAND)], adj_rim.at[pl.ds(BAND, BAND)], sems.at[6]
        ),
        pltpu.make_async_copy(cot_hbm.at[pl.ds(0, rim)], cot_rim.at[pl.ds(0, rim)], sems.at[7]),
        pltpu.make_async_copy(
            cot_hbm.at[pl.ds(rows - rim, rim)], cot_rim.at[pl.ds(rim, rim)], sems.at[8]
        ),
    ]
    for copy in scalars + copies:
        copy.start()
    feat[rows:] = jnp.zeros((block_rows, width), jnp.bfloat16)
    dense[...] = jnp.zeros_like(dense)
    for copy in scalars:
        copy.wait()
    write_places(off_ref, cnt_ref, place_ref, blocks, slots)
    place_copy = pltpu.make_async_copy(place_ref, place_out, sems.at[14])
    place_copy.start()
    for copy in copies[:5]:
        copy.wait()
    weight = weight_ref[...]
    bias = bias_ref[...]
    sums = jnp.zeros((8, width), jnp.float32)
    for step in range(0, count, 2):
        for block in (step, step + 1):
            places = places_of(place_ref, block + BAND, slots)
            agg_all[block * block_rows : (block + 1) * block_rows] = jnp.dot(
                row_of(adj, block, slots), pick(feat, places, block_rows),
                preferred_element_type=jnp.float32,
            ).astype(jnp.bfloat16)
        here = pl.ds(step * block_rows, 2 * block_rows)
        preact = jnp.dot(agg_all[here], weight, preferred_element_type=jnp.float32) + bias
        act[here], grad = activate(preact, cot[here])
        grad_ref[here] = grad
        sums = sums + column_sums(grad)
    act_out = pltpu.make_async_copy(act, act_hbm.at[pl.ds(rim, inner)], sems.at[11])
    act_out.start()
    sums_ref[...] = sums
    partial_ref[...] = weight_terms(agg_all[...], grad_ref[...])
    for copy in copies[5:]:
        copy.wait()
    for side, first in enumerate((0, blocks - BAND)):
        for row in range(BAND):
            here = pl.ds(row * block_rows, block_rows)
            for slot, place in enumerate(places_of(place_ref, first + row, slots)):
                dense[side, place, here] = adj_rim[side * BAND + row, slot]
    own_ref[:rim] = jnp.dot(
        side_by_side(dense, 0, BAND, 3 * BAND), feat[: 2 * rim],
        preferred_element_type=jnp.float32,
    )
    own_ref[rim:] = jnp.dot(
        side_by_side(dense, 1, 0, 2 * BAND), feat[rows - 2 * rim : rows],
        preferred_element_type=jnp.float32,
    )
    act_out.wait()
    place_copy.wait()


def rim_kernel(
    weight_ref, bias_ref, own_ref, first_ref, second_ref, dense, cot_ref, partial_ref, sums_ref,
    act_ref, grad_ref, send_ref, keep_ref,
    halo, agg_all, payload,
):
    rim, width = first_ref.shape
    odd = place_in_mesh() & 1
    halo[pl.ds(pl.multiple_of((1 - odd) * rim, rim), rim)] = first_ref[...]
    halo[pl.ds(pl.multiple_of(odd * rim, rim), rim)] = second_ref[...]
    weight = weight_ref[...]
    bias = bias_ref[...]
    sums = sums_ref[...]
    for side, first in enumerate((0, 2 * BAND)):
        here = pl.ds(side * rim, rim)
        agg = own_ref[here] + jnp.dot(
            side_by_side(dense, side, first, first + BAND), halo[here],
            preferred_element_type=jnp.float32,
        )
        agg = agg.astype(jnp.bfloat16)
        agg_all[here] = agg
        preact = jnp.dot(agg, weight, preferred_element_type=jnp.float32) + bias
        act_ref[here], grad = activate(preact, cot_ref[here])
        grad_ref[here] = grad
        sums = sums + column_sums(grad)
    half = width // 2
    partial = partial_ref[...] + weight_terms(agg_all[...], grad_ref[...])
    payload[0, :half] = partial[:half]
    payload[1, :half] = partial[half:]
    tail = jnp.zeros((TAIL, width), jnp.float32)
    payload[0, half:] = jnp.broadcast_to(jnp.sum(sums, axis=0, keepdims=True), tail.shape)
    payload[1, half:] = tail
    side = core_side()
    keep_ref[...] = payload[side]
    send_ref[...] = payload[1 - side].astype(send_ref.dtype)


def scatter_rows(places, upstream, adj_ref, spread):
    _, slots, block_rows, _ = adj_ref.shape
    for step, targets in enumerate(places):
        terms = jnp.dot(
            upstream[:, step * block_rows : (step + 1) * block_rows],
            row_of(adj_ref, step, slots),
            preferred_element_type=jnp.float32,
        )
        for slot, target in enumerate(targets):
            spread[target] += terms[:, slot * block_rows : (slot + 1) * block_rows]


def rim_back_kernel(
    weight_ref, dense, grad_ref, act_ref, act_in,
    act_hbm, spread, first_ref, second_ref, mark_ref,
    spill, sems,
):
    block_rows = dense.shape[3]
    rim = BAND * block_rows
    rows = act_hbm.shape[0]
    copies = [
        pltpu.make_async_copy(act_ref.at[pl.ds(0, rim)], act_hbm.at[pl.ds(0, rim)], sems.at[0]),
        pltpu.make_async_copy(
            act_ref.at[pl.ds(rim, rim)], act_hbm.at[pl.ds(rows - rim, rim)], sems.at[1]
        ),
    ]
    for copy in copies:
        copy.start()
    weight = weight_ref[...]
    for side, (inside, outside) in enumerate(((BAND, 0), (0, 2 * BAND))):
        terms = jnp.dot(
            to_upstream(weight, grad_ref[side * rim : (side + 1) * rim]),
            side_by_side(dense, side, 0, 3 * BAND),
            preferred_element_type=jnp.float32,
        )
        for block in range(2 * BAND):
            lane = (inside + block) * block_rows
            spread[side * 2 * BAND + block] = terms[:, lane : lane + block_rows]
        for block in range(BAND):
            lane = (outside + block) * block_rows
            here = pl.ds(side * rim + block * block_rows, block_rows)
            spill[here] = terms[:, lane : lane + block_rows].T.astype(jnp.bfloat16)
    odd = place_in_mesh() & 1
    first_ref[...] = spill[pl.ds(pl.multiple_of((1 - odd) * rim, rim), rim)]
    second_ref[...] = spill[pl.ds(pl.multiple_of(odd * rim, rim), rim)]
    mark_ref[...] = jnp.zeros_like(mark_ref)
    for copy in copies:
        copy.wait()


def inner_back_kernel(
    place_in, weight_ref, adj_ref, grad_ref, rim_spread,
    whole_hbm, edge_ref, mark_ref,
    place_ref, spread, out, sems,
):
    fetch = pltpu.make_async_copy(place_in, place_ref, sems.at[1])
    fetch.start()
    count, slots, block_rows, _ = adj_ref.shape
    blocks = place_ref.shape[0] // slots
    rim = BAND * block_rows
    spread[: 2 * BAND] = rim_spread[: 2 * BAND]
    spread[2 * BAND :] = jnp.zeros_like(spread[2 * BAND :])
    spread[blocks - 2 * BAND : blocks] = rim_spread[2 * BAND :]
    upstream = to_upstream(weight_ref[...], grad_ref[...])
    fetch.wait()
    scatter_rows(
        [places_of(place_ref, step + BAND, slots) for step in range(count)],
        upstream, adj_ref, spread,
    )
    for step in range(count):
        here = pl.ds(step * block_rows, block_rows)
        out[here] = spread[BAND + step].T.astype(jnp.bfloat16)
    finish = pltpu.make_async_copy(out, whole_hbm.at[pl.ds(rim, count * block_rows)], sems.at[0])
    finish.start()
    mark_ref[...] = jnp.zeros_like(mark_ref)
    for block in range(BAND):
        edge_ref[block * block_rows : (block + 1) * block_rows] = spread[block].T
        after = BAND + block
        edge_ref[after * block_rows : (after + 1) * block_rows] = spread[blocks - BAND + block].T
    finish.wait()


def add_kernel(parts, *refs):
    values = [ref[...].astype(jnp.float32) for ref in refs[:parts]]
    total = values[0] + values[1]
    if parts == 4:
        total = total + (values[2] + values[3])
    refs[-1][...] = total.astype(refs[-1].dtype)


def last_kernel(
    scale, own_ref, other_ref, edge_ref, first_ref, second_ref, whole_in,
    weight_out, bias_out, whole_hbm,
    out, sums, bias, sems,
):
    half = sums.shape[0] // 2
    rim = first_ref.shape[0]
    rows = whole_hbm.shape[0]
    copies = [
        pltpu.make_async_copy(sums, weight_out, sems.at[0]),
        pltpu.make_async_copy(bias, bias_out, sems.at[1]),
        pltpu.make_async_copy(out.at[pl.ds(0, rim)], whole_hbm.at[pl.ds(0, rim)], sems.at[2]),
        pltpu.make_async_copy(
            out.at[pl.ds(rim, rim)], whole_hbm.at[pl.ds(rows - rim, rim)], sems.at[3]
        ),
    ]
    side = core_side()
    own_rows = pl.ds(pl.multiple_of(side * half, half), half)
    other_rows = pl.ds(pl.multiple_of((1 - side) * half, half), half)
    own = own_ref[...].astype(jnp.float32) * scale
    other = other_ref[...].astype(jnp.float32) * scale
    sums[own_rows] = own[:half]
    sums[other_rows] = other[:half]
    copies[0].start()
    bias[...] = jnp.where(side == 0, own[half : half + 1], other[half : half + 1])
    copies[1].start()
    odd = place_in_mesh() & 1
    for base, spill_ref in (((1 - odd) * rim, first_ref), (odd * rim, second_ref)):
        here = pl.ds(pl.multiple_of(base, rim), rim)
        out[here] = (edge_ref[here] + spill_ref[...].astype(jnp.float32)).astype(jnp.bfloat16)
    for copy in copies[2:]:
        copy.start()
    for copy in copies:
        copy.wait()


def add(values, dtype, after=()):
    size = values[0].size
    return pl.pallas_call(
        functools.partial(add_kernel, len(values)),
        out_shape=jax.ShapeDtypeStruct(values[0].shape, dtype),
        in_specs=[pl.BlockSpec(memory_space=pltpu.VMEM)] * len(values)
        + [pl.BlockSpec(memory_space=pl.ANY)] * len(after),
        compiler_params=pltpu.CompilerParams(vmem_limit_bytes=2 * MIB),
        cost_estimate=pl.CostEstimate(
            flops=size * len(values), bytes_accessed=8 * size, transcendentals=0
        ),
        name="add_halves",
    )(*values, *after)


def swap(value, masks):
    pairs = [(i, i ^ mask) for i, mask in enumerate(masks) if mask]
    return lax.ppermute(value, AXES, pairs)


def with_next(value, count, closed):
    pairs = [(i, (i + 1 if i & 1 else i - 1) % count) for i in range(count)]
    return lax.ppermute(value, AXES, pairs if closed else pairs[1:-1])


def sum_halves(send, keep, count, core_bit, marks):
    others = [bit for bit in range(count.bit_length() - 1) if bit != core_bit]
    groups = [others[i : i + 2] for i in range(0, len(others), 2)]
    groups[0] = groups[0][::-1]
    total = add([keep, swap(send, [1 << core_bit] * count)], jnp.bfloat16, marks.get("core", ()))
    for step in range(len(groups)):
        masks = []
        for group in (groups[step], groups[len(groups) - 1 - step]):
            if len(groups[0]) != len(groups[-1]):
                group = groups[step]
            bits = [1 << bit for bit in group]
            if group[1:]:
                both = bits[0] | bits[1]
                near = group is groups[0]
                bits = [bits[0], both, bits[1]] if near else [*bits, both]
            masks.append(bits)
        parts = [total] + [
            swap(total, [masks[(i >> core_bit) & 1][k] for i in range(count)])
            for k in range(len(masks[0]))
        ]
        last = step == len(groups) - 1
        name = "last" if last else step
        total = add(parts, jnp.bfloat16, marks.get(name, ()))
    return total


def on_device(features, adj_values, adj_offset, adj_count, weight, bias_vector, cotangent):
    blocks, slots = adj_offset.shape
    block_rows = adj_values.shape[2]
    rows, width = features.shape
    rim = BAND * block_rows
    inner = rows - 2 * rim
    cols = lax.axis_size("cols")
    count = lax.axis_size("rows") * cols
    vmem = pl.BlockSpec(memory_space=pltpu.VMEM)
    hbm = pl.BlockSpec(memory_space=pltpu.HBM)
    anywhere = pl.BlockSpec(memory_space=pl.ANY)
    place_scratch = pltpu.SMEM((blocks * slots,), jnp.int32)
    bias_row = bias_vector.reshape(1, width)

    def in_hbm(value):
        return pltpu.with_memory_space_constraint(value, pltpu.HBM)

    def shape(*sizes, dtype=jnp.bfloat16):
        return jax.ShapeDtypeStruct(sizes, dtype)

    def params(mib):
        return pltpu.CompilerParams(vmem_limit_bytes=mib * MIB)

    def cost(share):
        return pl.CostEstimate(
            flops=int(1.2e9 * share), bytes_accessed=int(6e6 * share),
            transcendentals=int(8e5 * share),
        )

    offsets = in_hbm(adj_offset.T)
    counts = in_hbm(adj_count)
    core_bit = cols.bit_length() - 1
    first_rim, second_rim = pl.pallas_call(
        halo_kernel,
        out_shape=(shape(rim, width), shape(rim, width)),
        in_specs=[hbm],
        out_specs=(vmem, vmem),
        scratch_shapes=[pltpu.SemaphoreType.DMA((8,))],
        compiler_params=params(2),
        cost_estimate=cost(0.05),
        name="halo_rows",
    )(in_hbm(features))
    first_halo = swap(first_rim, [1] * count)
    second_halo = with_next(second_rim, count, True)
    (
        activated, places, grad_inner, partial, sums, weight_near, bias_near, dense, own_part,
        cot_rim, adj_inner,
    ) = pl.pallas_call(
        inner_kernel,
        out_shape=(
            shape(rows, width),
            shape(blocks * slots, dtype=jnp.int32),
            shape(inner, width),
            shape(width, width, dtype=jnp.float32),
            shape(8, width, dtype=jnp.float32),
            shape(width, width),
            shape(1, width, dtype=jnp.float32),
            shape(2, 3 * BAND + 1, rim, block_rows),
            shape(2 * rim, width, dtype=jnp.float32),
            shape(2 * rim, width),
            shape(blocks - 2 * BAND, slots, block_rows, block_rows),
        ),
        in_specs=[hbm] * 7,
        out_specs=(hbm, anywhere) + (vmem,) * 9,
        scratch_shapes=[
            pltpu.SMEM((slots, blocks), jnp.int32),
            pltpu.SMEM((blocks,), jnp.int32),
            place_scratch,
            pltpu.VMEM((rows + block_rows, width), jnp.bfloat16),
            pltpu.VMEM((2 * BAND, slots, block_rows, block_rows), jnp.bfloat16),
            pltpu.VMEM((inner, width), jnp.bfloat16),
            pltpu.VMEM((inner, width), jnp.bfloat16),
            pltpu.VMEM((inner, width), jnp.bfloat16),
            pltpu.SemaphoreType.DMA((15,)),
        ],
        compiler_params=params(20),
        cost_estimate=cost(0.5),
        name="inner_rows",
    )(
        offsets, counts,
        *(in_hbm(x) for x in (weight, bias_row, features, adj_values, cotangent)),
    )
    half_shape = (width // 2 + TAIL, width)
    act_rim, grad_rim, send, keep = pl.pallas_call(
        rim_kernel,
        out_shape=(
            shape(2 * rim, width),
            shape(2 * rim, width),
            shape(*half_shape),
            shape(*half_shape, dtype=jnp.float32),
        ),
        in_specs=[vmem] * 9,
        out_specs=(vmem,) * 4,
        scratch_shapes=[
            pltpu.VMEM((2 * rim, width), jnp.bfloat16),
            pltpu.VMEM((2 * rim, width), jnp.bfloat16),
            pltpu.VMEM((2,) + half_shape, jnp.float32),
        ],
        compiler_params=params(12),
        cost_estimate=cost(0.2),
        name="rim_rows",
    )(
        weight_near, bias_near, own_part, first_halo, second_halo, dense, cot_rim, partial, sums,
    )
    mark = shape(8, 128, dtype=jnp.float32)
    activated, rim_spread, first_spill, second_spill, first_mark = pl.pallas_call(
        rim_back_kernel,
        out_shape=(
            shape(rows, width),
            shape(4 * BAND, width, block_rows, dtype=jnp.float32),
            shape(rim, width),
            shape(rim, width),
            mark,
        ),
        in_specs=[vmem] * 4 + [hbm],
        out_specs=(hbm,) + (vmem,) * 4,
        scratch_shapes=[
            pltpu.VMEM((2 * rim, width), jnp.bfloat16),
            pltpu.SemaphoreType.DMA((2,)),
        ],
        input_output_aliases={4: 0},
        compiler_params=params(12),
        cost_estimate=cost(0.2),
        name="rim_rows_back",
    )(weight_near, dense, grad_rim, act_rim, activated)
    first_part = swap(first_spill, [1] * count)
    second_part = with_next(second_spill, count, False)
    grad_whole, edges, second_mark = pl.pallas_call(
        inner_back_kernel,
        out_shape=(shape(rows, width), shape(2 * rim, width, dtype=jnp.float32), mark),
        in_specs=[anywhere] + [vmem] * 4,
        out_specs=(hbm, vmem, vmem),
        scratch_shapes=[
            place_scratch,
            pltpu.VMEM((blocks + 1, width, block_rows), jnp.float32),
            pltpu.VMEM((inner, width), jnp.bfloat16),
            pltpu.SemaphoreType.DMA((2,)),
        ],
        compiler_params=params(12),
        cost_estimate=cost(0.3),
        name="inner_rows_back",
    )(places, weight_near, adj_inner, grad_inner, rim_spread)
    marks = {"core": (first_mark,), "last": (second_mark, second_part)}
    own_half = sum_halves(send, keep, count, core_bit, marks)
    other_half = swap(own_half, [1 << core_bit] * count)
    norm_scale = 1.0 / math.sqrt(rows * count)
    grad_weight, grad_bias, grad_features = pl.pallas_call(
        functools.partial(last_kernel, norm_scale),
        out_shape=(
            shape(width, width, dtype=jnp.float32),
            shape(1, width, dtype=jnp.float32),
            shape(rows, width),
        ),
        in_specs=[vmem] * 5 + [hbm],
        out_specs=(hbm, hbm, hbm),
        scratch_shapes=[
            pltpu.VMEM((2 * rim, width), jnp.bfloat16),
            pltpu.VMEM((width, width), jnp.float32),
            pltpu.VMEM((1, width), jnp.float32),
            pltpu.SemaphoreType.DMA((4,)),
        ],
        input_output_aliases={5: 2},
        compiler_params=params(8),
        name="last_step",
    )(own_half, other_half, edges, first_part, second_part, grad_whole)
    return (activated, grad_features, grad_weight, grad_bias.reshape(width))


def solution(mesh):
    return jax.shard_map(
        on_device,
        mesh=mesh,
        in_specs=(
            P(AXES, None),
            P(AXES, None, None, None),
            P(AXES, None),
            P(AXES),
            P(),
            P(),
            P(AXES, None),
        ),
        out_specs=(P(AXES, None), P(AXES, None), P(), P()),
        check_vma=False,
    )
```
